32 devices in a mesh: dp: 4 (over z), seq: 8 (over y, x, core).
Axes of the slice: x: 2, y: 2, z: 4, core: 2. Of those that a mesh axis runs over, the one named last changes fastest.
Arguments:
- block_input: bfloat16 [4, 1024, 2048], P('dp', 'seq'), may hold values from -6 to 6
- cotangent: bfloat16 [4, 1024, 2048], P('dp', 'seq'), may hold values from -6 to 6
- doc_lengths: int32 [4, 4], P('dp'), may hold values from 1 to 1021, as said below
- owners: int32 [16], replicated, may hold values from 0 to 3, as said below
- master: float32 [2048, 32, 2048], P('seq', 'dp'), may hold values from -1.06066017 to 1.06066017
- first_moment: float32 [2048, 32, 2048], P('seq', 'dp'), may hold values from -256 to 256
- second_moment: float32 [2048, 32, 2048], P('seq', 'dp'), may hold values from 0 to 6144
Outputs:
- block_output: bfloat16 [4, 1024, 2048], P('dp', 'seq')
- input_grad: float32 [4, 1024, 2048], P('dp', 'seq')
- owned_grads: float32 [2048, 32, 2048], P('seq', 'dp')
- new_first: float32 [2048, 32, 2048], P('seq', 'dp')
- new_second: float32 [2048, 32, 2048], P('seq', 'dp')
- new_master: float32 [2048, 32, 2048], P('seq', 'dp')
The draws below stay inside these ranges and needn't reach their ends.
Inputs may be any that keep to these rules, and one draw needn't show every extreme that they name: `owners`: no index of dp holds more than 8 units, and in every draw some index holds exactly 8. `doc_lengths`: each row holds 4 document lengths, each at least 1, that fill the 1024 positions of its sequence in order; in every draw some document has exactly 1021 positions.
All inputs are finite; a program needn't handle non-finite values.
Results may differ from the reference program's by a relative error of at most 0.012.
Values may be sent and summed in bfloat16 or wider, within the bound.
A program may use at most 704 MiB of HBM per device.

```python
import math
import jax
import jax.numpy as jnp
from jax import lax

D = 2048
H = 16
HD = 128
FF = 8192
SHARD_LEN = 128
SEQ_DEV = 1
NDOC = 4
STEP = 5
UNITS = 16
CAP = 8
SLOTS = 32
SEQ_LEN = 1024
SEQS = 4
TOKENS = 4096
N_DP = 4


def owner_table(key):
    key = jax.random.fold_in(key, 7)
    first_key, second_key, third_key = jax.random.split(key, 3)
    favored = jax.random.randint(first_key, (), 0, N_DP)
    shuffled = jax.random.permutation(second_key, SLOTS)
    slot_owner = jnp.arange(SLOTS, dtype=jnp.int32) // CAP
    score_rank = shuffled + jnp.where(slot_owner == favored, 0, SLOTS)
    picked = jnp.argsort(score_rank)[:UNITS]
    mixing = jax.random.permutation(third_key, UNITS)
    return slot_owner[picked][mixing].astype(jnp.int32)


def slot_scales(owners):
    unit_order = jnp.arange(UNITS, dtype=jnp.int32)
    matching = owners[:, None] == owners[None, :]
    before = unit_order[None, :] < unit_order[:, None]
    places = jnp.sum(jnp.where(matching & before, 1, 0), axis=1)
    unit_slot = owners * CAP + places
    slot_match = unit_slot[None, :] == jnp.arange(SLOTS, dtype=jnp.int32)[:, None]
    unit_of = jnp.sum(jnp.where(slot_match, unit_order[None, :] + 1, 0), axis=1) - 1
    ff_blocks = FF // D
    weight_std = jnp.where(unit_of < 3, D ** (-0.5), jnp.where(unit_of == 3, 8.0 * D ** (-0.5), jnp.where(unit_of < 4 + 2 * ff_blocks, D ** (-0.5), FF ** (-0.5))))
    grad_size = jnp.where(unit_of < 3, 0.5, jnp.where(unit_of == 3, 0.15, jnp.where(unit_of < 4 + 2 * ff_blocks, 0.3, 0.6)))
    weight_std = jnp.where(unit_of < 0, D ** (-0.5), weight_std)
    grad_size = jnp.where(unit_of < 0, 0.3, grad_size) * math.sqrt(TOKENS)
    return (weight_std.astype(jnp.float32), grad_size.astype(jnp.float32))


def draw_owners(key, part):
    return owner_table(key)


def draw_master(key, part):
    owners = owner_table(key)
    weight_std, grad_size = slot_scales(owners)
    key = jax.random.fold_in(key, 21)
    base = jnp.clip(jax.random.normal(key, (D, SLOTS, D), jnp.float32), -6.0, 6.0)
    return base * weight_std[None, :, None]


def draw_first_moment(key, part):
    owners = owner_table(key)
    weight_std, grad_size = slot_scales(owners)
    key = jax.random.fold_in(key, 22)
    base = jnp.clip(jax.random.normal(key, (D, SLOTS, D), jnp.float32), -6.0, 6.0)
    return base * grad_size[None, :, None]


def draw_second_moment(key, part):
    owners = owner_table(key)
    weight_std, grad_size = slot_scales(owners)
    key = jax.random.fold_in(key, 23)
    factor = jnp.exp(jax.random.uniform(key, (D, SLOTS, D), jnp.float32, 0.0, math.log(4.0)))
    return factor * (grad_size * grad_size)[None, :, None]


def draw_doc_lengths(key, part):
    key = jax.random.fold_in(key, 33)
    key_list = jax.random.split(key, 4)
    raw_weights = jax.random.randint(key_list[0], (SEQS, NDOC), 1, 1000)
    spread_lengths = 1 + raw_weights * (SEQ_LEN - NDOC) // jnp.sum(raw_weights, axis=1, keepdims=True)
    spread_lengths = spread_lengths.at[:, NDOC - 1].add(SEQ_LEN - jnp.sum(spread_lengths, axis=1))
    picked_seq = jax.random.randint(key_list[1], (N_DP,), 0, SEQ_DEV)
    row_ids = jnp.arange(SEQS, dtype=jnp.int32)
    is_long = row_ids % SEQ_DEV == picked_seq[row_ids // SEQ_DEV]
    is_longest = row_ids == picked_seq[0]
    head_len = jax.random.randint(key_list[2], (SEQS, 1), 1, SHARD_LEN // 2 + 1)
    tail_len = jax.random.randint(key_list[3], (SEQS, NDOC - 2), 1, max(1, SHARD_LEN // (2 * NDOC)) + 1)
    head_len = jnp.where(is_longest[:, None], 1, head_len)
    tail_len = jnp.where(is_longest[:, None], 1, tail_len)
    long_len = SEQ_LEN - head_len - jnp.sum(tail_len, axis=1, keepdims=True)
    spanning = jnp.concatenate([head_len, long_len, tail_len], axis=1)
    return jnp.where(is_long[:, None], spanning, spread_lengths).astype(jnp.int32)


def steps_of(key, shape, shards, smallest, largest):
    def one(dim, parts):
        steps = jax.random.uniform(jax.random.fold_in(jax.random.fold_in(key, 6), dim), (parts,), jnp.float32, smallest / len(shards), largest / len(shards))
        return jnp.repeat(jnp.exp(steps), shape[dim] // parts).reshape((-1,) + (1,) * (len(shape) - dim - 1))

    gain = one(*shards[0])
    for cut in shards[1:]:
        gain = gain * one(*cut)
    return gain


def scatter_about(key, dims, scale, reach, shards=(), kind=jnp.bfloat16):
    loudness = steps_of(key, dims, shards, -0.22, 0.18) if shards else 1.0
    drawn = jax.random.normal(key, dims, jnp.float32) * scale * loudness
    return jnp.minimum(jnp.maximum(drawn, -reach), reach).astype(kind)


def setup_inputs(seed: int = 0) -> dict:
    seeds = jax.random.split(jax.random.key(seed), 8)
    return {
        "block_input": scatter_about(seeds[0], (SEQS, SEQ_LEN, D), 1.0, 6.0, ((0, 4), (1, 8))),
        "cotangent": scatter_about(seeds[1], (SEQS, SEQ_LEN, D), 1.0, 6.0, ((0, 4), (1, 8))),
        "doc_lengths": draw_doc_lengths(jax.random.fold_in(seeds[7], 71), 0),
        "owners": draw_owners(jax.random.fold_in(seeds[7], 71), 0),
        "master": draw_master(jax.random.fold_in(seeds[7], 71), 0),
        "first_moment": draw_first_moment(jax.random.fold_in(seeds[7], 71), 0),
        "second_moment": draw_second_moment(jax.random.fold_in(seeds[7], 71), 0),
    }


@jax.custom_vjp
def low(v):
    return lax.optimization_barrier(v.astype(jnp.bfloat16)).astype(jnp.float32)

@jax.custom_vjp
def low_back(v):
    return v

def low_keep(v):
    return (low(v), None)

def low_pass(kept, grad):
    return (grad,)

def back_keep(v):
    return (v, None)

def back_low(kept, grad):
    return (low(grad),)
low.defvjp(low_keep, low_pass)
low_back.defvjp(back_keep, back_low)
highest = lax.Precision.HIGHEST
norm_eps = 1e-05
rope_base = 10000.0
beta_one = 0.5
beta_two = 0.5
learn_rate = 0.01
decay_rate = 0.1
adam_eps = 1e-08
masked_score = -1000000000.0

def unit_slots(owners, per_owner):
    unit_count = owners.shape[0]
    unit_order = jnp.arange(unit_count, dtype=jnp.int32)
    matching = owners[:, None] == owners[None, :]
    before = unit_order[None, :] < unit_order[:, None]
    places = lax.optimization_barrier(jnp.sum(jnp.where(matching & before, 1, 0), axis=1)).astype(jnp.int32)
    return (owners * per_owner + places).astype(jnp.int32)

def layer_norm(values):
    center = values - lax.optimization_barrier(jnp.mean(values, axis=-1, keepdims=True))
    spread = lax.optimization_barrier(jnp.mean(center * center, axis=-1, keepdims=True))
    return center * lax.rsqrt(spread + norm_eps)

def rope_tables(positions, head_dim):
    half_dim = head_dim // 2
    frequency = jnp.power(rope_base, -(jnp.arange(half_dim, dtype=jnp.float32) * 2.0) / head_dim)
    angles = positions[:, None] * frequency[None, :]
    cosine_half = jnp.cos(angles)
    sine_half = jnp.sin(angles)
    return (jnp.concatenate([cosine_half, cosine_half], axis=-1), jnp.concatenate([sine_half, sine_half], axis=-1))

def rotate(values, cosine, sine):
    half_dim = values.shape[-1] // 2
    turned = jnp.concatenate([-values[..., half_dim:], values[..., :half_dim]], axis=-1)
    return values * cosine + turned * sine

def head_attention(queries, key_rows, value_rows, allowed):
    scores = low_back(jnp.dot(queries, key_rows.T, precision=highest)) * HD ** (-0.5)
    scores = jnp.where(allowed, scores, masked_score)
    row_peak = lax.optimization_barrier(jnp.max(scores, axis=-1, keepdims=True))
    raised = jnp.exp(scores - row_peak)
    probability = raised / lax.optimization_barrier(jnp.sum(raised, axis=-1, keepdims=True))
    return jnp.dot(low(probability), value_rows, precision=highest)

def forward(tokens, unit_weights, allowed, cosine_table, sine_table):
    rounded = low(unit_weights)
    ff_blocks = FF // D
    normed = low(layer_norm(tokens))
    qkv_proj = low_back(jnp.dot(normed, rounded[:, 0:3, :].reshape(D, 3 * D), precision=highest))
    qkv_proj = qkv_proj.reshape(-1, 3, H, HD)
    queries = low(rotate(qkv_proj[:, 0], cosine_table, sine_table))
    key_rows = low(rotate(qkv_proj[:, 1], cosine_table, sine_table))
    value_rows = low(qkv_proj[:, 2])

    def one_head(triple):
        return head_attention(triple[0], triple[1], triple[2], allowed)
    attended = lax.map(jax.checkpoint(one_head), (jnp.moveaxis(queries, 1, 0), jnp.moveaxis(key_rows, 1, 0), jnp.moveaxis(value_rows, 1, 0)))
    merged = jnp.moveaxis(attended, 0, 1).reshape(-1, D)
    merged = low(low_back(merged))
    attn_out = low_back(jnp.dot(merged, rounded[:, 3, :], precision=highest))
    residual = tokens + attn_out
    normed_two = low(layer_norm(residual))
    up_proj = low_back(jnp.dot(normed_two, rounded[:, 4:4 + ff_blocks, :].reshape(D, FF), precision=highest))
    gate_proj = low_back(jnp.dot(normed_two, rounded[:, 4 + ff_blocks:4 + 2 * ff_blocks, :].reshape(D, FF), precision=highest))
    hidden = low(jax.nn.silu(gate_proj) * up_proj)
    down_full = jnp.moveaxis(rounded[:, 4 + 2 * ff_blocks:, :], 1, 0).reshape(FF, D)
    return residual + jnp.dot(hidden, down_full, precision=highest)

def reference(block_input, cotangent, doc_lengths, owners, master, first_moment, second_moment):
    slot_count = master.shape[1]
    per_owner = slot_count // N_DP
    unit_slot = unit_slots(owners, per_owner)
    unit_weights = jnp.take(master, unit_slot, axis=1)
    positions = jnp.arange(SEQ_LEN, dtype=jnp.int32)
    cosine_table, sine_table = rope_tables(positions.astype(jnp.float32), HD)
    cosine_table = cosine_table[:, None, :]
    sine_table = sine_table[:, None, :]

    def one_sequence(grad_sum, inputs_now):
        tokens, upstream, lengths = inputs_now
        doc_ends = jnp.cumsum(lengths)
        document = lax.optimization_barrier(jnp.sum((positions[:, None] >= doc_ends[None, :]).astype(jnp.int32), axis=1))
        allowed = (document[:, None] == document[None, :]) & (positions[None, :] <= positions[:, None])

        def apply_block(token_rows, weight_rows):
            return forward(token_rows, weight_rows, allowed, cosine_table, sine_table)
        result, pullback = jax.vjp(apply_block, tokens.astype(jnp.float32), unit_weights)
        token_grad, weight_grad = pullback(upstream.astype(jnp.float32))
        return (grad_sum + weight_grad, (result.astype(jnp.bfloat16), token_grad))
    grad_sum, (block_output, input_grad) = lax.scan(one_sequence, jnp.zeros(unit_weights.shape, jnp.float32), (block_input, cotangent, doc_lengths))
    slot_order = jnp.arange(slot_count, dtype=jnp.int32)
    occupied = jnp.any(unit_slot[None, :] == slot_order[:, None], axis=1)
    keep_slot = occupied.astype(jnp.float32)[None, :, None]
    owned_grads = jnp.zeros(master.shape, jnp.float32).at[:, unit_slot, :].set(grad_sum)
    new_first = (beta_one * first_moment + (1.0 - beta_one) * owned_grads) * keep_slot
    new_second = (beta_two * second_moment + (1.0 - beta_two) * owned_grads * owned_grads) * keep_slot
    fixed_first = new_first / (1.0 - beta_one ** STEP)
    fixed_second = new_second / (1.0 - beta_two ** STEP)
    new_master = (master - learn_rate * (fixed_first / (jnp.sqrt(fixed_second) + adam_eps) + decay_rate * master)) * keep_slot
    return (block_output, input_grad, owned_grads, new_first, new_second, new_master)
```

```python
import jax
import jax.numpy as jnp
from jax import lax
from jax.sharding import PartitionSpec as P

D = 2048
H = 16
HD = 128
FF = 8192
STEP = 5


norm_eps = 1e-05
rope_base = 10000.0
beta_one = 0.5
beta_two = 0.5
learn_rate = 0.01
decay_rate = 0.1
adam_eps = 1e-08
masked_score = -1000000000.0


def unit_slots(owners, per_owner):
    unit_count = owners.shape[0]
    unit_order = jnp.arange(unit_count, dtype=jnp.int32)
    matching = owners[:, None] == owners[None, :]
    before = unit_order[None, :] < unit_order[:, None]
    places = jnp.sum(jnp.where(matching & before, 1, 0), axis=1).astype(jnp.int32)
    return owners * per_owner + places


def norm_parts(values):
    center = values - jnp.mean(values, axis=-1, keepdims=True)
    spread = jnp.mean(center * center, axis=-1, keepdims=True)
    scale_inv = lax.rsqrt(spread + norm_eps)
    return (center * scale_inv, scale_inv)


def norm_back(normed, scale_inv, upstream):
    upstream_mean = jnp.mean(upstream, axis=-1, keepdims=True)
    cross_mean = jnp.mean(upstream * normed, axis=-1, keepdims=True)
    return scale_inv * (upstream - upstream_mean - normed * cross_mean)


def rope_tables(positions, head_dim):
    half_dim = head_dim // 2
    frequency = jnp.power(rope_base, -(jnp.arange(half_dim, dtype=jnp.float32) * 2.0) / head_dim)
    angles = positions[:, None] * frequency[None, :]
    cosine_half = jnp.cos(angles)
    sine_half = jnp.sin(angles)
    return (
        jnp.concatenate([cosine_half, cosine_half], axis=-1),
        jnp.concatenate([sine_half, sine_half], axis=-1),
    )


def rotate(values, cosine, sine):
    half_dim = values.shape[-1] // 2
    turned = jnp.concatenate([-values[..., half_dim:], values[..., :half_dim]], axis=-1)
    return values * cosine + turned * sine


def rotate_back(grads, cosine, sine):
    half_dim = grads.shape[-1] // 2
    scaled = grads * sine
    turned = jnp.concatenate([scaled[..., half_dim:], -scaled[..., :half_dim]], axis=-1)
    return grads * cosine + turned


def local(block_input, cotangent, doc_lengths, owners, master, first_moment, second_moment):
    n_seq = lax.axis_size("seq")
    n_dp = lax.axis_size("dp")
    seq_index = lax.axis_index("seq")
    dp_index = lax.axis_index("dp")
    core = seq_index % 2
    _, shard_len, width = block_input.shape
    rows = master.shape[0]
    per_owner = master.shape[1]
    chips = n_seq // 2
    sub = rows // n_dp
    wide = width // n_dp
    half = chips * sub
    heads = H // n_seq
    head_cols = heads * HD
    seq_len = shard_len * n_seq
    ff_blocks = FF // D
    first_slots = min(4, per_owner)
    unit_count = owners.shape[0]
    bf = jnp.bfloat16
    f32 = jnp.float32
    score_scale = float(HD) ** (-0.5)

    unit_slot = unit_slots(owners, per_owner)
    place = unit_slot - owners * per_owner
    all_slots = jnp.arange(n_dp * per_owner, dtype=jnp.int32)
    match = unit_slot[None, :] == all_slots[:, None]
    slot_unit = jnp.sum(
        jnp.where(match, jnp.arange(unit_count, dtype=jnp.int32)[None, :] + 1, 0), axis=1
    ) - 1
    slot_unit = slot_unit.reshape(n_dp, per_owner)
    own_units = lax.dynamic_index_in_dim(slot_unit, dp_index, 0, keepdims=False)
    is_col = (own_units >= 4) & (own_units < 4 + 2 * ff_blocks)
    chip_groups = [[2 * k + c for k in range(chips)] for c in range(2)]

    def shift_pairs(k):
        return [(d, (d + k) % n_dp) for d in range(n_dp)]

    sibling = [(i, i ^ 1) for i in range(n_seq)]

    def pack(slots, col_flags):
        count = slots.shape[1]
        low = slots.astype(bf)
        col = low.reshape(rows, count, chips, 2, n_dp, sub).transpose(4, 1, 0, 3, 2, 5)
        col = col.reshape(n_dp, count, rows, wide)
        row = low.reshape(n_dp, sub, count, n_dp, wide).transpose(0, 2, 3, 1, 4)
        row = row.reshape(n_dp, count, rows, wide)
        return jnp.where(col_flags[None, :, None, None], col, row)

    def exchange(packed):
        parts = [lax.dynamic_index_in_dim(packed, dp_index, 0, keepdims=False)]
        for k in range(1, n_dp):
            send = lax.dynamic_index_in_dim(packed, (dp_index + k) % n_dp, 0, keepdims=False)
            parts.append(lax.ppermute(send, "dp", shift_pairs(k)))
        return parts

    first_parts = exchange(pack(master[:, :first_slots], is_col[:first_slots]))
    shift_of = (dp_index - owners) % n_dp
    first_table = jnp.stack(first_parts).reshape(n_dp * first_slots, rows, wide)
    att = jnp.take(first_table, (shift_of * first_slots + place)[:4], axis=0)
    att_rows = att[:3].reshape(3, n_dp, sub, n_seq // n_dp, head_cols)
    att_rows = att_rows.transpose(1, 3, 0, 2, 4).reshape(n_seq, 3, sub, head_cols)
    att_rows = lax.all_to_all(att_rows, "seq", 0, 0)
    att_all = lax.all_gather(
        jnp.concatenate(
            [att_rows.reshape(n_seq * 3 * sub, head_cols), att[3].reshape(-1, head_cols)], axis=0
        ),
        "dp",
        axis=0,
    )
    cut = n_seq * 3 * sub
    qkv_weight = att_all[:, :cut].reshape(n_dp, n_seq, 3, sub, head_cols)
    qkv_weight = qkv_weight.transpose(1, 0, 3, 2, 4).reshape(width, 3 * head_cols)
    out_weight = att_all[:, cut:].reshape(n_dp, n_dp, sub, wide).transpose(0, 2, 1, 3)
    out_weight = out_weight.reshape(rows, width)

    tokens = block_input.astype(f32).reshape(shard_len, width)
    normed_one, inv_one = norm_parts(tokens)
    normed_one_all = lax.all_gather(normed_one.astype(bf), "seq", axis=0, tiled=True)
    qkv_proj = jnp.dot(normed_one_all, qkv_weight, preferred_element_type=f32)
    qkv_proj = qkv_proj.reshape(seq_len, 3, heads, HD)
    positions = jnp.arange(seq_len, dtype=jnp.int32)
    cosine, sine = rope_tables(positions.astype(f32), HD)
    cosine = cosine[:, None, :]
    sine = sine[:, None, :]
    queries = rotate(qkv_proj[:, 0], cosine, sine).astype(bf)
    keys = rotate(qkv_proj[:, 1], cosine, sine).astype(bf)
    values = qkv_proj[:, 2].astype(bf)
    doc_ends = jnp.cumsum(doc_lengths[0])
    doc = jnp.sum((positions[:, None] >= doc_ends[None, :]).astype(jnp.int32), axis=1)
    allowed = (doc[:, None] == doc[None, :]) & (positions[None, :] <= positions[:, None])
    scores = jnp.einsum("qhd,khd->hqk", queries, keys, preferred_element_type=f32) * score_scale
    scores = jnp.where(allowed[None], scores, masked_score)
    peak = jnp.max(scores, axis=-1, keepdims=True)
    raised = jnp.exp(scores - peak)
    prob = raised / jnp.sum(raised, axis=-1, keepdims=True)
    prob_low = prob.astype(bf)
    attended = jnp.einsum("hqk,khd->qhd", prob_low, values, preferred_element_type=f32)
    attended_low = attended.reshape(seq_len, head_cols).astype(bf)
    attn_part = jnp.dot(attended_low, out_weight, preferred_element_type=f32).astype(bf)
    attn_out = lax.psum_scatter(attn_part, "seq", scatter_dimension=0, tiled=True)
    residual = tokens + attn_out.astype(f32)
    normed_two, inv_two = norm_parts(residual)

    if per_owner > first_slots:
        second = exchange(pack(master[:, first_slots:], is_col[first_slots:]))
        second_slots = per_owner - first_slots
        table = jnp.concatenate(
            [first_table, jnp.stack(second).reshape(n_dp * second_slots, rows, wide)], axis=0
        )
        index = jnp.where(
            place < first_slots,
            shift_of * first_slots + place,
            n_dp * first_slots + shift_of * second_slots + place - first_slots,
        )
    else:
        table = first_table
        index = shift_of * first_slots + place
    ff = jnp.take(table, index[4:], axis=0)
    ug = ff[: 2 * ff_blocks]
    mine = lax.dynamic_slice_in_dim(ug, core * half, half, axis=2)
    given = lax.dynamic_slice_in_dim(ug, (1 - core) * half, half, axis=2)
    got = lax.ppermute(given, "seq", sibling)
    ug = jnp.where(
        core == 0, jnp.concatenate([mine, got], axis=1), jnp.concatenate([got, mine], axis=1)
    )
    up_weight = lax.all_gather(
        ug[:ff_blocks], "seq", axis=1, tiled=True, axis_index_groups=chip_groups
    )
    gate_weight = lax.all_gather(
        ug[ff_blocks:], "seq", axis=1, tiled=True, axis_index_groups=chip_groups
    )
    down = ff[2 * ff_blocks :].reshape(ff_blocks, n_dp, sub, wide).transpose(0, 2, 1, 3)
    down_weight = lax.all_gather(
        down.reshape(ff_blocks, sub, width), "seq", axis=1, tiled=True, axis_index_groups=chip_groups
    )

    def gather_tokens(part):
        every = lax.all_gather(part, "dp", axis=0, tiled=True)
        other = lax.ppermute(every, "seq", sibling)
        return jnp.where(
            core == 0,
            jnp.concatenate([every, other], axis=0),
            jnp.concatenate([other, every], axis=0),
        )

    def scatter_tokens(part):
        count = n_dp * shard_len
        kept = lax.dynamic_slice_in_dim(part, core * count, count, axis=0)
        sent = lax.dynamic_slice_in_dim(part, (1 - core) * count, count, axis=0)
        got = lax.ppermute(sent.astype(bf), "seq", sibling)
        total = (kept + got.astype(f32)).astype(bf)
        return lax.psum_scatter(total, "dp", scatter_dimension=0, tiled=True).astype(f32)

    upstream = cotangent.reshape(shard_len, width)
    upstream_all = gather_tokens(upstream)
    normed_two_all = gather_tokens(normed_two.astype(bf))
    up_proj = jnp.einsum("tr,jrc->tjc", normed_two_all, up_weight, preferred_element_type=f32)
    gate_proj = jnp.einsum("tr,jrc->tjc", normed_two_all, gate_weight, preferred_element_type=f32)
    gate_sig = jax.nn.sigmoid(gate_proj)
    silu_value = gate_proj * gate_sig
    hidden_low = (silu_value * up_proj).astype(bf)
    ff_out = scatter_tokens(
        jnp.einsum("tjh,jhc->tc", hidden_low, down_weight, preferred_element_type=f32)
    )
    block_output = (residual + ff_out).astype(bf).reshape(block_input.shape)
    hidden_grad = jnp.einsum("tc,jhc->tjh", upstream_all, down_weight, preferred_element_type=f32)
    up_grad_low = (hidden_grad * silu_value).astype(bf)
    gate_grad_low = (
        hidden_grad * up_proj * (gate_sig + gate_proj * gate_sig * (1.0 - gate_sig))
    ).astype(bf)

    def chip_sum(part):
        return lax.psum_scatter(
            part.astype(bf),
            "seq",
            scatter_dimension=1,
            tiled=True,
            axis_index_groups=chip_groups,
        )

    down_grad = chip_sum(
        jnp.einsum("tjh,tc->jhc", hidden_low, upstream_all, preferred_element_type=f32)
    )
    up_grad = chip_sum(
        jnp.einsum("tr,tjc->jrc", normed_two_all, up_grad_low, preferred_element_type=f32)
    )
    gate_grad = chip_sum(
        jnp.einsum("tr,tjc->jrc", normed_two_all, gate_grad_low, preferred_element_type=f32)
    )
    norm_two_grad = jnp.einsum("tjc,jrc->tr", up_grad_low, up_weight, preferred_element_type=f32)
    norm_two_grad = norm_two_grad + jnp.einsum(
        "tjc,jrc->tr", gate_grad_low, gate_weight, preferred_element_type=f32
    )
    norm_two_grad = scatter_tokens(norm_two_grad)
    residual_grad = upstream.astype(f32) + norm_back(normed_two, inv_two, norm_two_grad)
    residual_grad_all = lax.all_gather(residual_grad.astype(bf), "seq", axis=0, tiled=True)

    attended_grad = jnp.einsum(
        "tc,rc->tr", residual_grad_all, out_weight, preferred_element_type=f32
    )
    attended_grad = attended_grad.astype(bf).reshape(seq_len, heads, HD)
    value_grad = jnp.einsum("hqk,qhd->khd", prob_low, attended_grad, preferred_element_type=f32)
    prob_grad = jnp.einsum("qhd,khd->hqk", attended_grad, values, preferred_element_type=f32)
    inner_sum = jnp.sum(prob * prob_grad, axis=-1, keepdims=True)
    score_grad = (prob * (prob_grad - inner_sum) * score_scale).astype(bf)
    query_grad = jnp.einsum("hqk,khd->qhd", score_grad, keys, preferred_element_type=f32)
    key_grad = jnp.einsum("hqk,qhd->khd", score_grad, queries, preferred_element_type=f32)
    qkv_grad = jnp.stack(
        [
            rotate_back(query_grad, cosine, sine),
            rotate_back(key_grad, cosine, sine),
            value_grad,
        ],
        axis=1,
    )
    qkv_grad_low = qkv_grad.astype(bf).reshape(seq_len, 3 * head_cols)
    norm_one_part = jnp.einsum("tf,rf->tr", qkv_grad_low, qkv_weight, preferred_element_type=f32)
    norm_one_grad = lax.psum_scatter(
        norm_one_part.astype(bf), "seq", scatter_dimension=0, tiled=True
    ).astype(f32)
    input_grad = (residual_grad + norm_back(normed_one, inv_one, norm_one_grad)).reshape(
        block_input.shape
    )

    qkv_wgrad = jnp.einsum(
        "tr,tf->rf", normed_one_all, qkv_grad_low, preferred_element_type=f32
    ).astype(bf)
    qkv_wgrad = qkv_wgrad.reshape(n_seq, n_dp, sub, 3, head_cols).transpose(1, 0, 3, 2, 4)
    out_wgrad = jnp.einsum(
        "tr,tc->rc", attended_low, residual_grad_all, preferred_element_type=f32
    ).astype(bf)
    out_wgrad = out_wgrad.reshape(n_dp, sub, n_dp, wide).transpose(0, 2, 1, 3)
    att_wgrad = lax.psum_scatter(
        jnp.concatenate(
            [
                qkv_wgrad.reshape(n_dp, cut, head_cols),
                out_wgrad.reshape(n_dp, -1, head_cols),
            ],
            axis=1,
        ),
        "dp",
        scatter_dimension=0,
        tiled=True,
    ).reshape(-1, head_cols)
    qkv_piece = att_wgrad[:cut].reshape(n_seq, 3, sub, head_cols)
    qkv_piece = lax.all_to_all(qkv_piece, "seq", 0, 0)
    qkv_piece = qkv_piece.reshape(n_dp, n_seq // n_dp, 3, sub, head_cols).transpose(2, 0, 3, 1, 4)
    qkv_piece = qkv_piece.reshape(3, rows, wide)
    out_piece = att_wgrad[cut:].reshape(1, rows, wide)

    ug_grad = jnp.concatenate([up_grad, gate_grad], axis=0)
    kept = lax.dynamic_slice_in_dim(ug_grad, core * rows, rows, axis=1)
    sent = lax.dynamic_slice_in_dim(ug_grad, (1 - core) * rows, rows, axis=1)
    got = lax.ppermute(sent, "seq", sibling)
    ug_piece = jnp.where(
        core == 0, jnp.concatenate([kept, got], axis=2), jnp.concatenate([got, kept], axis=2)
    )
    down_piece = down_grad.reshape(ff_blocks, sub, n_dp, wide).transpose(0, 2, 1, 3)
    down_piece = down_piece.reshape(ff_blocks, rows, wide)
    ff_pieces = jnp.concatenate([ug_piece, down_piece], axis=0)

    def give_back(pieces, low_slot, high_slot, skipped):
        parts = []
        for k in range(n_dp):
            target = (dp_index + k) % n_dp
            units = lax.dynamic_index_in_dim(slot_unit, target, 0, keepdims=False)
            units = jnp.maximum(units[low_slot:high_slot] - skipped, 0)
            send = jnp.take(pieces, units, axis=0)
            parts.append(send if k == 0 else lax.ppermute(send, "dp", shift_pairs(k)))
        order = (dp_index - jnp.arange(n_dp, dtype=jnp.int32)) % n_dp
        return jnp.take(jnp.stack(parts), order, axis=0)

    def unpack(parts, col_flags):
        count = parts.shape[1]
        col = parts.reshape(n_dp, count, rows, 2, chips, sub).transpose(2, 1, 4, 3, 0, 5)
        col = col.reshape(rows, count, width)
        row = parts.reshape(n_dp, count, n_dp, sub, wide).transpose(0, 3, 1, 2, 4)
        row = row.reshape(rows, count, width)
        return jnp.where(col_flags[None, :, None], col, row)

    grads = []
    if per_owner > first_slots:
        late = give_back(ff_pieces, first_slots, per_owner, 4)
        grads.append(unpack(late, is_col[first_slots:]))
    every_piece = jnp.concatenate([qkv_piece, out_piece, ff_pieces], axis=0)
    early = give_back(every_piece, 0, first_slots, 0)
    grads.insert(0, unpack(early, is_col[:first_slots]))
    keep_slot = (own_units >= 0)[None, :, None]
    owned_grads = jnp.where(keep_slot, jnp.concatenate(grads, axis=1).astype(f32), 0.0)
    keep_slot = keep_slot.astype(f32)
    new_first = (beta_one * first_moment + (1.0 - beta_one) * owned_grads) * keep_slot
    new_second = (
        beta_two * second_moment + (1.0 - beta_two) * owned_grads * owned_grads
    ) * keep_slot
    fixed_first = new_first / (1.0 - beta_one**STEP)
    fixed_second = new_second / (1.0 - beta_two**STEP)
    new_master = (
        master
        - learn_rate * (fixed_first / (jnp.sqrt(fixed_second) + adam_eps) + decay_rate * master)
    ) * keep_slot
    return (block_output, input_grad, owned_grads, new_first, new_second, new_master)


def solution(mesh):
    placed = (
        P("dp", "seq", None),
        P("dp", "seq", None),
        P("dp", None),
        P(),
        P("seq", "dp", None),
        P("seq", "dp", None),
        P("seq", "dp", None),
    )
    return jax.shard_map(
        local,
        mesh=mesh,
        in_specs=placed,
        out_specs=(
            P("dp", "seq", None),
            P("dp", "seq", None),
            P("seq", "dp", None),
            P("seq", "dp", None),
            P("seq", "dp", None),
            P("seq", "dp", None),
        ),
        check_vma=False,
    )
```

```python
import functools

import jax
import jax.numpy as jnp
from jax import lax
from jax.experimental import pallas as pl
from jax.experimental.pallas import tpu as pltpu
from jax.sharding import PartitionSpec as P

D = 2048
H = 16
HD = 128
FF = 8192
STEP = 5
bf = jnp.bfloat16
f32 = jnp.float32
MESH = pl.DeviceIdType.MESH


norm_eps = 1e-05
rope_base = 10000.0
beta_one = 0.5
beta_two = 0.5
learn_rate = 0.01
decay_rate = 0.1
adam_eps = 1e-08
masked_score = -1000000000.0


def unit_slots(owners, per_owner):
    unit_count = owners.shape[0]
    unit_order = jnp.arange(unit_count, dtype=jnp.int32)
    matching = owners[:, None] == owners[None, :]
    before = unit_order[None, :] < unit_order[:, None]
    places = jnp.sum(jnp.where(matching & before, 1, 0), axis=1).astype(jnp.int32)
    return owners * per_owner + places


def norm_parts(values):
    center = values - jnp.mean(values, axis=-1, keepdims=True)
    spread = jnp.mean(center * center, axis=-1, keepdims=True)
    scale_inv = lax.rsqrt(spread + norm_eps)
    return (center * scale_inv, scale_inv)


def norm_back(normed, scale_inv, upstream):
    upstream_mean = jnp.mean(upstream, axis=-1, keepdims=True)
    cross_mean = jnp.mean(upstream * normed, axis=-1, keepdims=True)
    return scale_inv * (upstream - upstream_mean - normed * cross_mean)


def rope_tables(positions, head_dim):
    half_dim = head_dim // 2
    frequency = jnp.power(rope_base, -(jnp.arange(half_dim, dtype=jnp.float32) * 2.0) / head_dim)
    angles = positions[:, None] * frequency[None, :]
    cosine_half = jnp.cos(angles)
    sine_half = jnp.sin(angles)
    return (
        jnp.concatenate([cosine_half, cosine_half], axis=-1),
        jnp.concatenate([sine_half, sine_half], axis=-1),
    )


def rotate(values, cosine, sine):
    half_dim = values.shape[-1] // 2
    turned = jnp.concatenate([-values[..., half_dim:], values[..., :half_dim]], axis=-1)
    return values * cosine + turned * sine


def rotate_back(grads, cosine, sine):
    half_dim = grads.shape[-1] // 2
    scaled = grads * sine
    turned = jnp.concatenate([scaled[..., half_dim:], -scaled[..., :half_dim]], axis=-1)
    return grads * cosine + turned


def pack_kernel(n_dp, chips, first_slots, flags, m_ref, *outs):
    rb, slots, width = m_ref.shape
    rows, wide = outs[0].shape[2:]
    sub = rows // n_dp
    start = pl.program_id(0) * rb
    target = start // sub
    inner = start % sub
    for s in range(slots):
        out = outs[0] if s < first_slots else outs[1]
        t = s if s < first_slots else s - first_slots

        @pl.when(flags[s] == 1)
        def _():
            x = m_ref[:, s, :].astype(bf)
            for d in range(n_dp):
                pieces = [
                    x[:, (2 * k + c) * rows + d * sub : (2 * k + c) * rows + (d + 1) * sub]
                    for c in range(2)
                    for k in range(chips)
                ]
                out[d, t, pl.ds(pl.multiple_of(start, rb), rb), :] = jnp.concatenate(pieces, axis=1)

        @pl.when(flags[s] == 0)
        def _():
            x = m_ref[:, s, :].astype(bf)
            for g in range(n_dp):
                out[target, t, pl.ds(pl.multiple_of(g * sub + inner, rb), rb), :] = x[
                    :, g * wide : (g + 1) * wide
                ]

def pack(master, flags, n_dp, n_seq, first_slots):
    rows, slots, width = master.shape
    wide = width // n_dp
    rb = min(32, rows // n_dp)
    counts = [first_slots] + ([slots - first_slots] if slots > first_slots else [])
    return pl.pallas_call(
        functools.partial(pack_kernel, n_dp, n_seq // 2, first_slots),
        out_shape=[jax.ShapeDtypeStruct((n_dp, c, rows, wide), bf) for c in counts],
        grid_spec=pltpu.PrefetchScalarGridSpec(
            num_scalar_prefetch=1,
            grid=(rows // rb,),
            in_specs=[pl.BlockSpec((rb, slots, width), lambda i, f: (i, 0, 0))],
            out_specs=[
                pl.BlockSpec((n_dp, c, rows, wide), lambda i, f: (0, 0, 0, 0)) for c in counts
            ],
        ),
        compiler_params=pltpu.CompilerParams(vmem_limit_bytes=50 << 20),
        name="pack",
    )(flags, master)

def adam_kernel(n_dp, chips, first_slots, n_groups, kinds, *refs):
    cols = refs[:n_groups]
    rws = refs[n_groups:2*n_groups]
    m_ref, f_ref, s_ref, g_out, f_out, s_out, m_out = refs[2*n_groups:]
    rb, slots, width = m_ref.shape
    wide = width // n_dp
    rows = wide * n_dp // (2 * chips)
    sub = rows // n_dp
    half = chips * sub

    def finish(s, grad):
        g_out[:, s, :] = grad
        first = beta_one * f_ref[:, s, :] + (1.0 - beta_one) * grad
        second = beta_two * s_ref[:, s, :] + (1.0 - beta_two) * grad * grad
        f_out[:, s, :] = first
        s_out[:, s, :] = second
        fixed_first = first * (1.0 / (1.0 - beta_one**STEP))
        fixed_second = second * (1.0 / (1.0 - beta_two**STEP))
        old = m_ref[:, s, :]
        m_out[:, s, :] = old - learn_rate * (
            fixed_first / (jnp.sqrt(fixed_second) + adam_eps) + decay_rate * old
        )

    for s in range(slots):
        grp = 0 if s < first_slots else 1
        t = s if grp == 0 else s - first_slots

        @pl.when(kinds[s] == 1)
        def _():
            pieces = []
            for i in range(2 * chips):
                k, c = i // 2, i % 2
                for d in range(n_dp):
                    pieces.append(cols[grp][d, t, :, c * half + k * sub : c * half + (k + 1) * sub])
            finish(s, jnp.concatenate(pieces, axis=1).astype(f32))

        @pl.when(kinds[s] == 0)
        def _():
            pieces = [rws[grp][0, t, g, :, :] for g in range(n_dp)]
            finish(s, jnp.concatenate(pieces, axis=1).astype(f32))

        @pl.when(kinds[s] == 2)
        def _():
            zero = jnp.zeros((rb, width), f32)
            g_out[:, s, :] = zero
            f_out[:, s, :] = zero
            s_out[:, s, :] = zero
            m_out[:, s, :] = zero

def adam(kinds, grads, master, first_moment, second_moment, n_dp, n_seq, first_slots):
    rows, slots, width = master.shape
    wide = width // n_dp
    sub = rows // n_dp
    rb = min(16, sub)
    state = pl.BlockSpec((rb, slots, width), lambda i, k: (i, 0, 0))
    cols = [pl.BlockSpec((n_dp, g.shape[1], rb, wide), lambda i, k: (0, 0, i, 0)) for g in grads]
    rws = [
        pl.BlockSpec(
            (1, g.shape[1], n_dp, rb, wide),
            lambda i, k: (i * rb // sub, 0, 0, i % (sub // rb), 0),
        )
        for g in grads
    ]
    return pl.pallas_call(
        functools.partial(adam_kernel, n_dp, n_seq // 2, first_slots, len(grads)),
        out_shape=[jax.ShapeDtypeStruct(master.shape, f32)] * 4,
        grid_spec=pltpu.PrefetchScalarGridSpec(
            num_scalar_prefetch=1,
            grid=(rows // rb,),
            in_specs=cols + rws + [state] * 3,
            out_specs=[state] * 4,
        ),
        compiler_params=pltpu.CompilerParams(vmem_limit_bytes=50 << 20),
        name="adam",
    )(
        kinds,
        *grads,
        *[g.reshape(n_dp, g.shape[1], n_dp, sub, wide) for g in grads],
        master,
        first_moment,
        second_moment,
    )

ANY = pl.BlockSpec(memory_space=pl.ANY)
VMEM = pl.BlockSpec(memory_space=pltpu.VMEM)


def line_place(kind):
    seq_index = lax.axis_index("seq")
    core = lax.rem(seq_index, 2)
    if kind == "seq":
        return seq_index // 2, lax.axis_size("seq") // 2, core
    return lax.axis_index("dp"), lax.axis_size("dp"), core


def line_device(kind, position, core):
    if kind == "seq":
        return (lax.axis_index("dp"), position * 2 + core)
    return (position, lax.axis_index("seq") - lax.rem(lax.axis_index("seq"), 2) + core)


def line_block(kind, position, count, core):
    return position * 2 + core if kind == "seq" else core * count + position


def greet(devices):
    barrier = pltpu.get_barrier_semaphore()
    for device in devices:
        pl.semaphore_signal(barrier, inc=1, device_id=device, device_id_type=MESH)
    pl.semaphore_wait(barrier, len(devices))


def send(src, dst, send_sem, recv_sem, device):
    return pltpu.make_async_remote_copy(
        src_ref=src,
        dst_ref=dst,
        send_sem=send_sem,
        recv_sem=recv_sem,
        device_id=device,
        device_id_type=MESH,
    )


def gather_kernel(kind, x_ref, out_ref, own_sem, send_sem, recv_sem, pass_sem, take_sem):
    position, count, core = line_place(kind)
    peers = [lax.rem(position + k, count) for k in range(count)]
    sibling = line_device(kind, position, 1 - core)
    greet([line_device(kind, p, core) for p in peers[1:]] + [sibling])
    mine = line_block(kind, position, count, core)
    own = pltpu.make_async_copy(x_ref, out_ref.at[mine], own_sem)
    own.start()
    copies = []
    for k in range(count - 1, 0, -1):
        copy = send(
            x_ref, out_ref.at[mine], send_sem.at[k], recv_sem.at[k], line_device(kind, peers[k], core)
        )
        copy.start()
        copies.append((k, copy))
    first = send(x_ref, out_ref.at[mine], pass_sem.at[0], take_sem.at[0], sibling)
    first.start()
    passed = [first]
    for k, copy in reversed(copies):
        copy.wait_recv()
        block = out_ref.at[line_block(kind, lax.rem(position + count - k, count), count, core)]
        onward = send(block, block, pass_sem.at[k], take_sem.at[k], sibling)
        onward.start()
        passed.append(onward)
    for k, copy in copies:
        copy.wait_send()
    for onward in passed:
        onward.wait()
    own.wait()


def gather_blocks(x, kind, collective_id):
    count = lax.axis_size("seq") // 2 if kind == "seq" else lax.axis_size("dp")
    dma = pltpu.SemaphoreType.DMA
    return pl.pallas_call(
        functools.partial(gather_kernel, kind),
        out_shape=jax.ShapeDtypeStruct((2 * count,) + x.shape, x.dtype),
        in_specs=[ANY],
        out_specs=ANY,
        scratch_shapes=[dma, dma((count,)), dma((count,)), dma((count,)), dma((count,))],
        compiler_params=pltpu.CompilerParams(
            collective_id=collective_id, has_side_effects=True, vmem_limit_bytes=16 << 20
        ),
        name="gather_" + kind,
    )(x)


def sum_kernel(
    kind, x_ref, out_ref, taken, sent, arrived, pass_sem, take_sem, send_sem, recv_sem
):
    position, count, core = line_place(kind)
    peers = [lax.rem(position + k, count) for k in range(count)]
    sibling = line_device(kind, position, 1 - core)
    greet([line_device(kind, p, core) for p in peers[1:]] + [sibling])
    order = list(range(count - 1, 0, -1)) + [0]
    passed = {}
    for k in order:
        block = x_ref.at[line_block(kind, peers[k], count, 1 - core)]
        passed[k] = send(block, taken.at[k], pass_sem.at[k], take_sem.at[k], sibling)
        passed[k].start()
    copies = {}
    for k in order[:-1]:
        passed[k].wait_recv()
        own = x_ref[line_block(kind, peers[k], count, core)].astype(f32)
        sent[k] = (own + taken[k].astype(f32)).astype(sent.dtype)
        copies[k] = send(
            sent.at[k],
            arrived.at[k],
            send_sem.at[k],
            recv_sem.at[k],
            line_device(kind, peers[k], core),
        )
        copies[k].start()
    passed[0].wait_recv()
    total = x_ref[line_block(kind, position, count, core)].astype(f32) + taken[0].astype(f32)
    for k in range(1, count):
        copies[k].wait_recv()
        total = total + arrived[k].astype(f32)
    out_ref[...] = total
    for k in order:
        passed[k].wait_send()
    for k in order[:-1]:
        copies[k].wait_send()


def sum_blocks(x, kind, collective_id):
    blocks, rows, columns = x.shape
    count = blocks // 2
    dma = pltpu.SemaphoreType.DMA
    slots = pltpu.VMEM((count, rows, columns), x.dtype)
    return pl.pallas_call(
        functools.partial(sum_kernel, kind),
        out_shape=jax.ShapeDtypeStruct((rows, columns), f32),
        in_specs=[VMEM],
        out_specs=VMEM,
        scratch_shapes=[slots, slots, slots, dma((count,)), dma((count,)), dma((count,)), dma((count,))],
        compiler_params=pltpu.CompilerParams(
            collective_id=collective_id, has_side_effects=True, vmem_limit_bytes=40 << 20
        ),
        name="sum_" + kind,
    )(x)


def spread_kernel(
    qkv_ref, out_ref, qkv_all, out_all, own_sem, a_send, a_recv, z_send, z_recv, o_send, o_recv
):
    n_seq = lax.axis_size("seq")
    n_dp = lax.axis_size("dp")
    seq_index = lax.axis_index("seq")
    dp_index = lax.axis_index("dp")
    seq_peers = [lax.rem(seq_index + k, n_seq) for k in range(n_seq)]
    dp_peers = [lax.rem(dp_index + k, n_dp) for k in range(n_dp)]
    greet([(dp_index, p) for p in seq_peers[1:]] + [(p, seq_index) for p in dp_peers[1:]])
    own = [
        pltpu.make_async_copy(qkv_ref.at[seq_index], qkv_all.at[seq_index, dp_index], own_sem.at[0]),
        pltpu.make_async_copy(out_ref, out_all.at[dp_index], own_sem.at[1]),
    ]
    for copy in own:
        copy.start()
    landing = qkv_all.at[seq_index, dp_index]
    across = {}
    for k in range(1, n_seq):
        across[k] = send(
            qkv_ref.at[seq_peers[k]], landing, a_send.at[k], a_recv.at[k], (dp_index, seq_peers[k])
        )
        across[k].start()
    outs = {}
    for k in range(1, n_dp):
        outs[k] = send(
            out_ref, out_all.at[dp_index], o_send.at[k], o_recv.at[k], (dp_peers[k], seq_index)
        )
        outs[k].start()
    along = []
    for k in range(n_seq):
        source = lax.rem(seq_index + n_seq - k, n_seq)
        block = qkv_all.at[source, dp_index]
        if k == 0:
            block_src = qkv_ref.at[seq_index]
        else:
            across[k].wait_recv()
            block_src = block
        for j in range(n_dp - 1, 0, -1):
            copy = send(block_src, block, z_send.at[k, j], z_recv.at[k, j], (dp_peers[j], seq_index))
            copy.start()
            along.append(copy)
    for copy in along:
        copy.wait()
    for k in range(1, n_dp):
        outs[k].wait()
    for k in range(1, n_seq):
        across[k].wait_send()
    for copy in own:
        copy.wait()


def spread_attention(qkv, out, collective_id):
    n_seq = lax.axis_size("seq")
    n_dp = lax.axis_size("dp")
    dma = pltpu.SemaphoreType.DMA
    return pl.pallas_call(
        spread_kernel,
        out_shape=[
            jax.ShapeDtypeStruct((n_seq, n_dp) + qkv.shape[1:], qkv.dtype),
            jax.ShapeDtypeStruct((n_dp,) + out.shape, out.dtype),
        ],
        in_specs=[ANY, ANY],
        out_specs=[ANY, ANY],
        scratch_shapes=[
            dma((2,)),
            dma((n_seq,)),
            dma((n_seq,)),
            dma((n_seq, n_dp)),
            dma((n_seq, n_dp)),
            dma((n_dp,)),
            dma((n_dp,)),
        ],
        compiler_params=pltpu.CompilerParams(
            collective_id=collective_id, has_side_effects=True, vmem_limit_bytes=16 << 20
        ),
        name="spread_attention",
    )(qkv, out)


def collect_kernel(
    qkv_ref, out_ref, qkv_sum, out_sum, qkv_in, out_in, total, own_sem, z_send, z_recv, o_send, o_recv,
    a_send, a_recv
):
    n_seq = lax.axis_size("seq")
    n_dp = lax.axis_size("dp")
    seq_index = lax.axis_index("seq")
    dp_index = lax.axis_index("dp")
    seq_peers = [lax.rem(seq_index + k, n_seq) for k in range(n_seq)]
    dp_peers = [lax.rem(dp_index + k, n_dp) for k in range(n_dp)]
    greet([(dp_index, p) for p in seq_peers[1:]] + [(p, seq_index) for p in dp_peers[1:]])
    along = {}
    for k in list(range(1, n_seq)) + [0]:
        for j in range(n_dp - 1, 0, -1):
            along[k, j] = send(
                qkv_ref.at[seq_peers[k], dp_peers[j]],
                qkv_in.at[k, j],
                z_send.at[k, j],
                z_recv.at[k, j],
                (dp_peers[j], seq_index),
            )
            along[k, j].start()
    outs = {}
    for j in range(n_dp - 1, 0, -1):
        outs[j] = send(
            out_ref.at[dp_peers[j]], out_in.at[j], o_send.at[j], o_recv.at[j], (dp_peers[j], seq_index)
        )
        outs[j].start()
    across = {}
    for k in list(range(1, n_seq)) + [0]:
        value = qkv_ref[seq_peers[k], dp_index].astype(f32)
        for j in range(1, n_dp):
            along[k, j].wait_recv()
            value = value + qkv_in[k, j].astype(f32)
        total[k] = value.astype(total.dtype)
        if k:
            across[k] = send(
                total.at[k],
                qkv_sum.at[seq_index],
                a_send.at[k],
                a_recv.at[k],
                (dp_index, seq_peers[k]),
            )
            across[k].start()
    own = pltpu.make_async_copy(total.at[0], qkv_sum.at[seq_index], own_sem)
    own.start()
    value = out_ref[dp_index].astype(f32)
    for j in range(1, n_dp):
        outs[j].wait_recv()
        value = value + out_in[j].astype(f32)
    out_sum[...] = value.astype(out_sum.dtype)
    for copy in along.values():
        copy.wait_send()
    for copy in outs.values():
        copy.wait_send()
    for copy in across.values():
        copy.wait()
    own.wait()


def collect_attention(qkv, out, collective_id):
    n_seq = lax.axis_size("seq")
    n_dp = lax.axis_size("dp")
    dma = pltpu.SemaphoreType.DMA
    tail = qkv.shape[2:]
    return pl.pallas_call(
        collect_kernel,
        out_shape=[
            jax.ShapeDtypeStruct((n_seq,) + tail, qkv.dtype),
            jax.ShapeDtypeStruct(out.shape[1:], out.dtype),
        ],
        in_specs=[VMEM, VMEM],
        out_specs=[VMEM, VMEM],
        scratch_shapes=[
            pltpu.VMEM((n_seq, n_dp) + tail, qkv.dtype),
            pltpu.VMEM((n_dp,) + out.shape[1:], out.dtype),
            pltpu.VMEM((n_seq,) + tail, qkv.dtype),
            dma,
            dma((n_seq, n_dp)),
            dma((n_seq, n_dp)),
            dma((n_dp,)),
            dma((n_dp,)),
            dma((n_seq,)),
            dma((n_seq,)),
        ],
        compiler_params=pltpu.CompilerParams(
            collective_id=collective_id, has_side_effects=True, vmem_limit_bytes=40 << 20
        ),
        name="collect_attention",
    )(qkv, out)


def local(block_input, cotangent, doc_lengths, owners, master, first_moment, second_moment):
    n_seq = lax.axis_size("seq")
    n_dp = lax.axis_size("dp")
    seq_index = lax.axis_index("seq")
    dp_index = lax.axis_index("dp")
    core = seq_index % 2
    _, shard_len, width = block_input.shape
    rows = master.shape[0]
    per_owner = master.shape[1]
    chips = n_seq // 2
    sub = rows // n_dp
    wide = width // n_dp
    half = chips * sub
    heads = H // n_seq
    head_cols = heads * HD
    seq_len = shard_len * n_seq
    ff_blocks = FF // D
    first_slots = min(4, per_owner)
    unit_count = owners.shape[0]
    score_scale = float(HD) ** (-0.5)

    unit_slot = unit_slots(owners, per_owner)
    place = unit_slot - owners * per_owner
    all_slots = jnp.arange(n_dp * per_owner, dtype=jnp.int32)
    match = unit_slot[None, :] == all_slots[:, None]
    slot_unit = jnp.sum(
        jnp.where(match, jnp.arange(unit_count, dtype=jnp.int32)[None, :] + 1, 0), axis=1
    ) - 1
    slot_unit = slot_unit.reshape(n_dp, per_owner)
    own_units = lax.dynamic_index_in_dim(slot_unit, dp_index, 0, keepdims=False)
    is_col = (own_units >= 4) & (own_units < 4 + 2 * ff_blocks)
    chip_groups = [[2 * k + c for k in range(chips)] for c in range(2)]

    sibling = [(i, i ^ 1) for i in range(n_seq)]

    def exchange(packed):
        return lax.all_to_all(packed, "dp", 0, 0)

    packed = pack(master, is_col.astype(jnp.int32), n_dp, n_seq, first_slots)
    first_table = exchange(packed[0]).reshape(n_dp * first_slots, rows, wide)
    att = jnp.take(first_table, (owners * first_slots + place)[:4], axis=0)
    att_rows = att[:3].reshape(3, n_dp, sub, n_seq // n_dp, head_cols)
    att_rows = att_rows.transpose(1, 3, 2, 0, 4).reshape(n_seq, sub, 3 * head_cols)
    att_out = att[3].reshape(n_dp, sub, wide).transpose(1, 0, 2).reshape(sub, width)
    qkv_weight, out_weight = spread_attention(att_rows, att_out, 1)
    qkv_weight = qkv_weight.reshape(width, 3 * head_cols)
    out_weight = out_weight.reshape(rows, width)

    tokens = block_input.astype(f32).reshape(shard_len, width)
    normed_one, inv_one = norm_parts(tokens)
    normed_one_all = gather_blocks(normed_one.astype(bf), "seq", 2).reshape(seq_len, width)
    qkv_proj = jnp.dot(normed_one_all, qkv_weight, preferred_element_type=f32)
    qkv_proj = qkv_proj.reshape(seq_len, 3, heads, HD)
    positions = jnp.arange(seq_len, dtype=jnp.int32)
    cosine, sine = rope_tables(positions.astype(f32), HD)
    cosine = cosine[:, None, :]
    sine = sine[:, None, :]
    queries = rotate(qkv_proj[:, 0], cosine, sine).astype(bf)
    keys = rotate(qkv_proj[:, 1], cosine, sine).astype(bf)
    values = qkv_proj[:, 2].astype(bf)
    doc_ends = jnp.cumsum(doc_lengths[0])
    doc = jnp.sum((positions[:, None] >= doc_ends[None, :]).astype(jnp.int32), axis=1)
    allowed = (doc[:, None] == doc[None, :]) & (positions[None, :] <= positions[:, None])
    scores = jnp.einsum("qhd,khd->hqk", queries, keys, preferred_element_type=f32) * score_scale
    scores = jnp.where(allowed[None], scores, masked_score)
    peak = jnp.max(scores, axis=-1, keepdims=True)
    raised = jnp.exp(scores - peak)
    prob = raised / jnp.sum(raised, axis=-1, keepdims=True)
    prob_low = prob.astype(bf)
    attended = jnp.einsum("hqk,khd->qhd", prob_low, values, preferred_element_type=f32)
    attended_low = attended.reshape(seq_len, head_cols).astype(bf)
    attn_part = jnp.dot(attended_low, out_weight, preferred_element_type=f32).astype(bf)
    attn_out = sum_blocks(attn_part.reshape(n_seq, shard_len, width), "seq", 3)
    residual = tokens + attn_out
    normed_two, inv_two = norm_parts(residual)

    if per_owner > first_slots:
        second_slots = per_owner - first_slots
        second = exchange(packed[1]).reshape(n_dp * second_slots, rows, wide)
        table = jnp.concatenate([first_table, second], axis=0)
        index = jnp.where(
            place < first_slots,
            owners * first_slots + place,
            n_dp * first_slots + owners * second_slots + place - first_slots,
        )
    else:
        table = first_table
        index = owners * first_slots + place
    ff = jnp.take(table, index[4:], axis=0)
    ug = ff[: 2 * ff_blocks]
    mine = lax.dynamic_slice_in_dim(ug, core * half, half, axis=2)
    given = lax.dynamic_slice_in_dim(ug, (1 - core) * half, half, axis=2)
    got = lax.ppermute(given, "seq", sibling)
    ug = jnp.where(
        core == 0, jnp.concatenate([mine, got], axis=1), jnp.concatenate([got, mine], axis=1)
    )
    up_weight = lax.all_gather(
        ug[:ff_blocks], "seq", axis=1, tiled=True, axis_index_groups=chip_groups
    )
    gate_weight = lax.all_gather(
        ug[ff_blocks:], "seq", axis=1, tiled=True, axis_index_groups=chip_groups
    )
    down = ff[2 * ff_blocks :].reshape(ff_blocks, n_dp, sub, wide).transpose(0, 2, 1, 3)
    down_weight = lax.all_gather(
        down.reshape(ff_blocks, sub, width), "seq", axis=1, tiled=True, axis_index_groups=chip_groups
    )

    def gather_tokens(part):
        return gather_blocks(part, "dp", 4).reshape(-1, width)

    def scatter_tokens(part):
        return sum_blocks(part.astype(bf).reshape(2 * n_dp, shard_len, width), "dp", 5)

    upstream = cotangent.reshape(shard_len, width)
    upstream_all = gather_tokens(upstream)
    normed_two_all = gather_tokens(normed_two.astype(bf))
    up_proj = jnp.einsum("tr,jrc->tjc", normed_two_all, up_weight, preferred_element_type=f32)
    gate_proj = jnp.einsum("tr,jrc->tjc", normed_two_all, gate_weight, preferred_element_type=f32)
    gate_sig = jax.nn.sigmoid(gate_proj)
    silu_value = gate_proj * gate_sig
    hidden_low = (silu_value * up_proj).astype(bf)
    ff_out = scatter_tokens(
        jnp.einsum("tjh,jhc->tc", hidden_low, down_weight, preferred_element_type=f32)
    )
    block_output = (residual + ff_out).astype(bf).reshape(block_input.shape)
    hidden_grad = jnp.einsum("tc,jhc->tjh", upstream_all, down_weight, preferred_element_type=f32)
    up_grad_low = (hidden_grad * silu_value).astype(bf)
    gate_grad_low = (
        hidden_grad * up_proj * (gate_sig + gate_proj * gate_sig * (1.0 - gate_sig))
    ).astype(bf)

    def chip_sum(part):
        return lax.psum_scatter(
            part.astype(bf),
            "seq",
            scatter_dimension=1,
            tiled=True,
            axis_index_groups=chip_groups,
        )

    down_grad = chip_sum(
        jnp.einsum("tjh,tc->jhc", hidden_low, upstream_all, preferred_element_type=f32)
    )
    up_grad = chip_sum(
        jnp.einsum("tr,tjc->jrc", normed_two_all, up_grad_low, preferred_element_type=f32)
    )
    gate_grad = chip_sum(
        jnp.einsum("tr,tjc->jrc", normed_two_all, gate_grad_low, preferred_element_type=f32)
    )
    norm_two_grad = jnp.einsum("tjc,jrc->tr", up_grad_low, up_weight, preferred_element_type=f32)
    norm_two_grad = norm_two_grad + jnp.einsum(
        "tjc,jrc->tr", gate_grad_low, gate_weight, preferred_element_type=f32
    )
    norm_two_grad = scatter_tokens(norm_two_grad)
    residual_grad = upstream.astype(f32) + norm_back(normed_two, inv_two, norm_two_grad)
    residual_grad_all = gather_blocks(residual_grad.astype(bf), "seq", 2).reshape(seq_len, width)

    attended_grad = jnp.einsum(
        "tc,rc->tr", residual_grad_all, out_weight, preferred_element_type=f32
    )
    attended_grad = attended_grad.astype(bf).reshape(seq_len, heads, HD)
    value_grad = jnp.einsum("hqk,qhd->khd", prob_low, attended_grad, preferred_element_type=f32)
    prob_grad = jnp.einsum("qhd,khd->hqk", attended_grad, values, preferred_element_type=f32)
    inner_sum = jnp.sum(prob * prob_grad, axis=-1, keepdims=True)
    score_grad = (prob * (prob_grad - inner_sum) * score_scale).astype(bf)
    query_grad = jnp.einsum("hqk,khd->qhd", score_grad, keys, preferred_element_type=f32)
    key_grad = jnp.einsum("hqk,qhd->khd", score_grad, queries, preferred_element_type=f32)
    qkv_grad = jnp.stack(
        [
            rotate_back(query_grad, cosine, sine),
            rotate_back(key_grad, cosine, sine),
            value_grad,
        ],
        axis=1,
    )
    qkv_grad_low = qkv_grad.astype(bf).reshape(seq_len, 3 * head_cols)
    norm_one_part = jnp.einsum("tf,rf->tr", qkv_grad_low, qkv_weight, preferred_element_type=f32)
    norm_one_grad = sum_blocks(
        norm_one_part.astype(bf).reshape(n_seq, shard_len, width), "seq", 3
    )
    input_grad = (residual_grad + norm_back(normed_one, inv_one, norm_one_grad)).reshape(
        block_input.shape
    )

    qkv_wgrad = jnp.einsum(
        "tr,tf->rf", normed_one_all, qkv_grad_low, preferred_element_type=f32
    ).astype(bf)
    out_wgrad = jnp.einsum(
        "tr,tc->rc", attended_low, residual_grad_all, preferred_element_type=f32
    ).astype(bf)
    qkv_piece, out_piece = collect_attention(
        qkv_wgrad.reshape(n_seq, n_dp, sub, 3 * head_cols), out_wgrad.reshape(n_dp, sub, width), 6
    )
    qkv_piece = qkv_piece.reshape(n_dp, n_seq // n_dp, sub, 3, head_cols).transpose(3, 0, 2, 1, 4)
    qkv_piece = qkv_piece.reshape(3, rows, wide)
    out_piece = out_piece.reshape(sub, n_dp, wide).transpose(1, 0, 2).reshape(1, rows, wide)

    ug_grad = jnp.concatenate([up_grad, gate_grad], axis=0)
    kept = lax.dynamic_slice_in_dim(ug_grad, core * rows, rows, axis=1)
    sent = lax.dynamic_slice_in_dim(ug_grad, (1 - core) * rows, rows, axis=1)
    got = lax.ppermute(sent, "seq", sibling)
    ug_piece = jnp.where(
        core == 0, jnp.concatenate([kept, got], axis=2), jnp.concatenate([got, kept], axis=2)
    )
    down_piece = down_grad.reshape(ff_blocks, sub, n_dp, wide).transpose(0, 2, 1, 3)
    down_piece = down_piece.reshape(ff_blocks, rows, wide)
    ff_pieces = jnp.concatenate([ug_piece, down_piece], axis=0)

    def give_back(pieces, low_slot, high_slot, skipped):
        units = jnp.maximum(slot_unit[:, low_slot:high_slot] - skipped, 0)
        return lax.all_to_all(jnp.take(pieces, units, axis=0), "dp", 0, 0)

    grads = []
    if per_owner > first_slots:
        grads.append(give_back(ff_pieces, first_slots, per_owner, 4))
    every_piece = jnp.concatenate([qkv_piece, out_piece, ff_pieces], axis=0)
    grads.insert(0, give_back(every_piece, 0, first_slots, 0))
    kinds = jnp.where(own_units < 0, 2, is_col.astype(jnp.int32)).astype(jnp.int32)
    owned_grads, new_first, new_second, new_master = adam(
        kinds, grads, master, first_moment, second_moment, n_dp, n_seq, first_slots
    )
    return (block_output, input_grad, owned_grads, new_first, new_second, new_master)


def solution(mesh):
    placed = (
        P("dp", "seq", None),
        P("dp", "seq", None),
        P("dp", None),
        P(),
        P("seq", "dp", None),
        P("seq", "dp", None),
        P("seq", "dp", None),
    )
    return jax.shard_map(
        local,
        mesh=mesh,
        in_specs=placed,
        out_specs=(
            P("dp", "seq", None),
            P("dp", "seq", None),
            P("seq", "dp", None),
            P("seq", "dp", None),
            P("seq", "dp", None),
            P("seq", "dp", None),
        ),
        check_vma=False,
    )
```

```python
import functools

import jax
import jax.numpy as jnp
from jax import lax
from jax.experimental import pallas as pl
from jax.experimental.pallas import tpu as pltpu
from jax.sharding import PartitionSpec as P

D = 2048
H = 16
HD = 128
FF = 8192
STEP = 5
bf = jnp.bfloat16
f32 = jnp.float32
MESH = pl.DeviceIdType.MESH


norm_eps = 1e-05
rope_base = 10000.0
beta_one = 0.5
beta_two = 0.5
learn_rate = 0.01
decay_rate = 0.1
adam_eps = 1e-08
masked_score = -1000000000.0


def unit_slots(owners, per_owner):
    unit_count = owners.shape[0]
    unit_order = jnp.arange(unit_count, dtype=jnp.int32)
    matching = owners[:, None] == owners[None, :]
    before = unit_order[None, :] < unit_order[:, None]
    places = jnp.sum(jnp.where(matching & before, 1, 0), axis=1).astype(jnp.int32)
    return owners * per_owner + places


def norm_parts(values):
    center = values - jnp.mean(values, axis=-1, keepdims=True)
    spread = jnp.mean(center * center, axis=-1, keepdims=True)
    scale_inv = lax.rsqrt(spread + norm_eps)
    return (center * scale_inv, scale_inv)


def norm_back(normed, scale_inv, upstream):
    upstream_mean = jnp.mean(upstream, axis=-1, keepdims=True)
    cross_mean = jnp.mean(upstream * normed, axis=-1, keepdims=True)
    return scale_inv * (upstream - upstream_mean - normed * cross_mean)


def rope_tables(positions, head_dim):
    half_dim = head_dim // 2
    frequency = jnp.power(rope_base, -(jnp.arange(half_dim, dtype=jnp.float32) * 2.0) / head_dim)
    angles = positions[:, None] * frequency[None, :]
    cosine_half = jnp.cos(angles)
    sine_half = jnp.sin(angles)
    return (
        jnp.concatenate([cosine_half, cosine_half], axis=-1),
        jnp.concatenate([sine_half, sine_half], axis=-1),
    )


def rotate(values, cosine, sine):
    half_dim = values.shape[-1] // 2
    turned = jnp.concatenate([-values[..., half_dim:], values[..., :half_dim]], axis=-1)
    return values * cosine + turned * sine


def rotate_back(grads, cosine, sine):
    half_dim = grads.shape[-1] // 2
    scaled = grads * sine
    turned = jnp.concatenate([scaled[..., half_dim:], -scaled[..., :half_dim]], axis=-1)
    return grads * cosine + turned


def pack_kernel(n_dp, chips, first_slots, flags, m_ref, *outs):
    rb, slots, width = m_ref.shape
    rows, wide = outs[0].shape[2:]
    sub = rows // n_dp
    start = pl.program_id(0) * rb
    target = start // sub
    inner = start % sub
    turned = jnp.swapaxes(m_ref[...], 0, 1).astype(bf)
    for s in range(slots):
        out = outs[0] if s < first_slots else outs[1]
        t = s if s < first_slots else s - first_slots
        x = turned[s]

        @pl.when(flags[s] == 1)
        def _():
            for d in range(n_dp):
                pieces = [
                    x[:, (2 * k + c) * rows + d * sub : (2 * k + c) * rows + (d + 1) * sub]
                    for c in range(2)
                    for k in range(chips)
                ]
                out[d, t, pl.ds(pl.multiple_of(start, rb), rb), :] = jnp.concatenate(pieces, axis=1)

        @pl.when(flags[s] == 0)
        def _():
            for g in range(n_dp):
                out[target, t, pl.ds(pl.multiple_of(g * sub + inner, rb), rb), :] = x[
                    :, g * wide : (g + 1) * wide
                ]


def pack(master, flags, n_dp, n_seq, first_slots):
    rows, slots, width = master.shape
    wide = width // n_dp
    rb = min(32, rows // n_dp)
    counts = [first_slots] + ([slots - first_slots] if slots > first_slots else [])
    return pl.pallas_call(
        functools.partial(pack_kernel, n_dp, n_seq // 2, first_slots),
        out_shape=[jax.ShapeDtypeStruct((n_dp, c, rows, wide), bf) for c in counts],
        grid_spec=pltpu.PrefetchScalarGridSpec(
            num_scalar_prefetch=1,
            grid=(rows // rb,),
            in_specs=[pl.BlockSpec((rb, slots, width), lambda i, f: (i, 0, 0))],
            out_specs=[
                pl.BlockSpec((n_dp, c, rows, wide), lambda i, f: (0, 0, 0, 0)) for c in counts
            ],
        ),
        compiler_params=pltpu.CompilerParams(vmem_limit_bytes=50 << 20),
        name="pack",
    )(flags, master)


def adam_kernel(n_dp, chips, first_slots, n_groups, kinds, *refs):
    cols = refs[:n_groups]
    rws = refs[n_groups : 2 * n_groups]
    m_ref, f_ref, s_ref, keep_ref, g_out, f_out, s_out, m_out, held = refs[2 * n_groups :]
    rb, slots, width = m_ref.shape
    wide = width // n_dp
    rows = width // (2 * chips)
    sub = rows // n_dp
    half = chips * sub
    for s in range(slots):
        group = 0 if s < first_slots else 1
        t = s if group == 0 else s - first_slots

        @pl.when(kinds[s] == 1)
        def _():
            pieces = []
            for i in range(2 * chips):
                k, c = i // 2, i % 2
                for d in range(n_dp):
                    begin = c * half + k * sub
                    pieces.append(cols[group][d, t, :, begin : begin + sub])
            held[s] = jnp.concatenate(pieces, axis=1).astype(f32)

        @pl.when(kinds[s] == 0)
        def _():
            for g in range(n_dp):
                held[s, :, g * wide : (g + 1) * wide] = rws[group][0, t, g, :, :].astype(f32)

        @pl.when(kinds[s] == 2)
        def _():
            held[s] = jnp.zeros((rb, width), f32)

    grad = jnp.swapaxes(held[...], 0, 1)
    keep = keep_ref[...] > 0.0
    g_out[...] = grad
    first = jnp.where(keep, beta_one * f_ref[...] + (1.0 - beta_one) * grad, 0.0)
    f_out[...] = first
    second = jnp.where(keep, beta_two * s_ref[...] + (1.0 - beta_two) * grad * grad, 0.0)
    s_out[...] = second
    fixed_first = first * (1.0 / (1.0 - beta_one**STEP))
    fixed_second = second * (1.0 / (1.0 - beta_two**STEP))
    old = m_ref[...]
    step = fixed_first / (jnp.sqrt(fixed_second) + adam_eps) + decay_rate * old
    m_out[...] = jnp.where(keep, old - learn_rate * step, 0.0)


def adam(kinds, grads, master, first_moment, second_moment, n_dp, n_seq, first_slots):
    rows, slots, width = master.shape
    wide = width // n_dp
    sub = rows // n_dp
    rb = min(16, sub)
    state = pl.BlockSpec((rb, slots, width), lambda i, k: (i, 0, 0))
    cols = [pl.BlockSpec((n_dp, g.shape[1], rb, wide), lambda i, k: (0, 0, i, 0)) for g in grads]
    rws = [
        pl.BlockSpec(
            (1, g.shape[1], n_dp, rb, wide),
            lambda i, k: (i * rb // sub, 0, 0, i % (sub // rb), 0),
        )
        for g in grads
    ]
    keep = jnp.broadcast_to((kinds != 2).astype(f32)[None, :, None], (1, slots, width))
    return pl.pallas_call(
        functools.partial(adam_kernel, n_dp, n_seq // 2, first_slots, len(grads)),
        out_shape=[jax.ShapeDtypeStruct(master.shape, f32)] * 4,
        grid_spec=pltpu.PrefetchScalarGridSpec(
            num_scalar_prefetch=1,
            grid=(rows // rb,),
            in_specs=cols
            + rws
            + [state] * 3
            + [pl.BlockSpec((1, slots, width), lambda i, k: (0, 0, 0))],
            out_specs=[state] * 4,
            scratch_shapes=[pltpu.VMEM((slots, rb, width), f32)],
        ),
        compiler_params=pltpu.CompilerParams(vmem_limit_bytes=50 << 20),
        name="adam",
    )(
        kinds,
        *grads,
        *[g.reshape(n_dp, g.shape[1], n_dp, sub, wide) for g in grads],
        master,
        first_moment,
        second_moment,
        keep,
    )


ANY = pl.BlockSpec(memory_space=pl.ANY)
VMEM = pl.BlockSpec(memory_space=pltpu.VMEM)
DMA = pltpu.SemaphoreType.DMA


def comm_params(collective_id, mib):
    return pltpu.CompilerParams(
        collective_id=collective_id, has_side_effects=True, vmem_limit_bytes=mib << 20
    )


def takes(microseconds):
    return pl.CostEstimate(flops=0, bytes_accessed=int(microseconds * 3e6), transcendentals=0)


def places():
    n_seq = lax.axis_size("seq")
    n_dp = lax.axis_size("dp")
    return n_seq, n_dp, lax.axis_index("seq"), lax.axis_index("dp")


def greet(devices):
    barrier = pltpu.get_barrier_semaphore()
    for device in devices:
        pl.semaphore_signal(barrier, inc=1, device_id=device, device_id_type=MESH)
    pl.semaphore_wait(barrier, len(devices))


def send(src, dst, send_sem, recv_sem, device):
    return pltpu.make_async_remote_copy(
        src_ref=src,
        dst_ref=dst,
        send_sem=send_sem,
        recv_sem=recv_sem,
        device_id=device,
        device_id_type=MESH,
    )


def relay_gather(views, place, count, device_of, send_sem, recv_sem, arrived):
    def leg(view, way, step, block, target):
        ref = views[view](block)
        return send(ref, ref, send_sem.at[view, way, step], recv_sem.at[view, way, step], device_of(target))

    def going(way, step):
        block = place - (step - 1) if way == 0 else place + (step - 1)
        target = place + 1 if way == 0 else place - 1
        inside = (block >= 0) & (block < count) & (target >= 0) & (target < count)
        return block, target, inside

    for step in range(1, count):
        for way in range(2):
            block, target, inside = going(way, step)

            @pl.when(inside)
            def _():
                for view in range(len(views)):
                    leg(view, way, step, block, target).start()

        for way in range(2):
            block = place - step if way == 0 else place + step

            @pl.when((block >= 0) & (block < count))
            def _():
                for view in range(len(views)):
                    leg(view, way, step, block, lax.rem(place + 1, count)).wait_recv()
                arrived(block)

    for step in range(1, count):
        for way in range(2):
            block, target, inside = going(way, step)

            @pl.when(inside)
            def _():
                for view in range(len(views)):
                    leg(view, way, step, block, target).wait_send()


def relay_sum(owns, sent, came, place, count, device_of, send_sem, recv_sem, ready):
    views = range(len(owns))

    def leg(view, way, block, target):
        return send(
            sent[view].at[way, block],
            came[view].at[way, block],
            send_sem.at[view, way, block],
            recv_sem.at[view, way, block],
            device_of(target),
        )

    def going(way, step):
        block = count - 1 - step + place if way == 0 else step - (count - 1 - place)
        target = place + 1 if way == 0 else place - 1
        return block, target, (block < count if way == 0 else block >= 0)

    def behind(way):
        return place > 0 if way == 0 else place < count - 1

    for step in range(count - 1):
        for way in range(2):
            block, target, inside = going(way, step)

            @pl.when(inside)
            def _():
                ready(block)
                for view in views:

                    @pl.when(behind(way))
                    def _():
                        leg(view, way, block, target).wait_recv()
                        value = owns[view](block) + came[view][way, block].astype(f32)
                        sent[view][way, block] = value.astype(sent[view].dtype)

                    @pl.when(jnp.logical_not(behind(way)))
                    def _():
                        sent[view][way, block] = owns[view](block).astype(sent[view].dtype)

                    leg(view, way, block, target).start()

    ready(place)
    for way in range(2):

        @pl.when(behind(way))
        def _():
            for view in views:
                leg(view, way, place, lax.rem(place + 1, count)).wait_recv()

    totals = []
    for view in views:
        total = owns[view](place)
        for way in range(2):
            value = came[view][way, place].astype(f32)
            total = total + jnp.where(behind(way), value, 0.0)
        totals.append(total)
    for step in range(count - 1):
        for way in range(2):
            block, target, inside = going(way, step)

            @pl.when(inside)
            def _():
                for view in views:
                    leg(view, way, block, target).wait_send()

    return totals


def front_kernel(
    packed_ref, x_ref, table_ref, out_ref, own_sem, a_send, a_recv, send_sem, recv_sem, pass_sem, take_sem
):
    n_seq, n_dp, seq_index, dp_index = places()
    chips, chip, core = n_seq // 2, seq_index // 2, lax.rem(seq_index, 2)
    dp_peers = [lax.rem(dp_index + k, n_dp) for k in range(n_dp)]
    chip_peers = [lax.rem(chip + k, chips) for k in range(chips)]
    sibling = (dp_index, chip * 2 + 1 - core)
    greet(
        [(p, seq_index) for p in dp_peers[1:]]
        + [(dp_index, p * 2 + core) for p in chip_peers[1:]]
        + [sibling]
    )
    along = []
    for k in range(1, n_dp):
        copy = send(
            packed_ref.at[dp_peers[k]],
            table_ref.at[dp_index],
            a_send.at[k],
            a_recv.at[k],
            (dp_peers[k], seq_index),
        )
        copy.start()
        along.append(copy)
    own = [
        pltpu.make_async_copy(packed_ref.at[dp_index], table_ref.at[dp_index], own_sem.at[0]),
        pltpu.make_async_copy(x_ref, out_ref.at[seq_index], own_sem.at[1]),
    ]
    for copy in own:
        copy.start()
    spread_blocks(
        x_ref, out_ref, chips, chip, core, dp_index, sibling, send_sem, recv_sem, pass_sem, take_sem
    )
    for copy in along:
        copy.wait()
    for copy in own:
        copy.wait()


def spread_blocks(
    x_ref, out_ref, chips, chip, core, dp_index, sibling, send_sem, recv_sem, pass_sem, take_sem
):
    mine = out_ref.at[chip * 2 + core]
    copies = {}
    for k in range(chips - 1, 0, -1):
        device = (dp_index, lax.rem(chip + k, chips) * 2 + core)
        copies[k] = send(x_ref, mine, send_sem.at[k], recv_sem.at[k], device)
        copies[k].start()
    passed = [send(x_ref, mine, pass_sem.at[0], take_sem.at[0], sibling)]
    passed[0].start()
    for k in range(1, chips):
        copies[k].wait_recv()
        block = out_ref.at[lax.rem(chip + chips - k, chips) * 2 + core]
        onward = send(block, block, pass_sem.at[k], take_sem.at[k], sibling)
        onward.start()
        passed.append(onward)
    for copy in copies.values():
        copy.wait_send()
    for onward in passed:
        onward.wait()


def front(packed, x, collective_id):
    chips = lax.axis_size("seq") // 2
    n_dp = lax.axis_size("dp")
    return pl.pallas_call(
        front_kernel,
        out_shape=[
            jax.ShapeDtypeStruct(packed.shape, packed.dtype),
            jax.ShapeDtypeStruct((2 * chips,) + x.shape, x.dtype),
        ],
        in_specs=[ANY, ANY],
        out_specs=[ANY, ANY],
        scratch_shapes=[DMA((2,)), DMA((n_dp,)), DMA((n_dp,))] + [DMA((chips,))] * 4,
        compiler_params=comm_params(collective_id, 16),
        cost_estimate=takes(90),
        name="front",
    )(packed, x)


def gather_seq_kernel(x_ref, out_ref, own_sem, send_sem, recv_sem, pass_sem, take_sem):
    n_seq, n_dp, seq_index, dp_index = places()
    chips, chip, core = n_seq // 2, seq_index // 2, lax.rem(seq_index, 2)
    chip_peers = [lax.rem(chip + k, chips) for k in range(chips)]
    sibling = (dp_index, chip * 2 + 1 - core)
    greet([(dp_index, p * 2 + core) for p in chip_peers[1:]] + [sibling])
    own = pltpu.make_async_copy(x_ref, out_ref.at[seq_index], own_sem)
    own.start()
    spread_blocks(
        x_ref, out_ref, chips, chip, core, dp_index, sibling, send_sem, recv_sem, pass_sem, take_sem
    )
    own.wait()


def gather_seq(x, collective_id):
    chips = lax.axis_size("seq") // 2
    return pl.pallas_call(
        gather_seq_kernel,
        out_shape=jax.ShapeDtypeStruct((2 * chips,) + x.shape, x.dtype),
        in_specs=[ANY],
        out_specs=ANY,
        scratch_shapes=[DMA] + [DMA((chips,))] * 4,
        compiler_params=comm_params(collective_id, 16),
        cost_estimate=takes(28),
        name="gather_seq",
    )(x)


def gather_dp_kernel(x_ref, out_ref, own_sem, send_sem, recv_sem, pass_sem, take_sem):
    n_seq, n_dp, seq_index, dp_index = places()
    core = lax.rem(seq_index, 2)
    sibling = (dp_index, seq_index + 1 - 2 * core)
    greet([(lax.rem(dp_index + k, n_dp), seq_index) for k in range(1, n_dp)] + [sibling])
    own = pltpu.make_async_copy(x_ref, out_ref.at[core, dp_index], own_sem)
    own.start()
    own.wait()

    def onward(block):
        ref = out_ref.at[core, block]
        return send(ref, ref, pass_sem.at[block], take_sem.at[block], sibling)

    onward(dp_index).start()
    relay_gather(
        [lambda block: out_ref.at[core, block]],
        dp_index,
        n_dp,
        lambda place: (place, seq_index),
        send_sem,
        recv_sem,
        lambda block: onward(block).start(),
    )
    for block in range(n_dp):
        onward(block).wait_send()
        ref = out_ref.at[1 - core, block]
        send(ref, ref, pass_sem.at[block], take_sem.at[block], sibling).wait_recv()


def gather_dp(x, collective_id):
    n_dp = lax.axis_size("dp")
    return pl.pallas_call(
        gather_dp_kernel,
        out_shape=jax.ShapeDtypeStruct((2, n_dp) + x.shape, x.dtype),
        in_specs=[ANY],
        out_specs=ANY,
        scratch_shapes=[DMA, DMA((1, 2, n_dp)), DMA((1, 2, n_dp)), DMA((n_dp,)), DMA((n_dp,))],
        compiler_params=comm_params(collective_id, 16),
        cost_estimate=takes(40),
        name="gather_dp",
    )(x)


def sum_seq_kernel(x_ref, out_ref, taken, sent, arrived, pass_sem, take_sem, send_sem, recv_sem):
    n_seq, n_dp, seq_index, dp_index = places()
    chips, chip, core = n_seq // 2, seq_index // 2, lax.rem(seq_index, 2)
    peers = [lax.rem(chip + k, chips) for k in range(chips)]
    sibling = (dp_index, chip * 2 + 1 - core)
    greet([(dp_index, p * 2 + core) for p in peers[1:]] + [sibling])
    order = list(range(chips - 1, 0, -1)) + [0]
    passed = {}
    for k in order:
        block = x_ref.at[peers[k] * 2 + 1 - core]
        passed[k] = send(block, taken.at[k], pass_sem.at[k], take_sem.at[k], sibling)
        passed[k].start()
    copies = {}
    for k in order[:-1]:
        passed[k].wait_recv()
        own = x_ref[peers[k] * 2 + core].astype(f32)
        sent[k] = (own + taken[k].astype(f32)).astype(sent.dtype)
        device = (dp_index, peers[k] * 2 + core)
        copies[k] = send(sent.at[k], arrived.at[k], send_sem.at[k], recv_sem.at[k], device)
        copies[k].start()
    passed[0].wait_recv()
    total = x_ref[seq_index].astype(f32) + taken[0].astype(f32)
    for k in range(1, chips):
        copies[k].wait_recv()
        total = total + arrived[k].astype(f32)
    out_ref[...] = total
    for k in order:
        passed[k].wait_send()
    for k in order[:-1]:
        copies[k].wait_send()


def sum_seq(x, collective_id):
    blocks, rows, columns = x.shape
    chips = blocks // 2
    slots = pltpu.VMEM((chips, rows, columns), x.dtype)
    return pl.pallas_call(
        sum_seq_kernel,
        out_shape=jax.ShapeDtypeStruct((rows, columns), f32),
        in_specs=[VMEM],
        out_specs=VMEM,
        scratch_shapes=[slots, slots, slots] + [DMA((chips,))] * 4,
        compiler_params=comm_params(collective_id, 40),
        cost_estimate=takes(28),
        name="sum_seq",
    )(x)


def sum_dp_kernel(x_ref, out_ref, taken, sent, came, pass_sem, take_sem, send_sem, recv_sem):
    n_seq, n_dp, seq_index, dp_index = places()
    core = lax.rem(seq_index, 2)
    sibling = (dp_index, seq_index + 1 - 2 * core)
    greet([(lax.rem(dp_index + k, n_dp), seq_index) for k in range(1, n_dp)] + [sibling])

    def onward(block):
        return send(
            x_ref.at[1 - core, block], taken.at[block], pass_sem.at[block], take_sem.at[block], sibling
        )

    half = n_dp // 2
    for block in [b for k in range(half) for b in (n_dp - 1 - k, k)]:
        onward(block).start()
    waited = []

    def ready(block):
        onward(block).wait_recv()

    total = relay_sum(
        [lambda block: x_ref[core, block].astype(f32) + taken[block].astype(f32)],
        [sent],
        [came],
        dp_index,
        n_dp,
        lambda place: (place, seq_index),
        send_sem,
        recv_sem,
        ready,
    )[0]
    out_ref[...] = total
    for block in range(n_dp):
        onward(block).wait_send()


def sum_dp(x, collective_id):
    _, n_dp, rows, columns = x.shape
    slots = pltpu.VMEM((2, n_dp, rows, columns), x.dtype)
    return pl.pallas_call(
        sum_dp_kernel,
        out_shape=jax.ShapeDtypeStruct((rows, columns), f32),
        in_specs=[VMEM],
        out_specs=VMEM,
        scratch_shapes=[
            pltpu.VMEM((n_dp, rows, columns), x.dtype),
            slots,
            slots,
            DMA((n_dp,)),
            DMA((n_dp,)),
            DMA((1, 2, n_dp)),
            DMA((1, 2, n_dp)),
        ],
        compiler_params=comm_params(collective_id, 40),
        cost_estimate=takes(40),
        name="sum_dp",
    )(x)


def spread_kernel(
    qkv_ref, out_ref, qkv_all, out_all, own_sem, a_send, a_recv, send_sem, recv_sem
):
    n_seq, n_dp, seq_index, dp_index = places()
    seq_peers = [lax.rem(seq_index + k, n_seq) for k in range(n_seq)]
    greet(
        [(dp_index, p) for p in seq_peers[1:]]
        + [(lax.rem(dp_index + k, n_dp), seq_index) for k in range(1, n_dp)]
    )
    own = [
        pltpu.make_async_copy(qkv_ref.at[seq_index], qkv_all.at[seq_index, dp_index], own_sem.at[0]),
        pltpu.make_async_copy(out_ref, out_all.at[dp_index], own_sem.at[1]),
    ]
    for copy in own:
        copy.start()
    landing = qkv_all.at[seq_index, dp_index]
    across = []
    for k in range(1, n_seq):
        device = (dp_index, seq_peers[k])
        copy = send(qkv_ref.at[seq_peers[k]], landing, a_send.at[k], a_recv.at[k], device)
        copy.start()
        across.append(copy)
    for copy in own:
        copy.wait()
    for copy in across:
        copy.wait_recv()
    relay_gather(
        [lambda block: qkv_all.at[:, block], lambda block: out_all.at[block]],
        dp_index,
        n_dp,
        lambda place: (place, seq_index),
        send_sem,
        recv_sem,
        lambda block: None,
    )
    for copy in across:
        copy.wait_send()


def spread_attention(qkv, out, collective_id):
    n_seq = lax.axis_size("seq")
    n_dp = lax.axis_size("dp")
    return pl.pallas_call(
        spread_kernel,
        out_shape=[
            jax.ShapeDtypeStruct((n_seq, n_dp) + qkv.shape[1:], qkv.dtype),
            jax.ShapeDtypeStruct((n_dp,) + out.shape, out.dtype),
        ],
        in_specs=[ANY, ANY],
        out_specs=[ANY, ANY],
        scratch_shapes=[DMA((2,)), DMA((n_seq,)), DMA((n_seq,)), DMA((2, 2, n_dp)), DMA((2, 2, n_dp))],
        compiler_params=comm_params(collective_id, 16),
        cost_estimate=takes(75),
        name="spread_attention",
    )(qkv, out)


def collect_kernel(
    qkv_ref, out_ref, qkv_sum, out_sum, qkv_sent, qkv_came, out_sent, out_came, total, own_sem,
    send_sem, recv_sem, a_send, a_recv
):
    n_seq, n_dp, seq_index, dp_index = places()
    seq_peers = [lax.rem(seq_index + k, n_seq) for k in range(n_seq)]
    greet(
        [(dp_index, p) for p in seq_peers[1:]]
        + [(lax.rem(dp_index + k, n_dp), seq_index) for k in range(1, n_dp)]
    )
    sums = relay_sum(
        [lambda block: qkv_ref[:, block].astype(f32), lambda block: out_ref[block].astype(f32)],
        [qkv_sent, out_sent],
        [qkv_came, out_came],
        dp_index,
        n_dp,
        lambda place: (place, seq_index),
        send_sem,
        recv_sem,
        lambda block: None,
    )
    total[...] = sums[0].astype(total.dtype)
    across = []
    for k in range(1, n_seq):
        copy = send(
            total.at[seq_peers[k]],
            qkv_sum.at[seq_index],
            a_send.at[k],
            a_recv.at[k],
            (dp_index, seq_peers[k]),
        )
        copy.start()
        across.append(copy)
    own = pltpu.make_async_copy(total.at[seq_index], qkv_sum.at[seq_index], own_sem)
    own.start()
    out_sum[...] = sums[1].astype(out_sum.dtype)
    for copy in across:
        copy.wait()
    own.wait()


def collect_attention(qkv, out, collective_id):
    n_seq = lax.axis_size("seq")
    n_dp = lax.axis_size("dp")
    tail = qkv.shape[2:]
    q_slots = pltpu.VMEM((2, n_dp, n_seq) + tail, qkv.dtype)
    o_slots = pltpu.VMEM((2, n_dp) + out.shape[1:], out.dtype)
    return pl.pallas_call(
        collect_kernel,
        out_shape=[
            jax.ShapeDtypeStruct((n_seq,) + tail, qkv.dtype),
            jax.ShapeDtypeStruct(out.shape[1:], out.dtype),
        ],
        in_specs=[VMEM, VMEM],
        out_specs=[VMEM, VMEM],
        scratch_shapes=[
            q_slots,
            q_slots,
            o_slots,
            o_slots,
            pltpu.VMEM((n_seq,) + tail, qkv.dtype),
            DMA,
            DMA((2, 2, n_dp)),
            DMA((2, 2, n_dp)),
            DMA((n_seq,)),
            DMA((n_seq,)),
        ],
        compiler_params=comm_params(collective_id, 48),
        cost_estimate=takes(75),
        name="collect_attention",
    )(qkv, out)


def local(block_input, cotangent, doc_lengths, owners, master, first_moment, second_moment):
    n_seq = lax.axis_size("seq")
    n_dp = lax.axis_size("dp")
    seq_index = lax.axis_index("seq")
    dp_index = lax.axis_index("dp")
    core = seq_index % 2
    _, shard_len, width = block_input.shape
    rows = master.shape[0]
    per_owner = master.shape[1]
    chips = n_seq // 2
    sub = rows // n_dp
    wide = width // n_dp
    half = chips * sub
    heads = H // n_seq
    head_cols = heads * HD
    seq_len = shard_len * n_seq
    ff_blocks = FF // D
    first_slots = min(4, per_owner)
    unit_count = owners.shape[0]
    score_scale = float(HD) ** (-0.5)

    unit_slot = unit_slots(owners, per_owner)
    place = unit_slot - owners * per_owner
    all_slots = jnp.arange(n_dp * per_owner, dtype=jnp.int32)
    match = unit_slot[None, :] == all_slots[:, None]
    slot_unit = jnp.sum(
        jnp.where(match, jnp.arange(unit_count, dtype=jnp.int32)[None, :] + 1, 0), axis=1
    ) - 1
    slot_unit = slot_unit.reshape(n_dp, per_owner)
    own_units = lax.dynamic_index_in_dim(slot_unit, dp_index, 0, keepdims=False)
    is_col = (own_units >= 4) & (own_units < 4 + 2 * ff_blocks)
    chip_groups = [[2 * k + c for k in range(chips)] for c in range(2)]

    sibling = [(i, i ^ 1) for i in range(n_seq)]

    def exchange(packed):
        return lax.all_to_all(packed, "dp", 0, 0)

    tokens = block_input.astype(f32).reshape(shard_len, width)
    normed_one, inv_one = norm_parts(tokens)
    packed = pack(master, is_col.astype(jnp.int32), n_dp, n_seq, first_slots)
    first_table, normed_one_all = front(packed[0], normed_one.astype(bf), 2)
    first_table = first_table.reshape(n_dp * first_slots, rows, wide)
    normed_one_all = normed_one_all.reshape(seq_len, width)
    att = jnp.take(first_table, (owners * first_slots + place)[:4], axis=0)
    att_rows = att[:3].reshape(3, n_dp, sub, n_seq // n_dp, head_cols)
    att_rows = att_rows.transpose(1, 3, 2, 0, 4).reshape(n_seq, sub, 3 * head_cols)
    att_out = att[3].reshape(n_dp, sub, wide).transpose(1, 0, 2).reshape(sub, width)
    qkv_weight, out_weight = spread_attention(att_rows, att_out, 1)
    if per_owner > first_slots:
        late, qkv_weight = lax.optimization_barrier((packed[1], qkv_weight))
        late = exchange(late)
    qkv_weight = qkv_weight.reshape(width, 3 * head_cols)
    out_weight = out_weight.reshape(rows, width)

    qkv_proj = jnp.dot(normed_one_all, qkv_weight, preferred_element_type=f32)
    qkv_proj = qkv_proj.reshape(seq_len, 3, heads, HD)
    positions = jnp.arange(seq_len, dtype=jnp.int32)
    cosine, sine = rope_tables(positions.astype(f32), HD)
    cosine = cosine[:, None, :]
    sine = sine[:, None, :]
    queries = rotate(qkv_proj[:, 0], cosine, sine).astype(bf)
    keys = rotate(qkv_proj[:, 1], cosine, sine).astype(bf)
    values = qkv_proj[:, 2].astype(bf)
    doc_ends = jnp.cumsum(doc_lengths[0])
    doc = jnp.sum((positions[:, None] >= doc_ends[None, :]).astype(jnp.int32), axis=1)
    allowed = (doc[:, None] == doc[None, :]) & (positions[None, :] <= positions[:, None])
    scores = jnp.einsum("qhd,khd->hqk", queries, keys, preferred_element_type=f32) * score_scale
    scores = jnp.where(allowed[None], scores, masked_score)
    peak = jnp.max(scores, axis=-1, keepdims=True)
    raised = jnp.exp(scores - peak)
    prob = raised / jnp.sum(raised, axis=-1, keepdims=True)
    prob_low = prob.astype(bf)
    attended = jnp.einsum("hqk,khd->qhd", prob_low, values, preferred_element_type=f32)
    attended_low = attended.reshape(seq_len, head_cols).astype(bf)
    attn_part = jnp.dot(attended_low, out_weight, preferred_element_type=f32).astype(bf)
    attn_out = sum_seq(attn_part.reshape(n_seq, shard_len, width), 3)
    residual = tokens + attn_out
    normed_two, inv_two = norm_parts(residual)

    if per_owner > first_slots:
        second_slots = per_owner - first_slots
        late, normed_two = lax.optimization_barrier((late, normed_two))
        second = late.reshape(n_dp * second_slots, rows, wide)
        table = jnp.concatenate([first_table, second], axis=0)
        index = jnp.where(
            place < first_slots,
            owners * first_slots + place,
            n_dp * first_slots + owners * second_slots + place - first_slots,
        )
    else:
        table = first_table
        index = owners * first_slots + place
    ff = jnp.take(table, index[4:], axis=0)
    ug = ff[: 2 * ff_blocks]
    mine = lax.dynamic_slice_in_dim(ug, core * half, half, axis=2)
    given = lax.dynamic_slice_in_dim(ug, (1 - core) * half, half, axis=2)
    got = lax.ppermute(given, "seq", sibling)
    ug = jnp.where(
        core == 0, jnp.concatenate([mine, got], axis=1), jnp.concatenate([got, mine], axis=1)
    )
    up_weight = lax.all_gather(
        ug[:ff_blocks], "seq", axis=1, tiled=True, axis_index_groups=chip_groups
    )
    gate_weight = lax.all_gather(
        ug[ff_blocks:], "seq", axis=1, tiled=True, axis_index_groups=chip_groups
    )
    down = ff[2 * ff_blocks :].reshape(ff_blocks, n_dp, sub, wide).transpose(0, 2, 1, 3)
    down_weight = lax.all_gather(
        down.reshape(ff_blocks, sub, width), "seq", axis=1, tiled=True, axis_index_groups=chip_groups
    )

    def gather_tokens(part):
        return gather_dp(part, 4).reshape(-1, width)

    def scatter_tokens(part):
        return sum_dp(part.astype(bf).reshape(2, n_dp, shard_len, width), 5)

    upstream = cotangent.reshape(shard_len, width)
    every = lax.all_gather(upstream, "dp", axis=0, tiled=True)
    other = lax.ppermute(every, "seq", sibling)
    upstream_all = jnp.where(
        core == 0,
        jnp.concatenate([every, other], axis=0),
        jnp.concatenate([other, every], axis=0),
    )
    normed_two_all = gather_tokens(normed_two.astype(bf))
    up_proj = jnp.einsum("tr,jrc->tjc", normed_two_all, up_weight, preferred_element_type=f32)
    gate_proj = jnp.einsum("tr,jrc->tjc", normed_two_all, gate_weight, preferred_element_type=f32)
    gate_sig = jax.nn.sigmoid(gate_proj)
    silu_value = gate_proj * gate_sig
    hidden_low = (silu_value * up_proj).astype(bf)
    ff_out = scatter_tokens(
        jnp.einsum("tjh,jhc->tc", hidden_low, down_weight, preferred_element_type=f32)
    )
    block_output = (residual + ff_out).astype(bf).reshape(block_input.shape)
    hidden_grad = jnp.einsum("tc,jhc->tjh", upstream_all, down_weight, preferred_element_type=f32)
    up_grad_low = (hidden_grad * silu_value).astype(bf)
    gate_grad_low = (
        hidden_grad * up_proj * (gate_sig + gate_proj * gate_sig * (1.0 - gate_sig))
    ).astype(bf)

    def chip_sum(part):
        return lax.psum_scatter(
            part.astype(bf),
            "seq",
            scatter_dimension=1,
            tiled=True,
            axis_index_groups=chip_groups,
        )

    down_grad = chip_sum(
        jnp.einsum("tjh,tc->jhc", hidden_low, upstream_all, preferred_element_type=f32)
    )
    up_grad = chip_sum(
        jnp.einsum("tr,tjc->jrc", normed_two_all, up_grad_low, preferred_element_type=f32)
    )
    gate_grad = chip_sum(
        jnp.einsum("tr,tjc->jrc", normed_two_all, gate_grad_low, preferred_element_type=f32)
    )
    norm_two_grad = jnp.einsum("tjc,jrc->tr", up_grad_low, up_weight, preferred_element_type=f32)
    norm_two_grad = norm_two_grad + jnp.einsum(
        "tjc,jrc->tr", gate_grad_low, gate_weight, preferred_element_type=f32
    )
    norm_two_grad = scatter_tokens(norm_two_grad)
    residual_grad = upstream.astype(f32) + norm_back(normed_two, inv_two, norm_two_grad)
    residual_grad_all = gather_seq(residual_grad.astype(bf), 7).reshape(seq_len, width)

    attended_grad = jnp.einsum(
        "tc,rc->tr", residual_grad_all, out_weight, preferred_element_type=f32
    )
    attended_grad = attended_grad.astype(bf).reshape(seq_len, heads, HD)
    value_grad = jnp.einsum("hqk,qhd->khd", prob_low, attended_grad, preferred_element_type=f32)
    prob_grad = jnp.einsum("qhd,khd->hqk", attended_grad, values, preferred_element_type=f32)
    inner_sum = jnp.sum(prob * prob_grad, axis=-1, keepdims=True)
    score_grad = (prob * (prob_grad - inner_sum) * score_scale).astype(bf)
    query_grad = jnp.einsum("hqk,khd->qhd", score_grad, keys, preferred_element_type=f32)
    key_grad = jnp.einsum("hqk,qhd->khd", score_grad, queries, preferred_element_type=f32)
    qkv_grad = jnp.stack(
        [
            rotate_back(query_grad, cosine, sine),
            rotate_back(key_grad, cosine, sine),
            value_grad,
        ],
        axis=1,
    )
    qkv_grad_low = qkv_grad.astype(bf).reshape(seq_len, 3 * head_cols)
    norm_one_part = jnp.einsum("tf,rf->tr", qkv_grad_low, qkv_weight, preferred_element_type=f32)
    norm_one_grad = sum_seq(norm_one_part.astype(bf).reshape(n_seq, shard_len, width), 3)
    input_grad = (residual_grad + norm_back(normed_one, inv_one, norm_one_grad)).reshape(
        block_input.shape
    )

    qkv_wgrad = jnp.einsum(
        "tr,tf->rf", normed_one_all, qkv_grad_low, preferred_element_type=f32
    ).astype(bf)
    out_wgrad = jnp.einsum(
        "tr,tc->rc", attended_low, residual_grad_all, preferred_element_type=f32
    ).astype(bf)
    qkv_piece, out_piece = collect_attention(
        qkv_wgrad.reshape(n_seq, n_dp, sub, 3 * head_cols), out_wgrad.reshape(n_dp, sub, width), 6
    )
    qkv_piece = qkv_piece.reshape(n_dp, n_seq // n_dp, sub, 3, head_cols).transpose(3, 0, 2, 1, 4)
    qkv_piece = qkv_piece.reshape(3, rows, wide)
    out_piece = out_piece.reshape(sub, n_dp, wide).transpose(1, 0, 2).reshape(1, rows, wide)

    up_grad, gate_grad, down_grad, _ = lax.optimization_barrier(
        (up_grad, gate_grad, down_grad, residual_grad_all)
    )
    ug_grad = jnp.concatenate([up_grad, gate_grad], axis=0)
    kept = lax.dynamic_slice_in_dim(ug_grad, core * rows, rows, axis=1)
    sent = lax.dynamic_slice_in_dim(ug_grad, (1 - core) * rows, rows, axis=1)
    got = lax.ppermute(sent, "seq", sibling)
    ug_piece = jnp.where(
        core == 0, jnp.concatenate([kept, got], axis=2), jnp.concatenate([got, kept], axis=2)
    )
    down_piece = down_grad.reshape(ff_blocks, sub, n_dp, wide).transpose(0, 2, 1, 3)
    down_piece = down_piece.reshape(ff_blocks, rows, wide)
    ff_pieces = jnp.concatenate([ug_piece, down_piece], axis=0)

    def give_back(pieces, low_slot, high_slot, skipped):
        units = jnp.maximum(slot_unit[:, low_slot:high_slot] - skipped, 0)
        return lax.all_to_all(jnp.take(pieces, units, axis=0), "dp", 0, 0)

    grads = []
    if per_owner > first_slots:
        grads.append(give_back(ff_pieces, first_slots, per_owner, 4))
    every_piece = jnp.concatenate([qkv_piece, out_piece, ff_pieces], axis=0)
    grads.insert(0, give_back(every_piece, 0, first_slots, 0))
    kinds = jnp.where(own_units < 0, 2, is_col.astype(jnp.int32)).astype(jnp.int32)
    owned_grads, new_first, new_second, new_master = adam(
        kinds, grads, master, first_moment, second_moment, n_dp, n_seq, first_slots
    )
    return (block_output, input_grad, owned_grads, new_first, new_second, new_master)


def solution(mesh):
    placed = (
        P("dp", "seq", None),
        P("dp", "seq", None),
        P("dp", None),
        P(),
        P("seq", "dp", None),
        P("seq", "dp", None),
        P("seq", "dp", None),
    )
    return jax.shard_map(
        local,
        mesh=mesh,
        in_specs=placed,
        out_specs=(
            P("dp", "seq", None),
            P("dp", "seq", None),
            P("seq", "dp", None),
            P("seq", "dp", None),
            P("seq", "dp", None),
            P("seq", "dp", None),
        ),
        check_vma=False,
    )
```

```python
import functools

import jax
import jax.numpy as jnp
from jax import lax
from jax.experimental import pallas as pl
from jax.experimental.pallas import tpu as pltpu
from jax.sharding import PartitionSpec as P

D = 2048
H = 16
HD = 128
FF = 8192
STEP = 5
bf = jnp.bfloat16
f32 = jnp.float32
MESH = pl.DeviceIdType.MESH


norm_eps = 1e-05
rope_base = 10000.0
beta_one = 0.5
beta_two = 0.5
learn_rate = 0.01
decay_rate = 0.1
adam_eps = 1e-08
masked_score = -1000000000.0


def unit_slots(owners, per_owner):
    unit_count = owners.shape[0]
    unit_order = jnp.arange(unit_count, dtype=jnp.int32)
    matching = owners[:, None] == owners[None, :]
    before = unit_order[None, :] < unit_order[:, None]
    places = jnp.sum(jnp.where(matching & before, 1, 0), axis=1).astype(jnp.int32)
    return owners * per_owner + places


def norm_parts(values):
    center = values - jnp.mean(values, axis=-1, keepdims=True)
    spread = jnp.mean(center * center, axis=-1, keepdims=True)
    scale_inv = lax.rsqrt(spread + norm_eps)
    return (center * scale_inv, scale_inv)


def norm_back(normed, scale_inv, upstream):
    upstream_mean = jnp.mean(upstream, axis=-1, keepdims=True)
    cross_mean = jnp.mean(upstream * normed, axis=-1, keepdims=True)
    return scale_inv * (upstream - upstream_mean - normed * cross_mean)


def rope_tables(positions, head_dim):
    half_dim = head_dim // 2
    frequency = jnp.power(rope_base, -(jnp.arange(half_dim, dtype=jnp.float32) * 2.0) / head_dim)
    angles = positions[:, None] * frequency[None, :]
    cosine_half = jnp.cos(angles)
    sine_half = jnp.sin(angles)
    return (
        jnp.concatenate([cosine_half, cosine_half], axis=-1),
        jnp.concatenate([sine_half, sine_half], axis=-1),
    )


def rotate(values, cosine, sine):
    half_dim = values.shape[-1] // 2
    turned = jnp.concatenate([-values[..., half_dim:], values[..., :half_dim]], axis=-1)
    return values * cosine + turned * sine


def rotate_back(grads, cosine, sine):
    half_dim = grads.shape[-1] // 2
    scaled = grads * sine
    turned = jnp.concatenate([scaled[..., half_dim:], -scaled[..., :half_dim]], axis=-1)
    return grads * cosine + turned


def pack_kernel(n_dp, chips, first_slots, flags, m_ref, *outs):
    rb, slots, width = m_ref.shape
    rows, wide = outs[0].shape[2:]
    sub = rows // n_dp
    start = pl.program_id(0) * rb
    target = start // sub
    inner = start % sub
    turned = jnp.swapaxes(m_ref[...], 0, 1).astype(bf)
    for s in range(slots):
        out = outs[0] if s < first_slots else outs[1]
        t = s if s < first_slots else s - first_slots
        x = turned[s]

        @pl.when(flags[s] == 1)
        def _():
            for d in range(n_dp):
                pieces = [
                    x[:, (2 * k + c) * rows + d * sub : (2 * k + c) * rows + (d + 1) * sub]
                    for c in range(2)
                    for k in range(chips)
                ]
                out[d, t, pl.ds(pl.multiple_of(start, rb), rb), :] = jnp.concatenate(pieces, axis=1)

        @pl.when(flags[s] == 0)
        def _():
            for g in range(n_dp):
                out[target, t, pl.ds(pl.multiple_of(g * sub + inner, rb), rb), :] = x[
                    :, g * wide : (g + 1) * wide
                ]


def pack(master, flags, n_dp, n_seq, first_slots):
    rows, slots, width = master.shape
    wide = width // n_dp
    rb = min(32, rows // n_dp)
    counts = [first_slots] + ([slots - first_slots] if slots > first_slots else [])
    return pl.pallas_call(
        functools.partial(pack_kernel, n_dp, n_seq // 2, first_slots),
        out_shape=[jax.ShapeDtypeStruct((n_dp, c, rows, wide), bf) for c in counts],
        grid_spec=pltpu.PrefetchScalarGridSpec(
            num_scalar_prefetch=1,
            grid=(rows // rb,),
            in_specs=[pl.BlockSpec((rb, slots, width), lambda i, f: (i, 0, 0))],
            out_specs=[
                pl.BlockSpec((n_dp, c, rows, wide), lambda i, f: (0, 0, 0, 0)) for c in counts
            ],
        ),
        compiler_params=pltpu.CompilerParams(vmem_limit_bytes=50 << 20),
        name="pack",
    )(flags, master)


def adam_kernel(n_dp, chips, first_slots, n_groups, kinds, *refs):
    cols = refs[:n_groups]
    rws = refs[n_groups : 2 * n_groups]
    m_ref, f_ref, s_ref, keep_ref, g_out, f_out, s_out, m_out, held = refs[2 * n_groups :]
    rb, slots, width = m_ref.shape
    wide = width // n_dp
    rows = width // (2 * chips)
    sub = rows // n_dp
    half = chips * sub
    for s in range(slots):
        group = 0 if s < first_slots else 1
        t = s if group == 0 else s - first_slots

        @pl.when(kinds[s] == 1)
        def _():
            pieces = []
            for i in range(2 * chips):
                k, c = i // 2, i % 2
                for d in range(n_dp):
                    begin = c * half + k * sub
                    pieces.append(cols[group][d, t, :, begin : begin + sub])
            held[s] = jnp.concatenate(pieces, axis=1).astype(f32)

        @pl.when(kinds[s] == 0)
        def _():
            for g in range(n_dp):
                held[s, :, g * wide : (g + 1) * wide] = rws[group][0, t, g, :, :].astype(f32)

        @pl.when(kinds[s] == 2)
        def _():
            held[s] = jnp.zeros((rb, width), f32)

    grad = jnp.swapaxes(held[...], 0, 1)
    keep = keep_ref[...] > 0.0
    g_out[...] = grad
    first = jnp.where(keep, beta_one * f_ref[...] + (1.0 - beta_one) * grad, 0.0)
    f_out[...] = first
    second = jnp.where(keep, beta_two * s_ref[...] + (1.0 - beta_two) * grad * grad, 0.0)
    s_out[...] = second
    fixed_first = first * (1.0 / (1.0 - beta_one**STEP))
    fixed_second = second * (1.0 / (1.0 - beta_two**STEP))
    old = m_ref[...]
    step = fixed_first / (jnp.sqrt(fixed_second) + adam_eps) + decay_rate * old
    m_out[...] = jnp.where(keep, old - learn_rate * step, 0.0)


def adam(kinds, grads, master, first_moment, second_moment, n_dp, n_seq, first_slots):
    rows, slots, width = master.shape
    wide = width // n_dp
    sub = rows // n_dp
    rb = min(16, sub)
    state = pl.BlockSpec((rb, slots, width), lambda i, k: (i, 0, 0))
    cols = [pl.BlockSpec((n_dp, g.shape[1], rb, wide), lambda i, k: (0, 0, i, 0)) for g in grads]
    rws = [
        pl.BlockSpec(
            (1, g.shape[1], n_dp, rb, wide),
            lambda i, k: (i * rb // sub, 0, 0, i % (sub // rb), 0),
        )
        for g in grads
    ]
    keep = jnp.broadcast_to((kinds != 2).astype(f32)[None, :, None], (1, slots, width))
    return pl.pallas_call(
        functools.partial(adam_kernel, n_dp, n_seq // 2, first_slots, len(grads)),
        out_shape=[jax.ShapeDtypeStruct(master.shape, f32)] * 4,
        grid_spec=pltpu.PrefetchScalarGridSpec(
            num_scalar_prefetch=1,
            grid=(rows // rb,),
            in_specs=cols
            + rws
            + [state] * 3
            + [pl.BlockSpec((1, slots, width), lambda i, k: (0, 0, 0))],
            out_specs=[state] * 4,
            scratch_shapes=[pltpu.VMEM((slots, rb, width), f32)],
        ),
        compiler_params=pltpu.CompilerParams(vmem_limit_bytes=50 << 20),
        name="adam",
    )(
        kinds,
        *grads,
        *[g.reshape(n_dp, g.shape[1], n_dp, sub, wide) for g in grads],
        master,
        first_moment,
        second_moment,
        keep,
    )


ANY = pl.BlockSpec(memory_space=pl.ANY)
VMEM = pl.BlockSpec(memory_space=pltpu.VMEM)
DMA = pltpu.SemaphoreType.DMA


def comm_params(collective_id, mib):
    return pltpu.CompilerParams(
        collective_id=collective_id, has_side_effects=True, vmem_limit_bytes=mib << 20
    )


def takes(microseconds):
    return pl.CostEstimate(flops=0, bytes_accessed=int(microseconds * 3e6), transcendentals=0)


def places():
    n_seq = lax.axis_size("seq")
    n_dp = lax.axis_size("dp")
    return n_seq, n_dp, lax.axis_index("seq"), lax.axis_index("dp")


def greet(devices):
    barrier = pltpu.get_barrier_semaphore()
    for device in devices:
        pl.semaphore_signal(barrier, inc=1, device_id=device, device_id_type=MESH)
    pl.semaphore_wait(barrier, len(devices))


def send(src, dst, send_sem, recv_sem, device):
    return pltpu.make_async_remote_copy(
        src_ref=src,
        dst_ref=dst,
        send_sem=send_sem,
        recv_sem=recv_sem,
        device_id=device,
        device_id_type=MESH,
    )


def relay_gather(views, place, count, device_of, send_sem, recv_sem, arrived):
    def leg(view, way, step, block, target):
        ref = views[view](block)
        return send(ref, ref, send_sem.at[view, way, step], recv_sem.at[view, way, step], device_of(target))

    def going(way, step):
        block = place - (step - 1) if way == 0 else place + (step - 1)
        target = place + 1 if way == 0 else place - 1
        inside = (block >= 0) & (block < count) & (target >= 0) & (target < count)
        return block, target, inside

    for step in range(1, count):
        for way in range(2):
            block, target, inside = going(way, step)

            @pl.when(inside)
            def _():
                for view in range(len(views)):
                    leg(view, way, step, block, target).start()

        for way in range(2):
            block = place - step if way == 0 else place + step

            @pl.when((block >= 0) & (block < count))
            def _():
                for view in range(len(views)):
                    leg(view, way, step, block, lax.rem(place + 1, count)).wait_recv()
                arrived(block)

    for step in range(1, count):
        for way in range(2):
            block, target, inside = going(way, step)

            @pl.when(inside)
            def _():
                for view in range(len(views)):
                    leg(view, way, step, block, target).wait_send()


def relay_sum(owns, sent, came, place, count, device_of, send_sem, recv_sem, ready):
    views = range(len(owns))

    def spot(way, block, receiver):
        return jnp.where(block == receiver, count, block) if way else block

    def leg(view, way, block, target, receiver):
        return send(
            sent[view].at[block],
            came[view].at[spot(way, block, receiver)],
            send_sem.at[view, way, block],
            recv_sem.at[view, way, block],
            device_of(target),
        )

    def going(way, step):
        block = count - 1 - step + place if way == 0 else step - (count - 1 - place)
        target = place + 1 if way == 0 else place - 1
        return block, target, (block < count if way == 0 else block >= 0)

    def behind(way):
        return place > 0 if way == 0 else place < count - 1

    for step in range(count - 1):
        for way in range(2):
            block, target, inside = going(way, step)

            @pl.when(inside)
            def _():
                ready(block)
                for view in views:

                    @pl.when(behind(way))
                    def _():
                        leg(view, way, block, target, place).wait_recv()
                        value = owns[view](block) + came[view][block].astype(f32)
                        sent[view][block] = value.astype(sent[view].dtype)

                    @pl.when(jnp.logical_not(behind(way)))
                    def _():
                        sent[view][block] = owns[view](block).astype(sent[view].dtype)

                    leg(view, way, block, target, target).start()

    ready(place)
    for way in range(2):

        @pl.when(behind(way))
        def _():
            for view in views:
                leg(view, way, place, lax.rem(place + 1, count), place).wait_recv()

    totals = []
    for view in views:
        total = owns[view](place)
        for way in range(2):
            value = came[view][place if way == 0 else count].astype(f32)
            total = total + jnp.where(behind(way), value, 0.0)
        totals.append(total)
    for step in range(count - 1):
        for way in range(2):
            block, target, inside = going(way, step)

            @pl.when(inside)
            def _():
                for view in views:
                    leg(view, way, block, target, target).wait_send()

    return totals


def front_kernel(
    packed_ref, x_ref, table_ref, out_ref, own_sem, a_send, a_recv, send_sem, recv_sem, pass_sem, take_sem
):
    n_seq, n_dp, seq_index, dp_index = places()
    chips, chip, core = n_seq // 2, seq_index // 2, lax.rem(seq_index, 2)
    dp_peers = [lax.rem(dp_index + k, n_dp) for k in range(n_dp)]
    chip_peers = [lax.rem(chip + k, chips) for k in range(chips)]
    sibling = (dp_index, chip * 2 + 1 - core)
    greet(
        [(p, seq_index) for p in dp_peers[1:]]
        + [(dp_index, p * 2 + core) for p in chip_peers[1:]]
        + [sibling]
    )
    along = []
    for k in range(1, n_dp):
        copy = send(
            packed_ref.at[dp_peers[k]],
            table_ref.at[dp_index],
            a_send.at[k],
            a_recv.at[k],
            (dp_peers[k], seq_index),
        )
        copy.start()
        along.append(copy)
    own = [
        pltpu.make_async_copy(packed_ref.at[dp_index], table_ref.at[dp_index], own_sem.at[0]),
        pltpu.make_async_copy(x_ref, out_ref.at[seq_index], own_sem.at[1]),
    ]
    for copy in own:
        copy.start()
    spread_blocks(
        x_ref, out_ref, chips, chip, core, dp_index, sibling, send_sem, recv_sem, pass_sem, take_sem
    )
    for copy in along:
        copy.wait()
    for copy in own:
        copy.wait()


def spread_blocks(
    x_ref, out_ref, chips, chip, core, dp_index, sibling, send_sem, recv_sem, pass_sem, take_sem
):
    mine = out_ref.at[chip * 2 + core]
    copies = {}
    for k in range(chips - 1, 0, -1):
        device = (dp_index, lax.rem(chip + k, chips) * 2 + core)
        copies[k] = send(x_ref, mine, send_sem.at[k], recv_sem.at[k], device)
        copies[k].start()
    passed = [send(x_ref, mine, pass_sem.at[0], take_sem.at[0], sibling)]
    passed[0].start()
    for k in range(1, chips):
        copies[k].wait_recv()
        block = out_ref.at[lax.rem(chip + chips - k, chips) * 2 + core]
        onward = send(block, block, pass_sem.at[k], take_sem.at[k], sibling)
        onward.start()
        passed.append(onward)
    for copy in copies.values():
        copy.wait_send()
    for onward in passed:
        onward.wait()


def front(packed, x, collective_id):
    chips = lax.axis_size("seq") // 2
    n_dp = lax.axis_size("dp")
    return pl.pallas_call(
        front_kernel,
        out_shape=[
            jax.ShapeDtypeStruct(packed.shape, packed.dtype),
            jax.ShapeDtypeStruct((2 * chips,) + x.shape, x.dtype),
        ],
        in_specs=[ANY, ANY],
        out_specs=[ANY, ANY],
        scratch_shapes=[DMA((2,)), DMA((n_dp,)), DMA((n_dp,))] + [DMA((chips,))] * 4,
        compiler_params=comm_params(collective_id, 16),
        cost_estimate=takes(90),
        name="front",
    )(packed, x)


def gather_seq_kernel(x_ref, out_ref, own_sem, send_sem, recv_sem, pass_sem, take_sem):
    n_seq, n_dp, seq_index, dp_index = places()
    chips, chip, core = n_seq // 2, seq_index // 2, lax.rem(seq_index, 2)
    chip_peers = [lax.rem(chip + k, chips) for k in range(chips)]
    sibling = (dp_index, chip * 2 + 1 - core)
    greet([(dp_index, p * 2 + core) for p in chip_peers[1:]] + [sibling])
    own = pltpu.make_async_copy(x_ref, out_ref.at[seq_index], own_sem)
    own.start()
    spread_blocks(
        x_ref, out_ref, chips, chip, core, dp_index, sibling, send_sem, recv_sem, pass_sem, take_sem
    )
    own.wait()


def gather_seq(x, collective_id):
    chips = lax.axis_size("seq") // 2
    return pl.pallas_call(
        gather_seq_kernel,
        out_shape=jax.ShapeDtypeStruct((2 * chips,) + x.shape, x.dtype),
        in_specs=[ANY],
        out_specs=ANY,
        scratch_shapes=[DMA] + [DMA((chips,))] * 4,
        compiler_params=comm_params(collective_id, 16),
        cost_estimate=takes(28),
        name="gather_seq",
    )(x)


def gather_dp_kernel(x_ref, out_ref, own_sem, send_sem, recv_sem, pass_sem, take_sem):
    n_seq, n_dp, seq_index, dp_index = places()
    core = lax.rem(seq_index, 2)
    sibling = (dp_index, seq_index + 1 - 2 * core)
    greet([(lax.rem(dp_index + k, n_dp), seq_index) for k in range(1, n_dp)] + [sibling])
    own = pltpu.make_async_copy(x_ref, out_ref.at[core, dp_index], own_sem)
    own.start()
    own.wait()

    def onward(block):
        ref = out_ref.at[core, block]
        return send(ref, ref, pass_sem.at[block], take_sem.at[block], sibling)

    onward(dp_index).start()
    relay_gather(
        [lambda block: out_ref.at[core, block]],
        dp_index,
        n_dp,
        lambda place: (place, seq_index),
        send_sem,
        recv_sem,
        lambda block: onward(block).start(),
    )
    for block in range(n_dp):
        onward(block).wait_send()
        ref = out_ref.at[1 - core, block]
        send(ref, ref, pass_sem.at[block], take_sem.at[block], sibling).wait_recv()


def gather_dp(x, collective_id):
    n_dp = lax.axis_size("dp")
    return pl.pallas_call(
        gather_dp_kernel,
        out_shape=jax.ShapeDtypeStruct((2, n_dp) + x.shape, x.dtype),
        in_specs=[ANY],
        out_specs=ANY,
        scratch_shapes=[DMA, DMA((1, 2, n_dp)), DMA((1, 2, n_dp)), DMA((n_dp,)), DMA((n_dp,))],
        compiler_params=comm_params(collective_id, 16),
        cost_estimate=takes(40),
        name="gather_dp",
    )(x)


def sum_seq_kernel(x_ref, out_ref, taken, sent, arrived, pass_sem, take_sem, send_sem, recv_sem):
    n_seq, n_dp, seq_index, dp_index = places()
    chips, chip, core = n_seq // 2, seq_index // 2, lax.rem(seq_index, 2)
    peers = [lax.rem(chip + k, chips) for k in range(chips)]
    sibling = (dp_index, chip * 2 + 1 - core)
    greet([(dp_index, p * 2 + core) for p in peers[1:]] + [sibling])
    order = list(range(chips - 1, 0, -1)) + [0]
    passed = {}
    for k in order:
        block = x_ref.at[peers[k] * 2 + 1 - core]
        passed[k] = send(block, taken.at[k], pass_sem.at[k], take_sem.at[k], sibling)
        passed[k].start()
    copies = {}
    for k in order[:-1]:
        passed[k].wait_recv()
        own = x_ref[peers[k] * 2 + core].astype(f32)
        sent[k] = (own + taken[k].astype(f32)).astype(sent.dtype)
        device = (dp_index, peers[k] * 2 + core)
        copies[k] = send(sent.at[k], arrived.at[k], send_sem.at[k], recv_sem.at[k], device)
        copies[k].start()
    passed[0].wait_recv()
    total = x_ref[seq_index].astype(f32) + taken[0].astype(f32)
    for k in range(1, chips):
        copies[k].wait_recv()
        total = total + arrived[k].astype(f32)
    out_ref[...] = total
    for k in order:
        passed[k].wait_send()
    for k in order[:-1]:
        copies[k].wait_send()


def sum_seq(x, collective_id):
    blocks, rows, columns = x.shape
    chips = blocks // 2
    slots = pltpu.VMEM((chips, rows, columns), x.dtype)
    return pl.pallas_call(
        sum_seq_kernel,
        out_shape=jax.ShapeDtypeStruct((rows, columns), f32),
        in_specs=[VMEM],
        out_specs=VMEM,
        scratch_shapes=[slots, slots, slots] + [DMA((chips,))] * 4,
        compiler_params=comm_params(collective_id, 40),
        cost_estimate=takes(28),
        name="sum_seq",
    )(x)


def sum_dp_kernel(x_ref, out_ref, taken, sent, came, pass_sem, take_sem, send_sem, recv_sem):
    n_seq, n_dp, seq_index, dp_index = places()
    core = lax.rem(seq_index, 2)
    sibling = (dp_index, seq_index + 1 - 2 * core)
    greet([(lax.rem(dp_index + k, n_dp), seq_index) for k in range(1, n_dp)] + [sibling])

    def onward(block):
        return send(
            x_ref.at[1 - core, block], taken.at[block], pass_sem.at[block], take_sem.at[block], sibling
        )

    half = n_dp // 2
    for block in [b for k in range(half) for b in (n_dp - 1 - k, k)]:
        onward(block).start()
    waited = []

    def ready(block):
        onward(block).wait_recv()

    total = relay_sum(
        [lambda block: x_ref[core, block].astype(f32) + taken[block].astype(f32)],
        [sent],
        [came],
        dp_index,
        n_dp,
        lambda place: (place, seq_index),
        send_sem,
        recv_sem,
        ready,
    )[0]
    out_ref[...] = total
    for block in range(n_dp):
        onward(block).wait_send()


def sum_dp(x, collective_id):
    _, n_dp, rows, columns = x.shape
    return pl.pallas_call(
        sum_dp_kernel,
        out_shape=jax.ShapeDtypeStruct((rows, columns), f32),
        in_specs=[VMEM],
        out_specs=VMEM,
        scratch_shapes=[
            pltpu.VMEM((n_dp, rows, columns), x.dtype),
            pltpu.VMEM((n_dp, rows, columns), x.dtype),
            pltpu.VMEM((n_dp + 1, rows, columns), x.dtype),
            DMA((n_dp,)),
            DMA((n_dp,)),
            DMA((1, 2, n_dp)),
            DMA((1, 2, n_dp)),
        ],
        compiler_params=comm_params(collective_id, 40),
        cost_estimate=takes(40),
        name="sum_dp",
    )(x)


def spread_kernel(
    qkv_ref, out_ref, qkv_all, out_all, own_sem, a_send, a_recv, send_sem, recv_sem
):
    n_seq, n_dp, seq_index, dp_index = places()
    seq_peers = [lax.rem(seq_index + k, n_seq) for k in range(n_seq)]
    greet(
        [(dp_index, p) for p in seq_peers[1:]]
        + [(lax.rem(dp_index + k, n_dp), seq_index) for k in range(1, n_dp)]
    )
    own = [
        pltpu.make_async_copy(qkv_ref.at[seq_index], qkv_all.at[seq_index, dp_index], own_sem.at[0]),
        pltpu.make_async_copy(out_ref, out_all.at[dp_index], own_sem.at[1]),
    ]
    for copy in own:
        copy.start()
    landing = qkv_all.at[seq_index, dp_index]
    across = []
    for k in range(1, n_seq):
        device = (dp_index, seq_peers[k])
        copy = send(qkv_ref.at[seq_peers[k]], landing, a_send.at[k], a_recv.at[k], device)
        copy.start()
        across.append(copy)
    for copy in own:
        copy.wait()
    for copy in across:
        copy.wait_recv()
    relay_gather(
        [lambda block: qkv_all.at[:, block], lambda block: out_all.at[block]],
        dp_index,
        n_dp,
        lambda place: (place, seq_index),
        send_sem,
        recv_sem,
        lambda block: None,
    )
    for copy in across:
        copy.wait_send()


def spread_attention(qkv, out, collective_id):
    n_seq = lax.axis_size("seq")
    n_dp = lax.axis_size("dp")
    return pl.pallas_call(
        spread_kernel,
        out_shape=[
            jax.ShapeDtypeStruct((n_seq, n_dp) + qkv.shape[1:], qkv.dtype),
            jax.ShapeDtypeStruct((n_dp,) + out.shape, out.dtype),
        ],
        in_specs=[ANY, ANY],
        out_specs=[ANY, ANY],
        scratch_shapes=[DMA((2,)), DMA((n_seq,)), DMA((n_seq,)), DMA((2, 2, n_dp)), DMA((2, 2, n_dp))],
        compiler_params=comm_params(collective_id, 16),
        cost_estimate=takes(75),
        name="spread_attention",
    )(qkv, out)


def collect_kernel(
    qkv_ref, out_ref, qkv_sum, out_sum, qkv_sent, qkv_came, out_sent, out_came, total, own_sem,
    send_sem, recv_sem, a_send, a_recv
):
    n_seq, n_dp, seq_index, dp_index = places()
    seq_peers = [lax.rem(seq_index + k, n_seq) for k in range(n_seq)]
    greet(
        [(dp_index, p) for p in seq_peers[1:]]
        + [(lax.rem(dp_index + k, n_dp), seq_index) for k in range(1, n_dp)]
    )
    sums = relay_sum(
        [lambda block: qkv_ref[:, block].astype(f32), lambda block: out_ref[block].astype(f32)],
        [qkv_sent, out_sent],
        [qkv_came, out_came],
        dp_index,
        n_dp,
        lambda place: (place, seq_index),
        send_sem,
        recv_sem,
        lambda block: None,
    )
    total[...] = sums[0].astype(total.dtype)
    across = []
    for k in range(1, n_seq):
        copy = send(
            total.at[seq_peers[k]],
            qkv_sum.at[seq_index],
            a_send.at[k],
            a_recv.at[k],
            (dp_index, seq_peers[k]),
        )
        copy.start()
        across.append(copy)
    own = pltpu.make_async_copy(total.at[seq_index], qkv_sum.at[seq_index], own_sem)
    own.start()
    out_sum[...] = sums[1].astype(out_sum.dtype)
    for copy in across:
        copy.wait()
    own.wait()


def collect_attention(qkv, out, collective_id):
    n_seq = lax.axis_size("seq")
    n_dp = lax.axis_size("dp")
    tail = qkv.shape[2:]
    return pl.pallas_call(
        collect_kernel,
        out_shape=[
            jax.ShapeDtypeStruct((n_seq,) + tail, qkv.dtype),
            jax.ShapeDtypeStruct(out.shape[1:], out.dtype),
        ],
        in_specs=[VMEM, VMEM],
        out_specs=[VMEM, VMEM],
        scratch_shapes=[
            pltpu.VMEM((n_dp, n_seq) + tail, qkv.dtype),
            pltpu.VMEM((n_dp + 1, n_seq) + tail, qkv.dtype),
            pltpu.VMEM((n_dp,) + out.shape[1:], out.dtype),
            pltpu.VMEM((n_dp + 1,) + out.shape[1:], out.dtype),
            pltpu.VMEM((n_seq,) + tail, qkv.dtype),
            DMA,
            DMA((2, 2, n_dp)),
            DMA((2, 2, n_dp)),
            DMA((n_seq,)),
            DMA((n_seq,)),
        ],
        compiler_params=comm_params(collective_id, 48),
        cost_estimate=takes(75),
        name="collect_attention",
    )(qkv, out)


def ring_chip(place, chips):
    return jnp.where(place < chips // 2, 2 * place, 2 * (chips - 1 - place) + 1)


def ring_place(chip, chips):
    line = chip // 2
    return jnp.where(lax.rem(chip, 2) == 0, line, chips - 1 - line)


class Ring:
    def __init__(self, chips, chip, core, dp_index, send_sem, recv_sem):
        self.chips = chips
        self.place = ring_place(chip, chips)
        self.core = core
        self.dp_index = dp_index
        self.send_sem = send_sem
        self.recv_sem = recv_sem
        self.last = chips // 2

    def at(self, offset):
        return ring_chip(lax.rem(self.place + offset + self.chips, self.chips), self.chips)

    def device(self, way):
        return (self.dp_index, self.at(1 if way == 0 else -1) * 2 + self.core)

    def leg(self, view, way, step, src, dst):
        return send(
            src, dst, self.send_sem.at[view, way, step], self.recv_sem.at[view, way, step], self.device(way)
        )


def ring_gather_leg(ring, views, view, way, step, arriving):
    distance = step if arriving else step - 1
    block = ring.at(-distance if way == 0 else distance)
    ref = views[view](block, way if step == ring.last else None)
    return ring.leg(view, way, step - 1, ref, ref)


def pick_kernel(first_slots, ff_blocks, info, first_ref, *refs):
    late_ref = refs[0] if len(refs) == 5 else None
    mine_ref, given_ref, down_ref, piece_ref = refs[-4:]
    unit = pl.program_id(0)
    rows, wide = piece_ref.shape
    half = wide // 2
    sub, width = down_ref.shape[1:]
    groups = width // wide

    @pl.when(info[2, unit] == 0)
    def _():
        piece_ref[...] = first_ref[0]

    if late_ref is not None:

        @pl.when(info[2, unit] != 0)
        def _():
            piece_ref[...] = late_ref[0]

    @pl.when(unit < 2 * ff_blocks)
    def _():
        @pl.when(info[3, 0] == 0)
        def _():
            mine_ref[0] = piece_ref[:, :half]
            given_ref[0] = piece_ref[:, half:]

        @pl.when(info[3, 0] != 0)
        def _():
            mine_ref[0] = piece_ref[:, half:]
            given_ref[0] = piece_ref[:, :half]

    @pl.when(unit >= 2 * ff_blocks)
    def _():
        for g in range(groups):
            down_ref[0, :, g * wide : (g + 1) * wide] = piece_ref[g * sub : (g + 1) * sub, :]


def pick_ff(first_table, late_table, owners, place, core, ff_blocks, sub, first_slots):
    rows, wide = first_table.shape[1:]
    width = rows // sub * wide
    units = 3 * ff_blocks
    owners, place = owners[4:], place[4:]
    in_late = place >= first_slots
    late_slots = 1 if late_table is None else late_table.shape[0] // lax.axis_size("dp")
    info = jnp.stack(
        [
            owners * first_slots + jnp.minimum(place, first_slots - 1),
            owners * late_slots + jnp.maximum(place - first_slots, 0),
            in_late.astype(jnp.int32),
            jnp.full((units,), core, jnp.int32),
        ]
    ).astype(jnp.int32)
    tables = [first_table] if late_table is None else [first_table, late_table]
    specs = [
        pl.BlockSpec((1, rows, wide), lambda u, info: (info[0, u], 0, 0)),
        pl.BlockSpec((1, rows, wide), lambda u, info: (info[1, u], 0, 0)),
    ]
    side = pl.BlockSpec(
        (1, rows, wide // 2), lambda u, info: (jnp.minimum(u, 2 * ff_blocks - 1), 0, 0)
    )
    return pl.pallas_call(
        functools.partial(pick_kernel, first_slots, ff_blocks),
        out_shape=[
            jax.ShapeDtypeStruct((2 * ff_blocks, rows, wide // 2), bf),
            jax.ShapeDtypeStruct((2 * ff_blocks, rows, wide // 2), bf),
            jax.ShapeDtypeStruct((ff_blocks, sub, width), bf),
        ],
        grid_spec=pltpu.PrefetchScalarGridSpec(
            num_scalar_prefetch=1,
            grid=(units,),
            in_specs=specs[: len(tables)],
            out_specs=[
                side,
                side,
                pl.BlockSpec(
                    (1, sub, width), lambda u, info: (jnp.maximum(u - 2 * ff_blocks, 0), 0, 0)
                ),
            ],
            scratch_shapes=[pltpu.VMEM((rows, wide), bf)],
        ),
        compiler_params=pltpu.CompilerParams(vmem_limit_bytes=16 << 20),
        cost_estimate=takes(6),
        name="pick_ff",
    )(info, *tables)


def pick_attention_kernel(info, piece_ref, rows_ref, out_ref):
    unit = pl.program_id(0)
    blocks, sub, columns = rows_ref.shape
    step = columns // 3
    groups = out_ref.shape[1] // piece_ref.shape[2]
    wide = piece_ref.shape[2]
    share = wide // step
    for u in range(3):

        @pl.when(unit == u)
        def _():
            for block in range(blocks):
                g, h = block // share, block % share
                rows_ref[block, :, u * step : (u + 1) * step] = piece_ref[
                    0, g * sub : (g + 1) * sub, h * step : (h + 1) * step
                ]

    @pl.when(unit == 3)
    def _():
        for g in range(groups):
            out_ref[:, g * wide : (g + 1) * wide] = piece_ref[0, g * sub : (g + 1) * sub, :]


def pick_attention(first_table, index, n_seq, sub, width):
    rows, wide = first_table.shape[1:]
    columns = 3 * (width // n_seq)
    return pl.pallas_call(
        pick_attention_kernel,
        out_shape=[
            jax.ShapeDtypeStruct((n_seq, sub, columns), bf),
            jax.ShapeDtypeStruct((sub, width), bf),
        ],
        grid_spec=pltpu.PrefetchScalarGridSpec(
            num_scalar_prefetch=1,
            grid=(4,),
            in_specs=[pl.BlockSpec((1, rows, wide), lambda u, info: (info[u], 0, 0))],
            out_specs=[
                pl.BlockSpec((n_seq, sub, columns), lambda u, info: (0, 0, 0)),
                pl.BlockSpec((sub, width), lambda u, info: (0, 0)),
            ],
        ),
        compiler_params=pltpu.CompilerParams(vmem_limit_bytes=16 << 20),
        cost_estimate=takes(3),
        name="pick_attention",
    )(index.astype(jnp.int32), first_table)


def arrange_kernel(ff_blocks, units, ug_ref, down_ref, *refs):
    piece_ref = refs[-1]
    unit = units[pl.program_id(0)]
    rows, wide = piece_ref.shape[1:]
    sub, width = down_ref.shape[1:]
    groups = width // wide

    @pl.when((unit >= 4) & (unit < 4 + 2 * ff_blocks))
    def _():
        piece_ref[0] = ug_ref[0]

    @pl.when(unit >= 4 + 2 * ff_blocks)
    def _():
        for g in range(groups):
            piece_ref[0, g * sub : (g + 1) * sub, :] = down_ref[0, :, g * wide : (g + 1) * wide]

    if len(refs) == 3:
        qkv_ref, out_ref = refs[:2]
        blocks, _, columns = qkv_ref.shape
        step = columns // 3
        share = wide // step
        for u in range(3):

            @pl.when(unit == u)
            def _():
                for block in range(blocks):
                    g, h = block // share, block % share
                    piece_ref[0, g * sub : (g + 1) * sub, h * step : (h + 1) * step] = qkv_ref[
                        block, :, u * step : (u + 1) * step
                    ]

        @pl.when(unit == 3)
        def _():
            for g in range(groups):
                piece_ref[0, g * sub : (g + 1) * sub, :] = out_ref[:, g * wide : (g + 1) * wide]


def arrange(units, ug, down, attention):
    n_dp, slots = units.shape
    rows, wide = ug.shape[1:]
    sub, width = down.shape[1:]
    ff_blocks = down.shape[0]
    specs = [
        pl.BlockSpec(
            (1, rows, wide), lambda k, u: (jnp.clip(u[k] - 4, 0, 2 * ff_blocks - 1), 0, 0)
        ),
        pl.BlockSpec(
            (1, sub, width),
            lambda k, u: (jnp.clip(u[k] - 4 - 2 * ff_blocks, 0, ff_blocks - 1), 0, 0),
        ),
    ]
    if attention:
        specs.append(pl.BlockSpec(attention[0].shape, lambda k, u: (0, 0, 0)))
        specs.append(pl.BlockSpec(attention[1].shape, lambda k, u: (0, 0)))
    return pl.pallas_call(
        functools.partial(arrange_kernel, ff_blocks),
        out_shape=jax.ShapeDtypeStruct((n_dp * slots, rows, wide), bf),
        grid_spec=pltpu.PrefetchScalarGridSpec(
            num_scalar_prefetch=1,
            grid=(n_dp * slots,),
            in_specs=specs,
            out_specs=pl.BlockSpec((1, rows, wide), lambda k, u: (k, 0, 0)),
        ),
        compiler_params=pltpu.CompilerParams(vmem_limit_bytes=16 << 20),
        cost_estimate=takes(7),
        name="arrange",
    )(units.reshape(-1), ug, down, *attention).reshape(n_dp, slots, rows, wide)


def weights_kernel(
    mine_ref, given_ref, down_ref, x_ref, cot_ref, ug_all, down_all, x_all, cot_all,
    own_sem, side_send, side_recv, ring_send, ring_recv, send_sem, recv_sem, pass_sem, take_sem
):
    n_seq, n_dp, seq_index, dp_index = places()
    chips, chip, core = n_seq // 2, seq_index // 2, lax.rem(seq_index, 2)
    sibling = (dp_index, chip * 2 + 1 - core)
    ring = Ring(chips, chip, core, dp_index, ring_send, ring_recv)
    blocks = down_ref.shape[0]
    greet(
        [(lax.rem(dp_index + k, n_dp), seq_index) for k in range(1, n_dp)]
        + [sibling, ring.device(0), ring.device(1)]
    )
    sides = [
        send(
            given_ref.at[pl.ds(k * blocks, blocks)],
            ug_all.at[pl.ds(k * blocks, blocks), chip, core],
            side_send.at[k],
            side_recv.at[k],
            sibling,
        )
        for k in range(2)
    ]
    sides.append(send(cot_ref, cot_all.at[core], side_send.at[2], side_recv.at[2], sibling))
    own = [
        pltpu.make_async_copy(x_ref, x_all.at[core, dp_index], own_sem.at[0]),
        pltpu.make_async_copy(down_ref, down_all.at[:, chip], own_sem.at[1]),
        pltpu.make_async_copy(mine_ref, ug_all.at[:, chip, core], own_sem.at[2]),
        pltpu.make_async_copy(cot_ref, cot_all.at[core], own_sem.at[3]),
    ]
    for copy in sides + own:
        copy.start()

    def part_of(base, part):
        if part is None:
            return pl.ds(base, blocks)
        return pl.ds(base + part * (blocks // 2), blocks // 2)

    views = [
        lambda block, part: down_all.at[part_of(0, part), block],
        lambda block, part: ug_all.at[part_of(0, part), block],
        lambda block, part: ug_all.at[part_of(blocks, part), block],
    ]
    for copy in own:
        copy.wait()
    for view in range(3):
        if view:
            sides[view - 1].wait_recv()
        for way in range(2):
            ring_gather_leg(ring, views, view, way, 1, False).start()

    def onward(block):
        ref = x_all.at[core, block]
        return send(ref, ref, pass_sem.at[block], take_sem.at[block], sibling)

    onward(dp_index).start()
    relay_gather(
        [lambda block: x_all.at[core, block]],
        dp_index,
        n_dp,
        lambda place: (place, seq_index),
        send_sem,
        recv_sem,
        lambda block: onward(block).start(),
    )
    for step in range(2, ring.last + 1):
        for view in range(3):
            for way in range(2):
                ring_gather_leg(ring, views, view, way, step - 1, True).wait_recv()
                ring_gather_leg(ring, views, view, way, step, False).start()
    for view in range(3):
        for way in range(2):
            ring_gather_leg(ring, views, view, way, ring.last, True).wait_recv()
    for step in range(1, ring.last + 1):
        for view in range(3):
            for way in range(2):
                ring_gather_leg(ring, views, view, way, step, False).wait_send()
    for block in range(n_dp):
        onward(block).wait_send()
        ref = x_all.at[1 - core, block]
        send(ref, ref, pass_sem.at[block], take_sem.at[block], sibling).wait_recv()
    for copy in sides:
        copy.wait_send()
    ref = cot_all.at[1 - core]
    send(ref, ref, side_send.at[2], side_recv.at[2], sibling).wait_recv()


def gather_weights(mine, given, down, x, cot, collective_id):
    n_dp = lax.axis_size("dp")
    chips = lax.axis_size("seq") // 2
    units, rows, half = mine.shape
    blocks, sub, width = down.shape
    steps = chips // 2
    return pl.pallas_call(
        weights_kernel,
        out_shape=[
            jax.ShapeDtypeStruct((units, chips, 2, rows, half), bf),
            jax.ShapeDtypeStruct((blocks, chips, sub, width), bf),
            jax.ShapeDtypeStruct((2, n_dp) + x.shape, bf),
            jax.ShapeDtypeStruct((2,) + cot.shape, bf),
        ],
        in_specs=[ANY] * 5,
        out_specs=[ANY] * 4,
        scratch_shapes=[
            DMA((4,)),
            DMA((3,)),
            DMA((3,)),
            DMA((3, 2, steps)),
            DMA((3, 2, steps)),
            DMA((1, 2, n_dp)),
            DMA((1, 2, n_dp)),
            DMA((n_dp,)),
            DMA((n_dp,)),
        ],
        compiler_params=comm_params(collective_id, 16),
        cost_estimate=takes(100),
        name="gather_weights",
    )(mine, given, down, x, cot)


def grads_kernel(
    up_ref, gate_ref, down_ref, x_ref, y_ref, ug_out, down_out, x_out, y_out, *refs
):
    half_came, full_sent, full_came, mine = refs[0:3], refs[3:6], refs[6:9], refs[9:12]
    side_out, x_taken, y_taken, z_sent, z_came = refs[12:17]
    ring_send, ring_recv, z_send, z_recv, x_pass, x_take, y_pass, y_take = refs[17:25]
    side_send, side_recv, own_sem = refs[25:]
    n_seq, n_dp, seq_index, dp_index = places()
    chips, chip, core = n_seq // 2, seq_index // 2, lax.rem(seq_index, 2)
    sibling = (dp_index, chip * 2 + 1 - core)
    ring = Ring(chips, chip, core, dp_index, ring_send, ring_recv)
    owns = [down_ref, up_ref, gate_ref]
    blocks = down_ref.shape[0]
    pair = blocks // 2
    half = up_ref.shape[-1]
    greet(
        [(lax.rem(dp_index + k, n_dp), seq_index) for k in range(1, n_dp)]
        + [sibling, ring.device(0), ring.device(1)]
    )

    def leg(view, way, step):
        if step == 0:
            src = owns[view].at[pl.ds(way * pair, pair), ring.at(ring.last)]
            return ring.leg(view, way, step, src, half_came[view].at[way])
        src, dst = full_sent[view].at[step - 1, way], full_came[view].at[step - 1, way]
        return ring.leg(view, way, step, src, dst)

    def own_copy(view, way, step):
        distance = ring.last - step
        if step == ring.last:
            return pltpu.make_async_copy(
                owns[view].at[:, chip], mine[view], own_sem.at[view, 0, step - 1]
            )
        src = owns[view].at[:, ring.at(distance if way == 0 else -distance)]
        return pltpu.make_async_copy(
            src, full_sent[view].at[step - 1, way], own_sem.at[view, way, step - 1]
        )

    for view in range(3):
        for way in range(2):
            leg(view, way, 0).start()
    for step in range(1, ring.last + 1):
        for view in range(3):
            for way in range(2 if step < ring.last else 1):
                own_copy(view, way, step).start()

    def column_sum(ref, taken, out, pass_sem, take_sem, z):
        def onward(block):
            return send(
                ref.at[1 - core, block], taken.at[block], pass_sem.at[block], take_sem.at[block], sibling
            )

        for block in [b for k in range(n_dp // 2) for b in (n_dp - 1 - k, k)]:
            onward(block).start()
        total = relay_sum(
            [lambda block: ref[core, block].astype(f32) + taken[block].astype(f32)],
            [z_sent.at[z]],
            [z_came.at[z]],
            dp_index,
            n_dp,
            lambda place: (place, seq_index),
            z_send.at[z],
            z_recv.at[z],
            lambda block: onward(block).wait_recv(),
        )[0]
        out[...] = total
        for block in range(n_dp):
            onward(block).wait_send()

    def ring_step(step):
        for view in range(3):
            for way in range(2):
                own_copy(view, way, step).wait()
                leg(view, way, step - 1).wait_recv()
                for k in range(blocks) if step > 1 else range(way * pair, (way + 1) * pair):
                    value = full_sent[view][step - 1, way, k].astype(f32)
                    if step > 1:
                        value = value + full_came[view][step - 2, way, k].astype(f32)
                    else:
                        value = value + half_came[view][way, k - way * pair].astype(f32)
                    full_sent[view][step - 1, way, k] = value.astype(bf)
                leg(view, way, step).start()

    column_sum(x_ref, x_taken, x_out, x_pass, x_take, 0)
    for step in range(1, ring.last):
        ring_step(step)
    column_sum(y_ref, y_taken, y_out, y_pass, y_take, 1)
    for view in range(3):
        own_copy(view, 0, ring.last).wait()
        for way in range(2):
            leg(view, way, ring.last - 1).wait_recv()
        for k in range(blocks):
            if ring.last > 1:
                came = full_came[view]
                sums = [came[ring.last - 2, way, k].astype(f32) for way in range(2)]
                value = mine[view][k].astype(f32) + sums[0] + sums[1]
            else:
                came = half_came[view][k // pair, k % pair].astype(f32)
                value = mine[view][k].astype(f32) + came
            value = value.astype(bf)
            if view == 0:
                down_out[k] = value
            else:
                unit = (view - 1) * blocks + k

                @pl.when(core == 0)
                def _():
                    ug_out[unit, :, :half] = value[0]
                    side_out[unit] = value[1]

                @pl.when(core != 0)
                def _():
                    ug_out[unit, :, half:] = value[1]
                    side_out[unit] = value[0]

    place = pl.ds(pl.multiple_of(core * half, half), half)
    side = send(side_out, ug_out.at[:, :, place], side_send, side_recv, sibling)
    side.start()
    side.wait()
    for step in range(ring.last):
        for view in range(3):
            for way in range(2):
                leg(view, way, step).wait_send()


def sum_grads(up, gate, down, x, y, collective_id):
    blocks, chips, _, rows, half = up.shape
    _, _, sub, width = down.shape
    _, n_dp, tokens, _ = x.shape
    steps = chips // 2
    side = (2, rows, half)
    vmem = pltpu.VMEM
    return pl.pallas_call(
        grads_kernel,
        out_shape=[
            jax.ShapeDtypeStruct((2 * blocks, rows, 2 * half), bf),
            jax.ShapeDtypeStruct((blocks, sub, width), bf),
            jax.ShapeDtypeStruct((tokens, width), f32),
            jax.ShapeDtypeStruct((tokens, width), f32),
        ],
        in_specs=[ANY] * 3 + [VMEM] * 2,
        out_specs=[VMEM] * 4,
        scratch_shapes=[vmem((2, blocks // 2) + s, bf) for s in ((sub, width), side, side)]
        + [vmem((max(steps - 1, 1), 2, blocks) + s, bf) for s in ((sub, width), side, side)] * 2
        + [vmem((blocks,) + s, bf) for s in ((sub, width), side, side)]
        + [
            vmem((2 * blocks, rows, half), bf),
            vmem((n_dp, tokens, width), bf),
            vmem((n_dp, tokens, width), bf),
            vmem((2, n_dp, tokens, width), bf),
            vmem((2, n_dp + 1, tokens, width), bf),
            DMA((3, 2, steps)),
            DMA((3, 2, steps)),
            DMA((2, 1, 2, n_dp)),
            DMA((2, 1, 2, n_dp)),
            DMA((n_dp,)),
            DMA((n_dp,)),
            DMA((n_dp,)),
            DMA((n_dp,)),
            DMA,
            DMA,
            DMA((3, 2, steps)),
        ],
        compiler_params=comm_params(collective_id, 58),
        cost_estimate=takes(120),
        name="sum_grads",
    )(up, gate, down, x, y)


def local(block_input, cotangent, doc_lengths, owners, master, first_moment, second_moment):
    n_seq = lax.axis_size("seq")
    n_dp = lax.axis_size("dp")
    seq_index = lax.axis_index("seq")
    dp_index = lax.axis_index("dp")
    core = seq_index % 2
    _, shard_len, width = block_input.shape
    rows = master.shape[0]
    per_owner = master.shape[1]
    chips = n_seq // 2
    sub = rows // n_dp
    wide = width // n_dp
    half = chips * sub
    heads = H // n_seq
    head_cols = heads * HD
    seq_len = shard_len * n_seq
    ff_blocks = FF // D
    first_slots = min(4, per_owner)
    unit_count = owners.shape[0]
    score_scale = float(HD) ** (-0.5)

    unit_slot = unit_slots(owners, per_owner)
    place = unit_slot - owners * per_owner
    all_slots = jnp.arange(n_dp * per_owner, dtype=jnp.int32)
    match = unit_slot[None, :] == all_slots[:, None]
    slot_unit = jnp.sum(
        jnp.where(match, jnp.arange(unit_count, dtype=jnp.int32)[None, :] + 1, 0), axis=1
    ) - 1
    slot_unit = slot_unit.reshape(n_dp, per_owner)
    own_units = lax.dynamic_index_in_dim(slot_unit, dp_index, 0, keepdims=False)
    is_col = (own_units >= 4) & (own_units < 4 + 2 * ff_blocks)


    tokens = block_input.astype(f32).reshape(shard_len, width)
    normed_one, inv_one = norm_parts(tokens)
    packed = pack(master, is_col.astype(jnp.int32), n_dp, n_seq, first_slots)
    first_table, normed_one_all = front(packed[0], normed_one.astype(bf), 2)
    first_table = first_table.reshape(n_dp * first_slots, rows, wide)
    normed_one_all = normed_one_all.reshape(seq_len, width)
    att_rows, att_out = pick_attention(
        first_table, (owners * first_slots + place)[:4], n_seq, sub, width
    )
    qkv_weight, out_weight = spread_attention(att_rows, att_out, 1)
    if per_owner > first_slots:
        late, qkv_weight = lax.optimization_barrier((packed[1], qkv_weight))
        late = lax.all_to_all(late, "dp", 0, 0)
    qkv_weight = qkv_weight.reshape(width, 3 * head_cols)
    out_weight = out_weight.reshape(rows, width)

    qkv_proj = jnp.dot(normed_one_all, qkv_weight, preferred_element_type=f32)
    qkv_proj = qkv_proj.reshape(seq_len, 3, heads, HD)
    positions = jnp.arange(seq_len, dtype=jnp.int32)
    cosine, sine = rope_tables(positions.astype(f32), HD)
    cosine = cosine[:, None, :]
    sine = sine[:, None, :]
    queries = rotate(qkv_proj[:, 0], cosine, sine).astype(bf)
    keys = rotate(qkv_proj[:, 1], cosine, sine).astype(bf)
    values = qkv_proj[:, 2].astype(bf)
    doc_ends = jnp.cumsum(doc_lengths[0])
    doc = jnp.sum((positions[:, None] >= doc_ends[None, :]).astype(jnp.int32), axis=1)
    allowed = (doc[:, None] == doc[None, :]) & (positions[None, :] <= positions[:, None])
    scores = jnp.einsum("qhd,khd->hqk", queries, keys, preferred_element_type=f32) * score_scale
    scores = jnp.where(allowed[None], scores, masked_score)
    peak = jnp.max(scores, axis=-1, keepdims=True)
    raised = jnp.exp(scores - peak)
    prob = raised / jnp.sum(raised, axis=-1, keepdims=True)
    prob_low = prob.astype(bf)
    attended = jnp.einsum("hqk,khd->qhd", prob_low, values, preferred_element_type=f32)
    attended_low = attended.reshape(seq_len, head_cols).astype(bf)
    attn_part = jnp.dot(attended_low, out_weight, preferred_element_type=f32).astype(bf)
    attn_out = sum_seq(attn_part.reshape(n_seq, shard_len, width), 3)
    residual = tokens + attn_out
    normed_two, inv_two = norm_parts(residual)

    upstream = cotangent.reshape(shard_len, width)
    upstream_column = lax.all_gather(upstream, "dp", axis=0)
    if per_owner > first_slots:
        late, normed_two = lax.optimization_barrier((late, normed_two))
        late = late.reshape(-1, rows, wide)
    else:
        late = None
    mine, given, down = pick_ff(
        first_table, late, owners, place, core, ff_blocks, sub, first_slots
    )
    ug_weight, down_weight, normed_two_all, upstream_all = gather_weights(
        mine, given, down, normed_two.astype(bf), upstream_column, 4
    )
    up_weight = ug_weight[:ff_blocks].reshape(ff_blocks, width, half)
    gate_weight = ug_weight[ff_blocks:].reshape(ff_blocks, width, half)
    down_weight = down_weight.reshape(ff_blocks, half, width)
    normed_two_all = normed_two_all.reshape(-1, width)
    upstream_all = upstream_all.reshape(-1, width)
    up_proj = jnp.einsum("tr,jrc->tjc", normed_two_all, up_weight, preferred_element_type=f32)
    gate_proj = jnp.einsum("tr,jrc->tjc", normed_two_all, gate_weight, preferred_element_type=f32)
    gate_sig = jax.nn.sigmoid(gate_proj)
    silu_value = gate_proj * gate_sig
    hidden_low = (silu_value * up_proj).astype(bf)
    ff_part = jnp.einsum("tjh,jhc->tc", hidden_low, down_weight, preferred_element_type=f32)
    hidden_grad = jnp.einsum("tc,jhc->tjh", upstream_all, down_weight, preferred_element_type=f32)
    up_grad_low = (hidden_grad * silu_value).astype(bf)
    gate_grad_low = (
        hidden_grad * up_proj * (gate_sig + gate_proj * gate_sig * (1.0 - gate_sig))
    ).astype(bf)

    down_grad = jnp.einsum(
        "tjh,tc->jhc", hidden_low, upstream_all, preferred_element_type=f32
    ).astype(bf)
    up_grad = jnp.einsum(
        "tr,tjc->jrc", normed_two_all, up_grad_low, preferred_element_type=f32
    ).astype(bf)
    gate_grad = jnp.einsum(
        "tr,tjc->jrc", normed_two_all, gate_grad_low, preferred_element_type=f32
    ).astype(bf)
    norm_two_grad = jnp.einsum("tjc,jrc->tr", up_grad_low, up_weight, preferred_element_type=f32)
    norm_two_grad = norm_two_grad + jnp.einsum(
        "tjc,jrc->tr", gate_grad_low, gate_weight, preferred_element_type=f32
    )
    side = (ff_blocks, chips, 2, rows, half)
    column = (2, n_dp, shard_len, width)
    ug_piece, down_piece, norm_two_grad, ff_out = sum_grads(
        up_grad.reshape(side),
        gate_grad.reshape(side),
        down_grad.reshape(ff_blocks, chips, sub, width),
        norm_two_grad.astype(bf).reshape(column),
        ff_part.astype(bf).reshape(column),
        5,
    )
    block_output = (residual + ff_out).astype(bf).reshape(block_input.shape)
    grads = []
    if per_owner > first_slots:
        late = arrange(slot_unit[:, first_slots:], ug_piece, down_piece, ())
        grads.append(lax.all_to_all(late, "dp", 0, 0))
    residual_grad = upstream.astype(f32) + norm_back(normed_two, inv_two, norm_two_grad)
    residual_grad_all = gather_seq(residual_grad.astype(bf), 7).reshape(seq_len, width)

    attended_grad = jnp.einsum(
        "tc,rc->tr", residual_grad_all, out_weight, preferred_element_type=f32
    )
    attended_grad = attended_grad.astype(bf).reshape(seq_len, heads, HD)
    value_grad = jnp.einsum("hqk,qhd->khd", prob_low, attended_grad, preferred_element_type=f32)
    prob_grad = jnp.einsum("qhd,khd->hqk", attended_grad, values, preferred_element_type=f32)
    inner_sum = jnp.sum(prob * prob_grad, axis=-1, keepdims=True)
    score_grad = (prob * (prob_grad - inner_sum) * score_scale).astype(bf)
    query_grad = jnp.einsum("hqk,khd->qhd", score_grad, keys, preferred_element_type=f32)
    key_grad = jnp.einsum("hqk,qhd->khd", score_grad, queries, preferred_element_type=f32)
    qkv_grad = jnp.stack(
        [
            rotate_back(query_grad, cosine, sine),
            rotate_back(key_grad, cosine, sine),
            value_grad,
        ],
        axis=1,
    )
    qkv_grad_low = qkv_grad.astype(bf).reshape(seq_len, 3 * head_cols)
    norm_one_part = jnp.einsum("tf,rf->tr", qkv_grad_low, qkv_weight, preferred_element_type=f32)
    norm_one_grad = sum_seq(norm_one_part.astype(bf).reshape(n_seq, shard_len, width), 3)
    input_grad = (residual_grad + norm_back(normed_one, inv_one, norm_one_grad)).reshape(
        block_input.shape
    )

    qkv_wgrad = jnp.einsum(
        "tr,tf->rf", normed_one_all, qkv_grad_low, preferred_element_type=f32
    ).astype(bf)
    out_wgrad = jnp.einsum(
        "tr,tc->rc", attended_low, residual_grad_all, preferred_element_type=f32
    ).astype(bf)
    qkv_piece, out_piece = collect_attention(
        qkv_wgrad.reshape(n_seq, n_dp, sub, 3 * head_cols), out_wgrad.reshape(n_dp, sub, width), 6
    )
    early = arrange(slot_unit[:, :first_slots], ug_piece, down_piece, (qkv_piece, out_piece))
    grads.insert(0, lax.all_to_all(early, "dp", 0, 0))
    kinds = jnp.where(own_units < 0, 2, is_col.astype(jnp.int32)).astype(jnp.int32)
    owned_grads, new_first, new_second, new_master = adam(
        kinds, grads, master, first_moment, second_moment, n_dp, n_seq, first_slots
    )
    return (block_output, input_grad, owned_grads, new_first, new_second, new_master)


def solution(mesh):
    placed = (
        P("dp", "seq", None),
        P("dp", "seq", None),
        P("dp", None),
        P(),
        P("seq", "dp", None),
        P("seq", "dp", None),
        P("seq", "dp", None),
    )
    return jax.shard_map(
        local,
        mesh=mesh,
        in_specs=placed,
        out_specs=(
            P("dp", "seq", None),
            P("dp", "seq", None),
            P("seq", "dp", None),
            P("seq", "dp", None),
            P("seq", "dp", None),
            P("seq", "dp", None),
        ),
        check_vma=False,
    )
```

```python
import functools

import jax
import jax.numpy as jnp
from jax import lax
from jax.experimental import pallas as pl
from jax.experimental.pallas import tpu as pltpu
from jax.sharding import PartitionSpec as P

D = 2048
H = 16
HD = 128
FF = 8192
STEP = 5
bf = jnp.bfloat16
f32 = jnp.float32
MESH = pl.DeviceIdType.MESH


norm_eps = 1e-05
rope_base = 10000.0
beta_one = 0.5
beta_two = 0.5
learn_rate = 0.01
decay_rate = 0.1
adam_eps = 1e-08
masked_score = -1000000000.0


def unit_slots(owners, per_owner):
    unit_count = owners.shape[0]
    unit_order = jnp.arange(unit_count, dtype=jnp.int32)
    matching = owners[:, None] == owners[None, :]
    before = unit_order[None, :] < unit_order[:, None]
    places = jnp.sum(jnp.where(matching & before, 1, 0), axis=1).astype(jnp.int32)
    return owners * per_owner + places


def norm_parts(values):
    center = values - jnp.mean(values, axis=-1, keepdims=True)
    spread = jnp.mean(center * center, axis=-1, keepdims=True)
    scale_inv = lax.rsqrt(spread + norm_eps)
    return (center * scale_inv, scale_inv)


def norm_back(normed, scale_inv, upstream):
    upstream_mean = jnp.mean(upstream, axis=-1, keepdims=True)
    cross_mean = jnp.mean(upstream * normed, axis=-1, keepdims=True)
    return scale_inv * (upstream - upstream_mean - normed * cross_mean)


def rope_tables(positions, head_dim):
    half_dim = head_dim // 2
    frequency = jnp.power(rope_base, -(jnp.arange(half_dim, dtype=jnp.float32) * 2.0) / head_dim)
    angles = positions[:, None] * frequency[None, :]
    cosine_half = jnp.cos(angles)
    sine_half = jnp.sin(angles)
    return (
        jnp.concatenate([cosine_half, cosine_half], axis=-1),
        jnp.concatenate([sine_half, sine_half], axis=-1),
    )


def rotate(values, cosine, sine):
    half_dim = values.shape[-1] // 2
    turned = jnp.concatenate([-values[..., half_dim:], values[..., :half_dim]], axis=-1)
    return values * cosine + turned * sine


def rotate_back(grads, cosine, sine):
    half_dim = grads.shape[-1] // 2
    scaled = grads * sine
    turned = jnp.concatenate([scaled[..., half_dim:], -scaled[..., :half_dim]], axis=-1)
    return grads * cosine + turned


def pack_kernel(n_dp, chips, first_slots, flags, m_ref, *outs):
    rb, slots, width = m_ref.shape
    rows, wide = outs[0].shape[2:]
    sub = rows // n_dp
    start = pl.program_id(0) * rb
    target = start // sub
    inner = start % sub
    turned = jnp.swapaxes(m_ref[...], 0, 1).astype(bf)
    for s in range(slots):
        out = outs[0] if s < first_slots else outs[1]
        t = s if s < first_slots else s - first_slots
        x = turned[s]

        @pl.when(flags[s] == 1)
        def _():
            for d in range(n_dp):
                pieces = [
                    x[:, (2 * k + c) * rows + d * sub : (2 * k + c) * rows + (d + 1) * sub]
                    for c in range(2)
                    for k in range(chips)
                ]
                out[d, t, pl.ds(pl.multiple_of(start, rb), rb), :] = jnp.concatenate(pieces, axis=1)

        @pl.when(flags[s] == 0)
        def _():
            for g in range(n_dp):
                out[target, t, pl.ds(pl.multiple_of(g * sub + inner, rb), rb), :] = x[
                    :, g * wide : (g + 1) * wide
                ]


def pack(master, flags, n_dp, n_seq, first_slots):
    rows, slots, width = master.shape
    wide = width // n_dp
    rb = min(32, rows // n_dp)
    counts = [first_slots] + ([slots - first_slots] if slots > first_slots else [])
    return pl.pallas_call(
        functools.partial(pack_kernel, n_dp, n_seq // 2, first_slots),
        out_shape=[jax.ShapeDtypeStruct((n_dp, c, rows, wide), bf) for c in counts],
        grid_spec=pltpu.PrefetchScalarGridSpec(
            num_scalar_prefetch=1,
            grid=(rows // rb,),
            in_specs=[pl.BlockSpec((rb, slots, width), lambda i, f: (i, 0, 0))],
            out_specs=[
                pl.BlockSpec((n_dp, c, rows, wide), lambda i, f: (0, 0, 0, 0)) for c in counts
            ],
        ),
        compiler_params=pltpu.CompilerParams(vmem_limit_bytes=50 << 20),
        name="pack",
    )(flags, master)


def adam_kernel(n_dp, chips, first_slots, n_groups, kinds, *refs):
    cols = refs[:n_groups]
    rws = refs[n_groups : 2 * n_groups]
    m_ref, f_ref, s_ref, keep_ref, g_out, f_out, s_out, m_out, held = refs[2 * n_groups :]
    rb, slots, width = m_ref.shape
    wide = width // n_dp
    rows = width // (2 * chips)
    sub = rows // n_dp
    half = chips * sub
    for s in range(slots):
        group = 0 if s < first_slots else 1
        t = s if group == 0 else s - first_slots

        @pl.when(kinds[s] == 1)
        def _():
            pieces = []
            for i in range(2 * chips):
                k, c = i // 2, i % 2
                for d in range(n_dp):
                    begin = c * half + k * sub
                    pieces.append(cols[group][d, t, :, begin : begin + sub])
            held[s] = jnp.concatenate(pieces, axis=1).astype(f32)

        @pl.when(kinds[s] == 0)
        def _():
            for g in range(n_dp):
                held[s, :, g * wide : (g + 1) * wide] = rws[group][0, t, g, :, :].astype(f32)

        @pl.when(kinds[s] == 2)
        def _():
            held[s] = jnp.zeros((rb, width), f32)

    grad = jnp.swapaxes(held[...], 0, 1)
    keep = keep_ref[...] > 0.0
    g_out[...] = grad
    first = jnp.where(keep, beta_one * f_ref[...] + (1.0 - beta_one) * grad, 0.0)
    f_out[...] = first
    second = jnp.where(keep, beta_two * s_ref[...] + (1.0 - beta_two) * grad * grad, 0.0)
    s_out[...] = second
    fixed_first = first * (1.0 / (1.0 - beta_one**STEP))
    fixed_second = second * (1.0 / (1.0 - beta_two**STEP))
    old = m_ref[...]
    step = fixed_first / (jnp.sqrt(fixed_second) + adam_eps) + decay_rate * old
    m_out[...] = jnp.where(keep, old - learn_rate * step, 0.0)


def adam(kinds, grads, master, first_moment, second_moment, n_dp, n_seq, first_slots):
    rows, slots, width = master.shape
    wide = width // n_dp
    sub = rows // n_dp
    rb = min(16, sub)
    state = pl.BlockSpec((rb, slots, width), lambda i, k: (i, 0, 0))
    cols = [pl.BlockSpec((n_dp, g.shape[1], rb, wide), lambda i, k: (0, 0, i, 0)) for g in grads]
    rws = [
        pl.BlockSpec(
            (1, g.shape[1], n_dp, rb, wide),
            lambda i, k: (i * rb // sub, 0, 0, i % (sub // rb), 0),
        )
        for g in grads
    ]
    keep = jnp.broadcast_to((kinds != 2).astype(f32)[None, :, None], (1, slots, width))
    return pl.pallas_call(
        functools.partial(adam_kernel, n_dp, n_seq // 2, first_slots, len(grads)),
        out_shape=[jax.ShapeDtypeStruct(master.shape, f32)] * 4,
        grid_spec=pltpu.PrefetchScalarGridSpec(
            num_scalar_prefetch=1,
            grid=(rows // rb,),
            in_specs=cols
            + rws
            + [state] * 3
            + [pl.BlockSpec((1, slots, width), lambda i, k: (0, 0, 0))],
            out_specs=[state] * 4,
            scratch_shapes=[pltpu.VMEM((slots, rb, width), f32)],
        ),
        compiler_params=pltpu.CompilerParams(vmem_limit_bytes=50 << 20),
        name="adam",
    )(
        kinds,
        *grads,
        *[g.reshape(n_dp, g.shape[1], n_dp, sub, wide) for g in grads],
        master,
        first_moment,
        second_moment,
        keep,
    )


ANY = pl.BlockSpec(memory_space=pl.ANY)
VMEM = pl.BlockSpec(memory_space=pltpu.VMEM)
DMA = pltpu.SemaphoreType.DMA


def comm_params(collective_id, mib):
    return pltpu.CompilerParams(
        collective_id=collective_id, has_side_effects=True, vmem_limit_bytes=mib << 20
    )


def takes(microseconds):
    return pl.CostEstimate(flops=0, bytes_accessed=int(microseconds * 3e6), transcendentals=0)


def places():
    n_seq = lax.axis_size("seq")
    n_dp = lax.axis_size("dp")
    return n_seq, n_dp, lax.axis_index("seq"), lax.axis_index("dp")


def greet(devices):
    barrier = pltpu.get_barrier_semaphore()
    for device in devices:
        pl.semaphore_signal(barrier, inc=1, device_id=device, device_id_type=MESH)
    pl.semaphore_wait(barrier, len(devices))


def send(src, dst, send_sem, recv_sem, device):
    return pltpu.make_async_remote_copy(
        src_ref=src,
        dst_ref=dst,
        send_sem=send_sem,
        recv_sem=recv_sem,
        device_id=device,
        device_id_type=MESH,
    )


def relay_gather(views, place, count, device_of, send_sem, recv_sem, arrived, between=None):
    def leg(view, way, step, block, target):
        ref = views[view](block)
        return send(ref, ref, send_sem.at[view, way, step], recv_sem.at[view, way, step], device_of(target))

    def going(way, step):
        block = place - (step - 1) if way == 0 else place + (step - 1)
        target = place + 1 if way == 0 else place - 1
        inside = (block >= 0) & (block < count) & (target >= 0) & (target < count)
        return block, target, inside

    for step in range(1, count):
        for way in range(2):
            block, target, inside = going(way, step)

            @pl.when(inside)
            def _():
                for view in range(len(views)):
                    leg(view, way, step, block, target).start()

        for way in range(2):
            block = place - step if way == 0 else place + step

            @pl.when((block >= 0) & (block < count))
            def _():
                for view in range(len(views)):
                    leg(view, way, step, block, lax.rem(place + 1, count)).wait_recv()
                arrived(block)

        if between:
            between(step)

    for step in range(1, count):
        for way in range(2):
            block, target, inside = going(way, step)

            @pl.when(inside)
            def _():
                for view in range(len(views)):
                    leg(view, way, step, block, target).wait_send()


def relay_sum(owns, sent, came, place, count, device_of, send_sem, recv_sem, ready):
    views = range(len(owns))

    def spot(way, block, receiver):
        return jnp.where(block == receiver, count, block) if way else block

    def leg(view, way, block, target, receiver):
        return send(
            sent[view].at[block],
            came[view].at[spot(way, block, receiver)],
            send_sem.at[view, way, block],
            recv_sem.at[view, way, block],
            device_of(target),
        )

    def going(way, step):
        block = count - 1 - step + place if way == 0 else step - (count - 1 - place)
        target = place + 1 if way == 0 else place - 1
        return block, target, (block < count if way == 0 else block >= 0)

    def behind(way):
        return place > 0 if way == 0 else place < count - 1

    for step in range(count - 1):
        for way in range(2):
            block, target, inside = going(way, step)

            @pl.when(inside)
            def _():
                ready(block)
                for view in views:

                    @pl.when(behind(way))
                    def _():
                        leg(view, way, block, target, place).wait_recv()
                        value = owns[view](block) + came[view][block].astype(f32)
                        sent[view][block] = value.astype(sent[view].dtype)

                    @pl.when(jnp.logical_not(behind(way)))
                    def _():
                        sent[view][block] = owns[view](block).astype(sent[view].dtype)

                    leg(view, way, block, target, target).start()

    ready(place)
    for way in range(2):

        @pl.when(behind(way))
        def _():
            for view in views:
                leg(view, way, place, lax.rem(place + 1, count), place).wait_recv()

    totals = []
    for view in views:
        total = owns[view](place)
        for way in range(2):
            value = came[view][place if way == 0 else count].astype(f32)
            total = total + jnp.where(behind(way), value, 0.0)
        totals.append(total)
    for step in range(count - 1):
        for way in range(2):
            block, target, inside = going(way, step)

            @pl.when(inside)
            def _():
                for view in views:
                    leg(view, way, block, target, target).wait_send()

    return totals


def front_kernel(
    packed_ref, x_ref, table_ref, out_ref, own_sem, a_send, a_recv, send_sem, recv_sem, pass_sem, take_sem
):
    n_seq, n_dp, seq_index, dp_index = places()
    chips, chip, core = n_seq // 2, seq_index // 2, lax.rem(seq_index, 2)
    dp_peers = [lax.rem(dp_index + k, n_dp) for k in range(n_dp)]
    chip_peers = [lax.rem(chip + k, chips) for k in range(chips)]
    sibling = (dp_index, chip * 2 + 1 - core)
    greet(
        [(p, seq_index) for p in dp_peers[1:]]
        + [(dp_index, p * 2 + core) for p in chip_peers[1:]]
        + [sibling]
    )
    along = []
    for k in range(1, n_dp):
        copy = send(
            packed_ref.at[dp_peers[k]],
            table_ref.at[dp_index],
            a_send.at[k],
            a_recv.at[k],
            (dp_peers[k], seq_index),
        )
        copy.start()
        along.append(copy)
    own = [
        pltpu.make_async_copy(packed_ref.at[dp_index], table_ref.at[dp_index], own_sem.at[0]),
        pltpu.make_async_copy(x_ref, out_ref.at[seq_index], own_sem.at[1]),
    ]
    for copy in own:
        copy.start()
    spread_blocks(
        x_ref, out_ref, chips, chip, core, dp_index, sibling, send_sem, recv_sem, pass_sem, take_sem
    )
    for copy in along:
        copy.wait()
    for copy in own:
        copy.wait()


def spread_blocks(
    x_ref, out_ref, chips, chip, core, dp_index, sibling, send_sem, recv_sem, pass_sem, take_sem
):
    mine = out_ref.at[chip * 2 + core]
    copies = {}
    for k in range(chips - 1, 0, -1):
        device = (dp_index, lax.rem(chip + k, chips) * 2 + core)
        copies[k] = send(x_ref, mine, send_sem.at[k], recv_sem.at[k], device)
        copies[k].start()
    passed = [send(x_ref, mine, pass_sem.at[0], take_sem.at[0], sibling)]
    passed[0].start()
    for k in range(1, chips):
        copies[k].wait_recv()
        block = out_ref.at[lax.rem(chip + chips - k, chips) * 2 + core]
        onward = send(block, block, pass_sem.at[k], take_sem.at[k], sibling)
        onward.start()
        passed.append(onward)
    for copy in copies.values():
        copy.wait_send()
    for onward in passed:
        onward.wait()


def front(packed, x, collective_id):
    chips = lax.axis_size("seq") // 2
    n_dp = lax.axis_size("dp")
    return pl.pallas_call(
        front_kernel,
        out_shape=[
            jax.ShapeDtypeStruct(packed.shape, packed.dtype),
            jax.ShapeDtypeStruct((2 * chips,) + x.shape, x.dtype),
        ],
        in_specs=[VMEM, VMEM],
        out_specs=[ANY, ANY],
        scratch_shapes=[DMA((2,)), DMA((n_dp,)), DMA((n_dp,))] + [DMA((chips,))] * 4,
        compiler_params=comm_params(collective_id, 24),
        cost_estimate=takes(90),
        name="front",
    )(packed, x)


def gather_seq_kernel(x_ref, out_ref, own_sem, send_sem, recv_sem, pass_sem, take_sem):
    n_seq, n_dp, seq_index, dp_index = places()
    chips, chip, core = n_seq // 2, seq_index // 2, lax.rem(seq_index, 2)
    chip_peers = [lax.rem(chip + k, chips) for k in range(chips)]
    sibling = (dp_index, chip * 2 + 1 - core)
    greet([(dp_index, p * 2 + core) for p in chip_peers[1:]] + [sibling])
    own = pltpu.make_async_copy(x_ref, out_ref.at[seq_index], own_sem)
    own.start()
    spread_blocks(
        x_ref, out_ref, chips, chip, core, dp_index, sibling, send_sem, recv_sem, pass_sem, take_sem
    )
    own.wait()


def gather_seq(x, collective_id):
    chips = lax.axis_size("seq") // 2
    return pl.pallas_call(
        gather_seq_kernel,
        out_shape=jax.ShapeDtypeStruct((2 * chips,) + x.shape, x.dtype),
        in_specs=[VMEM],
        out_specs=ANY,
        scratch_shapes=[DMA] + [DMA((chips,))] * 4,
        compiler_params=comm_params(collective_id, 16),
        cost_estimate=takes(28),
        name="gather_seq",
    )(x)


def sum_seq_kernel(x_ref, out_ref, taken, sent, arrived, pass_sem, take_sem, send_sem, recv_sem):
    n_seq, n_dp, seq_index, dp_index = places()
    chips, chip, core = n_seq // 2, seq_index // 2, lax.rem(seq_index, 2)
    peers = [lax.rem(chip + k, chips) for k in range(chips)]
    sibling = (dp_index, chip * 2 + 1 - core)
    greet([(dp_index, p * 2 + core) for p in peers[1:]] + [sibling])
    order = list(range(chips - 1, 0, -1)) + [0]
    passed = {}
    for k in order:
        block = x_ref.at[peers[k] * 2 + 1 - core]
        passed[k] = send(block, taken.at[k], pass_sem.at[k], take_sem.at[k], sibling)
        passed[k].start()
    copies = {}
    for k in order[:-1]:
        passed[k].wait_recv()
        own = x_ref[peers[k] * 2 + core].astype(f32)
        sent[k] = (own + taken[k].astype(f32)).astype(sent.dtype)
        device = (dp_index, peers[k] * 2 + core)
        copies[k] = send(sent.at[k], arrived.at[k], send_sem.at[k], recv_sem.at[k], device)
        copies[k].start()
    passed[0].wait_recv()
    total = x_ref[seq_index].astype(f32) + taken[0].astype(f32)
    for k in range(1, chips):
        copies[k].wait_recv()
        total = total + arrived[k].astype(f32)
    out_ref[...] = total
    for k in order:
        passed[k].wait_send()
    for k in order[:-1]:
        copies[k].wait_send()


def sum_seq(x, collective_id):
    blocks, rows, columns = x.shape
    chips = blocks // 2
    slots = pltpu.VMEM((chips, rows, columns), x.dtype)
    return pl.pallas_call(
        sum_seq_kernel,
        out_shape=jax.ShapeDtypeStruct((rows, columns), f32),
        in_specs=[VMEM],
        out_specs=VMEM,
        scratch_shapes=[slots, slots, slots] + [DMA((chips,))] * 4,
        compiler_params=comm_params(collective_id, 40),
        cost_estimate=takes(28),
        name="sum_seq",
    )(x)


def collect_kernel(
    qkv_ref, out_ref, qkv_sum, out_sum, qkv_sent, qkv_came, out_sent, out_came, total, own_sem,
    send_sem, recv_sem, a_send, a_recv
):
    n_seq, n_dp, seq_index, dp_index = places()
    seq_peers = [lax.rem(seq_index + k, n_seq) for k in range(n_seq)]
    greet(
        [(dp_index, p) for p in seq_peers[1:]]
        + [(lax.rem(dp_index + k, n_dp), seq_index) for k in range(1, n_dp)]
    )
    sums = relay_sum(
        [lambda block: qkv_ref[:, block].astype(f32), lambda block: out_ref[block].astype(f32)],
        [qkv_sent, out_sent],
        [qkv_came, out_came],
        dp_index,
        n_dp,
        lambda place: (place, seq_index),
        send_sem,
        recv_sem,
        lambda block: None,
    )
    total[...] = sums[0].astype(total.dtype)
    across = []
    for k in range(1, n_seq):
        copy = send(
            total.at[seq_peers[k]],
            qkv_sum.at[seq_index],
            a_send.at[k],
            a_recv.at[k],
            (dp_index, seq_peers[k]),
        )
        copy.start()
        across.append(copy)
    own = pltpu.make_async_copy(total.at[seq_index], qkv_sum.at[seq_index], own_sem)
    own.start()
    out_sum[...] = sums[1].astype(out_sum.dtype)
    for copy in across:
        copy.wait()
    own.wait()


def collect_attention(qkv, out, collective_id):
    n_seq = lax.axis_size("seq")
    n_dp = lax.axis_size("dp")
    tail = qkv.shape[2:]
    return pl.pallas_call(
        collect_kernel,
        out_shape=[
            jax.ShapeDtypeStruct((n_seq,) + tail, qkv.dtype),
            jax.ShapeDtypeStruct(out.shape[1:], out.dtype),
        ],
        in_specs=[VMEM, VMEM],
        out_specs=[VMEM, VMEM],
        scratch_shapes=[
            pltpu.VMEM((n_dp, n_seq) + tail, qkv.dtype),
            pltpu.VMEM((n_dp + 1, n_seq) + tail, qkv.dtype),
            pltpu.VMEM((n_dp,) + out.shape[1:], out.dtype),
            pltpu.VMEM((n_dp + 1,) + out.shape[1:], out.dtype),
            pltpu.VMEM((n_seq,) + tail, qkv.dtype),
            DMA,
            DMA((2, 2, n_dp)),
            DMA((2, 2, n_dp)),
            DMA((n_seq,)),
            DMA((n_seq,)),
        ],
        compiler_params=comm_params(collective_id, 48),
        cost_estimate=takes(75),
        name="collect_attention",
    )(qkv, out)


def ring_chip(place, chips):
    return jnp.where(place < chips // 2, 2 * place, 2 * (chips - 1 - place) + 1)


def ring_place(chip, chips):
    line = chip // 2
    return jnp.where(lax.rem(chip, 2) == 0, line, chips - 1 - line)


class Ring:
    def __init__(self, chips, chip, core, dp_index, send_sem, recv_sem):
        self.chips = chips
        self.place = ring_place(chip, chips)
        self.core = core
        self.dp_index = dp_index
        self.send_sem = send_sem
        self.recv_sem = recv_sem
        self.last = chips // 2

    def at(self, offset):
        return ring_chip(lax.rem(self.place + offset + self.chips, self.chips), self.chips)

    def device(self, way):
        return (self.dp_index, self.at(1 if way == 0 else -1) * 2 + self.core)

    def leg(self, view, way, step, src, dst):
        return send(
            src, dst, self.send_sem.at[view, way, step], self.recv_sem.at[view, way, step], self.device(way)
        )


def arrange_kernel(ff_blocks, units, ug_ref, down_ref, *refs):
    piece_ref = refs[-1]
    unit = units[pl.program_id(0)]
    rows, wide = piece_ref.shape[1:]
    sub, width = down_ref.shape[1:]
    groups = width // wide

    @pl.when((unit >= 4) & (unit < 4 + 2 * ff_blocks))
    def _():
        piece_ref[0] = ug_ref[0]

    @pl.when(unit >= 4 + 2 * ff_blocks)
    def _():
        for g in range(groups):
            piece_ref[0, g * sub : (g + 1) * sub, :] = down_ref[0, :, g * wide : (g + 1) * wide]

    if len(refs) == 3:
        qkv_ref, out_ref = refs[:2]
        blocks, _, columns = qkv_ref.shape
        step = columns // 3
        share = wide // step
        for u in range(3):

            @pl.when(unit == u)
            def _():
                for block in range(blocks):
                    g, h = block // share, block % share
                    piece_ref[0, g * sub : (g + 1) * sub, h * step : (h + 1) * step] = qkv_ref[
                        block, :, u * step : (u + 1) * step
                    ]

        @pl.when(unit == 3)
        def _():
            for g in range(groups):
                piece_ref[0, g * sub : (g + 1) * sub, :] = out_ref[:, g * wide : (g + 1) * wide]


def arrange(units, ug, down, attention):
    n_dp, slots = units.shape
    rows, wide = ug.shape[1:]
    sub, width = down.shape[1:]
    ff_blocks = down.shape[0]
    specs = [
        pl.BlockSpec(
            (1, rows, wide), lambda k, u: (jnp.clip(u[k] - 4, 0, 2 * ff_blocks - 1), 0, 0)
        ),
        pl.BlockSpec(
            (1, sub, width),
            lambda k, u: (jnp.clip(u[k] - 4 - 2 * ff_blocks, 0, ff_blocks - 1), 0, 0),
        ),
    ]
    if attention:
        specs.append(pl.BlockSpec(attention[0].shape, lambda k, u: (0, 0, 0)))
        specs.append(pl.BlockSpec(attention[1].shape, lambda k, u: (0, 0)))
    return pl.pallas_call(
        functools.partial(arrange_kernel, ff_blocks),
        out_shape=jax.ShapeDtypeStruct((n_dp * slots, rows, wide), bf),
        grid_spec=pltpu.PrefetchScalarGridSpec(
            num_scalar_prefetch=1,
            grid=(n_dp * slots,),
            in_specs=specs,
            out_specs=pl.BlockSpec((1, rows, wide), lambda k, u: (k, 0, 0)),
        ),
        compiler_params=pltpu.CompilerParams(vmem_limit_bytes=16 << 20),
        cost_estimate=takes(7),
        name="arrange",
    )(units.reshape(-1), ug, down, *attention).reshape(n_dp, slots, rows, wide)


def grads_kernel(
    up_ref, gate_ref, down_ref, x_ref, y_ref, ug_out, down_out, x_out, y_out, *refs
):
    half_came, full_sent, full_came, mine = refs[0:3], refs[3:6], refs[6:9], refs[9:12]
    side_out, x_taken, y_taken, z_sent, z_came = refs[12:17]
    ring_send, ring_recv, z_send, z_recv, x_pass, x_take, y_pass, y_take = refs[17:25]
    side_send, side_recv, own_sem = refs[25:]
    n_seq, n_dp, seq_index, dp_index = places()
    chips, chip, core = n_seq // 2, seq_index // 2, lax.rem(seq_index, 2)
    sibling = (dp_index, chip * 2 + 1 - core)
    ring = Ring(chips, chip, core, dp_index, ring_send, ring_recv)
    owns = [down_ref, up_ref, gate_ref]
    blocks = down_ref.shape[0]
    pair = blocks // 2
    half = up_ref.shape[-1]
    greet(
        [(lax.rem(dp_index + k, n_dp), seq_index) for k in range(1, n_dp)]
        + [sibling, ring.device(0), ring.device(1)]
    )

    def leg(view, way, step):
        if step == 0:
            src = owns[view].at[pl.ds(way * pair, pair), ring.at(ring.last)]
            return ring.leg(view, way, step, src, half_came[view].at[way])
        src, dst = full_sent[view].at[step - 1, way], full_came[view].at[step - 1, way]
        return ring.leg(view, way, step, src, dst)

    def own_copy(view, way, step):
        distance = ring.last - step
        if step == ring.last:
            return pltpu.make_async_copy(
                owns[view].at[:, chip], mine[view], own_sem.at[view, 0, step - 1]
            )
        src = owns[view].at[:, ring.at(distance if way == 0 else -distance)]
        return pltpu.make_async_copy(
            src, full_sent[view].at[step - 1, way], own_sem.at[view, way, step - 1]
        )

    for view in range(3):
        for way in range(2):
            leg(view, way, 0).start()
    for step in range(1, ring.last + 1):
        for view in range(3):
            for way in range(2 if step < ring.last else 1):
                own_copy(view, way, step).start()

    def column_sum(ref, taken, out, pass_sem, take_sem, z):
        def onward(block):
            return send(
                ref.at[1 - core, block], taken.at[block], pass_sem.at[block], take_sem.at[block], sibling
            )

        for block in [b for k in range(n_dp // 2) for b in (n_dp - 1 - k, k)]:
            onward(block).start()
        total = relay_sum(
            [lambda block: ref[core, block].astype(f32) + taken[block].astype(f32)],
            [z_sent.at[z]],
            [z_came.at[z]],
            dp_index,
            n_dp,
            lambda place: (place, seq_index),
            z_send.at[z],
            z_recv.at[z],
            lambda block: onward(block).wait_recv(),
        )[0]
        out[...] = total
        for block in range(n_dp):
            onward(block).wait_send()

    def ring_step(step):
        for view in range(3):
            for way in range(2):
                own_copy(view, way, step).wait()
                leg(view, way, step - 1).wait_recv()
                for k in range(blocks) if step > 1 else range(way * pair, (way + 1) * pair):
                    value = full_sent[view][step - 1, way, k].astype(f32)
                    if step > 1:
                        value = value + full_came[view][step - 2, way, k].astype(f32)
                    else:
                        value = value + half_came[view][way, k - way * pair].astype(f32)
                    full_sent[view][step - 1, way, k] = value.astype(bf)
                leg(view, way, step).start()

    column_sum(x_ref, x_taken, x_out, x_pass, x_take, 0)
    for step in range(1, ring.last):
        ring_step(step)
    column_sum(y_ref, y_taken, y_out, y_pass, y_take, 1)
    for view in range(3):
        own_copy(view, 0, ring.last).wait()
        for way in range(2):
            leg(view, way, ring.last - 1).wait_recv()
        for k in range(blocks):
            if ring.last > 1:
                came = full_came[view]
                sums = [came[ring.last - 2, way, k].astype(f32) for way in range(2)]
                value = mine[view][k].astype(f32) + sums[0] + sums[1]
            else:
                came = half_came[view][k // pair, k % pair].astype(f32)
                value = mine[view][k].astype(f32) + came
            value = value.astype(bf)
            if view == 0:
                down_out[k] = value
            else:
                unit = (view - 1) * blocks + k

                @pl.when(core == 0)
                def _():
                    ug_out[unit, :, :half] = value[0]
                    side_out[unit] = value[1]

                @pl.when(core != 0)
                def _():
                    ug_out[unit, :, half:] = value[1]
                    side_out[unit] = value[0]

    place = pl.ds(pl.multiple_of(core * half, half), half)
    side = send(side_out, ug_out.at[:, :, place], side_send, side_recv, sibling)
    side.start()
    side.wait()
    for step in range(ring.last):
        for view in range(3):
            for way in range(2):
                leg(view, way, step).wait_send()


def sum_grads(up, gate, down, x, y, collective_id):
    blocks, chips, _, rows, half = up.shape
    _, _, sub, width = down.shape
    _, n_dp, tokens, _ = x.shape
    steps = chips // 2
    side = (2, rows, half)
    vmem = pltpu.VMEM
    return pl.pallas_call(
        grads_kernel,
        out_shape=[
            jax.ShapeDtypeStruct((2 * blocks, rows, 2 * half), bf),
            jax.ShapeDtypeStruct((blocks, sub, width), bf),
            jax.ShapeDtypeStruct((tokens, width), f32),
            jax.ShapeDtypeStruct((tokens, width), f32),
        ],
        in_specs=[ANY] * 3 + [VMEM] * 2,
        out_specs=[VMEM] * 4,
        scratch_shapes=[vmem((2, blocks // 2) + s, bf) for s in ((sub, width), side, side)]
        + [vmem((max(steps - 1, 1), 2, blocks) + s, bf) for s in ((sub, width), side, side)] * 2
        + [vmem((blocks,) + s, bf) for s in ((sub, width), side, side)]
        + [
            vmem((2 * blocks, rows, half), bf),
            vmem((n_dp, tokens, width), bf),
            vmem((n_dp, tokens, width), bf),
            vmem((2, n_dp, tokens, width), bf),
            vmem((2, n_dp + 1, tokens, width), bf),
            DMA((3, 2, steps)),
            DMA((3, 2, steps)),
            DMA((2, 1, 2, n_dp)),
            DMA((2, 1, 2, n_dp)),
            DMA((n_dp,)),
            DMA((n_dp,)),
            DMA((n_dp,)),
            DMA((n_dp,)),
            DMA,
            DMA,
            DMA((3, 2, steps)),
        ],
        compiler_params=comm_params(collective_id, 58),
        cost_estimate=takes(120),
        name="sum_grads",
    )(up, gate, down, x, y)


def turn_half(values):
    half = values.shape[-1] // 2
    return jnp.concatenate([-values[:, half:], values[:, :half]], axis=-1)


def forward_kernel(has_late, first_slots, ff_blocks, *refs):
    info, first_ref = refs[:2]
    refs = refs[2:]
    if has_late:
        late_ref, refs = refs[0], refs[1:]
    x1_ref, cos_ref, sin_ref, doc_row, doc_col, tokens_ref, cot_ref = refs[:7]
    qkv_all, out_all, query_out, key_out, value_out, mixed_out, stat_out, residual_out = refs[7:15]
    ug_all, down_all, x_all, cot_all = refs[15:19]
    att_stage, out_stage, part, taken, sent, arrived, x_stage = refs[19:26]
    mine_stage, given_stage, down_stage = refs[26:29]
    (own_sem, a_send, a_recv, w_send, w_recv, s_pass, s_take, s_send, s_recv, cot_send, cot_recv,
     late_send, late_recv, late_own, stage_own, side_send, side_recv, ring_send, ring_recv,
     send_sem, recv_sem, pass_sem, take_sem) = refs[29:52]
    late_tables = refs[52:]
    n_seq, n_dp, seq_index, dp_index = places()
    chips, chip, core = n_seq // 2, seq_index // 2, lax.rem(seq_index, 2)
    sibling = (dp_index, chip * 2 + 1 - core)
    seq_peers = [lax.rem(seq_index + k, n_seq) for k in range(n_seq)]
    dp_peers = [lax.rem(dp_index + k, n_dp) for k in range(n_dp)]
    rows, wide = first_ref.shape[1:]
    sub = rows // n_dp
    half = wide // 2
    step_cols = att_stage.shape[2] // 3
    share = wide // step_cols
    tokens, width = tokens_ref.shape
    greet([(dp_index, p) for p in seq_peers[1:]] + [(p, seq_index) for p in dp_peers[1:]])

    for u in range(3):
        for block in range(n_seq):
            g, h = block // share, block % share
            att_stage[block, :, u * step_cols : (u + 1) * step_cols] = first_ref[
                info[u], g * sub : (g + 1) * sub, h * step_cols : (h + 1) * step_cols
            ]
    for g in range(n_dp):
        out_stage[:, g * wide : (g + 1) * wide] = first_ref[info[3], g * sub : (g + 1) * sub, :]
    own = [
        pltpu.make_async_copy(att_stage.at[seq_index], qkv_all.at[seq_index, dp_index], own_sem.at[0]),
        pltpu.make_async_copy(out_stage, out_all.at[dp_index], own_sem.at[1]),
    ]
    cot_own = pltpu.make_async_copy(cot_ref, cot_all.at[core], own_sem.at[2])
    cot_copy = send(cot_ref, cot_all.at[core], cot_send, cot_recv, sibling)
    across = []
    for k in range(1, n_seq):
        copy = send(
            att_stage.at[seq_peers[k]],
            qkv_all.at[seq_index, dp_index],
            a_send.at[k],
            a_recv.at[k],
            (dp_index, seq_peers[k]),
        )
        copy.start()
        across.append(copy)
    for copy in own:
        copy.start()
    cot_copy.start()
    cot_own.start()
    for copy in own:
        copy.wait()
    for copy in across:
        copy.wait_recv()
    relay_gather(
        [lambda block: qkv_all.at[:, block], lambda block: out_all.at[block]],
        dp_index,
        n_dp,
        lambda place: (place, seq_index),
        w_send,
        w_recv,
        lambda block: None,
    )

    def band(c):
        return pl.ds(c * sub, sub)

    def late_copies(c):
        copies = []
        for k in range(1, n_dp):
            copies.append(
                send(
                    late_ref.at[dp_peers[k], :, band(c)],
                    late_tables[c].at[dp_index],
                    late_send.at[c, k],
                    late_recv.at[c, k],
                    (dp_peers[k], seq_index),
                )
            )
        return copies

    def late_own_copy(c):
        return pltpu.make_async_copy(
            late_ref.at[dp_index, :, band(c)], late_tables[c].at[dp_index], late_own.at[c]
        )

    def late_start(c):
        if not has_late or c >= n_dp:
            return
        if c:
            for copy in late_copies(c - 1):
                copy.wait_send()
        for copy in late_copies(c):
            copy.start()
        late_own_copy(c).start()

    late_start(0)

    seq_len = x1_ref.shape[0]
    heads = query_out.shape[1] // HD
    block_rows = min(256, seq_len)
    head_cols = heads * HD
    qkv_weight = qkv_all[...].reshape(width, 3 * head_cols)

    def project(b, carry):
        at = pl.ds(pl.multiple_of(b * block_rows, block_rows), block_rows)
        result = jnp.dot(x1_ref[at, :], qkv_weight, preferred_element_type=f32)
        cosine, sine = cos_ref[at, :], sin_ref[at, :]
        for h in range(heads):
            place = slice(h * HD, (h + 1) * HD)
            for part_id, out in ((0, query_out), (1, key_out)):
                begin = part_id * head_cols + h * HD
                values = result[:, begin : begin + HD]
                out[at, place] = (values * cosine + turn_half(values) * sine).astype(bf)
        value_out[at, :] = result[:, 2 * head_cols :].astype(bf)
        return carry

    lax.fori_loop(0, seq_len // block_rows, project, 0)

    def attend(b, carry):
        begin = pl.multiple_of(b * block_rows, block_rows)
        at = pl.ds(begin, block_rows)
        query_pos = begin + lax.broadcasted_iota(jnp.int32, (block_rows, seq_len), 0)
        key_pos = lax.broadcasted_iota(jnp.int32, (block_rows, seq_len), 1)
        allowed = (doc_col[at, :] == doc_row[...]) & (key_pos <= query_pos)
        for h in range(heads):
            place = slice(h * HD, (h + 1) * HD)
            scores = lax.dot_general(
                query_out[at, place],
                key_out[:, place],
                (((1,), (1,)), ((), ())),
                preferred_element_type=f32,
            )
            scores = jnp.where(allowed, scores * (float(HD) ** (-0.5)), masked_score)
            peak = jnp.max(scores, axis=-1, keepdims=True)
            raised = jnp.exp(scores - peak)
            total = jnp.sum(raised, axis=-1, keepdims=True)
            prob = (raised * (1.0 / total)).astype(bf)
            mixed = jnp.dot(prob, value_out[:, place], preferred_element_type=f32)
            mixed_out[at, place] = mixed.astype(bf)
            stat_out[at, place] = jnp.broadcast_to(peak + jnp.log(total), (block_rows, HD))
        return carry

    lax.fori_loop(0, seq_len // block_rows, attend, 0)
    out_weight = out_all[...].reshape(rows, width)

    def combine(b, carry):
        at = pl.ds(pl.multiple_of(b * tokens, tokens), tokens)
        part[b] = jnp.dot(mixed_out[at, :], out_weight, preferred_element_type=f32).astype(bf)
        return carry

    lax.fori_loop(0, n_seq, combine, 0)

    chip_peers = [lax.rem(chip + k, chips) for k in range(chips)]
    order = list(range(chips - 1, 0, -1)) + [0]
    passed = {}
    for k in order:
        block = part.at[chip_peers[k] * 2 + 1 - core]
        passed[k] = send(block, taken.at[k], s_pass.at[k], s_take.at[k], sibling)
        passed[k].start()
    copies = {}
    for k in order[:-1]:
        passed[k].wait_recv()
        value = part[chip_peers[k] * 2 + core].astype(f32)
        sent[k] = (value + taken[k].astype(f32)).astype(bf)
        device = (dp_index, chip_peers[k] * 2 + core)
        copies[k] = send(sent.at[k], arrived.at[k], s_send.at[k], s_recv.at[k], device)
        copies[k].start()

    ring = Ring(chips, chip, core, dp_index, None, None)
    pair = ff_blocks // 2

    def ring_leg(c, view, way, step, arriving):
        distance = step if arriving else step - 1
        block = ring.at(-distance if way == 0 else distance)
        begin = ff_blocks if view == 2 else 0
        units = pl.ds(begin, ff_blocks)
        if step == ring.last:
            units = pl.ds(begin + way * pair, pair)
        if view == 0:
            ref = down_all.at[units, block, :, pl.ds(c * wide, wide)]
        else:
            ref = ug_all.at[units, block, :, band(c)]
        return send(
            ref, ref, ring_send.at[c, view, way, step - 1], ring_recv.at[c, view, way, step - 1],
            ring.device(way),
        )

    def side_copy(c):
        return send(
            given_stage.at[c],
            ug_all.at[:, chip, core, band(c)],
            side_send.at[c],
            side_recv.at[c],
            sibling,
        )

    def begin_band(c):
        if has_late:
            for copy in late_copies(c):
                copy.wait_recv()
            late_own_copy(c).wait()
            late_start(c + 1)
            table = late_tables[c]
            late_slots = table.shape[1]
        for u in range(3 * ff_blocks):
            value = first_ref[info[4 + u], band(c), :]
            if has_late:
                code = info[4 + 3 * ff_blocks + u]
                other = table[code // late_slots, lax.rem(code, late_slots)]
                use_late = jnp.full(value.shape, info[4 + 6 * ff_blocks + u], jnp.int32) != 0
                value = jnp.where(use_late, other, value)
            if u < 2 * ff_blocks:
                left, right = value[:, :half], value[:, half:]

                @pl.when(core == 0)
                def _():
                    mine_stage[c, u] = left
                    given_stage[c, u] = right

                @pl.when(core != 0)
                def _():
                    mine_stage[c, u] = right
                    given_stage[c, u] = left
            else:
                down_stage[c, u - 2 * ff_blocks] = value
        side_copy(c).start()
        local = [
            pltpu.make_async_copy(mine_stage.at[c], ug_all.at[:, chip, core, band(c)], stage_own.at[c, 0]),
            pltpu.make_async_copy(
                down_stage.at[c], down_all.at[:, chip, :, pl.ds(c * wide, wide)], stage_own.at[c, 1]
            ),
        ]
        for copy in local:
            copy.start()
        for copy in local:
            copy.wait()
        side_copy(c).wait_recv()
        for view in range(3):
            for way in range(2):
                ring_leg(c, view, way, 1, False).start()

    def carry_band(c, step):
        for view in range(3):
            for way in range(2):
                ring_leg(c, view, way, step - 1, True).wait_recv()
                ring_leg(c, view, way, step, False).start()

    begin_band(0)
    passed[0].wait_recv()
    total = part[seq_index].astype(f32) + taken[0].astype(f32)
    for k in range(1, chips):
        copies[k].wait_recv()
        total = total + arrived[k].astype(f32)
    residual = tokens_ref[...] + total
    residual_out[...] = residual
    center = residual - jnp.mean(residual, axis=-1, keepdims=True)
    spread = jnp.mean(center * center, axis=-1, keepdims=True)
    x_stage[...] = (center * lax.rsqrt(spread + norm_eps)).astype(bf)
    for c in range(1, n_dp):
        begin_band(c)
        for step in range(2, ring.last + 1):
            carry_band(c - 1, step)

    own_x = pltpu.make_async_copy(x_stage, x_all.at[core, dp_index], own_sem.at[3])
    own_x.start()
    own_x.wait()

    def onward(block):
        ref = x_all.at[core, block]
        return send(ref, ref, pass_sem.at[block], take_sem.at[block], sibling)

    onward(dp_index).start()
    relay_gather(
        [lambda block: x_all.at[core, block]],
        dp_index,
        n_dp,
        lambda place: (place, seq_index),
        send_sem,
        recv_sem,
        lambda block: onward(block).start(),
        lambda step: carry_band(n_dp - 1, 2) if step == 1 and ring.last > 1 else None,
    )
    for step in range(3, ring.last + 1):
        carry_band(n_dp - 1, step)
    for c in range(n_dp):
        for view in range(3):
            for way in range(2):
                ring_leg(c, view, way, ring.last, True).wait_recv()
                for step in range(1, ring.last + 1):
                    ring_leg(c, view, way, step, False).wait_send()
        side_copy(c).wait_send()
        if has_late:
            if c == n_dp - 1:
                for copy in late_copies(c):
                    copy.wait_send()
    for block in range(n_dp):
        onward(block).wait_send()
        ref = x_all.at[1 - core, block]
        send(ref, ref, pass_sem.at[block], take_sem.at[block], sibling).wait_recv()
    for k in order:
        passed[k].wait_send()
    for k in order[:-1]:
        copies[k].wait_send()
    for copy in across:
        copy.wait_send()
    cot_copy.wait_send()
    cot_own.wait()
    ref = cot_all.at[1 - core]
    send(ref, ref, cot_send, cot_recv, sibling).wait_recv()


def forward(info, first_table, late, x1, cosine, sine, doc, tokens, cot, ff_blocks, first_slots, collective_id):
    n_seq = lax.axis_size("seq")
    n_dp = lax.axis_size("dp")
    chips = n_seq // 2
    rows, wide = first_table.shape[1:]
    sub = rows // n_dp
    half = wide // 2
    seq_len, width = x1.shape
    head_cols = width // n_seq
    shard = tokens.shape[0]
    steps = chips // 2
    vmem = pltpu.VMEM
    low = lambda *shape: jax.ShapeDtypeStruct(shape, bf)
    has_late = late is not None
    blocks = vmem((chips, shard, width), bf)
    return pl.pallas_call(
        functools.partial(forward_kernel, has_late, first_slots, ff_blocks),
        out_shape=[
            low(n_seq, n_dp, sub, 3 * head_cols),
            low(n_dp, sub, width),
            low(seq_len, head_cols),
            low(seq_len, head_cols),
            low(seq_len, head_cols),
            low(seq_len, head_cols),
            jax.ShapeDtypeStruct((seq_len, head_cols), f32),
            jax.ShapeDtypeStruct((shard, width), f32),
            low(2 * ff_blocks, chips, 2, rows, half),
            low(ff_blocks, chips, sub, width),
            low(2, n_dp, shard, width),
            low(2, n_dp, shard, width),
        ],
        in_specs=[pl.BlockSpec(memory_space=pltpu.SMEM), VMEM]
        + [ANY] * has_late
        + [VMEM] * 7,
        out_specs=[VMEM] * 8 + [ANY] * 4,
        scratch_shapes=[
            vmem((n_seq, sub, 3 * head_cols), bf),
            vmem((sub, width), bf),
            vmem((n_seq, shard, width), bf),
            blocks,
            blocks,
            blocks,
            vmem((shard, width), bf),
            vmem((n_dp, 2 * ff_blocks, sub, half), bf),
            vmem((n_dp, 2 * ff_blocks, sub, half), bf),
            vmem((n_dp, ff_blocks, sub, wide), bf),
            DMA((4,)),
            DMA((n_seq,)),
            DMA((n_seq,)),
            DMA((2, 2, n_dp)),
            DMA((2, 2, n_dp)),
            DMA((chips,)),
            DMA((chips,)),
            DMA((chips,)),
            DMA((chips,)),
            DMA,
            DMA,
            DMA((n_dp, n_dp)),
            DMA((n_dp, n_dp)),
            DMA((n_dp,)),
            DMA((n_dp, 2)),
            DMA((n_dp,)),
            DMA((n_dp,)),
            DMA((n_dp, 3, 2, steps)),
            DMA((n_dp, 3, 2, steps)),
            DMA((1, 2, n_dp)),
            DMA((1, 2, n_dp)),
            DMA((n_dp,)),
            DMA((n_dp,)),
        ]
        + [vmem((n_dp, late.shape[1], sub, wide), bf) for _ in range(n_dp if has_late else 0)],
        compiler_params=comm_params(collective_id, 58),
        cost_estimate=takes(230),
        name="forward",
    )(
        info,
        first_table,
        *([late] if has_late else []),
        x1,
        cosine,
        sine,
        doc[None, :],
        doc[:, None],
        tokens,
        cot,
    )


def local(block_input, cotangent, doc_lengths, owners, master, first_moment, second_moment):
    n_seq = lax.axis_size("seq")
    n_dp = lax.axis_size("dp")
    seq_index = lax.axis_index("seq")
    dp_index = lax.axis_index("dp")
    core = seq_index % 2
    _, shard_len, width = block_input.shape
    rows = master.shape[0]
    per_owner = master.shape[1]
    chips = n_seq // 2
    sub = rows // n_dp
    wide = width // n_dp
    half = chips * sub
    heads = H // n_seq
    head_cols = heads * HD
    seq_len = shard_len * n_seq
    ff_blocks = FF // D
    first_slots = min(4, per_owner)
    unit_count = owners.shape[0]
    score_scale = float(HD) ** (-0.5)

    unit_slot = unit_slots(owners, per_owner)
    place = unit_slot - owners * per_owner
    all_slots = jnp.arange(n_dp * per_owner, dtype=jnp.int32)
    match = unit_slot[None, :] == all_slots[:, None]
    slot_unit = jnp.sum(
        jnp.where(match, jnp.arange(unit_count, dtype=jnp.int32)[None, :] + 1, 0), axis=1
    ) - 1
    slot_unit = slot_unit.reshape(n_dp, per_owner)
    own_units = lax.dynamic_index_in_dim(slot_unit, dp_index, 0, keepdims=False)
    is_col = (own_units >= 4) & (own_units < 4 + 2 * ff_blocks)


    tokens = block_input.astype(f32).reshape(shard_len, width)
    normed_one, inv_one = norm_parts(tokens)
    packed = pack(master, is_col.astype(jnp.int32), n_dp, n_seq, first_slots)
    first_table, normed_one_all = front(packed[0], normed_one.astype(bf), 2)
    first_table = first_table.reshape(n_dp * first_slots, rows, wide)
    normed_one_all = normed_one_all.reshape(seq_len, width)
    upstream = cotangent.reshape(shard_len, width)
    upstream_column = lax.all_gather(upstream, "dp", axis=0)
    positions = jnp.arange(seq_len, dtype=jnp.int32)
    cosine, sine = rope_tables(positions.astype(f32), HD)
    doc_ends = jnp.cumsum(doc_lengths[0])
    doc = jnp.sum((positions[:, None] >= doc_ends[None, :]).astype(jnp.int32), axis=1)
    late_slots = per_owner - first_slots
    info = jnp.concatenate(
        [
            owners * first_slots + jnp.minimum(place, first_slots - 1),
            (owners * late_slots + jnp.maximum(place - first_slots, 0))[4:],
            (place >= first_slots)[4:],
        ]
    ).astype(jnp.int32)
    (
        qkv_weight,
        out_weight,
        queries,
        keys,
        values,
        attended_low,
        log_total,
        residual,
        ug_weight,
        down_weight,
        normed_two_all,
        upstream_all,
    ) = forward(
        info,
        first_table,
        packed[1] if late_slots else None,
        normed_one_all,
        cosine,
        sine,
        doc,
        tokens,
        upstream_column,
        ff_blocks,
        first_slots,
        1,
    )
    qkv_weight = qkv_weight.reshape(width, 3 * head_cols)
    out_weight = out_weight.reshape(rows, width)
    queries, keys, values = (a.reshape(seq_len, heads, HD) for a in (queries, keys, values))
    log_total = log_total.reshape(seq_len, heads, HD)[:, :, :1].transpose(1, 0, 2)
    cosine = cosine[:, None, :]
    sine = sine[:, None, :]
    normed_two, inv_two = norm_parts(residual)
    up_weight = ug_weight[:ff_blocks].reshape(ff_blocks, width, half)
    gate_weight = ug_weight[ff_blocks:].reshape(ff_blocks, width, half)
    down_weight = down_weight.reshape(ff_blocks, half, width)
    normed_two_all = normed_two_all.reshape(-1, width)
    upstream_all = upstream_all.reshape(-1, width)
    up_proj = jnp.einsum("tr,jrc->tjc", normed_two_all, up_weight, preferred_element_type=f32)
    gate_proj = jnp.einsum("tr,jrc->tjc", normed_two_all, gate_weight, preferred_element_type=f32)
    gate_sig = jax.nn.sigmoid(gate_proj)
    silu_value = gate_proj * gate_sig
    hidden_low = (silu_value * up_proj).astype(bf)
    ff_part = jnp.einsum("tjh,jhc->tc", hidden_low, down_weight, preferred_element_type=f32)
    hidden_grad = jnp.einsum("tc,jhc->tjh", upstream_all, down_weight, preferred_element_type=f32)
    up_grad_low = (hidden_grad * silu_value).astype(bf)
    gate_grad_low = (
        hidden_grad * up_proj * (gate_sig + gate_proj * gate_sig * (1.0 - gate_sig))
    ).astype(bf)

    down_grad = jnp.einsum(
        "tjh,tc->jhc", hidden_low, upstream_all, preferred_element_type=f32
    ).astype(bf)
    up_grad = jnp.einsum(
        "tr,tjc->jrc", normed_two_all, up_grad_low, preferred_element_type=f32
    ).astype(bf)
    gate_grad = jnp.einsum(
        "tr,tjc->jrc", normed_two_all, gate_grad_low, preferred_element_type=f32
    ).astype(bf)
    norm_two_grad = jnp.einsum("tjc,jrc->tr", up_grad_low, up_weight, preferred_element_type=f32)
    norm_two_grad = norm_two_grad + jnp.einsum(
        "tjc,jrc->tr", gate_grad_low, gate_weight, preferred_element_type=f32
    )
    side = (ff_blocks, chips, 2, rows, half)
    column = (2, n_dp, shard_len, width)
    ug_piece, down_piece, norm_two_grad, ff_out = sum_grads(
        up_grad.reshape(side),
        gate_grad.reshape(side),
        down_grad.reshape(ff_blocks, chips, sub, width),
        norm_two_grad.astype(bf).reshape(column),
        ff_part.astype(bf).reshape(column),
        5,
    )
    block_output = (residual + ff_out).astype(bf).reshape(block_input.shape)
    grads = []
    if per_owner > first_slots:
        late = arrange(slot_unit[:, first_slots:], ug_piece, down_piece, ())
        grads.append(lax.all_to_all(late, "dp", 0, 0))
    residual_grad = upstream.astype(f32) + norm_back(normed_two, inv_two, norm_two_grad)
    residual_grad_all = gather_seq(residual_grad.astype(bf), 7).reshape(seq_len, width)

    attended_grad = jnp.einsum(
        "tc,rc->tr", residual_grad_all, out_weight, preferred_element_type=f32
    )
    attended_grad = attended_grad.astype(bf).reshape(seq_len, heads, HD)
    allowed = (doc[:, None] == doc[None, :]) & (positions[None, :] <= positions[:, None])
    scores = jnp.einsum("qhd,khd->hqk", queries, keys, preferred_element_type=f32) * score_scale
    scores = jnp.where(allowed[None], scores, masked_score)
    prob = jnp.exp(scores - log_total)
    prob_low = prob.astype(bf)
    value_grad = jnp.einsum("hqk,qhd->khd", prob_low, attended_grad, preferred_element_type=f32)
    prob_grad = jnp.einsum("qhd,khd->hqk", attended_grad, values, preferred_element_type=f32)
    inner_sum = jnp.sum(prob * prob_grad, axis=-1, keepdims=True)
    score_grad = (prob * (prob_grad - inner_sum) * score_scale).astype(bf)
    query_grad = jnp.einsum("hqk,khd->qhd", score_grad, keys, preferred_element_type=f32)
    key_grad = jnp.einsum("hqk,qhd->khd", score_grad, queries, preferred_element_type=f32)
    qkv_grad = jnp.stack(
        [
            rotate_back(query_grad, cosine, sine),
            rotate_back(key_grad, cosine, sine),
            value_grad,
        ],
        axis=1,
    )
    qkv_grad_low = qkv_grad.astype(bf).reshape(seq_len, 3 * head_cols)
    norm_one_part = jnp.einsum("tf,rf->tr", qkv_grad_low, qkv_weight, preferred_element_type=f32)
    norm_one_grad = sum_seq(norm_one_part.astype(bf).reshape(n_seq, shard_len, width), 3)
    input_grad = (residual_grad + norm_back(normed_one, inv_one, norm_one_grad)).reshape(
        block_input.shape
    )

    qkv_wgrad = jnp.einsum(
        "tr,tf->rf", normed_one_all, qkv_grad_low, preferred_element_type=f32
    ).astype(bf)
    out_wgrad = jnp.einsum(
        "tr,tc->rc", attended_low, residual_grad_all, preferred_element_type=f32
    ).astype(bf)
    qkv_piece, out_piece = collect_attention(
        qkv_wgrad.reshape(n_seq, n_dp, sub, 3 * head_cols), out_wgrad.reshape(n_dp, sub, width), 6
    )
    early = arrange(slot_unit[:, :first_slots], ug_piece, down_piece, (qkv_piece, out_piece))
    grads.insert(0, lax.all_to_all(early, "dp", 0, 0))
    kinds = jnp.where(own_units < 0, 2, is_col.astype(jnp.int32)).astype(jnp.int32)
    owned_grads, new_first, new_second, new_master = adam(
        kinds, grads, master, first_moment, second_moment, n_dp, n_seq, first_slots
    )
    return (block_output, input_grad, owned_grads, new_first, new_second, new_master)


def solution(mesh):
    placed = (
        P("dp", "seq", None),
        P("dp", "seq", None),
        P("dp", None),
        P(),
        P("seq", "dp", None),
        P("seq", "dp", None),
        P("seq", "dp", None),
    )
    return jax.shard_map(
        local,
        mesh=mesh,
        in_specs=placed,
        out_specs=(
            P("dp", "seq", None),
            P("dp", "seq", None),
            P("seq", "dp", None),
            P("seq", "dp", None),
            P("seq", "dp", None),
            P("seq", "dp", None),
        ),
        check_vma=False,
    )
```

```python
import functools

import jax
import jax.numpy as jnp
from jax import lax
from jax.experimental import pallas as pl
from jax.experimental.pallas import tpu as pltpu
from jax.sharding import PartitionSpec as P

D = 2048
H = 16
HD = 128
FF = 8192
STEP = 5
bf = jnp.bfloat16
f32 = jnp.float32
MESH = pl.DeviceIdType.MESH


norm_eps = 1e-05
rope_base = 10000.0
beta_one = 0.5
beta_two = 0.5
learn_rate = 0.01
decay_rate = 0.1
adam_eps = 1e-08
masked_score = -1000000000.0


def unit_slots(owners, per_owner):
    unit_count = owners.shape[0]
    unit_order = jnp.arange(unit_count, dtype=jnp.int32)
    matching = owners[:, None] == owners[None, :]
    before = unit_order[None, :] < unit_order[:, None]
    places = jnp.sum(jnp.where(matching & before, 1, 0), axis=1).astype(jnp.int32)
    return owners * per_owner + places


def norm_parts(values):
    center = values - jnp.mean(values, axis=-1, keepdims=True)
    spread = jnp.mean(center * center, axis=-1, keepdims=True)
    scale_inv = lax.rsqrt(spread + norm_eps)
    return (center * scale_inv, scale_inv)


def norm_back(normed, scale_inv, upstream):
    upstream_mean = jnp.mean(upstream, axis=-1, keepdims=True)
    cross_mean = jnp.mean(upstream * normed, axis=-1, keepdims=True)
    return scale_inv * (upstream - upstream_mean - normed * cross_mean)


def rope_tables(positions, head_dim):
    half_dim = head_dim // 2
    frequency = jnp.power(rope_base, -(jnp.arange(half_dim, dtype=jnp.float32) * 2.0) / head_dim)
    angles = positions[:, None] * frequency[None, :]
    cosine_half = jnp.cos(angles)
    sine_half = jnp.sin(angles)
    return (
        jnp.concatenate([cosine_half, cosine_half], axis=-1),
        jnp.concatenate([sine_half, sine_half], axis=-1),
    )


def rotate(values, cosine, sine):
    half_dim = values.shape[-1] // 2
    turned = jnp.concatenate([-values[..., half_dim:], values[..., :half_dim]], axis=-1)
    return values * cosine + turned * sine


def rotate_back(grads, cosine, sine):
    half_dim = grads.shape[-1] // 2
    scaled = grads * sine
    turned = jnp.concatenate([scaled[..., half_dim:], -scaled[..., :half_dim]], axis=-1)
    return grads * cosine + turned


def pack_kernel(n_dp, chips, first_slots, flags, m_ref, *outs):
    rb, slots, width = m_ref.shape
    rows, wide = outs[0].shape[2:]
    sub = rows // n_dp
    start = pl.program_id(0) * rb
    target = start // sub
    inner = start % sub
    turned = jnp.swapaxes(m_ref[...], 0, 1).astype(bf)
    for s in range(slots):
        out = outs[0] if s < first_slots else outs[1]
        t = s if s < first_slots else s - first_slots
        x = turned[s]

        @pl.when(flags[s] == 1)
        def _():
            for d in range(n_dp):
                pieces = [
                    x[:, (2 * k + c) * rows + d * sub : (2 * k + c) * rows + (d + 1) * sub]
                    for c in range(2)
                    for k in range(chips)
                ]
                out[d, t, pl.ds(pl.multiple_of(start, rb), rb), :] = jnp.concatenate(pieces, axis=1)

        @pl.when(flags[s] == 0)
        def _():
            for g in range(n_dp):
                out[target, t, pl.ds(pl.multiple_of(g * sub + inner, rb), rb), :] = x[
                    :, g * wide : (g + 1) * wide
                ]


def pack(master, flags, n_dp, n_seq, first_slots):
    rows, slots, width = master.shape
    wide = width // n_dp
    rb = min(32, rows // n_dp)
    counts = [first_slots] + ([slots - first_slots] if slots > first_slots else [])
    return pl.pallas_call(
        functools.partial(pack_kernel, n_dp, n_seq // 2, first_slots),
        out_shape=[jax.ShapeDtypeStruct((n_dp, c, rows, wide), bf) for c in counts],
        grid_spec=pltpu.PrefetchScalarGridSpec(
            num_scalar_prefetch=1,
            grid=(rows // rb,),
            in_specs=[pl.BlockSpec((rb, slots, width), lambda i, f: (i, 0, 0))],
            out_specs=[
                pl.BlockSpec((n_dp, c, rows, wide), lambda i, f: (0, 0, 0, 0)) for c in counts
            ],
        ),
        compiler_params=pltpu.CompilerParams(vmem_limit_bytes=50 << 20),
        name="pack",
    )(flags, master)


def adam_kernel(n_dp, chips, first_slots, n_groups, n_kept, kinds, *refs):
    cols = refs[:n_groups]
    rws = refs[n_groups : 2 * n_groups]
    m_ref, f_ref, s_ref, keep_ref = refs[2 * n_groups : 2 * n_groups + 4]
    g_out, f_out, s_out, m_out, held = refs[2 * n_groups + 4 + n_kept :]
    rb, slots, width = m_ref.shape
    wide = width // n_dp
    rows = width // (2 * chips)
    sub = rows // n_dp
    half = chips * sub
    for s in range(slots):
        group = 0 if s < first_slots else 1
        t = s if group == 0 else s - first_slots

        @pl.when(kinds[s] == 1)
        def _():
            pieces = []
            for i in range(2 * chips):
                k, c = i // 2, i % 2
                for d in range(n_dp):
                    begin = c * half + k * sub
                    pieces.append(cols[group][d, t, :, begin : begin + sub])
            held[s] = jnp.concatenate(pieces, axis=1).astype(f32)

        @pl.when(kinds[s] == 0)
        def _():
            for g in range(n_dp):
                held[s, :, g * wide : (g + 1) * wide] = rws[group][0, t, g, :, :].astype(f32)

        @pl.when(kinds[s] == 2)
        def _():
            held[s] = jnp.zeros((rb, width), f32)

    grad = jnp.swapaxes(held[...], 0, 1)
    keep = keep_ref[...] > 0.0
    g_out[...] = grad
    first = jnp.where(keep, beta_one * f_ref[...] + (1.0 - beta_one) * grad, 0.0)
    f_out[...] = first
    second = jnp.where(keep, beta_two * s_ref[...] + (1.0 - beta_two) * grad * grad, 0.0)
    s_out[...] = second
    fixed_first = first * (1.0 / (1.0 - beta_one**STEP))
    fixed_second = second * (1.0 / (1.0 - beta_two**STEP))
    old = m_ref[...]
    step = fixed_first / (jnp.sqrt(fixed_second) + adam_eps) + decay_rate * old
    m_out[...] = jnp.where(keep, old - learn_rate * step, 0.0)


def adam(kinds, grads, master, first_moment, second_moment, n_dp, n_seq, first_slots, begin, kept):
    rows, slots, width = master.shape
    wide = width // n_dp
    sub = rows // n_dp
    size = grads[0].shape[2] // n_dp
    rb = min(16, size)
    steps = size // rb
    state = pl.BlockSpec(
        (rb, slots, width), lambda d, i, k: (d * (sub // rb) + begin // rb + i, 0, 0)
    )
    cols = [
        pl.BlockSpec((n_dp, g.shape[1], rb, wide), lambda d, i, k: (0, 0, d * steps + i, 0))
        for g in grads
    ]
    rws = [
        pl.BlockSpec((1, g.shape[1], n_dp, rb, wide), lambda d, i, k: (d, 0, 0, i, 0)) for g in grads
    ]
    keep = jnp.broadcast_to((kinds != 2).astype(f32)[None, :, None], (1, slots, width))
    first_kept = 1 + 2 * len(grads) + 4
    return pl.pallas_call(
        functools.partial(adam_kernel, n_dp, n_seq // 2, first_slots, len(grads), len(kept)),
        out_shape=[jax.ShapeDtypeStruct(master.shape, f32)] * 4,
        grid_spec=pltpu.PrefetchScalarGridSpec(
            num_scalar_prefetch=1,
            grid=(n_dp, steps),
            in_specs=cols
            + rws
            + [state] * 3
            + [pl.BlockSpec((1, slots, width), lambda d, i, k: (0, 0, 0))]
            + [pl.BlockSpec(memory_space=pl.ANY)] * len(kept),
            out_specs=[state] * 4,
            scratch_shapes=[pltpu.VMEM((slots, rb, width), f32)],
        ),
        input_output_aliases={first_kept + k: k for k in range(len(kept))},
        compiler_params=pltpu.CompilerParams(vmem_limit_bytes=50 << 20),
        cost_estimate=pl.CostEstimate(
            flops=0, bytes_accessed=int(150e6 * size / sub), transcendentals=0
        ),
        name="adam",
    )(
        kinds,
        *grads,
        *[g.reshape(n_dp, g.shape[1], n_dp, size, wide) for g in grads],
        master,
        first_moment,
        second_moment,
        keep,
        *kept,
    )


ANY = pl.BlockSpec(memory_space=pl.ANY)
VMEM = pl.BlockSpec(memory_space=pltpu.VMEM)
DMA = pltpu.SemaphoreType.DMA


def comm_params(collective_id, mib):
    return pltpu.CompilerParams(
        collective_id=collective_id, has_side_effects=True, vmem_limit_bytes=mib << 20
    )


def takes(microseconds):
    return pl.CostEstimate(flops=0, bytes_accessed=int(microseconds * 3e6), transcendentals=0)


def places():
    n_seq = lax.axis_size("seq")
    n_dp = lax.axis_size("dp")
    return n_seq, n_dp, lax.axis_index("seq"), lax.axis_index("dp")


def greet(devices):
    barrier = pltpu.get_barrier_semaphore()
    for device in devices:
        pl.semaphore_signal(barrier, inc=1, device_id=device, device_id_type=MESH)
    pl.semaphore_wait(barrier, len(devices))


def send(src, dst, send_sem, recv_sem, device):
    return pltpu.make_async_remote_copy(
        src_ref=src,
        dst_ref=dst,
        send_sem=send_sem,
        recv_sem=recv_sem,
        device_id=device,
        device_id_type=MESH,
    )


def relay_gather(views, place, count, device_of, send_sem, recv_sem, arrived, between=None):
    def leg(view, way, step, block, target):
        ref = views[view](block)
        return send(ref, ref, send_sem.at[view, way, step], recv_sem.at[view, way, step], device_of(target))

    def going(way, step):
        block = place - (step - 1) if way == 0 else place + (step - 1)
        target = place + 1 if way == 0 else place - 1
        inside = (block >= 0) & (block < count) & (target >= 0) & (target < count)
        return block, target, inside

    for step in range(1, count):
        for way in range(2):
            block, target, inside = going(way, step)

            @pl.when(inside)
            def _():
                for view in range(len(views)):
                    leg(view, way, step, block, target).start()

        for way in range(2):
            block = place - step if way == 0 else place + step

            @pl.when((block >= 0) & (block < count))
            def _():
                for view in range(len(views)):
                    leg(view, way, step, block, lax.rem(place + 1, count)).wait_recv()
                arrived(block)

        if between:
            between(step)

    for step in range(1, count):
        for way in range(2):
            block, target, inside = going(way, step)

            @pl.when(inside)
            def _():
                for view in range(len(views)):
                    leg(view, way, step, block, target).wait_send()


def relay_sum(owns, sent, came, place, count, device_of, send_sem, recv_sem, ready, between=None):
    views = range(len(owns))

    def spot(way, block, receiver):
        return jnp.where(block == receiver, count, block) if way else block

    def leg(view, way, block, target, receiver):
        return send(
            sent[view].at[block],
            came[view].at[spot(way, block, receiver)],
            send_sem.at[view, way, block],
            recv_sem.at[view, way, block],
            device_of(target),
        )

    def going(way, step):
        block = count - 1 - step + place if way == 0 else step - (count - 1 - place)
        target = place + 1 if way == 0 else place - 1
        return block, target, (block < count if way == 0 else block >= 0)

    def behind(way):
        return place > 0 if way == 0 else place < count - 1

    for step in range(count - 1):
        for way in range(2):
            block, target, inside = going(way, step)

            @pl.when(inside)
            def _():
                ready(block)
                for view in views:

                    @pl.when(behind(way))
                    def _():
                        leg(view, way, block, target, place).wait_recv()
                        value = owns[view](block) + came[view][block].astype(f32)
                        sent[view][block] = value.astype(sent[view].dtype)

                    @pl.when(jnp.logical_not(behind(way)))
                    def _():
                        sent[view][block] = owns[view](block).astype(sent[view].dtype)

                    leg(view, way, block, target, target).start()

        if between:
            between(step)

    ready(place)
    for way in range(2):

        @pl.when(behind(way))
        def _():
            for view in views:
                leg(view, way, place, lax.rem(place + 1, count), place).wait_recv()

    totals = []
    for view in views:
        total = owns[view](place)
        for way in range(2):
            value = came[view][place if way == 0 else count].astype(f32)
            total = total + jnp.where(behind(way), value, 0.0)
        totals.append(total)
    for step in range(count - 1):
        for way in range(2):
            block, target, inside = going(way, step)

            @pl.when(inside)
            def _():
                for view in views:
                    leg(view, way, block, target, target).wait_send()

    return totals


def front_kernel(
    packed_ref, x_ref, table_ref, out_ref, own_sem, a_send, a_recv, send_sem, recv_sem, pass_sem, take_sem
):
    n_seq, n_dp, seq_index, dp_index = places()
    chips, chip, core = n_seq // 2, seq_index // 2, lax.rem(seq_index, 2)
    dp_peers = [lax.rem(dp_index + k, n_dp) for k in range(n_dp)]
    chip_peers = [lax.rem(chip + k, chips) for k in range(chips)]
    sibling = (dp_index, chip * 2 + 1 - core)
    greet(
        [(p, seq_index) for p in dp_peers[1:]]
        + [(dp_index, p * 2 + core) for p in chip_peers[1:]]
        + [sibling]
    )
    along = []
    for k in range(1, n_dp):
        copy = send(
            packed_ref.at[dp_peers[k]],
            table_ref.at[dp_index],
            a_send.at[k],
            a_recv.at[k],
            (dp_peers[k], seq_index),
        )
        copy.start()
        along.append(copy)
    own = [
        pltpu.make_async_copy(packed_ref.at[dp_index], table_ref.at[dp_index], own_sem.at[0]),
        pltpu.make_async_copy(x_ref, out_ref.at[seq_index], own_sem.at[1]),
    ]
    for copy in own:
        copy.start()
    pass_on, finish = spread_blocks(
        x_ref, out_ref, chips, chip, core, dp_index, sibling, send_sem, recv_sem, pass_sem, take_sem
    )
    pass_on()
    finish()
    for copy in along:
        copy.wait()
    for copy in own:
        copy.wait()


def spread_blocks(
    x_ref, out_ref, chips, chip, core, dp_index, sibling, send_sem, recv_sem, pass_sem, take_sem
):
    mine = out_ref.at[chip * 2 + core]
    copies = {}
    for k in range(chips - 1, 0, -1):
        device = (dp_index, lax.rem(chip + k, chips) * 2 + core)
        copies[k] = send(x_ref, mine, send_sem.at[k], recv_sem.at[k], device)
        copies[k].start()
    passed = [send(x_ref, mine, pass_sem.at[0], take_sem.at[0], sibling)]
    passed[0].start()

    def pass_on():
        for k in range(1, chips):
            copies[k].wait_recv()
            block = out_ref.at[lax.rem(chip + chips - k, chips) * 2 + core]
            onward = send(block, block, pass_sem.at[k], take_sem.at[k], sibling)
            onward.start()
            passed.append(onward)

    def finish():
        for copy in copies.values():
            copy.wait_send()
        for onward in passed:
            onward.wait()

    return pass_on, finish


def front(packed, x, collective_id):
    chips = lax.axis_size("seq") // 2
    n_dp = lax.axis_size("dp")
    return pl.pallas_call(
        front_kernel,
        out_shape=[
            jax.ShapeDtypeStruct(packed.shape, packed.dtype),
            jax.ShapeDtypeStruct((2 * chips,) + x.shape, x.dtype),
        ],
        in_specs=[VMEM, VMEM],
        out_specs=[ANY, ANY],
        scratch_shapes=[DMA((2,)), DMA((n_dp,)), DMA((n_dp,))] + [DMA((chips,))] * 4,
        compiler_params=comm_params(collective_id, 24),
        cost_estimate=takes(90),
        name="front",
    )(packed, x)


def sum_seq_kernel(x_ref, out_ref, taken, sent, arrived, pass_sem, take_sem, send_sem, recv_sem):
    n_seq, n_dp, seq_index, dp_index = places()
    chips, chip, core = n_seq // 2, seq_index // 2, lax.rem(seq_index, 2)
    peers = [lax.rem(chip + k, chips) for k in range(chips)]
    sibling = (dp_index, chip * 2 + 1 - core)
    greet([(dp_index, p * 2 + core) for p in peers[1:]] + [sibling])
    order = list(range(chips - 1, 0, -1)) + [0]
    passed = {}
    for k in order:
        block = x_ref.at[peers[k] * 2 + 1 - core]
        passed[k] = send(block, taken.at[k], pass_sem.at[k], take_sem.at[k], sibling)
        passed[k].start()
    copies = {}
    for k in order[:-1]:
        passed[k].wait_recv()
        own = x_ref[peers[k] * 2 + core].astype(f32)
        sent[k] = (own + taken[k].astype(f32)).astype(sent.dtype)
        device = (dp_index, peers[k] * 2 + core)
        copies[k] = send(sent.at[k], arrived.at[k], send_sem.at[k], recv_sem.at[k], device)
        copies[k].start()
    passed[0].wait_recv()
    total = x_ref[seq_index].astype(f32) + taken[0].astype(f32)
    for k in range(1, chips):
        copies[k].wait_recv()
        total = total + arrived[k].astype(f32)
    out_ref[...] = total
    for k in order:
        passed[k].wait_send()
    for k in order[:-1]:
        copies[k].wait_send()


def sum_seq(x, collective_id):
    blocks, rows, columns = x.shape
    chips = blocks // 2
    slots = pltpu.VMEM((chips, rows, columns), x.dtype)
    return pl.pallas_call(
        sum_seq_kernel,
        out_shape=jax.ShapeDtypeStruct((rows, columns), f32),
        in_specs=[VMEM],
        out_specs=VMEM,
        scratch_shapes=[slots, slots, slots] + [DMA((chips,))] * 4,
        compiler_params=comm_params(collective_id, 40),
        cost_estimate=takes(28),
        name="sum_seq",
    )(x)


def collect_kernel(
    qkv_ref, out_ref, qkv_sum, out_sum, qkv_sent, qkv_came, out_sent, out_came, total, own_sem,
    send_sem, recv_sem, a_send, a_recv
):
    n_seq, n_dp, seq_index, dp_index = places()
    seq_peers = [lax.rem(seq_index + k, n_seq) for k in range(n_seq)]
    greet(
        [(dp_index, p) for p in seq_peers[1:]]
        + [(lax.rem(dp_index + k, n_dp), seq_index) for k in range(1, n_dp)]
    )
    sums = relay_sum(
        [lambda block: qkv_ref[:, block].astype(f32), lambda block: out_ref[block].astype(f32)],
        [qkv_sent, out_sent],
        [qkv_came, out_came],
        dp_index,
        n_dp,
        lambda place: (place, seq_index),
        send_sem,
        recv_sem,
        lambda block: None,
    )
    total[...] = sums[0].astype(total.dtype)
    across = []
    for k in range(1, n_seq):
        copy = send(
            total.at[seq_peers[k]],
            qkv_sum.at[seq_index],
            a_send.at[k],
            a_recv.at[k],
            (dp_index, seq_peers[k]),
        )
        copy.start()
        across.append(copy)
    own = pltpu.make_async_copy(total.at[seq_index], qkv_sum.at[seq_index], own_sem)
    own.start()
    out_sum[...] = sums[1].astype(out_sum.dtype)
    for copy in across:
        copy.wait()
    own.wait()


def collect_attention(qkv, out, collective_id):
    n_seq = lax.axis_size("seq")
    n_dp = lax.axis_size("dp")
    tail = qkv.shape[2:]
    return pl.pallas_call(
        collect_kernel,
        out_shape=[
            jax.ShapeDtypeStruct((n_seq,) + tail, qkv.dtype),
            jax.ShapeDtypeStruct(out.shape[1:], out.dtype),
        ],
        in_specs=[VMEM, VMEM],
        out_specs=[VMEM, VMEM],
        scratch_shapes=[
            pltpu.VMEM((n_dp, n_seq) + tail, qkv.dtype),
            pltpu.VMEM((n_dp + 1, n_seq) + tail, qkv.dtype),
            pltpu.VMEM((n_dp,) + out.shape[1:], out.dtype),
            pltpu.VMEM((n_dp + 1,) + out.shape[1:], out.dtype),
            pltpu.VMEM((n_seq,) + tail, qkv.dtype),
            DMA,
            DMA((2, 2, n_dp)),
            DMA((2, 2, n_dp)),
            DMA((n_seq,)),
            DMA((n_seq,)),
        ],
        compiler_params=comm_params(collective_id, 48),
        cost_estimate=takes(75),
        name="collect_attention",
    )(qkv, out)


def ring_chip(place, chips):
    return jnp.where(place < chips // 2, 2 * place, 2 * (chips - 1 - place) + 1)


def ring_place(chip, chips):
    line = chip // 2
    return jnp.where(lax.rem(chip, 2) == 0, line, chips - 1 - line)


class Ring:
    def __init__(self, chips, chip, core, dp_index, send_sem, recv_sem):
        self.chips = chips
        self.place = ring_place(chip, chips)
        self.core = core
        self.dp_index = dp_index
        self.send_sem = send_sem
        self.recv_sem = recv_sem
        self.last = chips // 2

    def at(self, offset):
        return ring_chip(lax.rem(self.place + offset + self.chips, self.chips), self.chips)

    def device(self, way):
        return (self.dp_index, self.at(1 if way == 0 else -1) * 2 + self.core)

    def leg(self, view, way, step, src, dst):
        return send(
            src, dst, self.send_sem.at[view, way, step], self.recv_sem.at[view, way, step], self.device(way)
        )


def arrange_kernel(ff_blocks, units, ug_ref, down_ref, *refs):
    piece_ref = refs[-1]
    unit = units[pl.program_id(0)]
    rows, wide = piece_ref.shape[1:]
    sub, width = down_ref.shape[1:]
    groups = width // wide

    @pl.when((unit >= 4) & (unit < 4 + 2 * ff_blocks))
    def _():
        piece_ref[0] = ug_ref[0]

    @pl.when(unit >= 4 + 2 * ff_blocks)
    def _():
        for g in range(groups):
            piece_ref[0, g * sub : (g + 1) * sub, :] = down_ref[0, :, g * wide : (g + 1) * wide]

    if len(refs) == 3:
        qkv_ref, out_ref = refs[:2]
        blocks, _, columns = qkv_ref.shape
        step = columns // 3
        share = wide // step
        for u in range(3):

            @pl.when(unit == u)
            def _():
                for block in range(blocks):
                    g, h = block // share, block % share
                    piece_ref[0, g * sub : (g + 1) * sub, h * step : (h + 1) * step] = qkv_ref[
                        block, :, u * step : (u + 1) * step
                    ]

        @pl.when(unit == 3)
        def _():
            for g in range(groups):
                piece_ref[0, g * sub : (g + 1) * sub, :] = out_ref[:, g * wide : (g + 1) * wide]


def arrange(units, ug, down, attention):
    n_dp, slots = units.shape
    rows, wide = ug.shape[1:]
    sub, width = down.shape[1:]
    ff_blocks = down.shape[0]
    specs = [
        pl.BlockSpec(
            (1, rows, wide), lambda k, u: (jnp.clip(u[k] - 4, 0, 2 * ff_blocks - 1), 0, 0)
        ),
        pl.BlockSpec(
            (1, sub, width),
            lambda k, u: (jnp.clip(u[k] - 4 - 2 * ff_blocks, 0, ff_blocks - 1), 0, 0),
        ),
    ]
    if attention:
        specs.append(pl.BlockSpec(attention[0].shape, lambda k, u: (0, 0, 0)))
        specs.append(pl.BlockSpec(attention[1].shape, lambda k, u: (0, 0)))
    return pl.pallas_call(
        functools.partial(arrange_kernel, ff_blocks),
        out_shape=jax.ShapeDtypeStruct((n_dp * slots, rows, wide), bf),
        grid_spec=pltpu.PrefetchScalarGridSpec(
            num_scalar_prefetch=1,
            grid=(n_dp * slots,),
            in_specs=specs,
            out_specs=pl.BlockSpec((1, rows, wide), lambda k, u: (k, 0, 0)),
        ),
        compiler_params=pltpu.CompilerParams(vmem_limit_bytes=16 << 20),
        cost_estimate=takes(7),
        name="arrange",
    )(units.reshape(-1), ug, down, *attention).reshape(n_dp, slots, rows, wide)


def column_sum(ref, taken, sent, came, send_sem, recv_sem, pass_sem, take_sem, between):
    n_seq, n_dp, seq_index, dp_index = places()
    core = lax.rem(seq_index, 2)
    sibling = (dp_index, seq_index + 1 - 2 * core)

    def onward(block):
        return send(
            ref.at[1 - core, block], taken.at[block], pass_sem.at[block], take_sem.at[block], sibling
        )

    for block in [b for k in range(n_dp // 2) for b in (n_dp - 1 - k, k)]:
        onward(block).start()
    total = relay_sum(
        [lambda block: ref[core, block].astype(f32) + taken[block].astype(f32)],
        [sent],
        [came],
        dp_index,
        n_dp,
        lambda place: (place, seq_index),
        send_sem,
        recv_sem,
        lambda block: onward(block).wait_recv(),
        between,
    )[0]
    for block in range(n_dp):
        onward(block).wait_send()
    return total


def grads_kernel(band, has_tokens, *refs):
    n_seq, n_dp, seq_index, dp_index = places()
    chips, chip, core = n_seq // 2, seq_index // 2, lax.rem(seq_index, 2)
    sibling = (dp_index, chip * 2 + 1 - core)
    refs = list(refs)

    def take(count):
        taken, refs[:count] = refs[:count], []
        return taken

    owns = take(3) if band else None
    (x_ref,) = take(1)
    tokens_ref = take(1)[0] if has_tokens else None
    outs = take(2) if band else None
    (x_out,) = take(1)
    tokens_out = take(1)[0] if has_tokens else None
    x_taken, z_sent, z_came, z_send, z_recv, x_pass, x_take = take(7)
    if has_tokens:
        token_own, token_send, token_recv, token_pass, token_take = take(5)
    greet(
        [(lax.rem(dp_index + k, n_dp), seq_index) for k in range(1, n_dp)]
        + [(dp_index, lax.rem(chip + k, chips) * 2 + core) for k in range(1, chips)]
        + [sibling]
    )
    if band:
        half_came, full_sent, full_came, mine = take(3), take(3), take(3), take(3)
        side_out, ring_send, ring_recv, side_send, side_recv, own_sem = take(6)
        ug_out, down_out = outs
        ring = Ring(chips, chip, core, dp_index, ring_send, ring_recv)
        begin, size = band
        blocks = down_out.shape[0]
        pair = blocks // 2
        half = ug_out.shape[2] // 2
        last = ring.last

        def own(view, place, way):
            if view == 0:
                units = pl.ds(0, blocks) if way is None else pl.ds(way * pair, pair)
                return owns[0].at[units, place, pl.ds(begin, size), :]
            columns = pl.ds(0, blocks * half) if way is None else pl.ds(way * pair * half, pair * half)
            return owns[view].at[place, :, :, pl.ds(begin, size), columns]

        def leg(view, way, step):
            if step == 0:
                src = own(view, ring.at(last), way)
                return ring.leg(view, way, step, src, half_came[view].at[way])
            src, dst = full_sent[view].at[step - 1, way], full_came[view].at[step - 1, way]
            return ring.leg(view, way, step, src, dst)

        def own_copy(view, way, step):
            distance = last - step
            if step == last:
                return pltpu.make_async_copy(
                    own(view, chip, None), mine[view], own_sem.at[view, 0, step - 1]
                )
            src = own(view, ring.at(distance if way == 0 else -distance), None)
            return pltpu.make_async_copy(
                src, full_sent[view].at[step - 1, way], own_sem.at[view, way, step - 1]
            )

        for view in range(3):
            for way in range(2):
                leg(view, way, 0).start()
        for step in range(1, last + 1):
            for view in range(3):
                for way in range(2 if step < last else 1):
                    own_copy(view, way, step).start()

        def ring_step(step):
            for view in range(3):
                for way in range(2):
                    own_copy(view, way, step).wait()
                    leg(view, way, step - 1).wait_recv()
                    full = full_sent[view]
                    if step > 1:
                        value = full[step - 1, way].astype(f32)
                        value = value + full_came[view][step - 2, way].astype(f32)
                        full[step - 1, way] = value.astype(bf)
                    elif view == 0:
                        units = slice(way * pair, (way + 1) * pair)
                        value = full[0, way, units].astype(f32) + half_came[0][way].astype(f32)
                        full[0, way, units] = value.astype(bf)
                    else:
                        columns = slice(way * pair * half, (way + 1) * pair * half)
                        value = full[0, way, :, :, :, columns].astype(f32)
                        value = value + half_came[view][way].astype(f32)
                        full[0, way, :, :, :, columns] = value.astype(bf)
                    leg(view, way, step).start()

    if has_tokens:
        own_tokens = pltpu.make_async_copy(tokens_ref, tokens_out.at[seq_index], token_own)
        own_tokens.start()
        pass_on, finish = spread_blocks(
            tokens_ref, tokens_out, chips, chip, core, dp_index, sibling,
            token_send, token_recv, token_pass, token_take,
        )

    def between(step):
        if step == 0:
            if band:
                for ring_at in range(1, last):
                    ring_step(ring_at)
            if has_tokens:
                pass_on()

    x_out[...] = column_sum(
        x_ref, x_taken, z_sent, z_came, z_send, z_recv, x_pass, x_take, between
    )
    if has_tokens:
        own_tokens.wait()
        finish()
    if not band:
        return
    for view in range(3):
        own_copy(view, 0, last).wait()
        for way in range(2):
            leg(view, way, last - 1).wait_recv()
        if last > 1:
            came = [full_came[view][last - 2, way].astype(f32) for way in range(2)]
            value = mine[view][...].astype(f32) + came[0] + came[1]
        else:
            axis = 0 if view == 0 else 3
            came = [half_came[view][way].astype(f32) for way in range(2)]
            value = mine[view][...].astype(f32) + jnp.concatenate(came, axis=axis)
        value = value.astype(bf)
        if view == 0:
            down_out[...] = value
            continue
        value = value.reshape(2, n_dp * size, blocks * half)
        for k in range(blocks):
            unit = (view - 1) * blocks + k

            @pl.when(core == 0)
            def _():
                ug_out[unit, :, :half] = value[0, :, k * half : (k + 1) * half]
                side_out[unit] = value[1, :, k * half : (k + 1) * half]

            @pl.when(core != 0)
            def _():
                ug_out[unit, :, half:] = value[1, :, k * half : (k + 1) * half]
                side_out[unit] = value[0, :, k * half : (k + 1) * half]

    place = pl.ds(pl.multiple_of(core * half, half), half)
    side = send(side_out, ug_out.at[:, :, place], side_send, side_recv, sibling)
    side.start()
    side.wait()
    for step in range(last):
        for view in range(3):
            for way in range(2):
                leg(view, way, step).wait_send()


def sum_grads(band, sums, x, tokens, collective_id):
    _, n_dp, shard, width = x.shape
    chips = lax.axis_size("seq") // 2
    steps = chips // 2
    vmem = pltpu.VMEM
    operands, in_specs, out_shape, out_specs = [], [], [], []
    scratch = [
        vmem((n_dp, shard, width), bf),
        vmem((n_dp, shard, width), bf),
        vmem((n_dp + 1, shard, width), bf),
        DMA((1, 2, n_dp)),
        DMA((1, 2, n_dp)),
        DMA((n_dp,)),
        DMA((n_dp,)),
    ]
    if tokens is not None:
        scratch += [DMA] + [DMA((chips,))] * 4
    if band:
        size = band[1]
        blocks = sums[0].shape[0]
        wide = sums[1].shape[-1]
        half = wide // blocks
        operands += sums
        in_specs += [ANY] * 3
        out_shape += [
            jax.ShapeDtypeStruct((2 * blocks, n_dp * size, 2 * half), bf),
            jax.ShapeDtypeStruct((blocks, size, width), bf),
        ]
        out_specs += [VMEM] * 2
        side = (2, n_dp, size)
        fulls = [(blocks, size, width), side + (wide,), side + (wide,)]
        halves = [(blocks // 2, size, width), side + (wide // 2,), side + (wide // 2,)]
        scratch += [vmem((2,) + s, bf) for s in halves]
        scratch += [vmem((max(steps - 1, 1), 2) + s, bf) for s in fulls] * 2
        scratch += [vmem(s, bf) for s in fulls]
        scratch += [
            vmem((2 * blocks, n_dp * size, half), bf),
            DMA((3, 2, steps)),
            DMA((3, 2, steps)),
            DMA,
            DMA,
            DMA((3, 2, steps)),
        ]
    operands.append(x)
    in_specs.append(VMEM)
    out_shape.append(jax.ShapeDtypeStruct((shard, width), f32))
    out_specs.append(VMEM)
    if tokens is not None:
        operands.append(tokens)
        in_specs.append(VMEM)
        out_shape.append(jax.ShapeDtypeStruct((2 * chips,) + tokens.shape, bf))
        out_specs.append(ANY)
    return pl.pallas_call(
        functools.partial(grads_kernel, band, tokens is not None),
        out_shape=out_shape,
        in_specs=in_specs,
        out_specs=out_specs,
        scratch_shapes=scratch,
        compiler_params=comm_params(collective_id, 56),
        cost_estimate=takes(75),
        name="sum_grads",
    )(*operands)


def turn_half(values):
    half = values.shape[-1] // 2
    return jnp.concatenate([-values[:, half:], values[:, :half]], axis=-1)


def forward_kernel(has_late, first_slots, ff_blocks, *refs):
    info, first_ref = refs[:2]
    refs = refs[2:]
    if has_late:
        late_ref, refs = refs[0], refs[1:]
    x1_ref, cos_ref, sin_ref, doc_row, doc_col, tokens_ref, cot_ref = refs[:7]
    qkv_all, out_all, query_out, key_out, value_out, mixed_out, stat_out, residual_out = refs[7:15]
    up_all, gate_all, down_all, x_all, cot_all = refs[15:20]
    ug_all = (up_all, gate_all)
    refs = refs[1:]
    att_stage, out_stage, part, taken, sent, arrived, x_stage = refs[19:26]
    mine_stage, given_stage, down_stage = refs[26:29]
    (own_sem, a_send, a_recv, w_send, w_recv, s_pass, s_take, s_send, s_recv, cot_send, cot_recv,
     late_send, late_recv, late_own, stage_own, side_send, side_recv, ring_send, ring_recv,
     send_sem, recv_sem, pass_sem, take_sem) = refs[29:52]
    late_tables = refs[52:]
    n_seq, n_dp, seq_index, dp_index = places()
    chips, chip, core = n_seq // 2, seq_index // 2, lax.rem(seq_index, 2)
    sibling = (dp_index, chip * 2 + 1 - core)
    seq_peers = [lax.rem(seq_index + k, n_seq) for k in range(n_seq)]
    dp_peers = [lax.rem(dp_index + k, n_dp) for k in range(n_dp)]
    rows, wide = first_ref.shape[1:]
    sub = rows // n_dp
    half = wide // 2
    step_cols = att_stage.shape[2] // 3
    share = wide // step_cols
    tokens, width = tokens_ref.shape
    greet([(dp_index, p) for p in seq_peers[1:]] + [(p, seq_index) for p in dp_peers[1:]])

    for u in range(3):
        for block in range(n_seq):
            g, h = block // share, block % share
            att_stage[block, :, u * step_cols : (u + 1) * step_cols] = first_ref[
                info[u], g * sub : (g + 1) * sub, h * step_cols : (h + 1) * step_cols
            ]
    for g in range(n_dp):
        out_stage[:, g * wide : (g + 1) * wide] = first_ref[info[3], g * sub : (g + 1) * sub, :]
    own = [
        pltpu.make_async_copy(att_stage.at[seq_index], qkv_all.at[seq_index, dp_index], own_sem.at[0]),
        pltpu.make_async_copy(out_stage, out_all.at[dp_index], own_sem.at[1]),
    ]
    cot_own = pltpu.make_async_copy(cot_ref, cot_all.at[core], own_sem.at[2])
    cot_copy = send(cot_ref, cot_all.at[core], cot_send, cot_recv, sibling)
    across = []
    for k in range(1, n_seq):
        copy = send(
            att_stage.at[seq_peers[k]],
            qkv_all.at[seq_index, dp_index],
            a_send.at[k],
            a_recv.at[k],
            (dp_index, seq_peers[k]),
        )
        copy.start()
        across.append(copy)
    for copy in own:
        copy.start()
    cot_copy.start()
    cot_own.start()
    for copy in own:
        copy.wait()
    for copy in across:
        copy.wait_recv()
    relay_gather(
        [lambda block: qkv_all.at[:, block], lambda block: out_all.at[block]],
        dp_index,
        n_dp,
        lambda place: (place, seq_index),
        w_send,
        w_recv,
        lambda block: None,
    )

    def band(c):
        return pl.ds(c * sub, sub)

    def late_copies(c):
        copies = []
        for k in range(1, n_dp):
            copies.append(
                send(
                    late_ref.at[dp_peers[k], :, band(c)],
                    late_tables[c].at[dp_index],
                    late_send.at[c, k],
                    late_recv.at[c, k],
                    (dp_peers[k], seq_index),
                )
            )
        return copies

    def late_own_copy(c):
        return pltpu.make_async_copy(
            late_ref.at[dp_index, :, band(c)], late_tables[c].at[dp_index], late_own.at[c]
        )

    def late_start(c):
        if not has_late or c >= n_dp:
            return
        if c:
            for copy in late_copies(c - 1):
                copy.wait_send()
        for copy in late_copies(c):
            copy.start()
        late_own_copy(c).start()

    late_start(0)

    seq_len = x1_ref.shape[0]
    heads = query_out.shape[1] // HD
    block_rows = min(256, seq_len)
    head_cols = heads * HD
    qkv_weight = qkv_all[...].reshape(width, 3 * head_cols)

    def project(b, carry):
        at = pl.ds(pl.multiple_of(b * block_rows, block_rows), block_rows)
        result = jnp.dot(x1_ref[at, :], qkv_weight, preferred_element_type=f32)
        cosine, sine = cos_ref[at, :], sin_ref[at, :]
        for h in range(heads):
            place = slice(h * HD, (h + 1) * HD)
            for part_id, out in ((0, query_out), (1, key_out)):
                begin = part_id * head_cols + h * HD
                values = result[:, begin : begin + HD]
                out[at, place] = (values * cosine + turn_half(values) * sine).astype(bf)
        value_out[at, :] = result[:, 2 * head_cols :].astype(bf)
        return carry

    lax.fori_loop(0, seq_len // block_rows, project, 0)

    def attend(b, carry):
        begin = pl.multiple_of(b * block_rows, block_rows)
        at = pl.ds(begin, block_rows)
        query_pos = begin + lax.broadcasted_iota(jnp.int32, (block_rows, seq_len), 0)
        key_pos = lax.broadcasted_iota(jnp.int32, (block_rows, seq_len), 1)
        allowed = (doc_col[at, :] == doc_row[...]) & (key_pos <= query_pos)
        for h in range(heads):
            place = slice(h * HD, (h + 1) * HD)
            scores = lax.dot_general(
                query_out[at, place],
                key_out[:, place],
                (((1,), (1,)), ((), ())),
                preferred_element_type=f32,
            )
            scores = jnp.where(allowed, scores * (float(HD) ** (-0.5)), masked_score)
            peak = jnp.max(scores, axis=-1, keepdims=True)
            raised = jnp.exp(scores - peak)
            total = jnp.sum(raised, axis=-1, keepdims=True)
            prob = (raised * (1.0 / total)).astype(bf)
            mixed = jnp.dot(prob, value_out[:, place], preferred_element_type=f32)
            mixed_out[at, place] = mixed.astype(bf)
            stat_out[at, place] = jnp.broadcast_to(peak + jnp.log(total), (block_rows, HD))
        return carry

    lax.fori_loop(0, seq_len // block_rows, attend, 0)
    out_weight = out_all[...].reshape(rows, width)

    def combine(b, carry):
        at = pl.ds(pl.multiple_of(b * tokens, tokens), tokens)
        part[b] = jnp.dot(mixed_out[at, :], out_weight, preferred_element_type=f32).astype(bf)
        return carry

    lax.fori_loop(0, n_seq, combine, 0)

    chip_peers = [lax.rem(chip + k, chips) for k in range(chips)]
    order = list(range(chips - 1, 0, -1)) + [0]
    passed = {}
    for k in order:
        block = part.at[chip_peers[k] * 2 + 1 - core]
        passed[k] = send(block, taken.at[k], s_pass.at[k], s_take.at[k], sibling)
        passed[k].start()
    copies = {}
    for k in order[:-1]:
        passed[k].wait_recv()
        value = part[chip_peers[k] * 2 + core].astype(f32)
        sent[k] = (value + taken[k].astype(f32)).astype(bf)
        device = (dp_index, chip_peers[k] * 2 + core)
        copies[k] = send(sent.at[k], arrived.at[k], s_send.at[k], s_recv.at[k], device)
        copies[k].start()

    ring = Ring(chips, chip, core, dp_index, None, None)
    pair = ff_blocks // 2

    def ring_leg(c, view, way, step, arriving):
        distance = step if arriving else step - 1
        block = ring.at(-distance if way == 0 else distance)
        units = pl.ds(way * pair, pair) if step == ring.last else pl.ds(0, ff_blocks)
        if view == 0:
            ref = down_all.at[units, block, :, pl.ds(c * wide, wide)]
        else:
            columns = pl.ds(0, ff_blocks * half)
            if step == ring.last:
                columns = pl.ds(way * pair * half, pair * half)
            ref = ug_all[view - 1].at[block, :, band(c), columns]
        return send(
            ref, ref, ring_send.at[c, view, way, step - 1], ring_recv.at[c, view, way, step - 1],
            ring.device(way),
        )

    def side_copies(c):
        return [
            send(
                given_stage.at[c, k],
                ug_all[k].at[chip, core, band(c)],
                side_send.at[c, k],
                side_recv.at[c, k],
                sibling,
            )
            for k in range(2)
        ]

    def begin_band(c):
        if has_late:
            for copy in late_copies(c):
                copy.wait_recv()
            late_own_copy(c).wait()
            late_start(c + 1)
            table = late_tables[c]
            late_slots = table.shape[1]
        for u in range(3 * ff_blocks):
            value = first_ref[info[4 + u], band(c), :]
            if has_late:
                code = info[4 + 3 * ff_blocks + u]
                other = table[code // late_slots, lax.rem(code, late_slots)]
                use_late = jnp.full(value.shape, info[4 + 6 * ff_blocks + u], jnp.int32) != 0
                value = jnp.where(use_late, other, value)
            if u < 2 * ff_blocks:
                left, right = value[:, :half], value[:, half:]
                k, j = u // ff_blocks, u % ff_blocks
                columns = slice(j * half, (j + 1) * half)

                @pl.when(core == 0)
                def _():
                    mine_stage[c, k, :, columns] = left
                    given_stage[c, k, :, columns] = right

                @pl.when(core != 0)
                def _():
                    mine_stage[c, k, :, columns] = right
                    given_stage[c, k, :, columns] = left
            else:
                down_stage[c, u - 2 * ff_blocks] = value
        for copy in side_copies(c):
            copy.start()
        local = [
            pltpu.make_async_copy(
                mine_stage.at[c, k], ug_all[k].at[chip, core, band(c)], stage_own.at[c, k]
            )
            for k in range(2)
        ]
        local.append(
            pltpu.make_async_copy(
                down_stage.at[c], down_all.at[:, chip, :, pl.ds(c * wide, wide)], stage_own.at[c, 2]
            )
        )
        for copy in local:
            copy.start()
        for copy in local:
            copy.wait()
        for copy in side_copies(c):
            copy.wait_recv()
        for view in range(3):
            for way in range(2):
                ring_leg(c, view, way, 1, False).start()

    def carry_band(c, step):
        for view in range(3):
            for way in range(2):
                ring_leg(c, view, way, step - 1, True).wait_recv()
                ring_leg(c, view, way, step, False).start()

    begin_band(0)
    passed[0].wait_recv()
    total = part[seq_index].astype(f32) + taken[0].astype(f32)
    for k in range(1, chips):
        copies[k].wait_recv()
        total = total + arrived[k].astype(f32)
    residual = tokens_ref[...] + total
    residual_out[...] = residual
    center = residual - jnp.mean(residual, axis=-1, keepdims=True)
    spread = jnp.mean(center * center, axis=-1, keepdims=True)
    x_stage[...] = (center * lax.rsqrt(spread + norm_eps)).astype(bf)
    for c in range(1, n_dp):
        begin_band(c)
        for step in range(2, ring.last + 1):
            carry_band(c - 1, step)

    own_x = pltpu.make_async_copy(x_stage, x_all.at[core, dp_index], own_sem.at[3])
    own_x.start()
    own_x.wait()

    def onward(block):
        ref = x_all.at[core, block]
        return send(ref, ref, pass_sem.at[block], take_sem.at[block], sibling)

    onward(dp_index).start()
    relay_gather(
        [lambda block: x_all.at[core, block]],
        dp_index,
        n_dp,
        lambda place: (place, seq_index),
        send_sem,
        recv_sem,
        lambda block: onward(block).start(),
        lambda step: carry_band(n_dp - 1, 2) if step == 1 and ring.last > 1 else None,
    )
    for step in range(3, ring.last + 1):
        carry_band(n_dp - 1, step)
    for c in range(n_dp):
        for view in range(3):
            for way in range(2):
                ring_leg(c, view, way, ring.last, True).wait_recv()
                for step in range(1, ring.last + 1):
                    ring_leg(c, view, way, step, False).wait_send()
        for copy in side_copies(c):
            copy.wait_send()
        if has_late:
            if c == n_dp - 1:
                for copy in late_copies(c):
                    copy.wait_send()
    for block in range(n_dp):
        onward(block).wait_send()
        ref = x_all.at[1 - core, block]
        send(ref, ref, pass_sem.at[block], take_sem.at[block], sibling).wait_recv()
    for k in order:
        passed[k].wait_send()
    for k in order[:-1]:
        copies[k].wait_send()
    for copy in across:
        copy.wait_send()
    cot_copy.wait_send()
    cot_own.wait()
    ref = cot_all.at[1 - core]
    send(ref, ref, cot_send, cot_recv, sibling).wait_recv()


def forward(info, first_table, late, x1, cosine, sine, doc, tokens, cot, ff_blocks, first_slots, collective_id):
    n_seq = lax.axis_size("seq")
    n_dp = lax.axis_size("dp")
    chips = n_seq // 2
    rows, wide = first_table.shape[1:]
    sub = rows // n_dp
    half = wide // 2
    seq_len, width = x1.shape
    head_cols = width // n_seq
    shard = tokens.shape[0]
    steps = chips // 2
    vmem = pltpu.VMEM
    low = lambda *shape: jax.ShapeDtypeStruct(shape, bf)
    has_late = late is not None
    blocks = vmem((chips, shard, width), bf)
    return pl.pallas_call(
        functools.partial(forward_kernel, has_late, first_slots, ff_blocks),
        out_shape=[
            low(n_seq, n_dp, sub, 3 * head_cols),
            low(n_dp, sub, width),
            low(seq_len, head_cols),
            low(seq_len, head_cols),
            low(seq_len, head_cols),
            low(seq_len, head_cols),
            jax.ShapeDtypeStruct((seq_len, head_cols), f32),
            jax.ShapeDtypeStruct((shard, width), f32),
            low(chips, 2, rows, ff_blocks * half),
            low(chips, 2, rows, ff_blocks * half),
            low(ff_blocks, chips, sub, width),
            low(2, n_dp, shard, width),
            low(2, n_dp, shard, width),
        ],
        in_specs=[pl.BlockSpec(memory_space=pltpu.SMEM), VMEM]
        + [ANY] * has_late
        + [VMEM] * 7,
        out_specs=[VMEM] * 8 + [ANY] * 5,
        scratch_shapes=[
            vmem((n_seq, sub, 3 * head_cols), bf),
            vmem((sub, width), bf),
            vmem((n_seq, shard, width), bf),
            blocks,
            blocks,
            blocks,
            vmem((shard, width), bf),
            vmem((n_dp, 2, sub, ff_blocks * half), bf),
            vmem((n_dp, 2, sub, ff_blocks * half), bf),
            vmem((n_dp, ff_blocks, sub, wide), bf),
            DMA((4,)),
            DMA((n_seq,)),
            DMA((n_seq,)),
            DMA((2, 2, n_dp)),
            DMA((2, 2, n_dp)),
            DMA((chips,)),
            DMA((chips,)),
            DMA((chips,)),
            DMA((chips,)),
            DMA,
            DMA,
            DMA((n_dp, n_dp)),
            DMA((n_dp, n_dp)),
            DMA((n_dp,)),
            DMA((n_dp, 3)),
            DMA((n_dp, 2)),
            DMA((n_dp, 2)),
            DMA((n_dp, 3, 2, steps)),
            DMA((n_dp, 3, 2, steps)),
            DMA((1, 2, n_dp)),
            DMA((1, 2, n_dp)),
            DMA((n_dp,)),
            DMA((n_dp,)),
        ]
        + [vmem((n_dp, late.shape[1], sub, wide), bf) for _ in range(n_dp if has_late else 0)],
        compiler_params=comm_params(collective_id, 58),
        cost_estimate=takes(230),
        name="forward",
    )(
        info,
        first_table,
        *([late] if has_late else []),
        x1,
        cosine,
        sine,
        doc[None, :],
        doc[:, None],
        tokens,
        cot,
    )


def local(block_input, cotangent, doc_lengths, owners, master, first_moment, second_moment):
    n_seq = lax.axis_size("seq")
    n_dp = lax.axis_size("dp")
    seq_index = lax.axis_index("seq")
    dp_index = lax.axis_index("dp")
    core = seq_index % 2
    _, shard_len, width = block_input.shape
    rows = master.shape[0]
    per_owner = master.shape[1]
    chips = n_seq // 2
    sub = rows // n_dp
    wide = width // n_dp
    half = chips * sub
    heads = H // n_seq
    head_cols = heads * HD
    seq_len = shard_len * n_seq
    ff_blocks = FF // D
    first_slots = min(4, per_owner)
    unit_count = owners.shape[0]
    score_scale = float(HD) ** (-0.5)

    unit_slot = unit_slots(owners, per_owner)
    place = unit_slot - owners * per_owner
    all_slots = jnp.arange(n_dp * per_owner, dtype=jnp.int32)
    match = unit_slot[None, :] == all_slots[:, None]
    slot_unit = jnp.sum(
        jnp.where(match, jnp.arange(unit_count, dtype=jnp.int32)[None, :] + 1, 0), axis=1
    ) - 1
    slot_unit = slot_unit.reshape(n_dp, per_owner)
    own_units = lax.dynamic_index_in_dim(slot_unit, dp_index, 0, keepdims=False)
    is_col = (own_units >= 4) & (own_units < 4 + 2 * ff_blocks)


    tokens = block_input.astype(f32).reshape(shard_len, width)
    normed_one, inv_one = norm_parts(tokens)
    packed = pack(master, is_col.astype(jnp.int32), n_dp, n_seq, first_slots)
    first_table, normed_one_all = front(packed[0], normed_one.astype(bf), 2)
    first_table = first_table.reshape(n_dp * first_slots, rows, wide)
    normed_one_all = normed_one_all.reshape(seq_len, width)
    upstream = cotangent.reshape(shard_len, width)
    upstream_column = lax.all_gather(upstream, "dp", axis=0)
    positions = jnp.arange(seq_len, dtype=jnp.int32)
    cosine, sine = rope_tables(positions.astype(f32), HD)
    doc_ends = jnp.cumsum(doc_lengths[0])
    doc = jnp.sum((positions[:, None] >= doc_ends[None, :]).astype(jnp.int32), axis=1)
    late_slots = per_owner - first_slots
    info = jnp.concatenate(
        [
            owners * first_slots + jnp.minimum(place, first_slots - 1),
            (owners * late_slots + jnp.maximum(place - first_slots, 0))[4:],
            (place >= first_slots)[4:],
        ]
    ).astype(jnp.int32)
    (
        qkv_weight,
        out_weight,
        queries,
        keys,
        values,
        attended_low,
        log_total,
        residual,
        up_weight,
        gate_weight,
        down_weight,
        normed_two_all,
        upstream_all,
    ) = forward(
        info,
        first_table,
        packed[1] if late_slots else None,
        normed_one_all,
        cosine,
        sine,
        doc,
        tokens,
        upstream_column,
        ff_blocks,
        first_slots,
        1,
    )
    qkv_weight = qkv_weight.reshape(width, 3 * head_cols)
    out_weight = out_weight.reshape(rows, width)
    queries, keys, values = (a.reshape(seq_len, heads, HD) for a in (queries, keys, values))
    log_total = log_total.reshape(seq_len, heads, HD)[:, :, :1].transpose(1, 0, 2)
    cosine = cosine[:, None, :]
    sine = sine[:, None, :]
    normed_two, inv_two = norm_parts(residual)
    columns = ff_blocks * half
    up_weight = up_weight.reshape(width, columns)
    gate_weight = gate_weight.reshape(width, columns)
    down_weight = down_weight.reshape(columns, width)
    normed_two_all = normed_two_all.reshape(-1, width)
    upstream_all = upstream_all.reshape(-1, width)

    def times(left, right, left_axis, right_axis):
        return lax.dot_general(
            left, right, (((left_axis,), (right_axis,)), ((), ())), preferred_element_type=f32
        )

    up_proj = times(normed_two_all, up_weight, 1, 0)
    gate_proj = times(normed_two_all, gate_weight, 1, 0)
    gate_sig = jax.nn.sigmoid(gate_proj)
    silu_value = gate_proj * gate_sig
    hidden_low = (silu_value * up_proj).astype(bf)
    hidden_grad = times(upstream_all, down_weight, 1, 1)
    up_grad_low = (hidden_grad * silu_value).astype(bf)
    gate_grad_low = (
        hidden_grad * up_proj * (gate_sig + gate_proj * gate_sig * (1.0 - gate_sig))
    ).astype(bf)
    norm_two_grad = times(up_grad_low, up_weight, 1, 1) + times(gate_grad_low, gate_weight, 1, 1)
    side = (chips, 2, n_dp, sub, columns)
    sums = [
        times(hidden_low, upstream_all, 0, 0).astype(bf).reshape(ff_blocks, chips, sub, width),
        times(normed_two_all, up_grad_low, 0, 0).astype(bf).reshape(side),
        times(normed_two_all, gate_grad_low, 0, 0).astype(bf).reshape(side),
    ]
    ff_part = times(hidden_low, down_weight, 1, 0)
    column = (2, n_dp, shard_len, width)
    bands = [(0, sub // 2), (sub // 2, sub // 2)] if sub % 32 == 0 else [(0, sub)]
    *pieces, norm_two_grad = sum_grads(
        bands[0], sums, norm_two_grad.astype(bf).reshape(column), None, 5
    )
    pieces = [pieces]
    residual_grad = upstream.astype(f32) + norm_back(normed_two, inv_two, norm_two_grad)
    late_grads = []
    if late_slots:
        send_now = arrange(slot_unit[:, first_slots:], *pieces[0], ())
        send_now, residual_grad = lax.optimization_barrier((send_now, residual_grad))
        late_grads.append(lax.all_to_all(send_now, "dp", 0, 0))
    *second, ff_out, residual_grad_all = sum_grads(
        bands[1] if len(bands) > 1 else None,
        sums,
        ff_part.astype(bf).reshape(column),
        residual_grad.astype(bf),
        7,
    )
    residual_grad_all = residual_grad_all.reshape(seq_len, width)
    block_output = (residual + ff_out).astype(bf).reshape(block_input.shape)
    if second:
        pieces.append(second)
        if late_slots:
            send_now = arrange(slot_unit[:, first_slots:], *second, ())
            send_now, residual_grad_all, late_grads[0] = lax.optimization_barrier(
                (send_now, residual_grad_all, late_grads[0])
            )
            late_grads.append(lax.all_to_all(send_now, "dp", 0, 0))
    attended_grad = jnp.einsum(
        "tc,rc->tr", residual_grad_all, out_weight, preferred_element_type=f32
    )
    attended_grad = attended_grad.astype(bf).reshape(seq_len, heads, HD)
    allowed = (doc[:, None] == doc[None, :]) & (positions[None, :] <= positions[:, None])
    scores = jnp.einsum("qhd,khd->hqk", queries, keys, preferred_element_type=f32) * score_scale
    scores = jnp.where(allowed[None], scores, masked_score)
    prob = jnp.exp(scores - log_total)
    prob_low = prob.astype(bf)
    value_grad = jnp.einsum("hqk,qhd->khd", prob_low, attended_grad, preferred_element_type=f32)
    prob_grad = jnp.einsum("qhd,khd->hqk", attended_grad, values, preferred_element_type=f32)
    inner_sum = jnp.sum(prob * prob_grad, axis=-1, keepdims=True)
    score_grad = (prob * (prob_grad - inner_sum) * score_scale).astype(bf)
    query_grad = jnp.einsum("hqk,khd->qhd", score_grad, keys, preferred_element_type=f32)
    key_grad = jnp.einsum("hqk,qhd->khd", score_grad, queries, preferred_element_type=f32)
    qkv_grad = jnp.stack(
        [
            rotate_back(query_grad, cosine, sine),
            rotate_back(key_grad, cosine, sine),
            value_grad,
        ],
        axis=1,
    )
    qkv_grad_low = qkv_grad.astype(bf).reshape(seq_len, 3 * head_cols)
    norm_one_part = jnp.einsum("tf,rf->tr", qkv_grad_low, qkv_weight, preferred_element_type=f32)
    norm_one_grad = sum_seq(norm_one_part.astype(bf).reshape(n_seq, shard_len, width), 3)
    qkv_wgrad = jnp.einsum(
        "tr,tf->rf", normed_one_all, qkv_grad_low, preferred_element_type=f32
    ).astype(bf)
    out_wgrad = jnp.einsum(
        "tr,tc->rc", attended_low, residual_grad_all, preferred_element_type=f32
    ).astype(bf)
    qkv_piece, out_piece = collect_attention(
        qkv_wgrad.reshape(n_seq, n_dp, sub, 3 * head_cols), out_wgrad.reshape(n_dp, sub, width), 6
    )
    kinds = jnp.where(own_units < 0, 2, is_col.astype(jnp.int32)).astype(jnp.int32)
    kept = ()
    came = None
    for k, (begin, size) in enumerate(bands):
        rows_now = slice(begin, begin + size)
        attention = (qkv_piece[:, rows_now], out_piece[rows_now])
        send_now = arrange(slot_unit[:, :first_slots], *pieces[k], attention)
        if came is not None:
            send_now, came, norm_one_grad = lax.optimization_barrier(
                (send_now, came, norm_one_grad)
            )
        elif late_grads:
            send_now, late_grads[-1] = lax.optimization_barrier((send_now, late_grads[-1]))
        came = lax.all_to_all(send_now, "dp", 0, 0)
        kept = adam(
            kinds,
            [came] + late_grads[k : k + 1],
            master,
            first_moment,
            second_moment,
            n_dp,
            n_seq,
            first_slots,
            begin,
            kept,
        )
    owned_grads, new_first, new_second, new_master = kept
    input_grad = (residual_grad + norm_back(normed_one, inv_one, norm_one_grad)).reshape(
        block_input.shape
    )
    return (block_output, input_grad, owned_grads, new_first, new_second, new_master)


def solution(mesh):
    placed = (
        P("dp", "seq", None),
        P("dp", "seq", None),
        P("dp", None),
        P(),
        P("seq", "dp", None),
        P("seq", "dp", None),
        P("seq", "dp", None),
    )
    return jax.shard_map(
        local,
        mesh=mesh,
        in_specs=placed,
        out_specs=(
            P("dp", "seq", None),
            P("dp", "seq", None),
            P("seq", "dp", None),
            P("seq", "dp", None),
            P("seq", "dp", None),
            P("seq", "dp", None),
        ),
        check_vma=False,
    )
```

```python
import functools

import jax
import jax.numpy as jnp
from jax import lax
from jax.experimental import pallas as pl
from jax.experimental.pallas import tpu as pltpu
from jax.sharding import PartitionSpec as P

D = 2048
H = 16
HD = 128
FF = 8192
STEP = 5
bf = jnp.bfloat16
f32 = jnp.float32
MESH = pl.DeviceIdType.MESH


norm_eps = 1e-05
rope_base = 10000.0
beta_one = 0.5
beta_two = 0.5
learn_rate = 0.01
decay_rate = 0.1
adam_eps = 1e-08
masked_score = -1000000000.0


def unit_slots(owners, per_owner):
    unit_count = owners.shape[0]
    unit_order = jnp.arange(unit_count, dtype=jnp.int32)
    matching = owners[:, None] == owners[None, :]
    before = unit_order[None, :] < unit_order[:, None]
    places = jnp.sum(jnp.where(matching & before, 1, 0), axis=1).astype(jnp.int32)
    return owners * per_owner + places


def norm_parts(values):
    center = values - jnp.mean(values, axis=-1, keepdims=True)
    spread = jnp.mean(center * center, axis=-1, keepdims=True)
    scale_inv = lax.rsqrt(spread + norm_eps)
    return (center * scale_inv, scale_inv)


def norm_back(normed, scale_inv, upstream):
    upstream_mean = jnp.mean(upstream, axis=-1, keepdims=True)
    cross_mean = jnp.mean(upstream * normed, axis=-1, keepdims=True)
    return scale_inv * (upstream - upstream_mean - normed * cross_mean)


def rope_tables(positions, head_dim):
    half_dim = head_dim // 2
    frequency = jnp.power(rope_base, -(jnp.arange(half_dim, dtype=jnp.float32) * 2.0) / head_dim)
    angles = positions[:, None] * frequency[None, :]
    cosine_half = jnp.cos(angles)
    sine_half = jnp.sin(angles)
    return (
        jnp.concatenate([cosine_half, cosine_half], axis=-1),
        jnp.concatenate([sine_half, sine_half], axis=-1),
    )


def rotate(values, cosine, sine):
    half_dim = values.shape[-1] // 2
    turned = jnp.concatenate([-values[..., half_dim:], values[..., :half_dim]], axis=-1)
    return values * cosine + turned * sine


def rotate_back(grads, cosine, sine):
    half_dim = grads.shape[-1] // 2
    scaled = grads * sine
    turned = jnp.concatenate([scaled[..., half_dim:], -scaled[..., :half_dim]], axis=-1)
    return grads * cosine + turned


def pack_kernel(n_dp, chips, first_slots, flags, m_ref, *outs):
    rb, slots, width = m_ref.shape
    rows, wide = outs[0].shape[2:]
    sub = rows // n_dp
    start = pl.program_id(0) * rb
    target = start // sub
    inner = start % sub
    turned = jnp.swapaxes(m_ref[...], 0, 1).astype(bf)
    for s in range(slots):
        out = outs[0] if s < first_slots else outs[1]
        t = s if s < first_slots else s - first_slots
        x = turned[s]

        @pl.when(flags[s] == 1)
        def _():
            for d in range(n_dp):
                pieces = [
                    x[:, (2 * k + c) * rows + d * sub : (2 * k + c) * rows + (d + 1) * sub]
                    for c in range(2)
                    for k in range(chips)
                ]
                out[d, t, pl.ds(pl.multiple_of(start, rb), rb), :] = jnp.concatenate(pieces, axis=1)

        @pl.when(flags[s] == 0)
        def _():
            for g in range(n_dp):
                out[target, t, pl.ds(pl.multiple_of(g * sub + inner, rb), rb), :] = x[
                    :, g * wide : (g + 1) * wide
                ]


def pack(master, flags, n_dp, n_seq, first_slots):
    rows, slots, width = master.shape
    wide = width // n_dp
    rb = min(32, rows // n_dp)
    counts = [first_slots] + ([slots - first_slots] if slots > first_slots else [])
    return pl.pallas_call(
        functools.partial(pack_kernel, n_dp, n_seq // 2, first_slots),
        out_shape=[jax.ShapeDtypeStruct((n_dp, c, rows, wide), bf) for c in counts],
        grid_spec=pltpu.PrefetchScalarGridSpec(
            num_scalar_prefetch=1,
            grid=(rows // rb,),
            in_specs=[pl.BlockSpec((rb, slots, width), lambda i, f: (i, 0, 0))],
            out_specs=[
                pl.BlockSpec((n_dp, c, rows, wide), lambda i, f: (0, 0, 0, 0)) for c in counts
            ],
        ),
        compiler_params=pltpu.CompilerParams(vmem_limit_bytes=50 << 20),
        name="pack",
    )(flags, master)


def adam_kernel(n_dp, chips, first_slots, n_groups, n_kept, kinds, *refs):
    cols = refs[:n_groups]
    rws = refs[n_groups : 2 * n_groups]
    m_ref, f_ref, s_ref, keep_ref = refs[2 * n_groups : 2 * n_groups + 4]
    g_out, f_out, s_out, m_out, held = refs[2 * n_groups + 4 + n_kept :]
    rb, slots, width = m_ref.shape
    wide = width // n_dp
    rows = width // (2 * chips)
    sub = rows // n_dp
    half = chips * sub
    for s in range(slots):
        group = 0 if s < first_slots else 1
        t = s if group == 0 else s - first_slots

        @pl.when(kinds[s] == 1)
        def _():
            pieces = []
            for i in range(2 * chips):
                k, c = i // 2, i % 2
                for d in range(n_dp):
                    begin = c * half + k * sub
                    pieces.append(cols[group][d, t, :, begin : begin + sub])
            held[s] = jnp.concatenate(pieces, axis=1).astype(f32)

        @pl.when(kinds[s] == 0)
        def _():
            for g in range(n_dp):
                held[s, :, g * wide : (g + 1) * wide] = rws[group][0, t, g, :, :].astype(f32)

        @pl.when(kinds[s] == 2)
        def _():
            held[s] = jnp.zeros((rb, width), f32)

    grad = jnp.swapaxes(held[...], 0, 1)
    keep = keep_ref[...] > 0.0
    g_out[...] = grad
    first = jnp.where(keep, beta_one * f_ref[...] + (1.0 - beta_one) * grad, 0.0)
    f_out[...] = first
    second = jnp.where(keep, beta_two * s_ref[...] + (1.0 - beta_two) * grad * grad, 0.0)
    s_out[...] = second
    fixed_first = first * (1.0 / (1.0 - beta_one**STEP))
    fixed_second = second * (1.0 / (1.0 - beta_two**STEP))
    old = m_ref[...]
    step = fixed_first / (jnp.sqrt(fixed_second) + adam_eps) + decay_rate * old
    m_out[...] = jnp.where(keep, old - learn_rate * step, 0.0)


def adam(kinds, grads, master, first_moment, second_moment, n_dp, n_seq, first_slots, begin, kept):
    rows, slots, width = master.shape
    wide = width // n_dp
    sub = rows // n_dp
    size = grads[0].shape[2] // n_dp
    rb = min(16, size)
    steps = size // rb
    state = pl.BlockSpec(
        (rb, slots, width), lambda d, i, k: (d * (sub // rb) + begin // rb + i, 0, 0)
    )
    cols = [
        pl.BlockSpec((n_dp, g.shape[1], rb, wide), lambda d, i, k: (0, 0, d * steps + i, 0))
        for g in grads
    ]
    rws = [
        pl.BlockSpec((1, g.shape[1], n_dp, rb, wide), lambda d, i, k: (d, 0, 0, i, 0)) for g in grads
    ]
    keep = jnp.broadcast_to((kinds != 2).astype(f32)[None, :, None], (1, slots, width))
    first_kept = 1 + 2 * len(grads) + 4
    return pl.pallas_call(
        functools.partial(adam_kernel, n_dp, n_seq // 2, first_slots, len(grads), len(kept)),
        out_shape=[jax.ShapeDtypeStruct(master.shape, f32)] * 4,
        grid_spec=pltpu.PrefetchScalarGridSpec(
            num_scalar_prefetch=1,
            grid=(n_dp, steps),
            in_specs=cols
            + rws
            + [state] * 3
            + [pl.BlockSpec((1, slots, width), lambda d, i, k: (0, 0, 0))]
            + [pl.BlockSpec(memory_space=pl.ANY)] * len(kept),
            out_specs=[state] * 4,
            scratch_shapes=[pltpu.VMEM((slots, rb, width), f32)],
        ),
        input_output_aliases={first_kept + k: k for k in range(len(kept))},
        compiler_params=pltpu.CompilerParams(vmem_limit_bytes=50 << 20),
        cost_estimate=pl.CostEstimate(
            flops=0, bytes_accessed=int(150e6 * size / sub), transcendentals=0
        ),
        name="adam",
    )(
        kinds,
        *grads,
        *[g.reshape(n_dp, g.shape[1], n_dp, size, wide) for g in grads],
        master,
        first_moment,
        second_moment,
        keep,
        *kept,
    )


ANY = pl.BlockSpec(memory_space=pl.ANY)
VMEM = pl.BlockSpec(memory_space=pltpu.VMEM)
DMA = pltpu.SemaphoreType.DMA


def comm_params(collective_id, mib):
    return pltpu.CompilerParams(
        collective_id=collective_id, has_side_effects=True, vmem_limit_bytes=mib << 20
    )


def takes(microseconds):
    return pl.CostEstimate(flops=0, bytes_accessed=int(microseconds * 3e6), transcendentals=0)


def places():
    n_seq = lax.axis_size("seq")
    n_dp = lax.axis_size("dp")
    return n_seq, n_dp, lax.axis_index("seq"), lax.axis_index("dp")


def greet(devices):
    barrier = pltpu.get_barrier_semaphore()
    for device in devices:
        pl.semaphore_signal(barrier, inc=1, device_id=device, device_id_type=MESH)
    pl.semaphore_wait(barrier, len(devices))


def send(src, dst, send_sem, recv_sem, device):
    return pltpu.make_async_remote_copy(
        src_ref=src,
        dst_ref=dst,
        send_sem=send_sem,
        recv_sem=recv_sem,
        device_id=device,
        device_id_type=MESH,
    )


def relay_gather(views, place, count, device_of, send_sem, recv_sem, arrived, between=None):
    def leg(view, way, step, block, target):
        ref = views[view](block)
        return send(ref, ref, send_sem.at[view, way, step], recv_sem.at[view, way, step], device_of(target))

    def going(way, step):
        block = place - (step - 1) if way == 0 else place + (step - 1)
        target = place + 1 if way == 0 else place - 1
        inside = (block >= 0) & (block < count) & (target >= 0) & (target < count)
        return block, target, inside

    for step in range(1, count):
        for way in range(2):
            block, target, inside = going(way, step)

            @pl.when(inside)
            def _():
                for view in range(len(views)):
                    leg(view, way, step, block, target).start()

        for way in range(2):
            block = place - step if way == 0 else place + step

            @pl.when((block >= 0) & (block < count))
            def _():
                for view in range(len(views)):
                    leg(view, way, step, block, lax.rem(place + 1, count)).wait_recv()
                arrived(block)

        if between:
            between(step)

    for step in range(1, count):
        for way in range(2):
            block, target, inside = going(way, step)

            @pl.when(inside)
            def _():
                for view in range(len(views)):
                    leg(view, way, step, block, target).wait_send()


def relay_sum(owns, sent, came, place, count, device_of, send_sem, recv_sem, ready, between=None):
    views = range(len(owns))

    def spot(way, block, receiver):
        return jnp.where(block == receiver, count, block) if way else block

    def leg(view, way, block, target, receiver):
        return send(
            sent[view].at[block],
            came[view].at[spot(way, block, receiver)],
            send_sem.at[view, way, block],
            recv_sem.at[view, way, block],
            device_of(target),
        )

    def going(way, step):
        block = count - 1 - step + place if way == 0 else step - (count - 1 - place)
        target = place + 1 if way == 0 else place - 1
        return block, target, (block < count if way == 0 else block >= 0)

    def behind(way):
        return place > 0 if way == 0 else place < count - 1

    for step in range(count - 1):
        for way in range(2):
            block, target, inside = going(way, step)

            @pl.when(inside)
            def _():
                ready(block)
                for view in views:

                    @pl.when(behind(way))
                    def _():
                        leg(view, way, block, target, place).wait_recv()
                        value = owns[view](block) + came[view][block].astype(f32)
                        sent[view][block] = value.astype(sent[view].dtype)

                    @pl.when(jnp.logical_not(behind(way)))
                    def _():
                        sent[view][block] = owns[view](block).astype(sent[view].dtype)

                    leg(view, way, block, target, target).start()

        if between:
            between(step)

    ready(place)
    for way in range(2):

        @pl.when(behind(way))
        def _():
            for view in views:
                leg(view, way, place, lax.rem(place + 1, count), place).wait_recv()

    totals = []
    for view in views:
        total = owns[view](place)
        for way in range(2):
            value = came[view][place if way == 0 else count].astype(f32)
            total = total + jnp.where(behind(way), value, 0.0)
        totals.append(total)
    for step in range(count - 1):
        for way in range(2):
            block, target, inside = going(way, step)

            @pl.when(inside)
            def _():
                for view in views:
                    leg(view, way, block, target, target).wait_send()

    return totals


def front_kernel(
    packed_ref, x_ref, table_ref, out_ref, own_sem, a_send, a_recv, send_sem, recv_sem, pass_sem, take_sem
):
    n_seq, n_dp, seq_index, dp_index = places()
    chips, chip, core = n_seq // 2, seq_index // 2, lax.rem(seq_index, 2)
    dp_peers = [lax.rem(dp_index + k, n_dp) for k in range(n_dp)]
    chip_peers = [lax.rem(chip + k, chips) for k in range(chips)]
    sibling = (dp_index, chip * 2 + 1 - core)
    greet(
        [(p, seq_index) for p in dp_peers[1:]]
        + [(dp_index, p * 2 + core) for p in chip_peers[1:]]
        + [sibling]
    )
    along = []
    for k in range(1, n_dp):
        copy = send(
            packed_ref.at[dp_peers[k]],
            table_ref.at[dp_index],
            a_send.at[k],
            a_recv.at[k],
            (dp_peers[k], seq_index),
        )
        copy.start()
        along.append(copy)
    own = [
        pltpu.make_async_copy(packed_ref.at[dp_index], table_ref.at[dp_index], own_sem.at[0]),
        pltpu.make_async_copy(x_ref, out_ref.at[seq_index], own_sem.at[1]),
    ]
    for copy in own:
        copy.start()
    pass_on, finish = spread_blocks(
        x_ref, out_ref, chips, chip, core, dp_index, sibling, send_sem, recv_sem, pass_sem, take_sem
    )
    pass_on()
    finish()
    for copy in along:
        copy.wait()
    for copy in own:
        copy.wait()


def spread_blocks(
    x_ref, out_ref, chips, chip, core, dp_index, sibling, send_sem, recv_sem, pass_sem, take_sem
):
    mine = out_ref.at[chip * 2 + core]
    copies = {}
    for k in range(chips - 1, 0, -1):
        device = (dp_index, lax.rem(chip + k, chips) * 2 + core)
        copies[k] = send(x_ref, mine, send_sem.at[k], recv_sem.at[k], device)
        copies[k].start()
    passed = [send(x_ref, mine, pass_sem.at[0], take_sem.at[0], sibling)]
    passed[0].start()

    def pass_on():
        for k in range(1, chips):
            copies[k].wait_recv()
            block = out_ref.at[lax.rem(chip + chips - k, chips) * 2 + core]
            onward = send(block, block, pass_sem.at[k], take_sem.at[k], sibling)
            onward.start()
            passed.append(onward)

    def finish():
        for copy in copies.values():
            copy.wait_send()
        for onward in passed:
            onward.wait()

    return pass_on, finish


def front(packed, x, collective_id):
    chips = lax.axis_size("seq") // 2
    n_dp = lax.axis_size("dp")
    return pl.pallas_call(
        front_kernel,
        out_shape=[
            jax.ShapeDtypeStruct(packed.shape, packed.dtype),
            jax.ShapeDtypeStruct((2 * chips,) + x.shape, x.dtype),
        ],
        in_specs=[VMEM, VMEM],
        out_specs=[ANY, ANY],
        scratch_shapes=[DMA((2,)), DMA((n_dp,)), DMA((n_dp,))] + [DMA((chips,))] * 4,
        compiler_params=comm_params(collective_id, 24),
        cost_estimate=takes(90),
        name="front",
    )(packed, x)


def sum_seq_kernel(x_ref, out_ref, taken, sent, arrived, pass_sem, take_sem, send_sem, recv_sem):
    n_seq, n_dp, seq_index, dp_index = places()
    chips, chip, core = n_seq // 2, seq_index // 2, lax.rem(seq_index, 2)
    peers = [lax.rem(chip + k, chips) for k in range(chips)]
    sibling = (dp_index, chip * 2 + 1 - core)
    greet([(dp_index, p * 2 + core) for p in peers[1:]] + [sibling])
    order = list(range(chips - 1, 0, -1)) + [0]
    passed = {}
    for k in order:
        block = x_ref.at[peers[k] * 2 + 1 - core]
        passed[k] = send(block, taken.at[k], pass_sem.at[k], take_sem.at[k], sibling)
        passed[k].start()
    copies = {}
    for k in order[:-1]:
        passed[k].wait_recv()
        own = x_ref[peers[k] * 2 + core].astype(f32)
        sent[k] = (own + taken[k].astype(f32)).astype(sent.dtype)
        device = (dp_index, peers[k] * 2 + core)
        copies[k] = send(sent.at[k], arrived.at[k], send_sem.at[k], recv_sem.at[k], device)
        copies[k].start()
    passed[0].wait_recv()
    total = x_ref[seq_index].astype(f32) + taken[0].astype(f32)
    for k in range(1, chips):
        copies[k].wait_recv()
        total = total + arrived[k].astype(f32)
    out_ref[...] = total
    for k in order:
        passed[k].wait_send()
    for k in order[:-1]:
        copies[k].wait_send()


def sum_seq(x, collective_id):
    blocks, rows, columns = x.shape
    chips = blocks // 2
    slots = pltpu.VMEM((chips, rows, columns), x.dtype)
    return pl.pallas_call(
        sum_seq_kernel,
        out_shape=jax.ShapeDtypeStruct((rows, columns), f32),
        in_specs=[VMEM],
        out_specs=VMEM,
        scratch_shapes=[slots, slots, slots] + [DMA((chips,))] * 4,
        compiler_params=comm_params(collective_id, 40),
        cost_estimate=takes(28),
        name="sum_seq",
    )(x)


def collect_kernel(
    qkv_ref, out_ref, qkv_sum, out_sum, qkv_sent, qkv_came, out_sent, out_came, total, own_sem,
    send_sem, recv_sem, a_send, a_recv
):
    n_seq, n_dp, seq_index, dp_index = places()
    seq_peers = [lax.rem(seq_index + k, n_seq) for k in range(n_seq)]
    greet(
        [(dp_index, p) for p in seq_peers[1:]]
        + [(lax.rem(dp_index + k, n_dp), seq_index) for k in range(1, n_dp)]
    )
    sums = relay_sum(
        [lambda block: qkv_ref[:, block].astype(f32), lambda block: out_ref[block].astype(f32)],
        [qkv_sent, out_sent],
        [qkv_came, out_came],
        dp_index,
        n_dp,
        lambda place: (place, seq_index),
        send_sem,
        recv_sem,
        lambda block: None,
    )
    total[...] = sums[0].astype(total.dtype)
    across = []
    for k in range(1, n_seq):
        copy = send(
            total.at[seq_peers[k]],
            qkv_sum.at[seq_index],
            a_send.at[k],
            a_recv.at[k],
            (dp_index, seq_peers[k]),
        )
        copy.start()
        across.append(copy)
    own = pltpu.make_async_copy(total.at[seq_index], qkv_sum.at[seq_index], own_sem)
    own.start()
    out_sum[...] = sums[1].astype(out_sum.dtype)
    for copy in across:
        copy.wait()
    own.wait()


def collect_attention(qkv, out, collective_id):
    n_seq = lax.axis_size("seq")
    n_dp = lax.axis_size("dp")
    tail = qkv.shape[2:]
    return pl.pallas_call(
        collect_kernel,
        out_shape=[
            jax.ShapeDtypeStruct((n_seq,) + tail, qkv.dtype),
            jax.ShapeDtypeStruct(out.shape[1:], out.dtype),
        ],
        in_specs=[VMEM, VMEM],
        out_specs=[VMEM, VMEM],
        scratch_shapes=[
            pltpu.VMEM((n_dp, n_seq) + tail, qkv.dtype),
            pltpu.VMEM((n_dp + 1, n_seq) + tail, qkv.dtype),
            pltpu.VMEM((n_dp,) + out.shape[1:], out.dtype),
            pltpu.VMEM((n_dp + 1,) + out.shape[1:], out.dtype),
            pltpu.VMEM((n_seq,) + tail, qkv.dtype),
            DMA,
            DMA((2, 2, n_dp)),
            DMA((2, 2, n_dp)),
            DMA((n_seq,)),
            DMA((n_seq,)),
        ],
        compiler_params=comm_params(collective_id, 48),
        cost_estimate=takes(75),
        name="collect_attention",
    )(qkv, out)


def ring_chip(place, chips):
    return jnp.where(place < chips // 2, 2 * place, 2 * (chips - 1 - place) + 1)


def ring_place(chip, chips):
    line = chip // 2
    return jnp.where(lax.rem(chip, 2) == 0, line, chips - 1 - line)


class Ring:
    def __init__(self, chips, chip, core, dp_index, send_sem, recv_sem):
        self.chips = chips
        self.place = ring_place(chip, chips)
        self.core = core
        self.dp_index = dp_index
        self.send_sem = send_sem
        self.recv_sem = recv_sem
        self.last = chips // 2

    def at(self, offset):
        return ring_chip(lax.rem(self.place + offset + self.chips, self.chips), self.chips)

    def device(self, way):
        return (self.dp_index, self.at(1 if way == 0 else -1) * 2 + self.core)

    def leg(self, view, way, step, src, dst):
        return send(
            src, dst, self.send_sem.at[view, way, step], self.recv_sem.at[view, way, step], self.device(way)
        )


def arrange_kernel(ff_blocks, units, ug_ref, down_ref, *refs):
    piece_ref = refs[-1]
    unit = units[pl.program_id(0)]
    rows, wide = piece_ref.shape[1:]
    sub, width = down_ref.shape[1:]
    groups = width // wide

    @pl.when((unit >= 4) & (unit < 4 + 2 * ff_blocks))
    def _():
        piece_ref[0] = ug_ref[0]

    @pl.when(unit >= 4 + 2 * ff_blocks)
    def _():
        for g in range(groups):
            piece_ref[0, g * sub : (g + 1) * sub, :] = down_ref[0, :, g * wide : (g + 1) * wide]

    if len(refs) == 3:
        qkv_ref, out_ref = refs[:2]
        blocks, _, columns = qkv_ref.shape
        step = columns // 3
        share = wide // step
        for u in range(3):

            @pl.when(unit == u)
            def _():
                for block in range(blocks):
                    g, h = block // share, block % share
                    piece_ref[0, g * sub : (g + 1) * sub, h * step : (h + 1) * step] = qkv_ref[
                        block, :, u * step : (u + 1) * step
                    ]

        @pl.when(unit == 3)
        def _():
            for g in range(groups):
                piece_ref[0, g * sub : (g + 1) * sub, :] = out_ref[:, g * wide : (g + 1) * wide]


def arrange(units, ug, down, attention):
    n_dp, slots = units.shape
    rows, wide = ug.shape[1:]
    sub, width = down.shape[1:]
    ff_blocks = down.shape[0]
    specs = [
        pl.BlockSpec(
            (1, rows, wide), lambda k, u: (jnp.clip(u[k] - 4, 0, 2 * ff_blocks - 1), 0, 0)
        ),
        pl.BlockSpec(
            (1, sub, width),
            lambda k, u: (jnp.clip(u[k] - 4 - 2 * ff_blocks, 0, ff_blocks - 1), 0, 0),
        ),
    ]
    if attention:
        specs.append(pl.BlockSpec(attention[0].shape, lambda k, u: (0, 0, 0)))
        specs.append(pl.BlockSpec(attention[1].shape, lambda k, u: (0, 0)))
    return pl.pallas_call(
        functools.partial(arrange_kernel, ff_blocks),
        out_shape=jax.ShapeDtypeStruct((n_dp * slots, rows, wide), bf),
        grid_spec=pltpu.PrefetchScalarGridSpec(
            num_scalar_prefetch=1,
            grid=(n_dp * slots,),
            in_specs=specs,
            out_specs=pl.BlockSpec((1, rows, wide), lambda k, u: (k, 0, 0)),
        ),
        compiler_params=pltpu.CompilerParams(vmem_limit_bytes=16 << 20),
        cost_estimate=takes(7),
        name="arrange",
    )(units.reshape(-1), ug, down, *attention).reshape(n_dp, slots, rows, wide)


def column_sums(refs, takens, sents, cames, send_sem, recv_sem, pass_sem, take_sem, between):
    n_seq, n_dp, seq_index, dp_index = places()
    core = lax.rem(seq_index, 2)
    sibling = (dp_index, seq_index + 1 - 2 * core)
    views = range(len(refs))

    def onward(view, block):
        return send(
            refs[view].at[1 - core, block],
            takens[view].at[block],
            pass_sem.at[view, block],
            take_sem.at[view, block],
            sibling,
        )

    for block in [b for k in range(n_dp // 2) for b in (n_dp - 1 - k, k)]:
        for view in views:
            onward(view, block).start()

    def ready(block):
        for view in views:
            onward(view, block).wait_recv()

    def own(view):
        return lambda block: refs[view][core, block].astype(f32) + takens[view][block].astype(f32)

    totals = relay_sum(
        [own(view) for view in views],
        sents,
        cames,
        dp_index,
        n_dp,
        lambda place: (place, seq_index),
        send_sem,
        recv_sem,
        ready,
        between,
    )
    for block in range(n_dp):
        for view in views:
            onward(view, block).wait_send()
    return totals


def grads_kernel(band, n_sums, has_tokens, *refs):
    n_seq, n_dp, seq_index, dp_index = places()
    chips, chip, core = n_seq // 2, seq_index // 2, lax.rem(seq_index, 2)
    sibling = (dp_index, chip * 2 + 1 - core)
    refs = list(refs)

    def take(count):
        taken, refs[:count] = refs[:count], []
        return taken

    owns = take(3) if band else None
    x_refs = take(n_sums)
    tokens_ref = take(1)[0] if has_tokens else None
    outs = take(2) if band else None
    x_outs = take(n_sums)
    tokens_out = take(1)[0] if has_tokens else None
    if n_sums:
        takens, sents, cames = take(n_sums), take(n_sums), take(n_sums)
        z_send, z_recv, x_pass, x_take = take(4)
    if has_tokens:
        token_own, token_send, token_recv, token_pass, token_take = take(5)
    greet(
        [(lax.rem(dp_index + k, n_dp), seq_index) for k in range(1, n_dp)]
        + [(dp_index, lax.rem(chip + k, chips) * 2 + core) for k in range(1, chips)]
        + [sibling]
    )
    if band:
        half_came, full_sent, full_came, mine = take(3), take(3), take(3), take(3)
        side_out, ring_send, ring_recv, side_send, side_recv, own_sem = take(6)
        ug_out, down_out = outs
        ring = Ring(chips, chip, core, dp_index, ring_send, ring_recv)
        begin, size = band
        blocks = down_out.shape[0]
        pair = blocks // 2
        half = ug_out.shape[2] // 2
        last = ring.last

        def own(view, place, way):
            if view == 0:
                units = pl.ds(0, blocks) if way is None else pl.ds(way * pair, pair)
                return owns[0].at[units, place, pl.ds(begin, size), :]
            columns = pl.ds(0, blocks * half) if way is None else pl.ds(way * pair * half, pair * half)
            return owns[view].at[place, :, :, pl.ds(begin, size), columns]

        def leg(view, way, step):
            if step == 0:
                src = own(view, ring.at(last), way)
                return ring.leg(view, way, step, src, half_came[view].at[way])
            src, dst = full_sent[view].at[step - 1, way], full_came[view].at[step - 1, way]
            return ring.leg(view, way, step, src, dst)

        def own_copy(view, way, step):
            distance = last - step
            if step == last:
                return pltpu.make_async_copy(
                    own(view, chip, None), mine[view], own_sem.at[view, 0, step - 1]
                )
            src = own(view, ring.at(distance if way == 0 else -distance), None)
            return pltpu.make_async_copy(
                src, full_sent[view].at[step - 1, way], own_sem.at[view, way, step - 1]
            )

        for view in range(3):
            for way in range(2):
                leg(view, way, 0).start()
        for step in range(1, last + 1):
            for view in range(3):
                for way in range(2 if step < last else 1):
                    own_copy(view, way, step).start()

        def ring_step(step):
            for view in range(3):
                for way in range(2):
                    own_copy(view, way, step).wait()
                    leg(view, way, step - 1).wait_recv()
                    full = full_sent[view]
                    if step > 1:
                        value = full[step - 1, way].astype(f32)
                        value = value + full_came[view][step - 2, way].astype(f32)
                        full[step - 1, way] = value.astype(bf)
                    elif view == 0:
                        units = slice(way * pair, (way + 1) * pair)
                        value = full[0, way, units].astype(f32) + half_came[0][way].astype(f32)
                        full[0, way, units] = value.astype(bf)
                    else:
                        columns = slice(way * pair * half, (way + 1) * pair * half)
                        value = full[0, way, :, :, :, columns].astype(f32)
                        value = value + half_came[view][way].astype(f32)
                        full[0, way, :, :, :, columns] = value.astype(bf)
                    leg(view, way, step).start()

    if has_tokens:
        own_tokens = pltpu.make_async_copy(tokens_ref, tokens_out.at[seq_index], token_own)
        own_tokens.start()
        pass_on, finish = spread_blocks(
            tokens_ref, tokens_out, chips, chip, core, dp_index, sibling,
            token_send, token_recv, token_pass, token_take,
        )

    def between(step):
        if step == 0:
            if band:
                for ring_at in range(1, last):
                    ring_step(ring_at)
            if has_tokens:
                pass_on()

    if n_sums:
        totals = column_sums(
            x_refs, takens, sents, cames, z_send, z_recv, x_pass, x_take, between
        )
        for out, total in zip(x_outs, totals):
            out[...] = total
    else:
        between(0)
    if has_tokens:
        own_tokens.wait()
        finish()
    if not band:
        return
    for view in range(3):
        own_copy(view, 0, last).wait()
        for way in range(2):
            leg(view, way, last - 1).wait_recv()
        if last > 1:
            came = [full_came[view][last - 2, way].astype(f32) for way in range(2)]
            value = mine[view][...].astype(f32) + came[0] + came[1]
        else:
            axis = 0 if view == 0 else 3
            came = [half_came[view][way].astype(f32) for way in range(2)]
            value = mine[view][...].astype(f32) + jnp.concatenate(came, axis=axis)
        value = value.astype(bf)
        if view == 0:
            down_out[...] = value
            continue
        value = value.reshape(2, n_dp * size, blocks * half)
        for k in range(blocks):
            unit = (view - 1) * blocks + k

            @pl.when(core == 0)
            def _():
                ug_out[unit, :, :half] = value[0, :, k * half : (k + 1) * half]
                side_out[unit] = value[1, :, k * half : (k + 1) * half]

            @pl.when(core != 0)
            def _():
                ug_out[unit, :, half:] = value[1, :, k * half : (k + 1) * half]
                side_out[unit] = value[0, :, k * half : (k + 1) * half]

    place = pl.ds(pl.multiple_of(core * half, half), half)
    side = send(side_out, ug_out.at[:, :, place], side_send, side_recv, sibling)
    side.start()
    side.wait()
    for step in range(last):
        for view in range(3):
            for way in range(2):
                leg(view, way, step).wait_send()


def sum_grads(band, sums, xs, tokens, shape, collective_id):
    n_dp, shard, width = shape
    chips = lax.axis_size("seq") // 2
    steps = chips // 2
    vmem = pltpu.VMEM
    operands, in_specs, out_shape, out_specs = [], [], [], []
    count = len(xs)
    scratch = []
    if count:
        scratch += [vmem((n_dp, shard, width), bf)] * (2 * count)
        scratch += [vmem((n_dp + 1, shard, width), bf)] * count
        scratch += [DMA((count, 2, n_dp))] * 2 + [DMA((count, n_dp))] * 2
    if tokens is not None:
        scratch += [DMA] + [DMA((chips,))] * 4
    if band:
        size = band[1]
        blocks = sums[0].shape[0]
        wide = sums[1].shape[-1]
        half = wide // blocks
        operands += sums
        in_specs += [ANY] * 3
        out_shape += [
            jax.ShapeDtypeStruct((2 * blocks, n_dp * size, 2 * half), bf),
            jax.ShapeDtypeStruct((blocks, size, width), bf),
        ]
        out_specs += [VMEM] * 2
        side = (2, n_dp, size)
        fulls = [(blocks, size, width), side + (wide,), side + (wide,)]
        halves = [(blocks // 2, size, width), side + (wide // 2,), side + (wide // 2,)]
        scratch += [vmem((2,) + s, bf) for s in halves]
        scratch += [vmem((max(steps - 1, 1), 2) + s, bf) for s in fulls] * 2
        scratch += [vmem(s, bf) for s in fulls]
        scratch += [
            vmem((2 * blocks, n_dp * size, half), bf),
            DMA((3, 2, steps)),
            DMA((3, 2, steps)),
            DMA,
            DMA,
            DMA((3, 2, steps)),
        ]
    operands += xs
    in_specs += [VMEM] * count
    out_shape += [jax.ShapeDtypeStruct((shard, width), f32)] * count
    out_specs += [VMEM] * count
    if tokens is not None:
        operands.append(tokens)
        in_specs.append(VMEM)
        out_shape.append(jax.ShapeDtypeStruct((2 * chips,) + tokens.shape, bf))
        out_specs.append(ANY)
    return pl.pallas_call(
        functools.partial(grads_kernel, band, count, tokens is not None),
        out_shape=out_shape,
        in_specs=in_specs,
        out_specs=out_specs,
        scratch_shapes=scratch,
        compiler_params=comm_params(collective_id, 58),
        cost_estimate=takes(75),
        name="sum_grads",
    )(*operands)


def attention_back_kernel(
    grad_ref, weight_ref, query_ref, key_ref, value_ref, mixed_ref, stat_ref, cos_ref, sin_ref, doc_row, doc_col, x_ref,
    qkv_out, qkv_weight_out, out_weight_out, mixed_grad, key_sum, value_sum
):
    seq_len, width = grad_ref.shape
    head_cols = query_ref.shape[1]
    heads = head_cols // HD
    block_rows = min(256, seq_len)
    scale = float(HD) ** (-0.5)

    def rows_of(b):
        return pl.ds(pl.multiple_of(b * block_rows, block_rows), block_rows)

    def times(left, right, left_axis, right_axis):
        return lax.dot_general(
            left, right, (((left_axis,), (right_axis,)), ((), ())), preferred_element_type=f32
        )

    def mix(b, carry):
        at = rows_of(b)
        mixed_grad[at, :] = times(grad_ref[at, :], weight_ref[...], 1, 1).astype(bf)
        return carry

    lax.fori_loop(0, seq_len // block_rows, mix, 0)
    key_sum[...] = jnp.zeros_like(key_sum)
    value_sum[...] = jnp.zeros_like(value_sum)

    def turned(grads, cosine, sine):
        scaled = grads * sine
        half = HD // 2
        other = jnp.concatenate([scaled[:, half:], -scaled[:, :half]], axis=-1)
        return grads * cosine + other

    def attend(b, carry):
        at = rows_of(b)
        begin = b * block_rows
        query_pos = begin + lax.broadcasted_iota(jnp.int32, (block_rows, seq_len), 0)
        key_pos = lax.broadcasted_iota(jnp.int32, (block_rows, seq_len), 1)
        allowed = (doc_col[at, :] == doc_row[...]) & (key_pos <= query_pos)
        for h in range(heads):
            place = slice(h * HD, (h + 1) * HD)
            query, part = query_ref[at, place], mixed_grad[at, place]
            scores = jnp.where(allowed, times(query, key_ref[:, place], 1, 1) * scale, masked_score)
            prob = jnp.exp(scores - stat_ref[at, h * HD : h * HD + 1])
            prob_grad = times(part, value_ref[:, place], 1, 1)
            inner = jnp.sum(prob * prob_grad, axis=-1, keepdims=True)
            score_grad = (prob * (prob_grad - inner) * scale).astype(bf)
            value_sum[:, place] += times(prob.astype(bf), part, 0, 0)
            key_sum[:, place] += times(score_grad, query, 0, 0)
            query_grad = times(score_grad, key_ref[:, place], 1, 0)
            qkv_out[at, place] = turned(query_grad, cos_ref[at, :], sin_ref[at, :]).astype(bf)
        return carry

    lax.fori_loop(0, seq_len // block_rows, attend, 0)

    def finish(b, carry):
        at = rows_of(b)
        for h in range(heads):
            place = slice(h * HD, (h + 1) * HD)
            grads = turned(key_sum[at, place], cos_ref[at, :], sin_ref[at, :])
            qkv_out[at, head_cols + h * HD : head_cols + (h + 1) * HD] = grads.astype(bf)
        qkv_out[at, 2 * head_cols :] = value_sum[at, :].astype(bf)
        return carry

    lax.fori_loop(0, seq_len // block_rows, finish, 0)
    columns = min(512, width)
    for c in range(width // columns):
        at = slice(c * columns, (c + 1) * columns)
        qkv_weight_out[at, :] = times(x_ref[:, at], qkv_out[...], 0, 0).astype(bf)
        out_weight_out[:, at] = times(mixed_ref[...], grad_ref[:, at], 0, 0).astype(bf)


def attention_back(grad, weight, query, key, value, mixed, stat, cosine, sine, doc, x):
    seq_len, width = grad.shape
    head_cols = query.shape[1]
    return pl.pallas_call(
        attention_back_kernel,
        out_shape=[
            jax.ShapeDtypeStruct((seq_len, 3 * head_cols), bf),
            jax.ShapeDtypeStruct((width, 3 * head_cols), bf),
            jax.ShapeDtypeStruct((head_cols, width), bf),
        ],
        in_specs=[VMEM] * 12,
        out_specs=[VMEM] * 3,
        scratch_shapes=[
            pltpu.VMEM((seq_len, head_cols), bf),
            pltpu.VMEM((seq_len, head_cols), f32),
            pltpu.VMEM((seq_len, head_cols), f32),
        ],
        compiler_params=pltpu.CompilerParams(vmem_limit_bytes=50 << 20),
        cost_estimate=takes(35),
        name="attention_back",
    )(grad, weight, query, key, value, mixed, stat, cosine, sine, doc[None, :], doc[:, None], x)


def turn_half(values):
    half = values.shape[-1] // 2
    return jnp.concatenate([-values[:, half:], values[:, :half]], axis=-1)


def forward_kernel(has_late, first_slots, ff_blocks, *refs):
    info, first_ref = refs[:2]
    refs = refs[2:]
    if has_late:
        late_ref, refs = refs[0], refs[1:]
    x1_ref, cos_ref, sin_ref, doc_row, doc_col, tokens_ref, cot_ref = refs[:7]
    qkv_all, out_all, query_out, key_out, value_out, mixed_out, stat_out, residual_out = refs[7:15]
    up_all, gate_all, down_all, x_all, cot_all = refs[15:20]
    ug_all = (up_all, gate_all)
    refs = refs[1:]
    att_stage, out_stage, part, taken, sent, arrived, x_stage = refs[19:26]
    mine_stage, given_stage, down_stage = refs[26:29]
    (own_sem, a_send, a_recv, w_send, w_recv, s_pass, s_take, s_send, s_recv, cot_send, cot_recv,
     late_send, late_recv, late_own, stage_own, side_send, side_recv, ring_send, ring_recv,
     send_sem, recv_sem, pass_sem, take_sem) = refs[29:52]
    late_tables = refs[52:]
    n_seq, n_dp, seq_index, dp_index = places()
    chips, chip, core = n_seq // 2, seq_index // 2, lax.rem(seq_index, 2)
    sibling = (dp_index, chip * 2 + 1 - core)
    seq_peers = [lax.rem(seq_index + k, n_seq) for k in range(n_seq)]
    dp_peers = [lax.rem(dp_index + k, n_dp) for k in range(n_dp)]
    rows, wide = first_ref.shape[1:]
    sub = rows // n_dp
    half = wide // 2
    step_cols = att_stage.shape[2] // 3
    share = wide // step_cols
    tokens, width = tokens_ref.shape
    greet([(dp_index, p) for p in seq_peers[1:]] + [(p, seq_index) for p in dp_peers[1:]])

    def band(c):
        return pl.ds(c * sub, sub)

    def late_copies(c):
        copies = []
        for k in range(1, n_dp):
            copies.append(
                send(
                    late_ref.at[dp_peers[k], :, band(c)],
                    late_tables[c].at[dp_index],
                    late_send.at[c, k],
                    late_recv.at[c, k],
                    (dp_peers[k], seq_index),
                )
            )
        return copies

    def late_own_copy(c):
        return pltpu.make_async_copy(
            late_ref.at[dp_index, :, band(c)], late_tables[c].at[dp_index], late_own.at[c]
        )

    def late_start(c):
        if not has_late or c >= n_dp:
            return
        if c:
            for copy in late_copies(c - 1):
                copy.wait_send()
        for copy in late_copies(c):
            copy.start()
        late_own_copy(c).start()

    late_start(0)

    for u in range(3):
        for block in range(n_seq):
            g, h = block // share, block % share
            att_stage[block, :, u * step_cols : (u + 1) * step_cols] = first_ref[
                info[u], g * sub : (g + 1) * sub, h * step_cols : (h + 1) * step_cols
            ]
    for g in range(n_dp):
        out_stage[:, g * wide : (g + 1) * wide] = first_ref[info[3], g * sub : (g + 1) * sub, :]
    own = [
        pltpu.make_async_copy(att_stage.at[seq_index], qkv_all.at[seq_index, dp_index], own_sem.at[0]),
        pltpu.make_async_copy(out_stage, out_all.at[dp_index], own_sem.at[1]),
    ]
    cot_own = pltpu.make_async_copy(cot_ref, cot_all.at[core], own_sem.at[2])
    cot_copy = send(cot_ref, cot_all.at[core], cot_send, cot_recv, sibling)
    across = []
    for k in range(1, n_seq):
        copy = send(
            att_stage.at[seq_peers[k]],
            qkv_all.at[seq_index, dp_index],
            a_send.at[k],
            a_recv.at[k],
            (dp_index, seq_peers[k]),
        )
        copy.start()
        across.append(copy)
    for copy in own:
        copy.start()
    cot_copy.start()
    cot_own.start()
    for copy in own:
        copy.wait()
    for copy in across:
        copy.wait_recv()
    relay_gather(
        [lambda block: qkv_all.at[:, block], lambda block: out_all.at[block]],
        dp_index,
        n_dp,
        lambda place: (place, seq_index),
        w_send,
        w_recv,
        lambda block: None,
    )

    seq_len = x1_ref.shape[0]
    heads = query_out.shape[1] // HD
    block_rows = min(256, seq_len)
    head_cols = heads * HD
    qkv_weight = qkv_all[...].reshape(width, 3 * head_cols)

    def project(b, carry):
        at = pl.ds(pl.multiple_of(b * block_rows, block_rows), block_rows)
        result = jnp.dot(x1_ref[at, :], qkv_weight, preferred_element_type=f32)
        cosine, sine = cos_ref[at, :], sin_ref[at, :]
        for h in range(heads):
            place = slice(h * HD, (h + 1) * HD)
            for part_id, out in ((0, query_out), (1, key_out)):
                begin = part_id * head_cols + h * HD
                values = result[:, begin : begin + HD]
                out[at, place] = (values * cosine + turn_half(values) * sine).astype(bf)
        value_out[at, :] = result[:, 2 * head_cols :].astype(bf)
        return carry

    lax.fori_loop(0, seq_len // block_rows, project, 0)

    def attend(b, carry):
        begin = pl.multiple_of(b * block_rows, block_rows)
        at = pl.ds(begin, block_rows)
        query_pos = begin + lax.broadcasted_iota(jnp.int32, (block_rows, seq_len), 0)
        key_pos = lax.broadcasted_iota(jnp.int32, (block_rows, seq_len), 1)
        allowed = (doc_col[at, :] == doc_row[...]) & (key_pos <= query_pos)
        for h in range(heads):
            place = slice(h * HD, (h + 1) * HD)
            scores = lax.dot_general(
                query_out[at, place],
                key_out[:, place],
                (((1,), (1,)), ((), ())),
                preferred_element_type=f32,
            )
            scores = jnp.where(allowed, scores * (float(HD) ** (-0.5)), masked_score)
            peak = jnp.max(scores, axis=-1, keepdims=True)
            raised = jnp.exp(scores - peak)
            total = jnp.sum(raised, axis=-1, keepdims=True)
            prob = (raised * (1.0 / total)).astype(bf)
            mixed = jnp.dot(prob, value_out[:, place], preferred_element_type=f32)
            mixed_out[at, place] = mixed.astype(bf)
            stat_out[at, place] = jnp.broadcast_to(peak + jnp.log(total), (block_rows, HD))
        return carry

    lax.fori_loop(0, seq_len // block_rows, attend, 0)
    out_weight = out_all[...].reshape(rows, width)

    def combine(b, carry):
        at = pl.ds(pl.multiple_of(b * tokens, tokens), tokens)
        part[b] = jnp.dot(mixed_out[at, :], out_weight, preferred_element_type=f32).astype(bf)
        return carry

    lax.fori_loop(0, n_seq, combine, 0)

    chip_peers = [lax.rem(chip + k, chips) for k in range(chips)]
    order = list(range(chips - 1, 0, -1)) + [0]
    passed = {}
    for k in order:
        block = part.at[chip_peers[k] * 2 + 1 - core]
        passed[k] = send(block, taken.at[k], s_pass.at[k], s_take.at[k], sibling)
        passed[k].start()
    copies = {}
    for k in order[:-1]:
        passed[k].wait_recv()
        value = part[chip_peers[k] * 2 + core].astype(f32)
        sent[k] = (value + taken[k].astype(f32)).astype(bf)
        device = (dp_index, chip_peers[k] * 2 + core)
        copies[k] = send(sent.at[k], arrived.at[k], s_send.at[k], s_recv.at[k], device)
        copies[k].start()

    ring = Ring(chips, chip, core, dp_index, None, None)
    pair = ff_blocks // 2

    def ring_leg(c, view, way, step, arriving):
        distance = step if arriving else step - 1
        block = ring.at(-distance if way == 0 else distance)
        units = pl.ds(way * pair, pair) if step == ring.last else pl.ds(0, ff_blocks)
        if view == 0:
            ref = down_all.at[units, block, :, pl.ds(c * wide, wide)]
        else:
            columns = pl.ds(0, ff_blocks * half)
            if step == ring.last:
                columns = pl.ds(way * pair * half, pair * half)
            ref = ug_all[view - 1].at[block, :, band(c), columns]
        return send(
            ref, ref, ring_send.at[c, view, way, step - 1], ring_recv.at[c, view, way, step - 1],
            ring.device(way),
        )

    def side_copies(c):
        return [
            send(
                given_stage.at[c, k],
                ug_all[k].at[chip, core, band(c)],
                side_send.at[c, k],
                side_recv.at[c, k],
                sibling,
            )
            for k in range(2)
        ]

    def begin_band(c):
        if has_late:
            for copy in late_copies(c):
                copy.wait_recv()
            late_own_copy(c).wait()
            late_start(c + 1)
            table = late_tables[c]
            late_slots = table.shape[1]
        for u in range(3 * ff_blocks):
            value = first_ref[info[4 + u], band(c), :]
            if has_late:
                code = info[4 + 3 * ff_blocks + u]
                other = table[code // late_slots, lax.rem(code, late_slots)]
                use_late = jnp.full(value.shape, info[4 + 6 * ff_blocks + u], jnp.int32) != 0
                value = jnp.where(use_late, other, value)
            if u < 2 * ff_blocks:
                left, right = value[:, :half], value[:, half:]
                k, j = u // ff_blocks, u % ff_blocks
                columns = slice(j * half, (j + 1) * half)

                @pl.when(core == 0)
                def _():
                    mine_stage[c, k, :, columns] = left
                    given_stage[c, k, :, columns] = right

                @pl.when(core != 0)
                def _():
                    mine_stage[c, k, :, columns] = right
                    given_stage[c, k, :, columns] = left
            else:
                down_stage[c, u - 2 * ff_blocks] = value
        for copy in side_copies(c):
            copy.start()
        local = [
            pltpu.make_async_copy(
                mine_stage.at[c, k], ug_all[k].at[chip, core, band(c)], stage_own.at[c, k]
            )
            for k in range(2)
        ]
        local.append(
            pltpu.make_async_copy(
                down_stage.at[c], down_all.at[:, chip, :, pl.ds(c * wide, wide)], stage_own.at[c, 2]
            )
        )
        for copy in local:
            copy.start()
        for copy in local:
            copy.wait()
        for copy in side_copies(c):
            copy.wait_recv()
        for view in range(3):
            for way in range(2):
                ring_leg(c, view, way, 1, False).start()

    def carry_band(c, step):
        for view in range(3):
            for way in range(2):
                ring_leg(c, view, way, step - 1, True).wait_recv()
                ring_leg(c, view, way, step, False).start()

    begin_band(0)
    passed[0].wait_recv()
    total = part[seq_index].astype(f32) + taken[0].astype(f32)
    for k in range(1, chips):
        copies[k].wait_recv()
        total = total + arrived[k].astype(f32)
    residual = tokens_ref[...] + total
    residual_out[...] = residual
    center = residual - jnp.mean(residual, axis=-1, keepdims=True)
    spread = jnp.mean(center * center, axis=-1, keepdims=True)
    x_stage[...] = (center * lax.rsqrt(spread + norm_eps)).astype(bf)
    for c in range(1, n_dp):
        begin_band(c)
        for step in range(2, ring.last + 1):
            carry_band(c - 1, step)

    own_x = pltpu.make_async_copy(x_stage, x_all.at[core, dp_index], own_sem.at[3])
    own_x.start()
    own_x.wait()

    def onward(block):
        ref = x_all.at[core, block]
        return send(ref, ref, pass_sem.at[block], take_sem.at[block], sibling)

    onward(dp_index).start()
    relay_gather(
        [lambda block: x_all.at[core, block]],
        dp_index,
        n_dp,
        lambda place: (place, seq_index),
        send_sem,
        recv_sem,
        lambda block: onward(block).start(),
        lambda step: carry_band(n_dp - 1, 2) if step == 1 and ring.last > 1 else None,
    )
    for step in range(3, ring.last + 1):
        carry_band(n_dp - 1, step)
    for c in range(n_dp):
        for view in range(3):
            for way in range(2):
                ring_leg(c, view, way, ring.last, True).wait_recv()
                for step in range(1, ring.last + 1):
                    ring_leg(c, view, way, step, False).wait_send()
        for copy in side_copies(c):
            copy.wait_send()
        if has_late:
            if c == n_dp - 1:
                for copy in late_copies(c):
                    copy.wait_send()
    for block in range(n_dp):
        onward(block).wait_send()
        ref = x_all.at[1 - core, block]
        send(ref, ref, pass_sem.at[block], take_sem.at[block], sibling).wait_recv()
    for k in order:
        passed[k].wait_send()
    for k in order[:-1]:
        copies[k].wait_send()
    for copy in across:
        copy.wait_send()
    cot_copy.wait_send()
    cot_own.wait()
    ref = cot_all.at[1 - core]
    send(ref, ref, cot_send, cot_recv, sibling).wait_recv()


def forward(info, first_table, late, x1, cosine, sine, doc, tokens, cot, ff_blocks, first_slots, collective_id):
    n_seq = lax.axis_size("seq")
    n_dp = lax.axis_size("dp")
    chips = n_seq // 2
    rows, wide = first_table.shape[1:]
    sub = rows // n_dp
    half = wide // 2
    seq_len, width = x1.shape
    head_cols = width // n_seq
    shard = tokens.shape[0]
    steps = chips // 2
    vmem = pltpu.VMEM
    low = lambda *shape: jax.ShapeDtypeStruct(shape, bf)
    has_late = late is not None
    blocks = vmem((chips, shard, width), bf)
    return pl.pallas_call(
        functools.partial(forward_kernel, has_late, first_slots, ff_blocks),
        out_shape=[
            low(n_seq, n_dp, sub, 3 * head_cols),
            low(n_dp, sub, width),
            low(seq_len, head_cols),
            low(seq_len, head_cols),
            low(seq_len, head_cols),
            low(seq_len, head_cols),
            jax.ShapeDtypeStruct((seq_len, head_cols), f32),
            jax.ShapeDtypeStruct((shard, width), f32),
            low(chips, 2, rows, ff_blocks * half),
            low(chips, 2, rows, ff_blocks * half),
            low(ff_blocks, chips, sub, width),
            low(2, n_dp, shard, width),
            low(2, n_dp, shard, width),
        ],
        in_specs=[pl.BlockSpec(memory_space=pltpu.SMEM), VMEM]
        + [ANY] * has_late
        + [VMEM] * 7,
        out_specs=[VMEM] * 8 + [ANY] * 5,
        scratch_shapes=[
            vmem((n_seq, sub, 3 * head_cols), bf),
            vmem((sub, width), bf),
            vmem((n_seq, shard, width), bf),
            blocks,
            blocks,
            blocks,
            vmem((shard, width), bf),
            vmem((n_dp, 2, sub, ff_blocks * half), bf),
            vmem((n_dp, 2, sub, ff_blocks * half), bf),
            vmem((n_dp, ff_blocks, sub, wide), bf),
            DMA((4,)),
            DMA((n_seq,)),
            DMA((n_seq,)),
            DMA((2, 2, n_dp)),
            DMA((2, 2, n_dp)),
            DMA((chips,)),
            DMA((chips,)),
            DMA((chips,)),
            DMA((chips,)),
            DMA,
            DMA,
            DMA((n_dp, n_dp)),
            DMA((n_dp, n_dp)),
            DMA((n_dp,)),
            DMA((n_dp, 3)),
            DMA((n_dp, 2)),
            DMA((n_dp, 2)),
            DMA((n_dp, 3, 2, steps)),
            DMA((n_dp, 3, 2, steps)),
            DMA((1, 2, n_dp)),
            DMA((1, 2, n_dp)),
            DMA((n_dp,)),
            DMA((n_dp,)),
        ]
        + [vmem((n_dp, late.shape[1], sub, wide), bf) for _ in range(n_dp if has_late else 0)],
        compiler_params=comm_params(collective_id, 58),
        cost_estimate=takes(230),
        name="forward",
    )(
        info,
        first_table,
        *([late] if has_late else []),
        x1,
        cosine,
        sine,
        doc[None, :],
        doc[:, None],
        tokens,
        cot,
    )


def local(block_input, cotangent, doc_lengths, owners, master, first_moment, second_moment):
    n_seq = lax.axis_size("seq")
    n_dp = lax.axis_size("dp")
    seq_index = lax.axis_index("seq")
    dp_index = lax.axis_index("dp")
    core = seq_index % 2
    _, shard_len, width = block_input.shape
    rows = master.shape[0]
    per_owner = master.shape[1]
    chips = n_seq // 2
    sub = rows // n_dp
    wide = width // n_dp
    half = chips * sub
    head_cols = H // n_seq * HD
    seq_len = shard_len * n_seq
    ff_blocks = FF // D
    first_slots = min(4, per_owner)
    unit_count = owners.shape[0]

    unit_slot = unit_slots(owners, per_owner)
    place = unit_slot - owners * per_owner
    all_slots = jnp.arange(n_dp * per_owner, dtype=jnp.int32)
    match = unit_slot[None, :] == all_slots[:, None]
    slot_unit = jnp.sum(
        jnp.where(match, jnp.arange(unit_count, dtype=jnp.int32)[None, :] + 1, 0), axis=1
    ) - 1
    slot_unit = slot_unit.reshape(n_dp, per_owner)
    own_units = lax.dynamic_index_in_dim(slot_unit, dp_index, 0, keepdims=False)
    is_col = (own_units >= 4) & (own_units < 4 + 2 * ff_blocks)


    tokens = block_input.astype(f32).reshape(shard_len, width)
    normed_one, inv_one = norm_parts(tokens)
    packed = pack(master, is_col.astype(jnp.int32), n_dp, n_seq, first_slots)
    first_table, normed_one_all = front(packed[0], normed_one.astype(bf), 2)
    first_table = first_table.reshape(n_dp * first_slots, rows, wide)
    normed_one_all = normed_one_all.reshape(seq_len, width)
    upstream = cotangent.reshape(shard_len, width)
    upstream_column = lax.all_gather(upstream, "dp", axis=0)
    positions = jnp.arange(seq_len, dtype=jnp.int32)
    cosine, sine = rope_tables(positions.astype(f32), HD)
    doc_ends = jnp.cumsum(doc_lengths[0])
    doc = jnp.sum((positions[:, None] >= doc_ends[None, :]).astype(jnp.int32), axis=1)
    late_slots = per_owner - first_slots
    info = jnp.concatenate(
        [
            owners * first_slots + jnp.minimum(place, first_slots - 1),
            (owners * late_slots + jnp.maximum(place - first_slots, 0))[4:],
            (place >= first_slots)[4:],
        ]
    ).astype(jnp.int32)
    (
        qkv_weight,
        out_weight,
        queries,
        keys,
        values,
        attended_low,
        log_total,
        residual,
        up_weight,
        gate_weight,
        down_weight,
        normed_two_all,
        upstream_all,
    ) = forward(
        info,
        first_table,
        packed[1] if late_slots else None,
        normed_one_all,
        cosine,
        sine,
        doc,
        tokens,
        upstream_column,
        ff_blocks,
        first_slots,
        1,
    )
    qkv_weight = qkv_weight.reshape(width, 3 * head_cols)
    out_weight = out_weight.reshape(rows, width)
    normed_two, inv_two = norm_parts(residual)
    columns = ff_blocks * half
    up_weight = up_weight.reshape(width, columns)
    gate_weight = gate_weight.reshape(width, columns)
    down_weight = down_weight.reshape(columns, width)
    normed_two_all = normed_two_all.reshape(-1, width)
    upstream_all = upstream_all.reshape(-1, width)

    def times(left, right, left_axis, right_axis):
        return lax.dot_general(
            left, right, (((left_axis,), (right_axis,)), ((), ())), preferred_element_type=f32
        )

    up_proj = times(normed_two_all, up_weight, 1, 0)
    gate_proj = times(normed_two_all, gate_weight, 1, 0)
    gate_sig = jax.nn.sigmoid(gate_proj)
    silu_value = gate_proj * gate_sig
    hidden_low = (silu_value * up_proj).astype(bf)
    hidden_grad = times(upstream_all, down_weight, 1, 1)
    up_grad_low = (hidden_grad * silu_value).astype(bf)
    gate_grad_low = (
        hidden_grad * up_proj * (gate_sig + gate_proj * gate_sig * (1.0 - gate_sig))
    ).astype(bf)
    norm_two_grad = times(up_grad_low, up_weight, 1, 1) + times(gate_grad_low, gate_weight, 1, 1)
    side = (chips, 2, n_dp, sub, columns)
    sums = [
        times(hidden_low, upstream_all, 0, 0).astype(bf).reshape(ff_blocks, chips, sub, width),
        times(normed_two_all, up_grad_low, 0, 0).astype(bf).reshape(side),
        times(normed_two_all, gate_grad_low, 0, 0).astype(bf).reshape(side),
    ]
    ff_part = times(hidden_low, down_weight, 1, 0)
    column = (2, n_dp, shard_len, width)
    bands = [(0, sub // 2), (sub // 2, sub // 2)] if sub % 32 == 0 else [(0, sub)]
    *pieces, norm_two_grad = sum_grads(
        bands[0], sums, [norm_two_grad.astype(bf).reshape(column)], None, column[1:], 5
    )
    pieces = [pieces]
    residual_grad = upstream.astype(f32) + norm_back(normed_two, inv_two, norm_two_grad)
    late_grads = []
    if late_slots:
        send_now = arrange(slot_unit[:, first_slots:], *pieces[0], ())
        send_now, residual_grad = lax.optimization_barrier((send_now, residual_grad))
        late_grads.append(lax.all_to_all(send_now, "dp", 0, 0))
    *second, ff_out, residual_grad_all = sum_grads(
        bands[1] if len(bands) > 1 else None,
        sums,
        [ff_part.astype(bf).reshape(column)],
        residual_grad.astype(bf),
        column[1:],
        7,
    )
    residual_grad_all = residual_grad_all.reshape(seq_len, width)
    block_output = (residual + ff_out).astype(bf).reshape(block_input.shape)
    if second:
        pieces.append(second)
        if late_slots:
            send_now = arrange(slot_unit[:, first_slots:], *second, ())
            send_now, residual_grad_all, late_grads[0] = lax.optimization_barrier(
                (send_now, residual_grad_all, late_grads[0])
            )
            late_grads.append(lax.all_to_all(send_now, "dp", 0, 0))
    qkv_grad_low, qkv_wgrad, out_wgrad = attention_back(
        residual_grad_all,
        out_weight,
        queries,
        keys,
        values,
        attended_low,
        log_total,
        cosine,
        sine,
        doc,
        normed_one_all,
    )
    norm_one_part = jnp.einsum("tf,rf->tr", qkv_grad_low, qkv_weight, preferred_element_type=f32)
    norm_one_grad = sum_seq(norm_one_part.astype(bf).reshape(n_seq, shard_len, width), 3)
    qkv_piece, out_piece = collect_attention(
        qkv_wgrad.reshape(n_seq, n_dp, sub, 3 * head_cols), out_wgrad.reshape(n_dp, sub, width), 6
    )
    kinds = jnp.where(own_units < 0, 2, is_col.astype(jnp.int32)).astype(jnp.int32)
    kept = ()
    came = None
    for k, (begin, size) in enumerate(bands):
        rows_now = slice(begin, begin + size)
        attention = (qkv_piece[:, rows_now], out_piece[rows_now])
        send_now = arrange(slot_unit[:, :first_slots], *pieces[k], attention)
        if came is not None:
            send_now, came, norm_one_grad = lax.optimization_barrier(
                (send_now, came, norm_one_grad)
            )
        elif late_grads:
            send_now, late_grads[-1] = lax.optimization_barrier((send_now, late_grads[-1]))
        came = lax.all_to_all(send_now, "dp", 0, 0)
        kept = adam(
            kinds,
            [came] + late_grads[k : k + 1],
            master,
            first_moment,
            second_moment,
            n_dp,
            n_seq,
            first_slots,
            begin,
            kept,
        )
    owned_grads, new_first, new_second, new_master = kept
    input_grad = (residual_grad + norm_back(normed_one, inv_one, norm_one_grad)).reshape(
        block_input.shape
    )
    return (block_output, input_grad, owned_grads, new_first, new_second, new_master)


def solution(mesh):
    placed = (
        P("dp", "seq", None),
        P("dp", "seq", None),
        P("dp", None),
        P(),
        P("seq", "dp", None),
        P("seq", "dp", None),
        P("seq", "dp", None),
    )
    return jax.shard_map(
        local,
        mesh=mesh,
        in_specs=placed,
        out_specs=(
            P("dp", "seq", None),
            P("dp", "seq", None),
            P("seq", "dp", None),
            P("seq", "dp", None),
            P("seq", "dp", None),
            P("seq", "dp", None),
        ),
        check_vma=False,
    )
```

```python
import functools

import jax
import jax.numpy as jnp
from jax import lax
from jax.experimental import pallas as pl
from jax.experimental.pallas import tpu as pltpu
from jax.sharding import PartitionSpec as P

D = 2048
H = 16
HD = 128
FF = 8192
STEP = 5
bf = jnp.bfloat16
f32 = jnp.float32
MESH = pl.DeviceIdType.MESH


norm_eps = 1e-05
rope_base = 10000.0
beta_one = 0.5
beta_two = 0.5
learn_rate = 0.01
decay_rate = 0.1
adam_eps = 1e-08
masked_score = -1000000000.0


def unit_slots(owners, per_owner):
    unit_count = owners.shape[0]
    unit_order = jnp.arange(unit_count, dtype=jnp.int32)
    matching = owners[:, None] == owners[None, :]
    before = unit_order[None, :] < unit_order[:, None]
    places = jnp.sum(jnp.where(matching & before, 1, 0), axis=1).astype(jnp.int32)
    return owners * per_owner + places


def norm_parts(values):
    center = values - jnp.mean(values, axis=-1, keepdims=True)
    spread = jnp.mean(center * center, axis=-1, keepdims=True)
    scale_inv = lax.rsqrt(spread + norm_eps)
    return (center * scale_inv, scale_inv)


def norm_back(normed, scale_inv, upstream):
    upstream_mean = jnp.mean(upstream, axis=-1, keepdims=True)
    cross_mean = jnp.mean(upstream * normed, axis=-1, keepdims=True)
    return scale_inv * (upstream - upstream_mean - normed * cross_mean)


def rope_tables(positions, head_dim):
    half_dim = head_dim // 2
    frequency = jnp.power(rope_base, -(jnp.arange(half_dim, dtype=jnp.float32) * 2.0) / head_dim)
    angles = positions[:, None] * frequency[None, :]
    cosine_half = jnp.cos(angles)
    sine_half = jnp.sin(angles)
    return (
        jnp.concatenate([cosine_half, cosine_half], axis=-1),
        jnp.concatenate([sine_half, sine_half], axis=-1),
    )


def rotate(values, cosine, sine):
    half_dim = values.shape[-1] // 2
    turned = jnp.concatenate([-values[..., half_dim:], values[..., :half_dim]], axis=-1)
    return values * cosine + turned * sine


def rotate_back(grads, cosine, sine):
    half_dim = grads.shape[-1] // 2
    scaled = grads * sine
    turned = jnp.concatenate([scaled[..., half_dim:], -scaled[..., :half_dim]], axis=-1)
    return grads * cosine + turned


def pack_kernel(n_dp, chips, first_slots, flags, m_ref, *outs):
    rb, slots, width = m_ref.shape
    rows, wide = outs[0].shape[2:]
    sub = rows // n_dp
    start = pl.program_id(0) * rb
    target = start // sub
    inner = start % sub
    turned = jnp.swapaxes(m_ref[...], 0, 1).astype(bf)
    for s in range(slots):
        out = outs[0] if s < first_slots else outs[1]
        t = s if s < first_slots else s - first_slots
        x = turned[s]

        @pl.when(flags[s] == 1)
        def _():
            for d in range(n_dp):
                pieces = [
                    x[:, (2 * k + c) * rows + d * sub : (2 * k + c) * rows + (d + 1) * sub]
                    for c in range(2)
                    for k in range(chips)
                ]
                out[d, t, pl.ds(pl.multiple_of(start, rb), rb), :] = jnp.concatenate(pieces, axis=1)

        @pl.when(flags[s] == 0)
        def _():
            for g in range(n_dp):
                out[target, t, pl.ds(pl.multiple_of(g * sub + inner, rb), rb), :] = x[
                    :, g * wide : (g + 1) * wide
                ]


def pack(master, flags, n_dp, n_seq, first_slots):
    rows, slots, width = master.shape
    wide = width // n_dp
    rb = min(32, rows // n_dp)
    counts = [first_slots] + ([slots - first_slots] if slots > first_slots else [])
    return pl.pallas_call(
        functools.partial(pack_kernel, n_dp, n_seq // 2, first_slots),
        out_shape=[jax.ShapeDtypeStruct((n_dp, c, rows, wide), bf) for c in counts],
        grid_spec=pltpu.PrefetchScalarGridSpec(
            num_scalar_prefetch=1,
            grid=(rows // rb,),
            in_specs=[pl.BlockSpec((rb, slots, width), lambda i, f: (i, 0, 0))],
            out_specs=[
                pl.BlockSpec((n_dp, c, rows, wide), lambda i, f: (0, 0, 0, 0)) for c in counts
            ],
        ),
        compiler_params=pltpu.CompilerParams(vmem_limit_bytes=50 << 20),
        name="pack",
    )(flags, master)


def adam_kernel(n_dp, chips, first_slots, n_groups, n_kept, kinds, *refs):
    cols = refs[:n_groups]
    rws = refs[n_groups : 2 * n_groups]
    m_ref, f_ref, s_ref, keep_ref = refs[2 * n_groups : 2 * n_groups + 4]
    g_out, f_out, s_out, m_out, held = refs[2 * n_groups + 4 + n_kept :]
    rb, slots, width = m_ref.shape
    wide = width // n_dp
    rows = width // (2 * chips)
    sub = rows // n_dp
    half = chips * sub
    for s in range(slots):
        group = 0 if s < first_slots else 1
        t = s if group == 0 else s - first_slots

        @pl.when(kinds[s] == 1)
        def _():
            pieces = []
            for i in range(2 * chips):
                k, c = i // 2, i % 2
                for d in range(n_dp):
                    begin = c * half + k * sub
                    pieces.append(cols[group][d, t, :, begin : begin + sub])
            held[s] = jnp.concatenate(pieces, axis=1).astype(f32)

        @pl.when(kinds[s] == 0)
        def _():
            for g in range(n_dp):
                held[s, :, g * wide : (g + 1) * wide] = rws[group][0, t, g, :, :].astype(f32)

        @pl.when(kinds[s] == 2)
        def _():
            held[s] = jnp.zeros((rb, width), f32)

    grad = jnp.swapaxes(held[...], 0, 1)
    keep = keep_ref[...] > 0.0
    g_out[...] = grad
    first = jnp.where(keep, beta_one * f_ref[...] + (1.0 - beta_one) * grad, 0.0)
    f_out[...] = first
    second = jnp.where(keep, beta_two * s_ref[...] + (1.0 - beta_two) * grad * grad, 0.0)
    s_out[...] = second
    fixed_first = first * (1.0 / (1.0 - beta_one**STEP))
    fixed_second = second * (1.0 / (1.0 - beta_two**STEP))
    old = m_ref[...]
    root = fixed_second * lax.rsqrt(jnp.maximum(fixed_second, 1e-37))
    step = fixed_first * pl.reciprocal(root + adam_eps, approx=True) + decay_rate * old
    m_out[...] = jnp.where(keep, old - learn_rate * step, 0.0)


def adam(kinds, grads, master, first_moment, second_moment, n_dp, n_seq, first_slots, begin, kept):
    rows, slots, width = master.shape
    wide = width // n_dp
    sub = rows // n_dp
    size = grads[0].shape[2] // n_dp
    rb = min(16, size)
    steps = size // rb
    state = pl.BlockSpec(
        (rb, slots, width), lambda d, i, k: (d * (sub // rb) + begin // rb + i, 0, 0)
    )
    cols = [
        pl.BlockSpec((n_dp, g.shape[1], rb, wide), lambda d, i, k: (0, 0, d * steps + i, 0))
        for g in grads
    ]
    rws = [
        pl.BlockSpec((1, g.shape[1], n_dp, rb, wide), lambda d, i, k: (d, 0, 0, i, 0)) for g in grads
    ]
    keep = jnp.broadcast_to((kinds != 2).astype(f32)[None, :, None], (1, slots, width))
    first_kept = 1 + 2 * len(grads) + 4
    return pl.pallas_call(
        functools.partial(adam_kernel, n_dp, n_seq // 2, first_slots, len(grads), len(kept)),
        out_shape=[jax.ShapeDtypeStruct(master.shape, f32)] * 4,
        grid_spec=pltpu.PrefetchScalarGridSpec(
            num_scalar_prefetch=1,
            grid=(n_dp, steps),
            in_specs=cols
            + rws
            + [state] * 3
            + [pl.BlockSpec((1, slots, width), lambda d, i, k: (0, 0, 0))]
            + [pl.BlockSpec(memory_space=pl.ANY)] * len(kept),
            out_specs=[state] * 4,
            scratch_shapes=[pltpu.VMEM((slots, rb, width), f32)],
        ),
        input_output_aliases={first_kept + k: k for k in range(len(kept))},
        compiler_params=pltpu.CompilerParams(vmem_limit_bytes=50 << 20),
        cost_estimate=pl.CostEstimate(
            flops=0, bytes_accessed=int(150e6 * size / sub), transcendentals=0
        ),
        name="adam",
    )(
        kinds,
        *grads,
        *[g.reshape(n_dp, g.shape[1], n_dp, size, wide) for g in grads],
        master,
        first_moment,
        second_moment,
        keep,
        *kept,
    )


ANY = pl.BlockSpec(memory_space=pl.ANY)
VMEM = pl.BlockSpec(memory_space=pltpu.VMEM)
DMA = pltpu.SemaphoreType.DMA


def comm_params(collective_id, mib):
    return pltpu.CompilerParams(
        collective_id=collective_id, has_side_effects=True, vmem_limit_bytes=mib << 20
    )


def takes(microseconds):
    return pl.CostEstimate(flops=0, bytes_accessed=int(microseconds * 3e6), transcendentals=0)


def places():
    n_seq = lax.axis_size("seq")
    n_dp = lax.axis_size("dp")
    return n_seq, n_dp, lax.axis_index("seq"), lax.axis_index("dp")


def greet(devices):
    barrier = pltpu.get_barrier_semaphore()
    for device in devices:
        pl.semaphore_signal(barrier, inc=1, device_id=device, device_id_type=MESH)
    pl.semaphore_wait(barrier, len(devices))


def send(src, dst, send_sem, recv_sem, device):
    return pltpu.make_async_remote_copy(
        src_ref=src,
        dst_ref=dst,
        send_sem=send_sem,
        recv_sem=recv_sem,
        device_id=device,
        device_id_type=MESH,
    )


def relay_gather(views, place, count, device_of, send_sem, recv_sem, arrived, between=None):
    def leg(view, way, step, block, target):
        ref = views[view](block)
        return send(ref, ref, send_sem.at[view, way, step], recv_sem.at[view, way, step], device_of(target))

    def going(way, step):
        block = place - (step - 1) if way == 0 else place + (step - 1)
        target = place + 1 if way == 0 else place - 1
        inside = (block >= 0) & (block < count) & (target >= 0) & (target < count)
        return block, target, inside

    for step in range(1, count):
        for way in range(2):
            block, target, inside = going(way, step)

            @pl.when(inside)
            def _():
                for view in range(len(views)):
                    leg(view, way, step, block, target).start()

        for way in range(2):
            block = place - step if way == 0 else place + step

            @pl.when((block >= 0) & (block < count))
            def _():
                for view in range(len(views)):
                    leg(view, way, step, block, lax.rem(place + 1, count)).wait_recv()
                arrived(block)

        if between:
            between(step)

    for step in range(1, count):
        for way in range(2):
            block, target, inside = going(way, step)

            @pl.when(inside)
            def _():
                for view in range(len(views)):
                    leg(view, way, step, block, target).wait_send()


def relay_sum(owns, sent, came, place, count, device_of, send_sem, recv_sem, ready, between=None):
    views = range(len(owns))

    def spot(way, block, receiver):
        return jnp.where(block == receiver, count, block) if way else block

    def leg(view, way, block, target, receiver):
        return send(
            sent[view].at[block],
            came[view].at[spot(way, block, receiver)],
            send_sem.at[view, way, block],
            recv_sem.at[view, way, block],
            device_of(target),
        )

    def going(way, step):
        block = count - 1 - step + place if way == 0 else step - (count - 1 - place)
        target = place + 1 if way == 0 else place - 1
        return block, target, (block < count if way == 0 else block >= 0)

    def behind(way):
        return place > 0 if way == 0 else place < count - 1

    for step in range(count - 1):
        for way in range(2):
            block, target, inside = going(way, step)

            @pl.when(inside)
            def _():
                ready(block)
                for view in views:

                    @pl.when(behind(way))
                    def _():
                        leg(view, way, block, target, place).wait_recv()
                        value = owns[view](block) + came[view][block].astype(f32)
                        sent[view][block] = value.astype(sent[view].dtype)

                    @pl.when(jnp.logical_not(behind(way)))
                    def _():
                        sent[view][block] = owns[view](block).astype(sent[view].dtype)

                    leg(view, way, block, target, target).start()

        if between:
            between(step)

    ready(place)
    for way in range(2):

        @pl.when(behind(way))
        def _():
            for view in views:
                leg(view, way, place, lax.rem(place + 1, count), place).wait_recv()

    totals = []
    for view in views:
        total = owns[view](place)
        for way in range(2):
            value = came[view][place if way == 0 else count].astype(f32)
            total = total + jnp.where(behind(way), value, 0.0)
        totals.append(total)
    for step in range(count - 1):
        for way in range(2):
            block, target, inside = going(way, step)

            @pl.when(inside)
            def _():
                for view in views:
                    leg(view, way, block, target, target).wait_send()

    return totals


def front_kernel(
    packed_ref, x_ref, table_ref, out_ref, own_sem, a_send, a_recv, send_sem, recv_sem, pass_sem, take_sem
):
    n_seq, n_dp, seq_index, dp_index = places()
    chips, chip, core = n_seq // 2, seq_index // 2, lax.rem(seq_index, 2)
    dp_peers = [lax.rem(dp_index + k, n_dp) for k in range(n_dp)]
    chip_peers = [lax.rem(chip + k, chips) for k in range(chips)]
    sibling = (dp_index, chip * 2 + 1 - core)
    greet(
        [(p, seq_index) for p in dp_peers[1:]]
        + [(dp_index, p * 2 + core) for p in chip_peers[1:]]
        + [sibling]
    )
    along = []
    for k in range(1, n_dp):
        copy = send(
            packed_ref.at[dp_peers[k]],
            table_ref.at[dp_index],
            a_send.at[k],
            a_recv.at[k],
            (dp_peers[k], seq_index),
        )
        copy.start()
        along.append(copy)
    own = [
        pltpu.make_async_copy(packed_ref.at[dp_index], table_ref.at[dp_index], own_sem.at[0]),
        pltpu.make_async_copy(x_ref, out_ref.at[seq_index], own_sem.at[1]),
    ]
    for copy in own:
        copy.start()
    pass_on, finish = spread_blocks(
        x_ref, out_ref, chips, chip, core, dp_index, sibling, send_sem, recv_sem, pass_sem, take_sem
    )
    pass_on()
    finish()
    for copy in along:
        copy.wait()
    for copy in own:
        copy.wait()


def spread_blocks(
    x_ref, out_ref, chips, chip, core, dp_index, sibling, send_sem, recv_sem, pass_sem, take_sem
):
    mine = out_ref.at[chip * 2 + core]
    copies = {}
    for k in range(chips - 1, 0, -1):
        device = (dp_index, lax.rem(chip + k, chips) * 2 + core)
        copies[k] = send(x_ref, mine, send_sem.at[k], recv_sem.at[k], device)
        copies[k].start()
    passed = [send(x_ref, mine, pass_sem.at[0], take_sem.at[0], sibling)]
    passed[0].start()

    def pass_on():
        for k in range(1, chips):
            copies[k].wait_recv()
            block = out_ref.at[lax.rem(chip + chips - k, chips) * 2 + core]
            onward = send(block, block, pass_sem.at[k], take_sem.at[k], sibling)
            onward.start()
            passed.append(onward)

    def finish():
        for copy in copies.values():
            copy.wait_send()
        for onward in passed:
            onward.wait()

    return pass_on, finish


def front(packed, x, collective_id):
    chips = lax.axis_size("seq") // 2
    n_dp = lax.axis_size("dp")
    return pl.pallas_call(
        front_kernel,
        out_shape=[
            jax.ShapeDtypeStruct(packed.shape, packed.dtype),
            jax.ShapeDtypeStruct((2 * chips,) + x.shape, x.dtype),
        ],
        in_specs=[VMEM, VMEM],
        out_specs=[ANY, ANY],
        scratch_shapes=[DMA((2,)), DMA((n_dp,)), DMA((n_dp,))] + [DMA((chips,))] * 4,
        compiler_params=comm_params(collective_id, 24),
        cost_estimate=takes(90),
        name="front",
    )(packed, x)


def sum_seq_kernel(x_ref, out_ref, taken, sent, arrived, pass_sem, take_sem, send_sem, recv_sem):
    n_seq, n_dp, seq_index, dp_index = places()
    chips, chip, core = n_seq // 2, seq_index // 2, lax.rem(seq_index, 2)
    peers = [lax.rem(chip + k, chips) for k in range(chips)]
    sibling = (dp_index, chip * 2 + 1 - core)
    greet([(dp_index, p * 2 + core) for p in peers[1:]] + [sibling])
    order = list(range(chips - 1, 0, -1)) + [0]
    passed = {}
    for k in order:
        block = x_ref.at[peers[k] * 2 + 1 - core]
        passed[k] = send(block, taken.at[k], pass_sem.at[k], take_sem.at[k], sibling)
        passed[k].start()
    copies = {}
    for k in order[:-1]:
        passed[k].wait_recv()
        own = x_ref[peers[k] * 2 + core].astype(f32)
        sent[k] = (own + taken[k].astype(f32)).astype(sent.dtype)
        device = (dp_index, peers[k] * 2 + core)
        copies[k] = send(sent.at[k], arrived.at[k], send_sem.at[k], recv_sem.at[k], device)
        copies[k].start()
    passed[0].wait_recv()
    total = x_ref[seq_index].astype(f32) + taken[0].astype(f32)
    for k in range(1, chips):
        copies[k].wait_recv()
        total = total + arrived[k].astype(f32)
    out_ref[...] = total
    for k in order:
        passed[k].wait_send()
    for k in order[:-1]:
        copies[k].wait_send()


def sum_seq(x, collective_id):
    blocks, rows, columns = x.shape
    chips = blocks // 2
    slots = pltpu.VMEM((chips, rows, columns), x.dtype)
    return pl.pallas_call(
        sum_seq_kernel,
        out_shape=jax.ShapeDtypeStruct((rows, columns), f32),
        in_specs=[VMEM],
        out_specs=VMEM,
        scratch_shapes=[slots, slots, slots] + [DMA((chips,))] * 4,
        compiler_params=comm_params(collective_id, 40),
        cost_estimate=takes(28),
        name="sum_seq",
    )(x)


def collect_kernel(
    qkv_ref, out_ref, qkv_sum, out_sum, qkv_sent, qkv_came, out_sent, out_came, total, own_sem,
    send_sem, recv_sem, a_send, a_recv
):
    n_seq, n_dp, seq_index, dp_index = places()
    seq_peers = [lax.rem(seq_index + k, n_seq) for k in range(n_seq)]
    greet(
        [(dp_index, p) for p in seq_peers[1:]]
        + [(lax.rem(dp_index + k, n_dp), seq_index) for k in range(1, n_dp)]
    )
    sums = relay_sum(
        [lambda block: qkv_ref[:, block].astype(f32), lambda block: out_ref[block].astype(f32)],
        [qkv_sent, out_sent],
        [qkv_came, out_came],
        dp_index,
        n_dp,
        lambda place: (place, seq_index),
        send_sem,
        recv_sem,
        lambda block: None,
    )
    total[...] = sums[0].astype(total.dtype)
    across = []
    for k in range(1, n_seq):
        copy = send(
            total.at[seq_peers[k]],
            qkv_sum.at[seq_index],
            a_send.at[k],
            a_recv.at[k],
            (dp_index, seq_peers[k]),
        )
        copy.start()
        across.append(copy)
    own = pltpu.make_async_copy(total.at[seq_index], qkv_sum.at[seq_index], own_sem)
    own.start()
    out_sum[...] = sums[1].astype(out_sum.dtype)
    for copy in across:
        copy.wait()
    own.wait()


def collect_attention(qkv, out, collective_id):
    n_seq = lax.axis_size("seq")
    n_dp = lax.axis_size("dp")
    tail = qkv.shape[2:]
    return pl.pallas_call(
        collect_kernel,
        out_shape=[
            jax.ShapeDtypeStruct((n_seq,) + tail, qkv.dtype),
            jax.ShapeDtypeStruct(out.shape[1:], out.dtype),
        ],
        in_specs=[VMEM, VMEM],
        out_specs=[VMEM, VMEM],
        scratch_shapes=[
            pltpu.VMEM((n_dp, n_seq) + tail, qkv.dtype),
            pltpu.VMEM((n_dp + 1, n_seq) + tail, qkv.dtype),
            pltpu.VMEM((n_dp,) + out.shape[1:], out.dtype),
            pltpu.VMEM((n_dp + 1,) + out.shape[1:], out.dtype),
            pltpu.VMEM((n_seq,) + tail, qkv.dtype),
            DMA,
            DMA((2, 2, n_dp)),
            DMA((2, 2, n_dp)),
            DMA((n_seq,)),
            DMA((n_seq,)),
        ],
        compiler_params=comm_params(collective_id, 48),
        cost_estimate=takes(75),
        name="collect_attention",
    )(qkv, out)


def ring_chip(place, chips):
    return jnp.where(place < chips // 2, 2 * place, 2 * (chips - 1 - place) + 1)


def ring_place(chip, chips):
    line = chip // 2
    return jnp.where(lax.rem(chip, 2) == 0, line, chips - 1 - line)


class Ring:
    def __init__(self, chips, chip, core, dp_index, send_sem, recv_sem):
        self.chips = chips
        self.place = ring_place(chip, chips)
        self.core = core
        self.dp_index = dp_index
        self.send_sem = send_sem
        self.recv_sem = recv_sem
        self.last = chips // 2

    def at(self, offset):
        return ring_chip(lax.rem(self.place + offset + self.chips, self.chips), self.chips)

    def device(self, way):
        return (self.dp_index, self.at(1 if way == 0 else -1) * 2 + self.core)

    def leg(self, view, way, step, src, dst):
        return send(
            src, dst, self.send_sem.at[view, way, step], self.recv_sem.at[view, way, step], self.device(way)
        )


def arrange_kernel(ff_blocks, units, ug_ref, down_ref, *refs):
    piece_ref = refs[-1]
    unit = units[pl.program_id(0)]
    rows, wide = piece_ref.shape[1:]
    sub, width = down_ref.shape[1:]
    groups = width // wide

    @pl.when((unit >= 4) & (unit < 4 + 2 * ff_blocks))
    def _():
        piece_ref[0] = ug_ref[0]

    @pl.when(unit >= 4 + 2 * ff_blocks)
    def _():
        for g in range(groups):
            piece_ref[0, g * sub : (g + 1) * sub, :] = down_ref[0, :, g * wide : (g + 1) * wide]

    if len(refs) == 3:
        qkv_ref, out_ref = refs[:2]
        blocks, _, columns = qkv_ref.shape
        step = columns // 3
        share = wide // step
        for u in range(3):

            @pl.when(unit == u)
            def _():
                for block in range(blocks):
                    g, h = block // share, block % share
                    piece_ref[0, g * sub : (g + 1) * sub, h * step : (h + 1) * step] = qkv_ref[
                        block, :, u * step : (u + 1) * step
                    ]

        @pl.when(unit == 3)
        def _():
            for g in range(groups):
                piece_ref[0, g * sub : (g + 1) * sub, :] = out_ref[:, g * wide : (g + 1) * wide]


def arrange(units, ug, down, attention):
    n_dp, slots = units.shape
    rows, wide = ug.shape[1:]
    sub, width = down.shape[1:]
    ff_blocks = down.shape[0]
    specs = [
        pl.BlockSpec(
            (1, rows, wide), lambda k, u: (jnp.clip(u[k] - 4, 0, 2 * ff_blocks - 1), 0, 0)
        ),
        pl.BlockSpec(
            (1, sub, width),
            lambda k, u: (jnp.clip(u[k] - 4 - 2 * ff_blocks, 0, ff_blocks - 1), 0, 0),
        ),
    ]
    if attention:
        specs.append(pl.BlockSpec(attention[0].shape, lambda k, u: (0, 0, 0)))
        specs.append(pl.BlockSpec(attention[1].shape, lambda k, u: (0, 0)))
    return pl.pallas_call(
        functools.partial(arrange_kernel, ff_blocks),
        out_shape=jax.ShapeDtypeStruct((n_dp * slots, rows, wide), bf),
        grid_spec=pltpu.PrefetchScalarGridSpec(
            num_scalar_prefetch=1,
            grid=(n_dp * slots,),
            in_specs=specs,
            out_specs=pl.BlockSpec((1, rows, wide), lambda k, u: (k, 0, 0)),
        ),
        compiler_params=pltpu.CompilerParams(vmem_limit_bytes=16 << 20),
        cost_estimate=takes(7),
        name="arrange",
    )(units.reshape(-1), ug, down, *attention).reshape(n_dp, slots, rows, wide)


def column_sums(refs, takens, sents, cames, send_sem, recv_sem, pass_sem, take_sem, between):
    n_seq, n_dp, seq_index, dp_index = places()
    core = lax.rem(seq_index, 2)
    sibling = (dp_index, seq_index + 1 - 2 * core)
    views = range(len(refs))

    def onward(view, block):
        return send(
            refs[view].at[1 - core, block],
            takens[view].at[block],
            pass_sem.at[view, block],
            take_sem.at[view, block],
            sibling,
        )

    for block in [b for k in range(n_dp // 2) for b in (n_dp - 1 - k, k)]:
        for view in views:
            onward(view, block).start()

    def ready(block):
        for view in views:
            onward(view, block).wait_recv()

    def own(view):
        return lambda block: refs[view][core, block].astype(f32) + takens[view][block].astype(f32)

    totals = relay_sum(
        [own(view) for view in views],
        sents,
        cames,
        dp_index,
        n_dp,
        lambda place: (place, seq_index),
        send_sem,
        recv_sem,
        ready,
        between,
    )
    for block in range(n_dp):
        for view in views:
            onward(view, block).wait_send()
    return totals


class BandSum:
    def __init__(self, band, owns, outs, scratch, chips, chip, core, dp_index, n_dp):
        self.begin, self.size = band
        self.owns, self.outs = owns, outs
        self.half_came, self.full_sent, self.full_came = scratch[0:3], scratch[3:6], scratch[6:9]
        self.mine, self.side_out = scratch[9:12], scratch[12]
        ring_send, ring_recv, self.side_send, self.side_recv, self.own_sem = scratch[13:]
        self.ring = Ring(chips, chip, core, dp_index, ring_send, ring_recv)
        self.chip, self.core, self.n_dp = chip, core, n_dp
        self.sibling = (dp_index, chip * 2 + 1 - core)
        self.blocks = outs[1].shape[0]
        self.pair = self.blocks // 2
        self.half = outs[0].shape[2] // 2

    def own(self, view, place, way):
        rows = pl.ds(self.begin, self.size)
        if view == 0:
            units = pl.ds(0, self.blocks) if way is None else pl.ds(way * self.pair, self.pair)
            return self.owns[0].at[units, place, rows, :]
        columns = pl.ds(0, self.blocks * self.half)
        if way is not None:
            columns = pl.ds(way * self.pair * self.half, self.pair * self.half)
        return self.owns[view].at[place, :, :, rows, columns]

    def leg(self, view, way, step):
        ring = self.ring
        if step == 0:
            src = self.own(view, ring.at(ring.last), way)
            return ring.leg(view, way, step, src, self.half_came[view].at[way])
        src = self.full_sent[view].at[step - 1, way]
        return ring.leg(view, way, step, src, self.full_came[view].at[step - 1, way])

    def own_copy(self, view, way, step):
        distance = self.ring.last - step
        if distance == 0:
            return pltpu.make_async_copy(
                self.own(view, self.chip, None), self.mine[view], self.own_sem.at[view, 0, step - 1]
            )
        src = self.own(view, self.ring.at(distance if way == 0 else -distance), None)
        return pltpu.make_async_copy(
            src, self.full_sent[view].at[step - 1, way], self.own_sem.at[view, way, step - 1]
        )

    def start(self):
        for view in range(3):
            for way in range(2):
                self.leg(view, way, 0).start()
        for step in range(1, self.ring.last + 1):
            for view in range(3):
                for way in range(2 if step < self.ring.last else 1):
                    self.own_copy(view, way, step).start()

    def steps(self):
        pair, half = self.pair, self.half
        for step in range(1, self.ring.last):
            for view in range(3):
                for way in range(2):
                    self.own_copy(view, way, step).wait()
                    self.leg(view, way, step - 1).wait_recv()
                    full = self.full_sent[view]
                    if step > 1:
                        value = full[step - 1, way].astype(f32)
                        value = value + self.full_came[view][step - 2, way].astype(f32)
                        full[step - 1, way] = value.astype(bf)
                    elif view == 0:
                        units = slice(way * pair, (way + 1) * pair)
                        value = full[0, way, units].astype(f32)
                        value = value + self.half_came[0][way].astype(f32)
                        full[0, way, units] = value.astype(bf)
                    else:
                        columns = slice(way * pair * half, (way + 1) * pair * half)
                        value = full[0, way, :, :, :, columns].astype(f32)
                        value = value + self.half_came[view][way].astype(f32)
                        full[0, way, :, :, :, columns] = value.astype(bf)
                    self.leg(view, way, step).start()

    def finish(self):
        ug_out, down_out = self.outs
        last, blocks, half = self.ring.last, self.blocks, self.half
        for view in range(3):
            self.own_copy(view, 0, last).wait()
            for way in range(2):
                self.leg(view, way, last - 1).wait_recv()
            if last > 1:
                came = [self.full_came[view][last - 2, way].astype(f32) for way in range(2)]
                value = self.mine[view][...].astype(f32) + came[0] + came[1]
            else:
                came = [self.half_came[view][way].astype(f32) for way in range(2)]
                other = jnp.concatenate(came, axis=0 if view == 0 else 3)
                value = self.mine[view][...].astype(f32) + other
            value = value.astype(bf)
            if view == 0:
                down_out[...] = value
                continue
            value = value.reshape(2, self.n_dp * self.size, blocks * half)
            for k in range(blocks):
                unit = (view - 1) * blocks + k

                @pl.when(self.core == 0)
                def _():
                    ug_out[unit, :, :half] = value[0, :, k * half : (k + 1) * half]
                    self.side_out[unit] = value[1, :, k * half : (k + 1) * half]

                @pl.when(self.core != 0)
                def _():
                    ug_out[unit, :, half:] = value[1, :, k * half : (k + 1) * half]
                    self.side_out[unit] = value[0, :, k * half : (k + 1) * half]

        place = pl.ds(pl.multiple_of(self.core * half, half), half)
        side = send(
            self.side_out, ug_out.at[:, :, place], self.side_send, self.side_recv, self.sibling
        )
        side.start()
        side.wait()

    def close(self):
        for step in range(self.ring.last):
            for view in range(3):
                for way in range(2):
                    self.leg(view, way, step).wait_send()


def grads_kernel(bands, late_slots, *refs):
    n_seq, n_dp, seq_index, dp_index = places()
    chips, chip, core = n_seq // 2, seq_index // 2, lax.rem(seq_index, 2)
    sibling = (dp_index, chip * 2 + 1 - core)
    refs = list(refs)

    def take(count):
        taken, refs[:count] = refs[:count], []
        return taken

    info, residual_ref, cot_ref = take(3)
    owns, x_refs = take(3), take(2)
    outs = [take(2) for _ in bands]
    grad_out, ff_out, tokens_out = take(3)
    late_out = take(1)[0] if late_slots else None
    scratch = [take(18) for _ in bands]
    takens, sents, cames = take(2), take(2), take(2)
    z_send, z_recv, x_pass, x_take = take(4)
    stage, token_own, token_send, token_recv, token_pass, token_take = take(6)
    greet(
        [(lax.rem(dp_index + k, n_dp), seq_index) for k in range(1, n_dp)]
        + [(dp_index, lax.rem(chip + k, chips) * 2 + core) for k in range(1, chips)]
        + [sibling]
    )
    sums = [
        BandSum(band, owns, out, memory, chips, chip, core, dp_index, n_dp)
        for band, out, memory in zip(bands, outs, scratch)
    ]
    sums[0].start()

    def between(step):
        if step == 0:
            sums[0].steps()
            for later in sums[1:]:
                later.start()

    norm_two_grad, ff_sum = column_sums(
        x_refs, takens, sents, cames, z_send, z_recv, x_pass, x_take, between
    )
    ff_out[...] = ff_sum
    residual = residual_ref[...]
    center = residual - jnp.mean(residual, axis=-1, keepdims=True)
    variance = jnp.mean(center * center, axis=-1, keepdims=True)
    scale_inv = lax.rsqrt(variance + norm_eps)
    grad = norm_back(center * scale_inv, scale_inv, norm_two_grad) + cot_ref[...].astype(f32)
    grad_out[...] = grad
    stage[...] = grad.astype(bf)
    own_tokens = pltpu.make_async_copy(stage, tokens_out.at[seq_index], token_own)
    own_tokens.start()
    pass_on, finish_tokens = spread_blocks(
        stage, tokens_out, chips, chip, core, dp_index, sibling,
        token_send, token_recv, token_pass, token_take,
    )
    for later in sums[1:]:
        later.steps()
    sums[0].finish()
    along = []
    if late_slots:
        late_stage, late_send, late_recv, late_own = take(4)
        ug_ref, down_ref = outs[0]
        blocks, size, width = down_ref.shape
        wide = ug_ref.shape[2]
        for k in range(n_dp * late_slots):
            unit = info[k]
            is_down = unit >= 4 + 2 * blocks
            for g in range(n_dp):
                rows = slice(g * size, (g + 1) * size)
                value = ug_ref[jnp.clip(unit - 4, 0, 2 * blocks - 1), rows, :]
                other = down_ref[
                    jnp.clip(unit - 4 - 2 * blocks, 0, blocks - 1), :, g * wide : (g + 1) * wide
                ]
                use_other = jnp.full(value.shape, is_down.astype(jnp.int32), jnp.int32) != 0
                late_stage[k // late_slots, k % late_slots, rows, :] = jnp.where(
                    use_other, other, value
                )
        for k in range(1, n_dp):
            target = lax.rem(dp_index + k, n_dp)
            along.append(
                send(
                    late_stage.at[target],
                    late_out.at[dp_index],
                    late_send.at[k],
                    late_recv.at[k],
                    (target, seq_index),
                )
            )
        along.append(
            pltpu.make_async_copy(late_stage.at[dp_index], late_out.at[dp_index], late_own)
        )
        for copy in along:
            copy.start()
    pass_on()
    for later in sums[1:]:
        later.finish()
    for band in sums:
        band.close()
    own_tokens.wait()
    finish_tokens()
    for copy in along:
        copy.wait()


def sum_grads(bands, late_units, residual, cot, sums, xs, collective_id):
    _, n_dp, shard, width = xs[0].shape
    chips = lax.axis_size("seq") // 2
    steps = chips // 2
    vmem = pltpu.VMEM
    blocks = sums[0].shape[0]
    wide = sums[1].shape[-1]
    half = wide // blocks
    late_slots = late_units.shape[1]
    out_shape, out_specs, scratch = [], [], []
    for _, size in bands:
        out_shape += [
            jax.ShapeDtypeStruct((2 * blocks, n_dp * size, 2 * half), bf),
            jax.ShapeDtypeStruct((blocks, size, width), bf),
        ]
        out_specs += [VMEM] * 2
        side = (2, n_dp, size)
        fulls = [(blocks, size, width), side + (wide,), side + (wide,)]
        halves = [(blocks // 2, size, width), side + (wide // 2,), side + (wide // 2,)]
        scratch += [vmem((2,) + s, bf) for s in halves]
        scratch += [vmem((max(steps - 1, 1), 2) + s, bf) for s in fulls] * 2
        scratch += [vmem(s, bf) for s in fulls]
        scratch += [
            vmem((2 * blocks, n_dp * size, half), bf),
            DMA((3, 2, steps)),
            DMA((3, 2, steps)),
            DMA,
            DMA,
            DMA((3, 2, steps)),
        ]
    out_shape += [jax.ShapeDtypeStruct((shard, width), f32)] * 2
    out_shape.append(jax.ShapeDtypeStruct((2 * chips, shard, width), bf))
    out_specs += [VMEM, VMEM, ANY]
    scratch += [vmem((n_dp, shard, width), bf)] * 4
    scratch += [vmem((n_dp + 1, shard, width), bf)] * 2
    scratch += [DMA((2, 2, n_dp))] * 2 + [DMA((2, n_dp))] * 2
    scratch += [vmem((shard, width), bf), DMA] + [DMA((chips,))] * 4
    if late_slots:
        piece = (n_dp, late_slots, n_dp * bands[0][1], 2 * half)
        out_shape.append(jax.ShapeDtypeStruct(piece, bf))
        out_specs.append(ANY)
        scratch += [vmem(piece, bf), DMA((n_dp,)), DMA((n_dp,)), DMA]
    return pl.pallas_call(
        functools.partial(grads_kernel, bands, late_slots),
        out_shape=out_shape,
        in_specs=[pl.BlockSpec(memory_space=pltpu.SMEM), VMEM, VMEM] + [ANY] * 3 + [VMEM] * 2,
        out_specs=out_specs,
        scratch_shapes=scratch,
        compiler_params=comm_params(collective_id, 60),
        cost_estimate=takes(130),
        name="sum_grads",
    )(late_units.reshape(-1) if late_slots else jnp.zeros((1,), jnp.int32), residual, cot, *sums, *xs)


def attention_back_kernel(
    grad_ref, weight_ref, query_ref, key_ref, value_ref, mixed_ref, stat_ref, cos_ref, sin_ref, doc_row, doc_col, x_ref,
    qkv_out, qkv_weight_out, out_weight_out, mixed_grad, key_sum, value_sum
):
    seq_len, width = grad_ref.shape
    head_cols = query_ref.shape[1]
    heads = head_cols // HD
    block_rows = min(256, seq_len)
    scale = float(HD) ** (-0.5)

    def rows_of(b):
        return pl.ds(pl.multiple_of(b * block_rows, block_rows), block_rows)

    def times(left, right, left_axis, right_axis):
        return lax.dot_general(
            left, right, (((left_axis,), (right_axis,)), ((), ())), preferred_element_type=f32
        )

    def mix(b, carry):
        at = rows_of(b)
        mixed_grad[at, :] = times(grad_ref[at, :], weight_ref[...], 1, 1).astype(bf)
        return carry

    lax.fori_loop(0, seq_len // block_rows, mix, 0)
    key_sum[...] = jnp.zeros_like(key_sum)
    value_sum[...] = jnp.zeros_like(value_sum)

    def turned(grads, cosine, sine):
        scaled = grads * sine
        half = HD // 2
        other = jnp.concatenate([scaled[:, half:], -scaled[:, :half]], axis=-1)
        return grads * cosine + other

    def attend(b, carry):
        at = rows_of(b)
        begin = b * block_rows
        query_pos = begin + lax.broadcasted_iota(jnp.int32, (block_rows, seq_len), 0)
        key_pos = lax.broadcasted_iota(jnp.int32, (block_rows, seq_len), 1)
        allowed = (doc_col[at, :] == doc_row[...]) & (key_pos <= query_pos)
        for h in range(heads):
            place = slice(h * HD, (h + 1) * HD)
            query, part = query_ref[at, place], mixed_grad[at, place]
            scores = jnp.where(allowed, times(query, key_ref[:, place], 1, 1) * scale, masked_score)
            prob = jnp.exp(scores - stat_ref[at, h * HD : h * HD + 1])
            prob_grad = times(part, value_ref[:, place], 1, 1)
            inner = jnp.sum(prob * prob_grad, axis=-1, keepdims=True)
            score_grad = (prob * (prob_grad - inner) * scale).astype(bf)
            value_sum[:, place] += times(prob.astype(bf), part, 0, 0)
            key_sum[:, place] += times(score_grad, query, 0, 0)
            query_grad = times(score_grad, key_ref[:, place], 1, 0)
            qkv_out[at, place] = turned(query_grad, cos_ref[at, :], sin_ref[at, :]).astype(bf)
        return carry

    lax.fori_loop(0, seq_len // block_rows, attend, 0)

    def finish(b, carry):
        at = rows_of(b)
        for h in range(heads):
            place = slice(h * HD, (h + 1) * HD)
            grads = turned(key_sum[at, place], cos_ref[at, :], sin_ref[at, :])
            qkv_out[at, head_cols + h * HD : head_cols + (h + 1) * HD] = grads.astype(bf)
        qkv_out[at, 2 * head_cols :] = value_sum[at, :].astype(bf)
        return carry

    lax.fori_loop(0, seq_len // block_rows, finish, 0)
    columns = min(512, width)
    for c in range(width // columns):
        at = slice(c * columns, (c + 1) * columns)
        qkv_weight_out[at, :] = times(x_ref[:, at], qkv_out[...], 0, 0).astype(bf)
        out_weight_out[:, at] = times(mixed_ref[...], grad_ref[:, at], 0, 0).astype(bf)


def attention_back(grad, weight, query, key, value, mixed, stat, cosine, sine, doc, x):
    seq_len, width = grad.shape
    head_cols = query.shape[1]
    return pl.pallas_call(
        attention_back_kernel,
        out_shape=[
            jax.ShapeDtypeStruct((seq_len, 3 * head_cols), bf),
            jax.ShapeDtypeStruct((width, 3 * head_cols), bf),
            jax.ShapeDtypeStruct((head_cols, width), bf),
        ],
        in_specs=[VMEM] * 12,
        out_specs=[VMEM] * 3,
        scratch_shapes=[
            pltpu.VMEM((seq_len, head_cols), bf),
            pltpu.VMEM((seq_len, head_cols), f32),
            pltpu.VMEM((seq_len, head_cols), f32),
        ],
        compiler_params=pltpu.CompilerParams(vmem_limit_bytes=50 << 20),
        cost_estimate=takes(35),
        name="attention_back",
    )(grad, weight, query, key, value, mixed, stat, cosine, sine, doc[None, :], doc[:, None], x)


def turn_half(values):
    half = values.shape[-1] // 2
    return jnp.concatenate([-values[:, half:], values[:, :half]], axis=-1)


def forward_kernel(has_late, first_slots, ff_blocks, *refs):
    info, first_ref = refs[:2]
    refs = refs[2:]
    if has_late:
        late_ref, refs = refs[0], refs[1:]
    x1_ref, cos_ref, sin_ref, doc_row, doc_col, tokens_ref, cot_ref = refs[:7]
    qkv_all, out_all, query_out, key_out, value_out, mixed_out, stat_out, residual_out = refs[7:15]
    up_all, gate_all, down_all, x_all, cot_all = refs[15:20]
    ug_all = (up_all, gate_all)
    refs = refs[1:]
    att_stage, out_stage, part, taken, sent, arrived, x_stage = refs[19:26]
    mine_stage, given_stage, down_stage = refs[26:29]
    (own_sem, a_send, a_recv, w_send, w_recv, s_pass, s_take, s_send, s_recv, cot_send, cot_recv,
     late_send, late_recv, late_own, stage_own, side_send, side_recv, ring_send, ring_recv,
     send_sem, recv_sem, pass_sem, take_sem) = refs[29:52]
    late_tables = refs[52:]
    n_seq, n_dp, seq_index, dp_index = places()
    chips, chip, core = n_seq // 2, seq_index // 2, lax.rem(seq_index, 2)
    sibling = (dp_index, chip * 2 + 1 - core)
    seq_peers = [lax.rem(seq_index + k, n_seq) for k in range(n_seq)]
    dp_peers = [lax.rem(dp_index + k, n_dp) for k in range(n_dp)]
    rows, wide = first_ref.shape[1:]
    sub = rows // n_dp
    half = wide // 2
    step_cols = att_stage.shape[2] // 3
    share = wide // step_cols
    tokens, width = tokens_ref.shape
    greet([(dp_index, p) for p in seq_peers[1:]] + [(p, seq_index) for p in dp_peers[1:]])

    def band(c):
        return pl.ds(c * sub, sub)

    def late_copies(c):
        copies = []
        for k in range(1, n_dp):
            copies.append(
                send(
                    late_ref.at[dp_peers[k], :, band(c)],
                    late_tables[c].at[dp_index],
                    late_send.at[c, k],
                    late_recv.at[c, k],
                    (dp_peers[k], seq_index),
                )
            )
        return copies

    def late_own_copy(c):
        return pltpu.make_async_copy(
            late_ref.at[dp_index, :, band(c)], late_tables[c].at[dp_index], late_own.at[c]
        )

    def late_start(c):
        if not has_late or c >= n_dp:
            return
        if c:
            for copy in late_copies(c - 1):
                copy.wait_send()
        for copy in late_copies(c):
            copy.start()
        late_own_copy(c).start()

    late_start(0)

    for u in range(3):
        for block in range(n_seq):
            g, h = block // share, block % share
            att_stage[block, :, u * step_cols : (u + 1) * step_cols] = first_ref[
                info[u], g * sub : (g + 1) * sub, h * step_cols : (h + 1) * step_cols
            ]
    for g in range(n_dp):
        out_stage[:, g * wide : (g + 1) * wide] = first_ref[info[3], g * sub : (g + 1) * sub, :]
    own = [
        pltpu.make_async_copy(att_stage.at[seq_index], qkv_all.at[seq_index, dp_index], own_sem.at[0]),
        pltpu.make_async_copy(out_stage, out_all.at[dp_index], own_sem.at[1]),
    ]
    cot_own = pltpu.make_async_copy(cot_ref, cot_all.at[core], own_sem.at[2])
    cot_copy = send(cot_ref, cot_all.at[core], cot_send, cot_recv, sibling)
    across = []
    for k in range(1, n_seq):
        copy = send(
            att_stage.at[seq_peers[k]],
            qkv_all.at[seq_index, dp_index],
            a_send.at[k],
            a_recv.at[k],
            (dp_index, seq_peers[k]),
        )
        copy.start()
        across.append(copy)
    for copy in own:
        copy.start()
    cot_copy.start()
    cot_own.start()
    for copy in own:
        copy.wait()
    for copy in across:
        copy.wait_recv()
    relay_gather(
        [lambda block: qkv_all.at[:, block], lambda block: out_all.at[block]],
        dp_index,
        n_dp,
        lambda place: (place, seq_index),
        w_send,
        w_recv,
        lambda block: None,
    )

    seq_len = x1_ref.shape[0]
    heads = query_out.shape[1] // HD
    block_rows = min(256, seq_len)
    head_cols = heads * HD
    qkv_weight = qkv_all[...].reshape(width, 3 * head_cols)

    def project(b, carry):
        at = pl.ds(pl.multiple_of(b * block_rows, block_rows), block_rows)
        result = jnp.dot(x1_ref[at, :], qkv_weight, preferred_element_type=f32)
        cosine, sine = cos_ref[at, :], sin_ref[at, :]
        for h in range(heads):
            place = slice(h * HD, (h + 1) * HD)
            for part_id, out in ((0, query_out), (1, key_out)):
                begin = part_id * head_cols + h * HD
                values = result[:, begin : begin + HD]
                out[at, place] = (values * cosine + turn_half(values) * sine).astype(bf)
        value_out[at, :] = result[:, 2 * head_cols :].astype(bf)
        return carry

    lax.fori_loop(0, seq_len // block_rows, project, 0)

    def attend(b, carry):
        begin = pl.multiple_of(b * block_rows, block_rows)
        at = pl.ds(begin, block_rows)
        query_pos = begin + lax.broadcasted_iota(jnp.int32, (block_rows, seq_len), 0)
        key_pos = lax.broadcasted_iota(jnp.int32, (block_rows, seq_len), 1)
        allowed = (doc_col[at, :] == doc_row[...]) & (key_pos <= query_pos)
        for h in range(heads):
            place = slice(h * HD, (h + 1) * HD)
            scores = lax.dot_general(
                query_out[at, place],
                key_out[:, place],
                (((1,), (1,)), ((), ())),
                preferred_element_type=f32,
            )
            scores = jnp.where(allowed, scores * (float(HD) ** (-0.5)), masked_score)
            peak = jnp.max(scores, axis=-1, keepdims=True)
            raised = jnp.exp(scores - peak)
            total = jnp.sum(raised, axis=-1, keepdims=True)
            prob = (raised * (1.0 / total)).astype(bf)
            mixed = jnp.dot(prob, value_out[:, place], preferred_element_type=f32)
            mixed_out[at, place] = mixed.astype(bf)
            stat_out[at, place] = jnp.broadcast_to(peak + jnp.log(total), (block_rows, HD))
        return carry

    lax.fori_loop(0, seq_len // block_rows, attend, 0)
    out_weight = out_all[...].reshape(rows, width)

    def combine(b, carry):
        at = pl.ds(pl.multiple_of(b * tokens, tokens), tokens)
        part[b] = jnp.dot(mixed_out[at, :], out_weight, preferred_element_type=f32).astype(bf)
        return carry

    lax.fori_loop(0, n_seq, combine, 0)

    chip_peers = [lax.rem(chip + k, chips) for k in range(chips)]
    order = list(range(chips - 1, 0, -1)) + [0]
    passed = {}
    for k in order:
        block = part.at[chip_peers[k] * 2 + 1 - core]
        passed[k] = send(block, taken.at[k], s_pass.at[k], s_take.at[k], sibling)
        passed[k].start()
    copies = {}
    for k in order[:-1]:
        passed[k].wait_recv()
        value = part[chip_peers[k] * 2 + core].astype(f32)
        sent[k] = (value + taken[k].astype(f32)).astype(bf)
        device = (dp_index, chip_peers[k] * 2 + core)
        copies[k] = send(sent.at[k], arrived.at[k], s_send.at[k], s_recv.at[k], device)
        copies[k].start()

    ring = Ring(chips, chip, core, dp_index, None, None)
    pair = ff_blocks // 2

    def ring_leg(c, view, way, step, arriving):
        distance = step if arriving else step - 1
        block = ring.at(-distance if way == 0 else distance)
        units = pl.ds(way * pair, pair) if step == ring.last else pl.ds(0, ff_blocks)
        if view == 0:
            ref = down_all.at[units, block, :, pl.ds(c * wide, wide)]
        else:
            columns = pl.ds(0, ff_blocks * half)
            if step == ring.last:
                columns = pl.ds(way * pair * half, pair * half)
            ref = ug_all[view - 1].at[block, :, band(c), columns]
        return send(
            ref, ref, ring_send.at[c, view, way, step - 1], ring_recv.at[c, view, way, step - 1],
            ring.device(way),
        )

    def side_copies(c):
        return [
            send(
                given_stage.at[c, k],
                ug_all[k].at[chip, core, band(c)],
                side_send.at[c, k],
                side_recv.at[c, k],
                sibling,
            )
            for k in range(2)
        ]

    def begin_band(c):
        if has_late:
            for copy in late_copies(c):
                copy.wait_recv()
            late_own_copy(c).wait()
            late_start(c + 1)
            table = late_tables[c]
            late_slots = table.shape[1]
        for u in range(3 * ff_blocks):
            value = first_ref[info[4 + u], band(c), :]
            if has_late:
                code = info[4 + 3 * ff_blocks + u]
                other = table[code // late_slots, lax.rem(code, late_slots)]
                use_late = jnp.full(value.shape, info[4 + 6 * ff_blocks + u], jnp.int32) != 0
                value = jnp.where(use_late, other, value)
            if u < 2 * ff_blocks:
                left, right = value[:, :half], value[:, half:]
                k, j = u // ff_blocks, u % ff_blocks
                columns = slice(j * half, (j + 1) * half)

                @pl.when(core == 0)
                def _():
                    mine_stage[c, k, :, columns] = left
                    given_stage[c, k, :, columns] = right

                @pl.when(core != 0)
                def _():
                    mine_stage[c, k, :, columns] = right
                    given_stage[c, k, :, columns] = left
            else:
                down_stage[c, u - 2 * ff_blocks] = value
        for copy in side_copies(c):
            copy.start()
        local = [
            pltpu.make_async_copy(
                mine_stage.at[c, k], ug_all[k].at[chip, core, band(c)], stage_own.at[c, k]
            )
            for k in range(2)
        ]
        local.append(
            pltpu.make_async_copy(
                down_stage.at[c], down_all.at[:, chip, :, pl.ds(c * wide, wide)], stage_own.at[c, 2]
            )
        )
        for copy in local:
            copy.start()
        for copy in local:
            copy.wait()
        for copy in side_copies(c):
            copy.wait_recv()
        for view in range(3):
            for way in range(2):
                ring_leg(c, view, way, 1, False).start()

    def carry_band(c, step):
        for view in range(3):
            for way in range(2):
                ring_leg(c, view, way, step - 1, True).wait_recv()
                ring_leg(c, view, way, step, False).start()

    begin_band(0)
    passed[0].wait_recv()
    total = part[seq_index].astype(f32) + taken[0].astype(f32)
    for k in range(1, chips):
        copies[k].wait_recv()
        total = total + arrived[k].astype(f32)
    residual = tokens_ref[...] + total
    residual_out[...] = residual
    center = residual - jnp.mean(residual, axis=-1, keepdims=True)
    spread = jnp.mean(center * center, axis=-1, keepdims=True)
    x_stage[...] = (center * lax.rsqrt(spread + norm_eps)).astype(bf)
    for c in range(1, n_dp):
        begin_band(c)
        for step in range(2, ring.last + 1):
            carry_band(c - 1, step)

    own_x = pltpu.make_async_copy(x_stage, x_all.at[core, dp_index], own_sem.at[3])
    own_x.start()
    own_x.wait()

    def onward(block):
        ref = x_all.at[core, block]
        return send(ref, ref, pass_sem.at[block], take_sem.at[block], sibling)

    onward(dp_index).start()
    relay_gather(
        [lambda block: x_all.at[core, block]],
        dp_index,
        n_dp,
        lambda place: (place, seq_index),
        send_sem,
        recv_sem,
        lambda block: onward(block).start(),
        lambda step: carry_band(n_dp - 1, 2) if step == 1 and ring.last > 1 else None,
    )
    for step in range(3, ring.last + 1):
        carry_band(n_dp - 1, step)
    for c in range(n_dp):
        for view in range(3):
            for way in range(2):
                ring_leg(c, view, way, ring.last, True).wait_recv()
                for step in range(1, ring.last + 1):
                    ring_leg(c, view, way, step, False).wait_send()
        for copy in side_copies(c):
            copy.wait_send()
        if has_late:
            if c == n_dp - 1:
                for copy in late_copies(c):
                    copy.wait_send()
    for block in range(n_dp):
        onward(block).wait_send()
        ref = x_all.at[1 - core, block]
        send(ref, ref, pass_sem.at[block], take_sem.at[block], sibling).wait_recv()
    for k in order:
        passed[k].wait_send()
    for k in order[:-1]:
        copies[k].wait_send()
    for copy in across:
        copy.wait_send()
    cot_copy.wait_send()
    cot_own.wait()
    ref = cot_all.at[1 - core]
    send(ref, ref, cot_send, cot_recv, sibling).wait_recv()


def forward(info, first_table, late, x1, cosine, sine, doc, tokens, cot, ff_blocks, first_slots, collective_id):
    n_seq = lax.axis_size("seq")
    n_dp = lax.axis_size("dp")
    chips = n_seq // 2
    rows, wide = first_table.shape[1:]
    sub = rows // n_dp
    half = wide // 2
    seq_len, width = x1.shape
    head_cols = width // n_seq
    shard = tokens.shape[0]
    steps = chips // 2
    vmem = pltpu.VMEM
    low = lambda *shape: jax.ShapeDtypeStruct(shape, bf)
    has_late = late is not None
    blocks = vmem((chips, shard, width), bf)
    return pl.pallas_call(
        functools.partial(forward_kernel, has_late, first_slots, ff_blocks),
        out_shape=[
            low(n_seq, n_dp, sub, 3 * head_cols),
            low(n_dp, sub, width),
            low(seq_len, head_cols),
            low(seq_len, head_cols),
            low(seq_len, head_cols),
            low(seq_len, head_cols),
            jax.ShapeDtypeStruct((seq_len, head_cols), f32),
            jax.ShapeDtypeStruct((shard, width), f32),
            low(chips, 2, rows, ff_blocks * half),
            low(chips, 2, rows, ff_blocks * half),
            low(ff_blocks, chips, sub, width),
            low(2, n_dp, shard, width),
            low(2, n_dp, shard, width),
        ],
        in_specs=[pl.BlockSpec(memory_space=pltpu.SMEM), VMEM]
        + [ANY] * has_late
        + [VMEM] * 7,
        out_specs=[VMEM] * 8 + [ANY] * 5,
        scratch_shapes=[
            vmem((n_seq, sub, 3 * head_cols), bf),
            vmem((sub, width), bf),
            vmem((n_seq, shard, width), bf),
            blocks,
            blocks,
            blocks,
            vmem((shard, width), bf),
            vmem((n_dp, 2, sub, ff_blocks * half), bf),
            vmem((n_dp, 2, sub, ff_blocks * half), bf),
            vmem((n_dp, ff_blocks, sub, wide), bf),
            DMA((4,)),
            DMA((n_seq,)),
            DMA((n_seq,)),
            DMA((2, 2, n_dp)),
            DMA((2, 2, n_dp)),
            DMA((chips,)),
            DMA((chips,)),
            DMA((chips,)),
            DMA((chips,)),
            DMA,
            DMA,
            DMA((n_dp, n_dp)),
            DMA((n_dp, n_dp)),
            DMA((n_dp,)),
            DMA((n_dp, 3)),
            DMA((n_dp, 2)),
            DMA((n_dp, 2)),
            DMA((n_dp, 3, 2, steps)),
            DMA((n_dp, 3, 2, steps)),
            DMA((1, 2, n_dp)),
            DMA((1, 2, n_dp)),
            DMA((n_dp,)),
            DMA((n_dp,)),
        ]
        + [vmem((n_dp, late.shape[1], sub, wide), bf) for _ in range(n_dp if has_late else 0)],
        compiler_params=comm_params(collective_id, 58),
        cost_estimate=takes(230),
        name="forward",
    )(
        info,
        first_table,
        *([late] if has_late else []),
        x1,
        cosine,
        sine,
        doc[None, :],
        doc[:, None],
        tokens,
        cot,
    )


def local(block_input, cotangent, doc_lengths, owners, master, first_moment, second_moment):
    n_seq = lax.axis_size("seq")
    n_dp = lax.axis_size("dp")
    seq_index = lax.axis_index("seq")
    dp_index = lax.axis_index("dp")
    core = seq_index % 2
    _, shard_len, width = block_input.shape
    rows = master.shape[0]
    per_owner = master.shape[1]
    chips = n_seq // 2
    sub = rows // n_dp
    wide = width // n_dp
    half = chips * sub
    head_cols = H // n_seq * HD
    seq_len = shard_len * n_seq
    ff_blocks = FF // D
    first_slots = min(4, per_owner)
    unit_count = owners.shape[0]

    unit_slot = unit_slots(owners, per_owner)
    place = unit_slot - owners * per_owner
    all_slots = jnp.arange(n_dp * per_owner, dtype=jnp.int32)
    match = unit_slot[None, :] == all_slots[:, None]
    slot_unit = jnp.sum(
        jnp.where(match, jnp.arange(unit_count, dtype=jnp.int32)[None, :] + 1, 0), axis=1
    ) - 1
    slot_unit = slot_unit.reshape(n_dp, per_owner)
    own_units = lax.dynamic_index_in_dim(slot_unit, dp_index, 0, keepdims=False)
    is_col = (own_units >= 4) & (own_units < 4 + 2 * ff_blocks)


    tokens = block_input.astype(f32).reshape(shard_len, width)
    normed_one, inv_one = norm_parts(tokens)
    packed = pack(master, is_col.astype(jnp.int32), n_dp, n_seq, first_slots)
    first_table, normed_one_all = front(packed[0], normed_one.astype(bf), 2)
    first_table = first_table.reshape(n_dp * first_slots, rows, wide)
    normed_one_all = normed_one_all.reshape(seq_len, width)
    upstream = cotangent.reshape(shard_len, width)
    upstream_column = lax.all_gather(upstream, "dp", axis=0)
    positions = jnp.arange(seq_len, dtype=jnp.int32)
    cosine, sine = rope_tables(positions.astype(f32), HD)
    doc_ends = jnp.cumsum(doc_lengths[0])
    doc = jnp.sum((positions[:, None] >= doc_ends[None, :]).astype(jnp.int32), axis=1)
    late_slots = per_owner - first_slots
    info = jnp.concatenate(
        [
            owners * first_slots + jnp.minimum(place, first_slots - 1),
            (owners * late_slots + jnp.maximum(place - first_slots, 0))[4:],
            (place >= first_slots)[4:],
        ]
    ).astype(jnp.int32)
    (
        qkv_weight,
        out_weight,
        queries,
        keys,
        values,
        attended_low,
        log_total,
        residual,
        up_weight,
        gate_weight,
        down_weight,
        normed_two_all,
        upstream_all,
    ) = forward(
        info,
        first_table,
        packed[1] if late_slots else None,
        normed_one_all,
        cosine,
        sine,
        doc,
        tokens,
        upstream_column,
        ff_blocks,
        first_slots,
        1,
    )
    qkv_weight = qkv_weight.reshape(width, 3 * head_cols)
    out_weight = out_weight.reshape(rows, width)
    normed_two, inv_two = norm_parts(residual)
    columns = ff_blocks * half
    up_weight = up_weight.reshape(width, columns)
    gate_weight = gate_weight.reshape(width, columns)
    down_weight = down_weight.reshape(columns, width)
    normed_two_all = normed_two_all.reshape(-1, width)
    upstream_all = upstream_all.reshape(-1, width)

    def times(left, right, left_axis, right_axis):
        return lax.dot_general(
            left, right, (((left_axis,), (right_axis,)), ((), ())), preferred_element_type=f32
        )

    up_proj = times(normed_two_all, up_weight, 1, 0)
    gate_proj = times(normed_two_all, gate_weight, 1, 0)
    gate_sig = jax.nn.sigmoid(gate_proj)
    silu_value = gate_proj * gate_sig
    hidden_low = (silu_value * up_proj).astype(bf)
    hidden_grad = times(upstream_all, down_weight, 1, 1)
    up_grad_low = (hidden_grad * silu_value).astype(bf)
    gate_grad_low = (
        hidden_grad * up_proj * (gate_sig + gate_proj * gate_sig * (1.0 - gate_sig))
    ).astype(bf)
    norm_two_grad = times(up_grad_low, up_weight, 1, 1) + times(gate_grad_low, gate_weight, 1, 1)
    side = (chips, 2, n_dp, sub, columns)
    sums = [
        times(hidden_low, upstream_all, 0, 0).astype(bf).reshape(ff_blocks, chips, sub, width),
        times(normed_two_all, up_grad_low, 0, 0).astype(bf).reshape(side),
        times(normed_two_all, gate_grad_low, 0, 0).astype(bf).reshape(side),
    ]
    ff_part = times(hidden_low, down_weight, 1, 0)
    column = (2, n_dp, shard_len, width)
    bands = [(0, sub // 2), (sub // 2, sub // 2)] if sub % 32 == 0 else [(0, sub)]
    back = sum_grads(
        bands,
        slot_unit[:, first_slots:],
        residual,
        upstream,
        sums,
        [norm_two_grad.astype(bf).reshape(column), ff_part.astype(bf).reshape(column)],
        5,
    )
    pieces = [back[2 * k : 2 * k + 2] for k in range(len(bands))]
    residual_grad, ff_out, residual_grad_all = back[2 * len(bands) : 2 * len(bands) + 3]
    residual_grad_all = residual_grad_all.reshape(seq_len, width)
    block_output = (residual + ff_out).astype(bf).reshape(block_input.shape)
    late_grads = []
    if late_slots:
        late_grads.append(back[-1])
        for now in pieces[1:]:
            send_now = arrange(slot_unit[:, first_slots:], *now, ())
            send_now, residual_grad_all = lax.optimization_barrier((send_now, residual_grad_all))
            late_grads.append(lax.all_to_all(send_now, "dp", 0, 0))
    qkv_grad_low, qkv_wgrad, out_wgrad = attention_back(
        residual_grad_all,
        out_weight,
        queries,
        keys,
        values,
        attended_low,
        log_total,
        cosine,
        sine,
        doc,
        normed_one_all,
    )
    norm_one_part = jnp.einsum("tf,rf->tr", qkv_grad_low, qkv_weight, preferred_element_type=f32)
    norm_one_grad = sum_seq(norm_one_part.astype(bf).reshape(n_seq, shard_len, width), 3)
    qkv_piece, out_piece = collect_attention(
        qkv_wgrad.reshape(n_seq, n_dp, sub, 3 * head_cols), out_wgrad.reshape(n_dp, sub, width), 6
    )
    kinds = jnp.where(own_units < 0, 2, is_col.astype(jnp.int32)).astype(jnp.int32)
    kept = ()
    came = None
    for k, (begin, size) in enumerate(bands):
        rows_now = slice(begin, begin + size)
        attention = (qkv_piece[:, rows_now], out_piece[rows_now])
        send_now = arrange(slot_unit[:, :first_slots], *pieces[k], attention)
        if came is not None:
            send_now, came, norm_one_grad = lax.optimization_barrier(
                (send_now, came, norm_one_grad)
            )
        elif late_grads:
            send_now, late_grads[-1] = lax.optimization_barrier((send_now, late_grads[-1]))
        came = lax.all_to_all(send_now, "dp", 0, 0)
        kept = adam(
            kinds,
            [came] + late_grads[k : k + 1],
            master,
            first_moment,
            second_moment,
            n_dp,
            n_seq,
            first_slots,
            begin,
            kept,
        )
    owned_grads, new_first, new_second, new_master = kept
    input_grad = (residual_grad + norm_back(normed_one, inv_one, norm_one_grad)).reshape(
        block_input.shape
    )
    return (block_output, input_grad, owned_grads, new_first, new_second, new_master)


def solution(mesh):
    placed = (
        P("dp", "seq", None),
        P("dp", "seq", None),
        P("dp", None),
        P(),
        P("seq", "dp", None),
        P("seq", "dp", None),
        P("seq", "dp", None),
    )
    return jax.shard_map(
        local,
        mesh=mesh,
        in_specs=placed,
        out_specs=(
            P("dp", "seq", None),
            P("dp", "seq", None),
            P("seq", "dp", None),
            P("seq", "dp", None),
            P("seq", "dp", None),
            P("seq", "dp", None),
        ),
        check_vma=False,
    )
```

```python
import functools

import jax
import jax.numpy as jnp
from jax import lax
from jax.experimental import pallas as pl
from jax.experimental.pallas import tpu as pltpu
from jax.sharding import PartitionSpec as P

D = 2048
H = 16
HD = 128
FF = 8192
STEP = 5
bf = jnp.bfloat16
f32 = jnp.float32
MESH = pl.DeviceIdType.MESH


norm_eps = 1e-05
rope_base = 10000.0
beta_one = 0.5
beta_two = 0.5
learn_rate = 0.01
decay_rate = 0.1
adam_eps = 1e-08
masked_score = -1000000000.0


def unit_slots(owners, per_owner):
    unit_count = owners.shape[0]
    unit_order = jnp.arange(unit_count, dtype=jnp.int32)
    matching = owners[:, None] == owners[None, :]
    before = unit_order[None, :] < unit_order[:, None]
    places = jnp.sum(jnp.where(matching & before, 1, 0), axis=1).astype(jnp.int32)
    return owners * per_owner + places


def norm_parts(values):
    center = values - jnp.mean(values, axis=-1, keepdims=True)
    spread = jnp.mean(center * center, axis=-1, keepdims=True)
    scale_inv = lax.rsqrt(spread + norm_eps)
    return (center * scale_inv, scale_inv)


def norm_back(normed, scale_inv, upstream):
    upstream_mean = jnp.mean(upstream, axis=-1, keepdims=True)
    cross_mean = jnp.mean(upstream * normed, axis=-1, keepdims=True)
    return scale_inv * (upstream - upstream_mean - normed * cross_mean)


def rope_tables(positions, head_dim):
    half_dim = head_dim // 2
    frequency = jnp.power(rope_base, -(jnp.arange(half_dim, dtype=jnp.float32) * 2.0) / head_dim)
    angles = positions[:, None] * frequency[None, :]
    cosine_half = jnp.cos(angles)
    sine_half = jnp.sin(angles)
    return (
        jnp.concatenate([cosine_half, cosine_half], axis=-1),
        jnp.concatenate([sine_half, sine_half], axis=-1),
    )


def rotate(values, cosine, sine):
    half_dim = values.shape[-1] // 2
    turned = jnp.concatenate([-values[..., half_dim:], values[..., :half_dim]], axis=-1)
    return values * cosine + turned * sine


def rotate_back(grads, cosine, sine):
    half_dim = grads.shape[-1] // 2
    scaled = grads * sine
    turned = jnp.concatenate([scaled[..., half_dim:], -scaled[..., :half_dim]], axis=-1)
    return grads * cosine + turned


def pack_kernel(n_dp, chips, first_slots, flags, m_ref, *outs):
    rb, slots, width = m_ref.shape
    rows, wide = outs[0].shape[2:]
    sub = rows // n_dp
    start = pl.program_id(0) * rb
    target = start // sub
    inner = start % sub
    turned = jnp.swapaxes(m_ref[...], 0, 1).astype(bf)
    for s in range(slots):
        out = outs[0] if s < first_slots else outs[1]
        t = s if s < first_slots else s - first_slots
        x = turned[s]

        @pl.when(flags[s] == 1)
        def _():
            for d in range(n_dp):
                pieces = [
                    x[:, (2 * k + c) * rows + d * sub : (2 * k + c) * rows + (d + 1) * sub]
                    for c in range(2)
                    for k in range(chips)
                ]
                out[d, t, pl.ds(pl.multiple_of(start, rb), rb), :] = jnp.concatenate(pieces, axis=1)

        @pl.when(flags[s] == 0)
        def _():
            for g in range(n_dp):
                out[target, t, pl.ds(pl.multiple_of(g * sub + inner, rb), rb), :] = x[
                    :, g * wide : (g + 1) * wide
                ]


def pack(master, flags, n_dp, n_seq, first_slots):
    rows, slots, width = master.shape
    wide = width // n_dp
    rb = min(32, rows // n_dp)
    counts = [first_slots] + ([slots - first_slots] if slots > first_slots else [])
    return pl.pallas_call(
        functools.partial(pack_kernel, n_dp, n_seq // 2, first_slots),
        out_shape=[jax.ShapeDtypeStruct((n_dp, c, rows, wide), bf) for c in counts],
        grid_spec=pltpu.PrefetchScalarGridSpec(
            num_scalar_prefetch=1,
            grid=(rows // rb,),
            in_specs=[pl.BlockSpec((rb, slots, width), lambda i, f: (i, 0, 0))],
            out_specs=[
                pl.BlockSpec((n_dp, c, rows, wide), lambda i, f: (0, 0, 0, 0)) for c in counts
            ],
        ),
        compiler_params=pltpu.CompilerParams(vmem_limit_bytes=50 << 20),
        name="pack",
    )(flags, master)


def adam_kernel(n_dp, chips, first_slots, n_groups, n_kept, kinds, *refs):
    cols = refs[:n_groups]
    rws = refs[n_groups : 2 * n_groups]
    m_ref, f_ref, s_ref, keep_ref = refs[2 * n_groups : 2 * n_groups + 4]
    g_out, f_out, s_out, m_out, held = refs[2 * n_groups + 4 + n_kept :]
    rb, slots, width = m_ref.shape
    wide = width // n_dp
    rows = width // (2 * chips)
    sub = rows // n_dp
    half = chips * sub
    for s in range(slots):
        group = 0 if s < first_slots else 1
        t = s if group == 0 else s - first_slots

        @pl.when(kinds[s] == 1)
        def _():
            pieces = []
            for i in range(2 * chips):
                k, c = i // 2, i % 2
                for d in range(n_dp):
                    begin = c * half + k * sub
                    pieces.append(cols[group][d, t, :, begin : begin + sub])
            held[s] = jnp.concatenate(pieces, axis=1).astype(f32)

        @pl.when(kinds[s] == 0)
        def _():
            for g in range(n_dp):
                held[s, :, g * wide : (g + 1) * wide] = rws[group][0, t, g, :, :].astype(f32)

        @pl.when(kinds[s] == 2)
        def _():
            held[s] = jnp.zeros((rb, width), f32)

    grad = jnp.swapaxes(held[...], 0, 1)
    keep = keep_ref[...] > 0.0
    g_out[...] = grad
    first = jnp.where(keep, beta_one * f_ref[...] + (1.0 - beta_one) * grad, 0.0)
    f_out[...] = first
    second = jnp.where(keep, beta_two * s_ref[...] + (1.0 - beta_two) * grad * grad, 0.0)
    s_out[...] = second
    fixed_first = first * (1.0 / (1.0 - beta_one**STEP))
    fixed_second = second * (1.0 / (1.0 - beta_two**STEP))
    old = m_ref[...]
    root = fixed_second * lax.rsqrt(jnp.maximum(fixed_second, 1e-37))
    step = fixed_first * pl.reciprocal(root + adam_eps, approx=True) + decay_rate * old
    m_out[...] = jnp.where(keep, old - learn_rate * step, 0.0)


def adam(kinds, grads, master, first_moment, second_moment, n_dp, n_seq, first_slots, begin, kept):
    rows, slots, width = master.shape
    wide = width // n_dp
    sub = rows // n_dp
    size = grads[0].shape[2] // n_dp
    rb = min(16, size)
    steps = size // rb
    state = pl.BlockSpec(
        (rb, slots, width), lambda d, i, k: (d * (sub // rb) + begin // rb + i, 0, 0)
    )
    cols = [
        pl.BlockSpec((n_dp, g.shape[1], rb, wide), lambda d, i, k: (0, 0, d * steps + i, 0))
        for g in grads
    ]
    rws = [
        pl.BlockSpec((1, g.shape[1], n_dp, rb, wide), lambda d, i, k: (d, 0, 0, i, 0)) for g in grads
    ]
    keep = jnp.broadcast_to((kinds != 2).astype(f32)[None, :, None], (1, slots, width))
    first_kept = 1 + 2 * len(grads) + 4
    return pl.pallas_call(
        functools.partial(adam_kernel, n_dp, n_seq // 2, first_slots, len(grads), len(kept)),
        out_shape=[jax.ShapeDtypeStruct(master.shape, f32)] * 4,
        grid_spec=pltpu.PrefetchScalarGridSpec(
            num_scalar_prefetch=1,
            grid=(n_dp, steps),
            in_specs=cols
            + rws
            + [state] * 3
            + [pl.BlockSpec((1, slots, width), lambda d, i, k: (0, 0, 0))]
            + [pl.BlockSpec(memory_space=pl.ANY)] * len(kept),
            out_specs=[state] * 4,
            scratch_shapes=[pltpu.VMEM((slots, rb, width), f32)],
        ),
        input_output_aliases={first_kept + k: k for k in range(len(kept))},
        compiler_params=pltpu.CompilerParams(vmem_limit_bytes=50 << 20),
        cost_estimate=pl.CostEstimate(
            flops=0, bytes_accessed=int(150e6 * size / sub), transcendentals=0
        ),
        name="adam",
    )(
        kinds,
        *grads,
        *[g.reshape(n_dp, g.shape[1], n_dp, size, wide) for g in grads],
        master,
        first_moment,
        second_moment,
        keep,
        *kept,
    )


ANY = pl.BlockSpec(memory_space=pl.ANY)
VMEM = pl.BlockSpec(memory_space=pltpu.VMEM)
DMA = pltpu.SemaphoreType.DMA


def comm_params(collective_id, mib):
    return pltpu.CompilerParams(
        collective_id=collective_id, has_side_effects=True, vmem_limit_bytes=mib << 20
    )


def takes(microseconds):
    return pl.CostEstimate(flops=0, bytes_accessed=int(microseconds * 3e6), transcendentals=0)


def places():
    n_seq = lax.axis_size("seq")
    n_dp = lax.axis_size("dp")
    return n_seq, n_dp, lax.axis_index("seq"), lax.axis_index("dp")


def greet(devices):
    barrier = pltpu.get_barrier_semaphore()
    for device in devices:
        pl.semaphore_signal(barrier, inc=1, device_id=device, device_id_type=MESH)
    pl.semaphore_wait(barrier, len(devices))


def send(src, dst, send_sem, recv_sem, device):
    return pltpu.make_async_remote_copy(
        src_ref=src,
        dst_ref=dst,
        send_sem=send_sem,
        recv_sem=recv_sem,
        device_id=device,
        device_id_type=MESH,
    )


def relay_gather(views, place, count, device_of, send_sem, recv_sem, arrived, between=None, during=None):
    def leg(view, way, step, block, target):
        ref = views[view](block)
        return send(ref, ref, send_sem.at[view, way, step], recv_sem.at[view, way, step], device_of(target))

    def going(way, step):
        block = place - (step - 1) if way == 0 else place + (step - 1)
        target = place + 1 if way == 0 else place - 1
        inside = (block >= 0) & (block < count) & (target >= 0) & (target < count)
        return block, target, inside

    for step in range(1, count):
        for way in range(2):
            block, target, inside = going(way, step)

            @pl.when(inside)
            def _():
                for view in range(len(views)):
                    leg(view, way, step, block, target).start()

        if during:
            during(step)

        for way in range(2):
            block = place - step if way == 0 else place + step

            @pl.when((block >= 0) & (block < count))
            def _():
                for view in range(len(views)):
                    leg(view, way, step, block, lax.rem(place + 1, count)).wait_recv()
                arrived(block)

        if between:
            between(step)

    for step in range(1, count):
        for way in range(2):
            block, target, inside = going(way, step)

            @pl.when(inside)
            def _():
                for view in range(len(views)):
                    leg(view, way, step, block, target).wait_send()


def relay_sum(owns, sent, came, place, count, device_of, send_sem, recv_sem, ready, between=None):
    views = range(len(owns))

    def spot(way, block, receiver):
        return jnp.where(block == receiver, count, block) if way else block

    def leg(view, way, block, target, receiver):
        return send(
            sent[view].at[block],
            came[view].at[spot(way, block, receiver)],
            send_sem.at[view, way, block],
            recv_sem.at[view, way, block],
            device_of(target),
        )

    def going(way, step):
        block = count - 1 - step + place if way == 0 else step - (count - 1 - place)
        target = place + 1 if way == 0 else place - 1
        return block, target, (block < count if way == 0 else block >= 0)

    def behind(way):
        return place > 0 if way == 0 else place < count - 1

    for step in range(count - 1):
        for way in range(2):
            block, target, inside = going(way, step)

            @pl.when(inside)
            def _():
                ready(block)
                for view in views:

                    @pl.when(behind(way))
                    def _():
                        leg(view, way, block, target, place).wait_recv()
                        value = owns[view](block) + came[view][block].astype(f32)
                        sent[view][block] = value.astype(sent[view].dtype)

                    @pl.when(jnp.logical_not(behind(way)))
                    def _():
                        sent[view][block] = owns[view](block).astype(sent[view].dtype)

                    leg(view, way, block, target, target).start()

        if between:
            between(step)

    ready(place)
    for way in range(2):

        @pl.when(behind(way))
        def _():
            for view in views:
                leg(view, way, place, lax.rem(place + 1, count), place).wait_recv()

    totals = []
    for view in views:
        total = owns[view](place)
        for way in range(2):
            value = came[view][place if way == 0 else count].astype(f32)
            total = total + jnp.where(behind(way), value, 0.0)
        totals.append(total)
    for step in range(count - 1):
        for way in range(2):
            block, target, inside = going(way, step)

            @pl.when(inside)
            def _():
                for view in views:
                    leg(view, way, block, target, target).wait_send()

    return totals


def front_kernel(
    packed_ref, x_ref, table_ref, out_ref, own_sem, a_send, a_recv, send_sem, recv_sem, pass_sem, take_sem
):
    n_seq, n_dp, seq_index, dp_index = places()
    chips, chip, core = n_seq // 2, seq_index // 2, lax.rem(seq_index, 2)
    dp_peers = [lax.rem(dp_index + k, n_dp) for k in range(n_dp)]
    chip_peers = [lax.rem(chip + k, chips) for k in range(chips)]
    sibling = (dp_index, chip * 2 + 1 - core)
    greet(
        [(p, seq_index) for p in dp_peers[1:]]
        + [(dp_index, p * 2 + core) for p in chip_peers[1:]]
        + [sibling]
    )
    along = []
    for k in range(1, n_dp):
        copy = send(
            packed_ref.at[dp_peers[k]],
            table_ref.at[dp_index],
            a_send.at[k],
            a_recv.at[k],
            (dp_peers[k], seq_index),
        )
        copy.start()
        along.append(copy)
    own = [
        pltpu.make_async_copy(packed_ref.at[dp_index], table_ref.at[dp_index], own_sem.at[0]),
        pltpu.make_async_copy(x_ref, out_ref.at[seq_index], own_sem.at[1]),
    ]
    for copy in own:
        copy.start()
    pass_on, finish = spread_blocks(
        x_ref, out_ref, chips, chip, core, dp_index, sibling, send_sem, recv_sem, pass_sem, take_sem
    )
    pass_on()
    finish()
    for copy in along:
        copy.wait()
    for copy in own:
        copy.wait()


def spread_blocks(
    x_ref, out_ref, chips, chip, core, dp_index, sibling, send_sem, recv_sem, pass_sem, take_sem
):
    mine = out_ref.at[chip * 2 + core]
    copies = {}
    for k in range(chips - 1, 0, -1):
        device = (dp_index, lax.rem(chip + k, chips) * 2 + core)
        copies[k] = send(x_ref, mine, send_sem.at[k], recv_sem.at[k], device)
        copies[k].start()
    passed = [send(x_ref, mine, pass_sem.at[0], take_sem.at[0], sibling)]
    passed[0].start()

    def pass_on():
        for k in range(1, chips):
            copies[k].wait_recv()
            block = out_ref.at[lax.rem(chip + chips - k, chips) * 2 + core]
            onward = send(block, block, pass_sem.at[k], take_sem.at[k], sibling)
            onward.start()
            passed.append(onward)

    def finish():
        for copy in copies.values():
            copy.wait_send()
        for onward in passed:
            onward.wait()

    return pass_on, finish


def front(packed, x, collective_id):
    chips = lax.axis_size("seq") // 2
    n_dp = lax.axis_size("dp")
    return pl.pallas_call(
        front_kernel,
        out_shape=[
            jax.ShapeDtypeStruct(packed.shape, packed.dtype),
            jax.ShapeDtypeStruct((2 * chips,) + x.shape, x.dtype),
        ],
        in_specs=[VMEM, VMEM],
        out_specs=[ANY, ANY],
        scratch_shapes=[DMA((2,)), DMA((n_dp,)), DMA((n_dp,))] + [DMA((chips,))] * 4,
        compiler_params=comm_params(collective_id, 24),
        cost_estimate=takes(90),
        name="front",
    )(packed, x)


def sum_seq_kernel(x_ref, out_ref, taken, sent, arrived, pass_sem, take_sem, send_sem, recv_sem):
    n_seq, n_dp, seq_index, dp_index = places()
    chips, chip, core = n_seq // 2, seq_index // 2, lax.rem(seq_index, 2)
    peers = [lax.rem(chip + k, chips) for k in range(chips)]
    sibling = (dp_index, chip * 2 + 1 - core)
    greet([(dp_index, p * 2 + core) for p in peers[1:]] + [sibling])
    order = list(range(chips - 1, 0, -1)) + [0]
    passed = {}
    for k in order:
        block = x_ref.at[peers[k] * 2 + 1 - core]
        passed[k] = send(block, taken.at[k], pass_sem.at[k], take_sem.at[k], sibling)
        passed[k].start()
    copies = {}
    for k in order[:-1]:
        passed[k].wait_recv()
        own = x_ref[peers[k] * 2 + core].astype(f32)
        sent[k] = (own + taken[k].astype(f32)).astype(sent.dtype)
        device = (dp_index, peers[k] * 2 + core)
        copies[k] = send(sent.at[k], arrived.at[k], send_sem.at[k], recv_sem.at[k], device)
        copies[k].start()
    passed[0].wait_recv()
    total = x_ref[seq_index].astype(f32) + taken[0].astype(f32)
    for k in range(1, chips):
        copies[k].wait_recv()
        total = total + arrived[k].astype(f32)
    out_ref[...] = total
    for k in order:
        passed[k].wait_send()
    for k in order[:-1]:
        copies[k].wait_send()


def sum_seq(x, collective_id):
    blocks, rows, columns = x.shape
    chips = blocks // 2
    slots = pltpu.VMEM((chips, rows, columns), x.dtype)
    return pl.pallas_call(
        sum_seq_kernel,
        out_shape=jax.ShapeDtypeStruct((rows, columns), f32),
        in_specs=[VMEM],
        out_specs=VMEM,
        scratch_shapes=[slots, slots, slots] + [DMA((chips,))] * 4,
        compiler_params=comm_params(collective_id, 40),
        cost_estimate=takes(28),
        name="sum_seq",
    )(x)


def collect_kernel(
    qkv_ref, out_ref, qkv_sum, out_sum, qkv_sent, qkv_came, out_sent, out_came, total, own_sem,
    send_sem, recv_sem, a_send, a_recv
):
    n_seq, n_dp, seq_index, dp_index = places()
    seq_peers = [lax.rem(seq_index + k, n_seq) for k in range(n_seq)]
    greet(
        [(dp_index, p) for p in seq_peers[1:]]
        + [(lax.rem(dp_index + k, n_dp), seq_index) for k in range(1, n_dp)]
    )
    sums = relay_sum(
        [lambda block: qkv_ref[:, block].astype(f32), lambda block: out_ref[block].astype(f32)],
        [qkv_sent, out_sent],
        [qkv_came, out_came],
        dp_index,
        n_dp,
        lambda place: (place, seq_index),
        send_sem,
        recv_sem,
        lambda block: None,
    )
    total[...] = sums[0].astype(total.dtype)
    across = []
    for k in range(1, n_seq):
        copy = send(
            total.at[seq_peers[k]],
            qkv_sum.at[seq_index],
            a_send.at[k],
            a_recv.at[k],
            (dp_index, seq_peers[k]),
        )
        copy.start()
        across.append(copy)
    own = pltpu.make_async_copy(total.at[seq_index], qkv_sum.at[seq_index], own_sem)
    own.start()
    out_sum[...] = sums[1].astype(out_sum.dtype)
    for copy in across:
        copy.wait()
    own.wait()


def collect_attention(qkv, out, collective_id):
    n_seq = lax.axis_size("seq")
    n_dp = lax.axis_size("dp")
    tail = qkv.shape[2:]
    return pl.pallas_call(
        collect_kernel,
        out_shape=[
            jax.ShapeDtypeStruct((n_seq,) + tail, qkv.dtype),
            jax.ShapeDtypeStruct(out.shape[1:], out.dtype),
        ],
        in_specs=[VMEM, VMEM],
        out_specs=[VMEM, VMEM],
        scratch_shapes=[
            pltpu.VMEM((n_dp, n_seq) + tail, qkv.dtype),
            pltpu.VMEM((n_dp + 1, n_seq) + tail, qkv.dtype),
            pltpu.VMEM((n_dp,) + out.shape[1:], out.dtype),
            pltpu.VMEM((n_dp + 1,) + out.shape[1:], out.dtype),
            pltpu.VMEM((n_seq,) + tail, qkv.dtype),
            DMA,
            DMA((2, 2, n_dp)),
            DMA((2, 2, n_dp)),
            DMA((n_seq,)),
            DMA((n_seq,)),
        ],
        compiler_params=comm_params(collective_id, 48),
        cost_estimate=takes(75),
        name="collect_attention",
    )(qkv, out)


def ring_chip(place, chips):
    return jnp.where(place < chips // 2, 2 * place, 2 * (chips - 1 - place) + 1)


def ring_place(chip, chips):
    line = chip // 2
    return jnp.where(lax.rem(chip, 2) == 0, line, chips - 1 - line)


class Ring:
    def __init__(self, chips, chip, core, dp_index, send_sem, recv_sem):
        self.chips = chips
        self.place = ring_place(chip, chips)
        self.core = core
        self.dp_index = dp_index
        self.send_sem = send_sem
        self.recv_sem = recv_sem
        self.last = chips // 2

    def at(self, offset):
        return ring_chip(lax.rem(self.place + offset + self.chips, self.chips), self.chips)

    def device(self, way):
        return (self.dp_index, self.at(1 if way == 0 else -1) * 2 + self.core)

    def leg(self, view, way, step, src, dst):
        return send(
            src, dst, self.send_sem.at[view, way, step], self.recv_sem.at[view, way, step], self.device(way)
        )


def arrange_kernel(ff_blocks, units, ug_ref, down_ref, *refs):
    piece_ref = refs[-1]
    unit = units[pl.program_id(0)]
    rows, wide = piece_ref.shape[1:]
    sub, width = down_ref.shape[1:]
    groups = width // wide

    @pl.when((unit >= 4) & (unit < 4 + 2 * ff_blocks))
    def _():
        piece_ref[0] = ug_ref[0]

    @pl.when(unit >= 4 + 2 * ff_blocks)
    def _():
        for g in range(groups):
            piece_ref[0, g * sub : (g + 1) * sub, :] = down_ref[0, :, g * wide : (g + 1) * wide]

    if len(refs) == 3:
        qkv_ref, out_ref = refs[:2]
        blocks, _, columns = qkv_ref.shape
        step = columns // 3
        share = wide // step
        for u in range(3):

            @pl.when(unit == u)
            def _():
                for block in range(blocks):
                    g, h = block // share, block % share
                    piece_ref[0, g * sub : (g + 1) * sub, h * step : (h + 1) * step] = qkv_ref[
                        block, :, u * step : (u + 1) * step
                    ]

        @pl.when(unit == 3)
        def _():
            for g in range(groups):
                piece_ref[0, g * sub : (g + 1) * sub, :] = out_ref[:, g * wide : (g + 1) * wide]


def arrange(units, ug, down, attention):
    n_dp, slots = units.shape
    rows, wide = ug.shape[1:]
    sub, width = down.shape[1:]
    ff_blocks = down.shape[0]
    specs = [
        pl.BlockSpec(
            (1, rows, wide), lambda k, u: (jnp.clip(u[k] - 4, 0, 2 * ff_blocks - 1), 0, 0)
        ),
        pl.BlockSpec(
            (1, sub, width),
            lambda k, u: (jnp.clip(u[k] - 4 - 2 * ff_blocks, 0, ff_blocks - 1), 0, 0),
        ),
    ]
    if attention:
        specs.append(pl.BlockSpec(attention[0].shape, lambda k, u: (0, 0, 0)))
        specs.append(pl.BlockSpec(attention[1].shape, lambda k, u: (0, 0)))
    return pl.pallas_call(
        functools.partial(arrange_kernel, ff_blocks),
        out_shape=jax.ShapeDtypeStruct((n_dp * slots, rows, wide), bf),
        grid_spec=pltpu.PrefetchScalarGridSpec(
            num_scalar_prefetch=1,
            grid=(n_dp * slots,),
            in_specs=specs,
            out_specs=pl.BlockSpec((1, rows, wide), lambda k, u: (k, 0, 0)),
        ),
        compiler_params=pltpu.CompilerParams(vmem_limit_bytes=16 << 20),
        cost_estimate=takes(7),
        name="arrange",
    )(units.reshape(-1), ug, down, *attention).reshape(n_dp, slots, rows, wide)


def column_sums(refs, takens, sents, cames, send_sem, recv_sem, pass_sem, take_sem, between):
    n_seq, n_dp, seq_index, dp_index = places()
    core = lax.rem(seq_index, 2)
    sibling = (dp_index, seq_index + 1 - 2 * core)
    views = range(len(refs))

    def onward(view, block):
        return send(
            refs[view].at[1 - core, block],
            takens[view].at[block],
            pass_sem.at[view, block],
            take_sem.at[view, block],
            sibling,
        )

    for block in [b for k in range(n_dp // 2) for b in (n_dp - 1 - k, k)]:
        for view in views:
            onward(view, block).start()

    def ready(block):
        for view in views:
            onward(view, block).wait_recv()

    def own(view):
        return lambda block: refs[view][core, block].astype(f32) + takens[view][block].astype(f32)

    totals = relay_sum(
        [own(view) for view in views],
        sents,
        cames,
        dp_index,
        n_dp,
        lambda place: (place, seq_index),
        send_sem,
        recv_sem,
        ready,
        between,
    )
    for block in range(n_dp):
        for view in views:
            onward(view, block).wait_send()
    return totals


def ff_kernel(
    x_hbm, up_hbm, gate_hbm, down_hbm, cot_ref, ff_out, grad_out, down_grad, up_grad, gate_grad,
    x_ref, up_ref, gate_ref, down_ref, cot_all, hidden, up_low, gate_low, up_factor, gate_factor, stage, narrow, grad_stage,
    load_sem, grad_sem, stage_sem, narrow_sem, own_sem, send_sem, recv_sem, pass_sem, take_sem
):
    n_seq, n_dp, seq_index, dp_index = places()
    core = lax.rem(seq_index, 2)
    sibling = (dp_index, seq_index + 1 - 2 * core)
    loads = [
        pltpu.make_async_copy(src, dst, load_sem.at[k])
        for k, (src, dst) in enumerate(
            ((x_hbm, x_ref), (up_hbm, up_ref), (gate_hbm, gate_ref), (down_hbm, down_ref))
        )
    ]
    for load in loads:
        load.start()
    greet([(lax.rem(dp_index + k, n_dp), seq_index) for k in range(1, n_dp)] + [sibling])
    own = pltpu.make_async_copy(cot_ref, cot_all.at[core, dp_index], own_sem)
    own.start()
    own.wait()

    def onward(block):
        ref = cot_all.at[core, block]
        return send(ref, ref, pass_sem.at[block], take_sem.at[block], sibling)

    onward(dp_index).start()
    count, width = x_ref.shape
    columns = up_ref.shape[1]
    shard = cot_ref.shape[0]
    block_rows = 2 * shard
    blocks = count // block_rows

    def rows_of(b):
        return pl.ds(pl.multiple_of(b * block_rows, block_rows), block_rows)

    def times(left, right, left_axis, right_axis):
        return lax.dot_general(
            left, right, (((left_axis,), (right_axis,)), ((), ())), preferred_element_type=f32
        )

    def put(index, buffer, sem, value, dst):
        slot = lax.rem(index, 2)

        def copy(to):
            return pltpu.make_async_copy(buffer.at[slot], to, sem.at[slot])

        @pl.when(index >= 2)
        def _():
            copy(dst).wait()

        buffer[slot] = value
        copy(dst).start()

    def drain(buffer, sem, dst):
        for slot in range(2):
            pltpu.make_async_copy(buffer.at[slot], dst, sem.at[slot]).wait()

    def ahead(b, carry):
        at = rows_of(b)
        up = times(x_ref[at, :], up_ref[...], 1, 0)
        gate = times(x_ref[at, :], gate_ref[...], 1, 0)
        sig = jax.nn.sigmoid(gate)
        silu = gate * sig
        hidden[at, :] = (silu * up).astype(bf)
        up_factor[at, :] = silu
        gate_factor[at, :] = up * (sig + silu * (1.0 - sig))
        return carry

    def across(b, carry):
        at = rows_of(b)
        put(b, stage, stage_sem, times(hidden[at, :], down_ref[...], 1, 0).astype(bf), ff_out.at[at, :])
        return carry

    def back(place):
        ref = cot_all.at[1 - core, place]
        send(ref, ref, pass_sem.at[place], take_sem.at[place], sibling).wait_recv()
        lines = [
            pl.ds(pl.multiple_of((c * n_dp + place) * shard, shard), shard) for c in range(2)
        ]

        def both(source):
            return jnp.concatenate([source[line, :] for line in lines], axis=0)

        cot = jnp.concatenate([cot_all[c, place] for c in range(2)], axis=0)
        hidden_grad = times(cot, down_ref[...], 1, 1)
        up_part = (hidden_grad * both(up_factor)).astype(bf)
        gate_part = (hidden_grad * both(gate_factor)).astype(bf)
        value = times(up_part, up_ref[...], 1, 1) + times(gate_part, gate_ref[...], 1, 1)
        value = value.astype(bf)
        copies = []
        for c, line in enumerate(lines):
            up_low[line, :] = up_part[c * shard : (c + 1) * shard]
            gate_low[line, :] = gate_part[c * shard : (c + 1) * shard]
            grad_stage[c] = value[c * shard : (c + 1) * shard]
            copies.append(
                pltpu.make_async_copy(grad_stage.at[c], grad_out.at[line, :], grad_sem.at[c])
            )
            copies[c].start()
        for copy in copies:
            copy.wait()

    def back_at(distance):
        for place in (dp_index - distance, dp_index + distance):

            @pl.when((place >= 0) & (place < n_dp))
            def _():
                back(place)

    def work(step):
        if step == 1:
            for load in loads[:3]:
                load.wait()
            lax.fori_loop(0, blocks, ahead, 0)
            loads[3].wait()
        if step == 2 or n_dp == 2:
            back(dp_index)
        if step > 1:
            back_at(step - 1)
        if step == n_dp - 1:
            lax.fori_loop(0, blocks, across, 0)

    relay_gather(
        [lambda block: cot_all.at[core, block]],
        dp_index,
        n_dp,
        lambda place: (place, seq_index),
        send_sem,
        recv_sem,
        lambda block: onward(block).start(),
        during=work,
    )
    back_at(n_dp - 1)
    for block in range(n_dp):
        onward(block).wait_send()
    down_rows = min(256, columns)
    down_blocks = columns // down_rows
    cot_rows = cot_all[...].reshape(count, width)
    for b in range(down_blocks):
        at = slice(b * down_rows, (b + 1) * down_rows)
        value = times(hidden[:, at], cot_rows, 0, 0).astype(bf)
        put(b + blocks, stage.at[:, pl.ds(0, down_rows)], stage_sem, value, down_grad.at[at, :])
    side_blocks = width // 256
    for k, (low, out) in enumerate(((up_low, up_grad), (gate_low, gate_grad))):
        for b in range(side_blocks):
            at = slice(b * 256, (b + 1) * 256)
            value = times(x_ref[:, at], low[...], 0, 0).astype(bf)
            put(k * side_blocks + b, narrow, narrow_sem, value, out.at[at, :])
    drain(stage.at[:, pl.ds(0, down_rows)], stage_sem, down_grad.at[pl.ds(0, down_rows), :])
    drain(narrow, narrow_sem, gate_grad.at[pl.ds(0, 256), :])


def feed_forward(x, up, gate, down, cot, collective_id):
    n_dp = lax.axis_size("dp")
    count, width = x.shape
    columns = up.shape[1]
    shard = cot.shape[0]
    vmem = pltpu.VMEM
    low = lambda *shape: jax.ShapeDtypeStruct(shape, bf)
    return pl.pallas_call(
        ff_kernel,
        out_shape=[
            low(count, width),
            low(count, width),
            low(columns, width),
            low(width, columns),
            low(width, columns),
        ],
        in_specs=[ANY] * 4 + [VMEM],
        out_specs=[ANY] * 5,
        scratch_shapes=[
            vmem((count, width), bf),
            vmem((width, columns), bf),
            vmem((width, columns), bf),
            vmem((columns, width), bf),
            vmem((2, n_dp, shard, width), bf),
            vmem((count, columns), bf),
            vmem((count, columns), bf),
            vmem((count, columns), bf),
            vmem((count, columns), f32),
            vmem((count, columns), f32),
            vmem((2, 2 * shard, width), bf),
            vmem((2, 256, columns), bf),
            vmem((2, shard, width), bf),
            DMA((4,)),
            DMA((2,)),
            DMA((2,)),
            DMA((2,)),
            DMA,
            DMA((1, 2, n_dp)),
            DMA((1, 2, n_dp)),
            DMA((n_dp,)),
            DMA((n_dp,)),
        ],
        compiler_params=comm_params(collective_id, 58),
        cost_estimate=takes(60),
        name="feed_forward",
    )(x, up, gate, down, cot)


class BandSum:
    def __init__(self, band, owns, outs, scratch, chips, chip, core, dp_index, n_dp):
        self.begin, self.size = band
        self.owns, self.outs = owns, outs
        self.half_came, self.full_sent, self.full_came = scratch[0:3], scratch[3:6], scratch[6:9]
        self.mine, self.side_out = scratch[9:12], scratch[12]
        ring_send, ring_recv, self.side_send, self.side_recv, self.own_sem = scratch[13:]
        self.ring = Ring(chips, chip, core, dp_index, ring_send, ring_recv)
        self.chip, self.core, self.n_dp = chip, core, n_dp
        self.sibling = (dp_index, chip * 2 + 1 - core)
        self.blocks = outs[1].shape[0]
        self.pair = self.blocks // 2
        self.half = outs[0].shape[2] // 2

    def own(self, view, place, way):
        rows = pl.ds(self.begin, self.size)
        if view == 0:
            units = pl.ds(0, self.blocks) if way is None else pl.ds(way * self.pair, self.pair)
            return self.owns[0].at[units, place, rows, :]
        columns = pl.ds(0, self.blocks * self.half)
        if way is not None:
            columns = pl.ds(way * self.pair * self.half, self.pair * self.half)
        return self.owns[view].at[place, :, :, rows, columns]

    def leg(self, view, way, step):
        ring = self.ring
        if step == 0:
            src = self.own(view, ring.at(ring.last), way)
            return ring.leg(view, way, step, src, self.half_came[view].at[way])
        src = self.full_sent[view].at[step - 1, way]
        return ring.leg(view, way, step, src, self.full_came[view].at[step - 1, way])

    def own_copy(self, view, way, step):
        distance = self.ring.last - step
        if distance == 0:
            return pltpu.make_async_copy(
                self.own(view, self.chip, None), self.mine[view], self.own_sem.at[view, 0, step - 1]
            )
        src = self.own(view, self.ring.at(distance if way == 0 else -distance), None)
        return pltpu.make_async_copy(
            src, self.full_sent[view].at[step - 1, way], self.own_sem.at[view, way, step - 1]
        )

    def start(self):
        for view in range(3):
            for way in range(2):
                self.leg(view, way, 0).start()
        for step in range(1, self.ring.last + 1):
            for view in range(3):
                for way in range(2 if step < self.ring.last else 1):
                    self.own_copy(view, way, step).start()

    def steps(self):
        pair, half = self.pair, self.half
        for step in range(1, self.ring.last):
            for view in range(3):
                for way in range(2):
                    self.own_copy(view, way, step).wait()
                    self.leg(view, way, step - 1).wait_recv()
                    full = self.full_sent[view]
                    if step > 1:
                        value = full[step - 1, way].astype(f32)
                        value = value + self.full_came[view][step - 2, way].astype(f32)
                        full[step - 1, way] = value.astype(bf)
                    elif view == 0:
                        units = slice(way * pair, (way + 1) * pair)
                        value = full[0, way, units].astype(f32)
                        value = value + self.half_came[0][way].astype(f32)
                        full[0, way, units] = value.astype(bf)
                    else:
                        columns = slice(way * pair * half, (way + 1) * pair * half)
                        value = full[0, way, :, :, :, columns].astype(f32)
                        value = value + self.half_came[view][way].astype(f32)
                        full[0, way, :, :, :, columns] = value.astype(bf)
                    self.leg(view, way, step).start()

    def finish(self):
        ug_out, down_out = self.outs
        last, blocks, half = self.ring.last, self.blocks, self.half
        for view in range(3):
            self.own_copy(view, 0, last).wait()
            for way in range(2):
                self.leg(view, way, last - 1).wait_recv()
            if last > 1:
                came = [self.full_came[view][last - 2, way].astype(f32) for way in range(2)]
                value = self.mine[view][...].astype(f32) + came[0] + came[1]
            else:
                came = [self.half_came[view][way].astype(f32) for way in range(2)]
                other = jnp.concatenate(came, axis=0 if view == 0 else 3)
                value = self.mine[view][...].astype(f32) + other
            value = value.astype(bf)
            if view == 0:
                down_out[...] = value
                continue
            value = value.reshape(2, self.n_dp * self.size, blocks * half)
            for k in range(blocks):
                unit = (view - 1) * blocks + k

                @pl.when(self.core == 0)
                def _():
                    ug_out[unit, :, :half] = value[0, :, k * half : (k + 1) * half]
                    self.side_out[unit] = value[1, :, k * half : (k + 1) * half]

                @pl.when(self.core != 0)
                def _():
                    ug_out[unit, :, half:] = value[1, :, k * half : (k + 1) * half]
                    self.side_out[unit] = value[0, :, k * half : (k + 1) * half]

        place = pl.ds(pl.multiple_of(self.core * half, half), half)
        side = send(
            self.side_out, ug_out.at[:, :, place], self.side_send, self.side_recv, self.sibling
        )
        side.start()
        side.wait()

    def close(self):
        for step in range(self.ring.last):
            for view in range(3):
                for way in range(2):
                    self.leg(view, way, step).wait_send()


def grads_kernel(bands, late_slots, *refs):
    n_seq, n_dp, seq_index, dp_index = places()
    chips, chip, core = n_seq // 2, seq_index // 2, lax.rem(seq_index, 2)
    sibling = (dp_index, chip * 2 + 1 - core)
    refs = list(refs)

    def take(count):
        taken, refs[:count] = refs[:count], []
        return taken

    info, residual_ref, cot_ref = take(3)
    owns, x_refs = take(3), take(2)
    outs = [take(2) for _ in bands]
    grad_out, ff_out, tokens_out = take(3)
    late_out = take(1)[0] if late_slots else None
    scratch = [take(18) for _ in bands]
    takens, sents, cames = take(2), take(2), take(2)
    z_send, z_recv, x_pass, x_take = take(4)
    stage, token_own, token_send, token_recv, token_pass, token_take = take(6)
    greet(
        [(lax.rem(dp_index + k, n_dp), seq_index) for k in range(1, n_dp)]
        + [(dp_index, lax.rem(chip + k, chips) * 2 + core) for k in range(1, chips)]
        + [sibling]
    )
    sums = [
        BandSum(band, owns, out, memory, chips, chip, core, dp_index, n_dp)
        for band, out, memory in zip(bands, outs, scratch)
    ]
    sums[0].start()

    def between(step):
        if step == 0:
            sums[0].steps()
            for later in sums[1:]:
                later.start()

    norm_two_grad, ff_sum = column_sums(
        x_refs, takens, sents, cames, z_send, z_recv, x_pass, x_take, between
    )
    ff_out[...] = ff_sum
    residual = residual_ref[...]
    center = residual - jnp.mean(residual, axis=-1, keepdims=True)
    variance = jnp.mean(center * center, axis=-1, keepdims=True)
    scale_inv = lax.rsqrt(variance + norm_eps)
    grad = norm_back(center * scale_inv, scale_inv, norm_two_grad) + cot_ref[...].astype(f32)
    grad_out[...] = grad
    stage[...] = grad.astype(bf)
    own_tokens = pltpu.make_async_copy(stage, tokens_out.at[seq_index], token_own)
    own_tokens.start()
    pass_on, finish_tokens = spread_blocks(
        stage, tokens_out, chips, chip, core, dp_index, sibling,
        token_send, token_recv, token_pass, token_take,
    )
    for later in sums[1:]:
        later.steps()
    sums[0].finish()
    along = []
    if late_slots:
        late_stage, late_send, late_recv, late_own = take(4)
        ug_ref, down_ref = outs[0]
        blocks, size, width = down_ref.shape
        wide = ug_ref.shape[2]
        for k in range(n_dp * late_slots):
            unit = info[k]
            is_down = unit >= 4 + 2 * blocks
            for g in range(n_dp):
                rows = slice(g * size, (g + 1) * size)
                value = ug_ref[jnp.clip(unit - 4, 0, 2 * blocks - 1), rows, :]
                other = down_ref[
                    jnp.clip(unit - 4 - 2 * blocks, 0, blocks - 1), :, g * wide : (g + 1) * wide
                ]
                use_other = jnp.full(value.shape, is_down.astype(jnp.int32), jnp.int32) != 0
                late_stage[k // late_slots, k % late_slots, rows, :] = jnp.where(
                    use_other, other, value
                )
        for k in range(1, n_dp):
            target = lax.rem(dp_index + k, n_dp)
            along.append(
                send(
                    late_stage.at[target],
                    late_out.at[dp_index],
                    late_send.at[k],
                    late_recv.at[k],
                    (target, seq_index),
                )
            )
        along.append(
            pltpu.make_async_copy(late_stage.at[dp_index], late_out.at[dp_index], late_own)
        )
        for copy in along:
            copy.start()
    pass_on()
    for later in sums[1:]:
        later.finish()
    for band in sums:
        band.close()
    own_tokens.wait()
    finish_tokens()
    for copy in along:
        copy.wait()


def sum_grads(bands, late_units, residual, cot, sums, xs, collective_id):
    _, n_dp, shard, width = xs[0].shape
    chips = lax.axis_size("seq") // 2
    steps = chips // 2
    vmem = pltpu.VMEM
    blocks = sums[0].shape[0]
    wide = sums[1].shape[-1]
    half = wide // blocks
    late_slots = late_units.shape[1]
    out_shape, out_specs, scratch = [], [], []
    for _, size in bands:
        out_shape += [
            jax.ShapeDtypeStruct((2 * blocks, n_dp * size, 2 * half), bf),
            jax.ShapeDtypeStruct((blocks, size, width), bf),
        ]
        out_specs += [VMEM] * 2
        side = (2, n_dp, size)
        fulls = [(blocks, size, width), side + (wide,), side + (wide,)]
        halves = [(blocks // 2, size, width), side + (wide // 2,), side + (wide // 2,)]
        scratch += [vmem((2,) + s, bf) for s in halves]
        scratch += [vmem((max(steps - 1, 1), 2) + s, bf) for s in fulls] * 2
        scratch += [vmem(s, bf) for s in fulls]
        scratch += [
            vmem((2 * blocks, n_dp * size, half), bf),
            DMA((3, 2, steps)),
            DMA((3, 2, steps)),
            DMA,
            DMA,
            DMA((3, 2, steps)),
        ]
    out_shape += [jax.ShapeDtypeStruct((shard, width), f32)] * 2
    out_shape.append(jax.ShapeDtypeStruct((2 * chips, shard, width), bf))
    out_specs += [VMEM, VMEM, ANY]
    scratch += [vmem((n_dp, shard, width), bf)] * 4
    scratch += [vmem((n_dp + 1, shard, width), bf)] * 2
    scratch += [DMA((2, 2, n_dp))] * 2 + [DMA((2, n_dp))] * 2
    scratch += [vmem((shard, width), bf), DMA] + [DMA((chips,))] * 4
    if late_slots:
        piece = (n_dp, late_slots, n_dp * bands[0][1], 2 * half)
        out_shape.append(jax.ShapeDtypeStruct(piece, bf))
        out_specs.append(ANY)
        scratch += [vmem(piece, bf), DMA((n_dp,)), DMA((n_dp,)), DMA]
    return pl.pallas_call(
        functools.partial(grads_kernel, bands, late_slots),
        out_shape=out_shape,
        in_specs=[pl.BlockSpec(memory_space=pltpu.SMEM), VMEM, VMEM] + [ANY] * 3 + [VMEM] * 2,
        out_specs=out_specs,
        scratch_shapes=scratch,
        compiler_params=comm_params(collective_id, 60),
        cost_estimate=takes(130),
        name="sum_grads",
    )(late_units.reshape(-1) if late_slots else jnp.zeros((1,), jnp.int32), residual, cot, *sums, *xs)


def attention_back_kernel(
    grad_ref, weight_ref, query_ref, key_ref, value_ref, mixed_ref, stat_ref, cos_ref, sin_ref, doc_row, doc_col, x_ref,
    qkv_out, qkv_weight_out, out_weight_out, mixed_grad, key_sum, value_sum
):
    seq_len, width = grad_ref.shape
    head_cols = query_ref.shape[1]
    heads = head_cols // HD
    block_rows = min(256, seq_len)
    scale = float(HD) ** (-0.5)

    def rows_of(b):
        return pl.ds(pl.multiple_of(b * block_rows, block_rows), block_rows)

    def times(left, right, left_axis, right_axis):
        return lax.dot_general(
            left, right, (((left_axis,), (right_axis,)), ((), ())), preferred_element_type=f32
        )

    def mix(b, carry):
        at = rows_of(b)
        mixed_grad[at, :] = times(grad_ref[at, :], weight_ref[...], 1, 1).astype(bf)
        return carry

    lax.fori_loop(0, seq_len // block_rows, mix, 0)
    key_sum[...] = jnp.zeros_like(key_sum)
    value_sum[...] = jnp.zeros_like(value_sum)

    def turned(grads, cosine, sine):
        scaled = grads * sine
        half = HD // 2
        other = jnp.concatenate([scaled[:, half:], -scaled[:, :half]], axis=-1)
        return grads * cosine + other

    def attend(b, carry):
        at = rows_of(b)
        begin = b * block_rows
        query_pos = begin + lax.broadcasted_iota(jnp.int32, (block_rows, seq_len), 0)
        key_pos = lax.broadcasted_iota(jnp.int32, (block_rows, seq_len), 1)
        allowed = (doc_col[at, :] == doc_row[...]) & (key_pos <= query_pos)
        for h in range(heads):
            place = slice(h * HD, (h + 1) * HD)
            query, part = query_ref[at, place], mixed_grad[at, place]
            scores = jnp.where(allowed, times(query, key_ref[:, place], 1, 1) * scale, masked_score)
            prob = jnp.exp(scores - stat_ref[at, h * HD : h * HD + 1])
            prob_grad = times(part, value_ref[:, place], 1, 1)
            inner = jnp.sum(prob * prob_grad, axis=-1, keepdims=True)
            score_grad = (prob * (prob_grad - inner) * scale).astype(bf)
            value_sum[:, place] += times(prob.astype(bf), part, 0, 0)
            key_sum[:, place] += times(score_grad, query, 0, 0)
            query_grad = times(score_grad, key_ref[:, place], 1, 0)
            qkv_out[at, place] = turned(query_grad, cos_ref[at, :], sin_ref[at, :]).astype(bf)
        return carry

    lax.fori_loop(0, seq_len // block_rows, attend, 0)

    def finish(b, carry):
        at = rows_of(b)
        for h in range(heads):
            place = slice(h * HD, (h + 1) * HD)
            grads = turned(key_sum[at, place], cos_ref[at, :], sin_ref[at, :])
            qkv_out[at, head_cols + h * HD : head_cols + (h + 1) * HD] = grads.astype(bf)
        qkv_out[at, 2 * head_cols :] = value_sum[at, :].astype(bf)
        return carry

    lax.fori_loop(0, seq_len // block_rows, finish, 0)
    columns = min(512, width)
    for c in range(width // columns):
        at = slice(c * columns, (c + 1) * columns)
        qkv_weight_out[at, :] = times(x_ref[:, at], qkv_out[...], 0, 0).astype(bf)
        out_weight_out[:, at] = times(mixed_ref[...], grad_ref[:, at], 0, 0).astype(bf)


def attention_back(grad, weight, query, key, value, mixed, stat, cosine, sine, doc, x):
    seq_len, width = grad.shape
    head_cols = query.shape[1]
    return pl.pallas_call(
        attention_back_kernel,
        out_shape=[
            jax.ShapeDtypeStruct((seq_len, 3 * head_cols), bf),
            jax.ShapeDtypeStruct((width, 3 * head_cols), bf),
            jax.ShapeDtypeStruct((head_cols, width), bf),
        ],
        in_specs=[VMEM] * 12,
        out_specs=[VMEM] * 3,
        scratch_shapes=[
            pltpu.VMEM((seq_len, head_cols), bf),
            pltpu.VMEM((seq_len, head_cols), f32),
            pltpu.VMEM((seq_len, head_cols), f32),
        ],
        compiler_params=pltpu.CompilerParams(vmem_limit_bytes=50 << 20),
        cost_estimate=takes(35),
        name="attention_back",
    )(grad, weight, query, key, value, mixed, stat, cosine, sine, doc[None, :], doc[:, None], x)


def turn_half(values):
    half = values.shape[-1] // 2
    return jnp.concatenate([-values[:, half:], values[:, :half]], axis=-1)


def forward_kernel(has_late, first_slots, ff_blocks, *refs):
    info, first_ref = refs[:2]
    refs = refs[2:]
    if has_late:
        late_ref, refs = refs[0], refs[1:]
    x1_ref, cos_ref, sin_ref, doc_row, doc_col, tokens_ref = refs[:6]
    refs = (None,) + refs
    qkv_all, out_all, query_out, key_out, value_out, mixed_out, stat_out, residual_out = refs[7:15]
    up_all, gate_all, down_all, x_all = refs[15:19]
    ug_all = (up_all, gate_all)
    att_stage, out_stage, part, taken, sent, arrived, x_stage = refs[19:26]
    mine_stage, given_stage, down_stage = refs[26:29]
    (own_sem, a_send, a_recv, w_send, w_recv, s_pass, s_take, s_send, s_recv,
     late_send, late_recv, late_own, stage_own, side_send, side_recv, ring_send, ring_recv,
     send_sem, recv_sem, pass_sem, take_sem) = refs[29:50]
    late_tables = refs[50:]
    n_seq, n_dp, seq_index, dp_index = places()
    chips, chip, core = n_seq // 2, seq_index // 2, lax.rem(seq_index, 2)
    sibling = (dp_index, chip * 2 + 1 - core)
    seq_peers = [lax.rem(seq_index + k, n_seq) for k in range(n_seq)]
    dp_peers = [lax.rem(dp_index + k, n_dp) for k in range(n_dp)]
    rows, wide = first_ref.shape[1:]
    sub = rows // n_dp
    half = wide // 2
    step_cols = att_stage.shape[2] // 3
    share = wide // step_cols
    tokens, width = tokens_ref.shape
    greet([(dp_index, p) for p in seq_peers[1:]] + [(p, seq_index) for p in dp_peers[1:]])

    def band(c):
        return pl.ds(c * sub, sub)

    def late_copies(c):
        copies = []
        for k in range(1, n_dp):
            copies.append(
                send(
                    late_ref.at[dp_peers[k], :, band(c)],
                    late_tables[c].at[dp_index],
                    late_send.at[c, k],
                    late_recv.at[c, k],
                    (dp_peers[k], seq_index),
                )
            )
        return copies

    def late_own_copy(c):
        return pltpu.make_async_copy(
            late_ref.at[dp_index, :, band(c)], late_tables[c].at[dp_index], late_own.at[c]
        )

    def late_start(c):
        if not has_late or c >= n_dp:
            return
        if c:
            for copy in late_copies(c - 1):
                copy.wait_send()
        for copy in late_copies(c):
            copy.start()
        late_own_copy(c).start()

    late_start(0)

    for u in range(3):
        for block in range(n_seq):
            g, h = block // share, block % share
            att_stage[block, :, u * step_cols : (u + 1) * step_cols] = first_ref[
                info[u], g * sub : (g + 1) * sub, h * step_cols : (h + 1) * step_cols
            ]
    for g in range(n_dp):
        out_stage[:, g * wide : (g + 1) * wide] = first_ref[info[3], g * sub : (g + 1) * sub, :]
    own = [
        pltpu.make_async_copy(att_stage.at[seq_index], qkv_all.at[seq_index, dp_index], own_sem.at[0]),
        pltpu.make_async_copy(out_stage, out_all.at[dp_index], own_sem.at[1]),
    ]
    across = []
    for k in range(1, n_seq):
        copy = send(
            att_stage.at[seq_peers[k]],
            qkv_all.at[seq_index, dp_index],
            a_send.at[k],
            a_recv.at[k],
            (dp_index, seq_peers[k]),
        )
        copy.start()
        across.append(copy)
    for copy in own:
        copy.start()
    for copy in own:
        copy.wait()
    for copy in across:
        copy.wait_recv()
    relay_gather(
        [lambda block: qkv_all.at[:, block], lambda block: out_all.at[block]],
        dp_index,
        n_dp,
        lambda place: (place, seq_index),
        w_send,
        w_recv,
        lambda block: None,
    )

    seq_len = x1_ref.shape[0]
    heads = query_out.shape[1] // HD
    block_rows = min(256, seq_len)
    head_cols = heads * HD
    qkv_weight = qkv_all[...].reshape(width, 3 * head_cols)

    def project(b, carry):
        at = pl.ds(pl.multiple_of(b * block_rows, block_rows), block_rows)
        result = jnp.dot(x1_ref[at, :], qkv_weight, preferred_element_type=f32)
        cosine, sine = cos_ref[at, :], sin_ref[at, :]
        for h in range(heads):
            place = slice(h * HD, (h + 1) * HD)
            for part_id, out in ((0, query_out), (1, key_out)):
                begin = part_id * head_cols + h * HD
                values = result[:, begin : begin + HD]
                out[at, place] = (values * cosine + turn_half(values) * sine).astype(bf)
        value_out[at, :] = result[:, 2 * head_cols :].astype(bf)
        return carry

    lax.fori_loop(0, seq_len // block_rows, project, 0)

    def attend(b, carry):
        begin = pl.multiple_of(b * block_rows, block_rows)
        at = pl.ds(begin, block_rows)
        query_pos = begin + lax.broadcasted_iota(jnp.int32, (block_rows, seq_len), 0)
        key_pos = lax.broadcasted_iota(jnp.int32, (block_rows, seq_len), 1)
        allowed = (doc_col[at, :] == doc_row[...]) & (key_pos <= query_pos)
        for h in range(heads):
            place = slice(h * HD, (h + 1) * HD)
            scores = lax.dot_general(
                query_out[at, place],
                key_out[:, place],
                (((1,), (1,)), ((), ())),
                preferred_element_type=f32,
            )
            scores = jnp.where(allowed, scores * (float(HD) ** (-0.5)), masked_score)
            peak = jnp.max(scores, axis=-1, keepdims=True)
            raised = jnp.exp(scores - peak)
            total = jnp.sum(raised, axis=-1, keepdims=True)
            prob = (raised * (1.0 / total)).astype(bf)
            mixed = jnp.dot(prob, value_out[:, place], preferred_element_type=f32)
            mixed_out[at, place] = mixed.astype(bf)
            stat_out[at, place] = jnp.broadcast_to(peak + jnp.log(total), (block_rows, HD))
        return carry

    lax.fori_loop(0, seq_len // block_rows, attend, 0)
    out_weight = out_all[...].reshape(rows, width)

    def combine(b, carry):
        at = pl.ds(pl.multiple_of(b * tokens, tokens), tokens)
        part[b] = jnp.dot(mixed_out[at, :], out_weight, preferred_element_type=f32).astype(bf)
        return carry

    lax.fori_loop(0, n_seq, combine, 0)

    chip_peers = [lax.rem(chip + k, chips) for k in range(chips)]
    order = list(range(chips - 1, 0, -1)) + [0]
    passed = {}
    for k in order:
        block = part.at[chip_peers[k] * 2 + 1 - core]
        passed[k] = send(block, taken.at[k], s_pass.at[k], s_take.at[k], sibling)
        passed[k].start()
    copies = {}
    for k in order[:-1]:
        passed[k].wait_recv()
        value = part[chip_peers[k] * 2 + core].astype(f32)
        sent[k] = (value + taken[k].astype(f32)).astype(bf)
        device = (dp_index, chip_peers[k] * 2 + core)
        copies[k] = send(sent.at[k], arrived.at[k], s_send.at[k], s_recv.at[k], device)
        copies[k].start()

    ring = Ring(chips, chip, core, dp_index, None, None)
    pair = ff_blocks // 2

    def ring_leg(c, view, way, step, arriving):
        distance = step if arriving else step - 1
        block = ring.at(-distance if way == 0 else distance)
        units = pl.ds(way * pair, pair) if step == ring.last else pl.ds(0, ff_blocks)
        if view == 0:
            ref = down_all.at[units, block, :, pl.ds(c * wide, wide)]
        else:
            columns = pl.ds(0, ff_blocks * half)
            if step == ring.last:
                columns = pl.ds(way * pair * half, pair * half)
            ref = ug_all[view - 1].at[block, :, band(c), columns]
        return send(
            ref, ref, ring_send.at[c, view, way, step - 1], ring_recv.at[c, view, way, step - 1],
            ring.device(way),
        )

    def side_copies(c):
        return [
            send(
                given_stage.at[c, k],
                ug_all[k].at[chip, core, band(c)],
                side_send.at[c, k],
                side_recv.at[c, k],
                sibling,
            )
            for k in range(2)
        ]

    def begin_band(c):
        if has_late:
            for copy in late_copies(c):
                copy.wait_recv()
            late_own_copy(c).wait()
            late_start(c + 1)
            table = late_tables[c]
            late_slots = table.shape[1]
        for u in range(3 * ff_blocks):
            value = first_ref[info[4 + u], band(c), :]
            if has_late:
                code = info[4 + 3 * ff_blocks + u]
                other = table[code // late_slots, lax.rem(code, late_slots)]
                use_late = jnp.full(value.shape, info[4 + 6 * ff_blocks + u], jnp.int32) != 0
                value = jnp.where(use_late, other, value)
            if u < 2 * ff_blocks:
                left, right = value[:, :half], value[:, half:]
                k, j = u // ff_blocks, u % ff_blocks
                columns = slice(j * half, (j + 1) * half)

                @pl.when(core == 0)
                def _():
                    mine_stage[c, k, :, columns] = left
                    given_stage[c, k, :, columns] = right

                @pl.when(core != 0)
                def _():
                    mine_stage[c, k, :, columns] = right
                    given_stage[c, k, :, columns] = left
            else:
                down_stage[c, u - 2 * ff_blocks] = value
        for copy in side_copies(c):
            copy.start()
        local = [
            pltpu.make_async_copy(
                mine_stage.at[c, k], ug_all[k].at[chip, core, band(c)], stage_own.at[c, k]
            )
            for k in range(2)
        ]
        local.append(
            pltpu.make_async_copy(
                down_stage.at[c], down_all.at[:, chip, :, pl.ds(c * wide, wide)], stage_own.at[c, 2]
            )
        )
        for copy in local:
            copy.start()
        for copy in local:
            copy.wait()
        for copy in side_copies(c):
            copy.wait_recv()
        for view in range(3):
            for way in range(2):
                ring_leg(c, view, way, 1, False).start()

    def carry_band(c, step):
        for view in range(3):
            for way in range(2):
                ring_leg(c, view, way, step - 1, True).wait_recv()
                ring_leg(c, view, way, step, False).start()

    begin_band(0)
    passed[0].wait_recv()
    total = part[seq_index].astype(f32) + taken[0].astype(f32)
    for k in range(1, chips):
        copies[k].wait_recv()
        total = total + arrived[k].astype(f32)
    residual = tokens_ref[...] + total
    residual_out[...] = residual
    center = residual - jnp.mean(residual, axis=-1, keepdims=True)
    spread = jnp.mean(center * center, axis=-1, keepdims=True)
    x_stage[...] = (center * lax.rsqrt(spread + norm_eps)).astype(bf)
    for c in range(1, n_dp):
        begin_band(c)
        for step in range(2, ring.last + 1):
            carry_band(c - 1, step)

    own_x = pltpu.make_async_copy(x_stage, x_all.at[core, dp_index], own_sem.at[3])
    own_x.start()
    own_x.wait()

    def onward(block):
        ref = x_all.at[core, block]
        return send(ref, ref, pass_sem.at[block], take_sem.at[block], sibling)

    onward(dp_index).start()
    relay_gather(
        [lambda block: x_all.at[core, block]],
        dp_index,
        n_dp,
        lambda place: (place, seq_index),
        send_sem,
        recv_sem,
        lambda block: onward(block).start(),
        lambda step: carry_band(n_dp - 1, 2) if step == 1 and ring.last > 1 else None,
    )
    for step in range(3, ring.last + 1):
        carry_band(n_dp - 1, step)
    for c in range(n_dp):
        for view in range(3):
            for way in range(2):
                ring_leg(c, view, way, ring.last, True).wait_recv()
                for step in range(1, ring.last + 1):
                    ring_leg(c, view, way, step, False).wait_send()
        for copy in side_copies(c):
            copy.wait_send()
        if has_late:
            if c == n_dp - 1:
                for copy in late_copies(c):
                    copy.wait_send()
    for block in range(n_dp):
        onward(block).wait_send()
        ref = x_all.at[1 - core, block]
        send(ref, ref, pass_sem.at[block], take_sem.at[block], sibling).wait_recv()
    for k in order:
        passed[k].wait_send()
    for k in order[:-1]:
        copies[k].wait_send()
    for copy in across:
        copy.wait_send()


def forward(info, first_table, late, x1, cosine, sine, doc, tokens, ff_blocks, first_slots, collective_id):
    n_seq = lax.axis_size("seq")
    n_dp = lax.axis_size("dp")
    chips = n_seq // 2
    rows, wide = first_table.shape[1:]
    sub = rows // n_dp
    half = wide // 2
    seq_len, width = x1.shape
    head_cols = width // n_seq
    shard = tokens.shape[0]
    steps = chips // 2
    vmem = pltpu.VMEM
    low = lambda *shape: jax.ShapeDtypeStruct(shape, bf)
    has_late = late is not None
    blocks = vmem((chips, shard, width), bf)
    return pl.pallas_call(
        functools.partial(forward_kernel, has_late, first_slots, ff_blocks),
        out_shape=[
            low(n_seq, n_dp, sub, 3 * head_cols),
            low(n_dp, sub, width),
            low(seq_len, head_cols),
            low(seq_len, head_cols),
            low(seq_len, head_cols),
            low(seq_len, head_cols),
            jax.ShapeDtypeStruct((seq_len, head_cols), f32),
            jax.ShapeDtypeStruct((shard, width), f32),
            low(chips, 2, rows, ff_blocks * half),
            low(chips, 2, rows, ff_blocks * half),
            low(ff_blocks, chips, sub, width),
            low(2, n_dp, shard, width),
        ],
        in_specs=[pl.BlockSpec(memory_space=pltpu.SMEM), VMEM]
        + [ANY] * has_late
        + [VMEM] * 6,
        out_specs=[VMEM] * 8 + [ANY] * 4,
        scratch_shapes=[
            vmem((n_seq, sub, 3 * head_cols), bf),
            vmem((sub, width), bf),
            vmem((n_seq, shard, width), bf),
            blocks,
            blocks,
            blocks,
            vmem((shard, width), bf),
            vmem((n_dp, 2, sub, ff_blocks * half), bf),
            vmem((n_dp, 2, sub, ff_blocks * half), bf),
            vmem((n_dp, ff_blocks, sub, wide), bf),
            DMA((4,)),
            DMA((n_seq,)),
            DMA((n_seq,)),
            DMA((2, 2, n_dp)),
            DMA((2, 2, n_dp)),
            DMA((chips,)),
            DMA((chips,)),
            DMA((chips,)),
            DMA((chips,)),
            DMA((n_dp, n_dp)),
            DMA((n_dp, n_dp)),
            DMA((n_dp,)),
            DMA((n_dp, 3)),
            DMA((n_dp, 2)),
            DMA((n_dp, 2)),
            DMA((n_dp, 3, 2, steps)),
            DMA((n_dp, 3, 2, steps)),
            DMA((1, 2, n_dp)),
            DMA((1, 2, n_dp)),
            DMA((n_dp,)),
            DMA((n_dp,)),
        ]
        + [vmem((n_dp, late.shape[1], sub, wide), bf) for _ in range(n_dp if has_late else 0)],
        compiler_params=comm_params(collective_id, 58),
        cost_estimate=takes(230),
        name="forward",
    )(
        info,
        first_table,
        *([late] if has_late else []),
        x1,
        cosine,
        sine,
        doc[None, :],
        doc[:, None],
        tokens,
    )


def local(block_input, cotangent, doc_lengths, owners, master, first_moment, second_moment):
    n_seq = lax.axis_size("seq")
    n_dp = lax.axis_size("dp")
    seq_index = lax.axis_index("seq")
    dp_index = lax.axis_index("dp")
    core = seq_index % 2
    _, shard_len, width = block_input.shape
    rows = master.shape[0]
    per_owner = master.shape[1]
    chips = n_seq // 2
    sub = rows // n_dp
    wide = width // n_dp
    half = chips * sub
    head_cols = H // n_seq * HD
    seq_len = shard_len * n_seq
    ff_blocks = FF // D
    first_slots = min(4, per_owner)
    unit_count = owners.shape[0]

    unit_slot = unit_slots(owners, per_owner)
    place = unit_slot - owners * per_owner
    all_slots = jnp.arange(n_dp * per_owner, dtype=jnp.int32)
    match = unit_slot[None, :] == all_slots[:, None]
    slot_unit = jnp.sum(
        jnp.where(match, jnp.arange(unit_count, dtype=jnp.int32)[None, :] + 1, 0), axis=1
    ) - 1
    slot_unit = slot_unit.reshape(n_dp, per_owner)
    own_units = lax.dynamic_index_in_dim(slot_unit, dp_index, 0, keepdims=False)
    is_col = (own_units >= 4) & (own_units < 4 + 2 * ff_blocks)


    tokens = block_input.astype(f32).reshape(shard_len, width)
    normed_one, inv_one = norm_parts(tokens)
    packed = pack(master, is_col.astype(jnp.int32), n_dp, n_seq, first_slots)
    first_table, normed_one_all = front(packed[0], normed_one.astype(bf), 2)
    first_table = first_table.reshape(n_dp * first_slots, rows, wide)
    normed_one_all = normed_one_all.reshape(seq_len, width)
    upstream = cotangent.reshape(shard_len, width)
    positions = jnp.arange(seq_len, dtype=jnp.int32)
    cosine, sine = rope_tables(positions.astype(f32), HD)
    doc_ends = jnp.cumsum(doc_lengths[0])
    doc = jnp.sum((positions[:, None] >= doc_ends[None, :]).astype(jnp.int32), axis=1)
    late_slots = per_owner - first_slots
    info = jnp.concatenate(
        [
            owners * first_slots + jnp.minimum(place, first_slots - 1),
            (owners * late_slots + jnp.maximum(place - first_slots, 0))[4:],
            (place >= first_slots)[4:],
        ]
    ).astype(jnp.int32)
    (
        qkv_weight,
        out_weight,
        queries,
        keys,
        values,
        attended_low,
        log_total,
        residual,
        up_weight,
        gate_weight,
        down_weight,
        normed_two_all,
    ) = forward(
        info,
        first_table,
        packed[1] if late_slots else None,
        normed_one_all,
        cosine,
        sine,
        doc,
        tokens,
        ff_blocks,
        first_slots,
        1,
    )
    qkv_weight = qkv_weight.reshape(width, 3 * head_cols)
    out_weight = out_weight.reshape(rows, width)
    normed_two, inv_two = norm_parts(residual)
    columns = ff_blocks * half
    up_weight = up_weight.reshape(width, columns)
    gate_weight = gate_weight.reshape(width, columns)
    down_weight = down_weight.reshape(columns, width)
    normed_two_all = normed_two_all.reshape(-1, width)
    ff_part, norm_two_part, down_grad, up_grad, gate_grad = feed_forward(
        normed_two_all, up_weight, gate_weight, down_weight, upstream, 7
    )
    side = (chips, 2, n_dp, sub, columns)
    sums = [
        down_grad.reshape(ff_blocks, chips, sub, width),
        up_grad.reshape(side),
        gate_grad.reshape(side),
    ]
    column = (2, n_dp, shard_len, width)
    bands = [(0, sub // 2), (sub // 2, sub // 2)] if sub % 32 == 0 else [(0, sub)]
    back = sum_grads(
        bands,
        slot_unit[:, first_slots:],
        residual,
        upstream,
        sums,
        [norm_two_part.reshape(column), ff_part.reshape(column)],
        5,
    )
    pieces = [back[2 * k : 2 * k + 2] for k in range(len(bands))]
    residual_grad, ff_out, residual_grad_all = back[2 * len(bands) : 2 * len(bands) + 3]
    residual_grad_all = residual_grad_all.reshape(seq_len, width)
    block_output = (residual + ff_out).astype(bf).reshape(block_input.shape)
    late_grads = []
    if late_slots:
        late_grads.append(back[-1])
        for now in pieces[1:]:
            send_now = arrange(slot_unit[:, first_slots:], *now, ())
            send_now, residual_grad_all = lax.optimization_barrier((send_now, residual_grad_all))
            late_grads.append(lax.all_to_all(send_now, "dp", 0, 0))
    qkv_grad_low, qkv_wgrad, out_wgrad = attention_back(
        residual_grad_all,
        out_weight,
        queries,
        keys,
        values,
        attended_low,
        log_total,
        cosine,
        sine,
        doc,
        normed_one_all,
    )
    norm_one_part = jnp.einsum("tf,rf->tr", qkv_grad_low, qkv_weight, preferred_element_type=f32)
    norm_one_grad = sum_seq(norm_one_part.astype(bf).reshape(n_seq, shard_len, width), 3)
    qkv_piece, out_piece = collect_attention(
        qkv_wgrad.reshape(n_seq, n_dp, sub, 3 * head_cols), out_wgrad.reshape(n_dp, sub, width), 6
    )
    kinds = jnp.where(own_units < 0, 2, is_col.astype(jnp.int32)).astype(jnp.int32)
    kept = ()
    came = None
    for k, (begin, size) in enumerate(bands):
        rows_now = slice(begin, begin + size)
        attention = (qkv_piece[:, rows_now], out_piece[rows_now])
        send_now = arrange(slot_unit[:, :first_slots], *pieces[k], attention)
        if came is not None:
            send_now, came, norm_one_grad = lax.optimization_barrier(
                (send_now, came, norm_one_grad)
            )
        elif late_grads:
            send_now, late_grads[-1] = lax.optimization_barrier((send_now, late_grads[-1]))
        came = lax.all_to_all(send_now, "dp", 0, 0)
        kept = adam(
            kinds,
            [came] + late_grads[k : k + 1],
            master,
            first_moment,
            second_moment,
            n_dp,
            n_seq,
            first_slots,
            begin,
            kept,
        )
    owned_grads, new_first, new_second, new_master = kept
    input_grad = (residual_grad + norm_back(normed_one, inv_one, norm_one_grad)).reshape(
        block_input.shape
    )
    return (block_output, input_grad, owned_grads, new_first, new_second, new_master)


def solution(mesh):
    placed = (
        P("dp", "seq", None),
        P("dp", "seq", None),
        P("dp", None),
        P(),
        P("seq", "dp", None),
        P("seq", "dp", None),
        P("seq", "dp", None),
    )
    return jax.shard_map(
        local,
        mesh=mesh,
        in_specs=placed,
        out_specs=(
            P("dp", "seq", None),
            P("dp", "seq", None),
            P("seq", "dp", None),
            P("seq", "dp", None),
            P("seq", "dp", None),
            P("seq", "dp", None),
        ),
        check_vma=False,
    )
```

```python
import functools

import jax
import jax.numpy as jnp
from jax import lax
from jax.experimental import pallas as pl
from jax.experimental.pallas import tpu as pltpu
from jax.sharding import PartitionSpec as P

D = 2048
H = 16
HD = 128
FF = 8192
STEP = 5
bf = jnp.bfloat16
f32 = jnp.float32
MESH = pl.DeviceIdType.MESH


norm_eps = 1e-05
rope_base = 10000.0
beta_one = 0.5
beta_two = 0.5
learn_rate = 0.01
decay_rate = 0.1
adam_eps = 1e-08
masked_score = -1000000000.0


def unit_slots(owners, per_owner):
    unit_count = owners.shape[0]
    unit_order = jnp.arange(unit_count, dtype=jnp.int32)
    matching = owners[:, None] == owners[None, :]
    before = unit_order[None, :] < unit_order[:, None]
    places = jnp.sum(jnp.where(matching & before, 1, 0), axis=1).astype(jnp.int32)
    return owners * per_owner + places


def norm_parts(values):
    center = values - jnp.mean(values, axis=-1, keepdims=True)
    spread = jnp.mean(center * center, axis=-1, keepdims=True)
    scale_inv = lax.rsqrt(spread + norm_eps)
    return (center * scale_inv, scale_inv)


def norm_back(normed, scale_inv, upstream):
    upstream_mean = jnp.mean(upstream, axis=-1, keepdims=True)
    cross_mean = jnp.mean(upstream * normed, axis=-1, keepdims=True)
    return scale_inv * (upstream - upstream_mean - normed * cross_mean)


def rope_tables(positions, head_dim):
    half_dim = head_dim // 2
    frequency = jnp.power(rope_base, -(jnp.arange(half_dim, dtype=jnp.float32) * 2.0) / head_dim)
    angles = positions[:, None] * frequency[None, :]
    cosine_half = jnp.cos(angles)
    sine_half = jnp.sin(angles)
    return (
        jnp.concatenate([cosine_half, cosine_half], axis=-1),
        jnp.concatenate([sine_half, sine_half], axis=-1),
    )


def rotate(values, cosine, sine):
    half_dim = values.shape[-1] // 2
    turned = jnp.concatenate([-values[..., half_dim:], values[..., :half_dim]], axis=-1)
    return values * cosine + turned * sine


def rotate_back(grads, cosine, sine):
    half_dim = grads.shape[-1] // 2
    scaled = grads * sine
    turned = jnp.concatenate([scaled[..., half_dim:], -scaled[..., :half_dim]], axis=-1)
    return grads * cosine + turned


def pack_kernel(n_dp, chips, first_slots, flags, m_ref, *outs):
    rb, slots, width = m_ref.shape
    rows, wide = outs[0].shape[2:]
    sub = rows // n_dp
    start = pl.program_id(0) * rb
    target = start // sub
    inner = start % sub
    turned = jnp.swapaxes(m_ref[...], 0, 1).astype(bf)
    for s in range(slots):
        out = outs[0] if s < first_slots else outs[1]
        t = s if s < first_slots else s - first_slots
        x = turned[s]

        @pl.when(flags[s] == 1)
        def _():
            for d in range(n_dp):
                pieces = [
                    x[:, (2 * k + c) * rows + d * sub : (2 * k + c) * rows + (d + 1) * sub]
                    for c in range(2)
                    for k in range(chips)
                ]
                out[d, t, pl.ds(pl.multiple_of(start, rb), rb), :] = jnp.concatenate(pieces, axis=1)

        @pl.when(flags[s] == 0)
        def _():
            for g in range(n_dp):
                out[target, t, pl.ds(pl.multiple_of(g * sub + inner, rb), rb), :] = x[
                    :, g * wide : (g + 1) * wide
                ]


def pack(master, flags, n_dp, n_seq, first_slots):
    rows, slots, width = master.shape
    wide = width // n_dp
    rb = min(32, rows // n_dp)
    counts = [first_slots] + ([slots - first_slots] if slots > first_slots else [])
    return pl.pallas_call(
        functools.partial(pack_kernel, n_dp, n_seq // 2, first_slots),
        out_shape=[jax.ShapeDtypeStruct((n_dp, c, rows, wide), bf) for c in counts],
        grid_spec=pltpu.PrefetchScalarGridSpec(
            num_scalar_prefetch=1,
            grid=(rows // rb,),
            in_specs=[pl.BlockSpec((rb, slots, width), lambda i, f: (i, 0, 0))],
            out_specs=[
                pl.BlockSpec((n_dp, c, rows, wide), lambda i, f: (0, 0, 0, 0)) for c in counts
            ],
        ),
        compiler_params=pltpu.CompilerParams(vmem_limit_bytes=50 << 20),
        name="pack",
    )(flags, master)


def adam_kernel(n_dp, chips, first_slots, n_groups, n_kept, kinds, *refs):
    cols = refs[:n_groups]
    rws = refs[n_groups : 2 * n_groups]
    m_ref, f_ref, s_ref, keep_ref = refs[2 * n_groups : 2 * n_groups + 4]
    g_out, f_out, s_out, m_out, held = refs[2 * n_groups + 4 + n_kept :]
    rb, slots, width = m_ref.shape
    wide = width // n_dp
    rows = width // (2 * chips)
    sub = rows // n_dp
    half = chips * sub
    for s in range(slots):
        group = 0 if s < first_slots else 1
        t = s if group == 0 else s - first_slots

        @pl.when(kinds[s] == 1)
        def _():
            pieces = []
            for i in range(2 * chips):
                k, c = i // 2, i % 2
                for d in range(n_dp):
                    begin = c * half + k * sub
                    pieces.append(cols[group][d, t, :, begin : begin + sub])
            held[s] = jnp.concatenate(pieces, axis=1).astype(f32)

        @pl.when(kinds[s] == 0)
        def _():
            for g in range(n_dp):
                held[s, :, g * wide : (g + 1) * wide] = rws[group][0, t, g, :, :].astype(f32)

        @pl.when(kinds[s] == 2)
        def _():
            held[s] = jnp.zeros((rb, width), f32)

    grad = jnp.swapaxes(held[...], 0, 1)
    keep = keep_ref[...] > 0.0
    g_out[...] = grad
    first = jnp.where(keep, beta_one * f_ref[...] + (1.0 - beta_one) * grad, 0.0)
    f_out[...] = first
    second = jnp.where(keep, beta_two * s_ref[...] + (1.0 - beta_two) * grad * grad, 0.0)
    s_out[...] = second
    fixed_first = first * (1.0 / (1.0 - beta_one**STEP))
    fixed_second = second * (1.0 / (1.0 - beta_two**STEP))
    old = m_ref[...]
    root = fixed_second * lax.rsqrt(jnp.maximum(fixed_second, 1e-37))
    step = fixed_first * pl.reciprocal(root + adam_eps, approx=True) + decay_rate * old
    m_out[...] = jnp.where(keep, old - learn_rate * step, 0.0)


def adam(kinds, grads, master, first_moment, second_moment, n_dp, n_seq, first_slots, begin, kept):
    rows, slots, width = master.shape
    wide = width // n_dp
    sub = rows // n_dp
    size = grads[0].shape[2] // n_dp
    rb = min(16, size)
    steps = size // rb
    state = pl.BlockSpec(
        (rb, slots, width), lambda d, i, k: (d * (sub // rb) + begin // rb + i, 0, 0)
    )
    cols = [
        pl.BlockSpec((n_dp, g.shape[1], rb, wide), lambda d, i, k: (0, 0, d * steps + i, 0))
        for g in grads
    ]
    rws = [
        pl.BlockSpec((1, g.shape[1], n_dp, rb, wide), lambda d, i, k: (d, 0, 0, i, 0)) for g in grads
    ]
    keep = jnp.broadcast_to((kinds != 2).astype(f32)[None, :, None], (1, slots, width))
    first_kept = 1 + 2 * len(grads) + 4
    return pl.pallas_call(
        functools.partial(adam_kernel, n_dp, n_seq // 2, first_slots, len(grads), len(kept)),
        out_shape=[jax.ShapeDtypeStruct(master.shape, f32)] * 4,
        grid_spec=pltpu.PrefetchScalarGridSpec(
            num_scalar_prefetch=1,
            grid=(n_dp, steps),
            in_specs=cols
            + rws
            + [state] * 3
            + [pl.BlockSpec((1, slots, width), lambda d, i, k: (0, 0, 0))]
            + [pl.BlockSpec(memory_space=pl.ANY)] * len(kept),
            out_specs=[state] * 4,
            scratch_shapes=[pltpu.VMEM((slots, rb, width), f32)],
        ),
        input_output_aliases={first_kept + k: k for k in range(len(kept))},
        compiler_params=pltpu.CompilerParams(vmem_limit_bytes=50 << 20),
        cost_estimate=pl.CostEstimate(
            flops=0, bytes_accessed=int(150e6 * size / sub), transcendentals=0
        ),
        name="adam",
    )(
        kinds,
        *grads,
        *[g.reshape(n_dp, g.shape[1], n_dp, size, wide) for g in grads],
        master,
        first_moment,
        second_moment,
        keep,
        *kept,
    )


ANY = pl.BlockSpec(memory_space=pl.ANY)
VMEM = pl.BlockSpec(memory_space=pltpu.VMEM)
DMA = pltpu.SemaphoreType.DMA


def comm_params(collective_id, mib):
    return pltpu.CompilerParams(
        collective_id=collective_id, has_side_effects=True, vmem_limit_bytes=mib << 20
    )


def takes(microseconds):
    return pl.CostEstimate(flops=0, bytes_accessed=int(microseconds * 3e6), transcendentals=0)


def places():
    n_seq = lax.axis_size("seq")
    n_dp = lax.axis_size("dp")
    return n_seq, n_dp, lax.axis_index("seq"), lax.axis_index("dp")


def greet(devices):
    barrier = pltpu.get_barrier_semaphore()
    for device in devices:
        pl.semaphore_signal(barrier, inc=1, device_id=device, device_id_type=MESH)
    pl.semaphore_wait(barrier, len(devices))


def send(src, dst, send_sem, recv_sem, device):
    return pltpu.make_async_remote_copy(
        src_ref=src,
        dst_ref=dst,
        send_sem=send_sem,
        recv_sem=recv_sem,
        device_id=device,
        device_id_type=MESH,
    )


def relay_gather(views, place, count, device_of, send_sem, recv_sem, arrived, between=None, during=None):
    def leg(view, way, step, block, target):
        ref = views[view](block)
        return send(ref, ref, send_sem.at[view, way, step], recv_sem.at[view, way, step], device_of(target))

    def going(way, step):
        block = place - (step - 1) if way == 0 else place + (step - 1)
        target = place + 1 if way == 0 else place - 1
        inside = (block >= 0) & (block < count) & (target >= 0) & (target < count)
        return block, target, inside

    for step in range(1, count):
        for way in range(2):
            block, target, inside = going(way, step)

            @pl.when(inside)
            def _():
                for view in range(len(views)):
                    leg(view, way, step, block, target).start()

        if during:
            during(step)

        for way in range(2):
            block = place - step if way == 0 else place + step

            @pl.when((block >= 0) & (block < count))
            def _():
                for view in range(len(views)):
                    leg(view, way, step, block, lax.rem(place + 1, count)).wait_recv()
                arrived(block)

        if between:
            between(step)

    for step in range(1, count):
        for way in range(2):
            block, target, inside = going(way, step)

            @pl.when(inside)
            def _():
                for view in range(len(views)):
                    leg(view, way, step, block, target).wait_send()


def relay_sum(owns, sent, came, place, count, device_of, send_sem, recv_sem, ready, between=None):
    views = range(len(owns))

    def spot(way, block, receiver):
        return jnp.where(block == receiver, count, block) if way else block

    def leg(view, way, block, target, receiver):
        return send(
            sent[view].at[block],
            came[view].at[spot(way, block, receiver)],
            send_sem.at[view, way, block],
            recv_sem.at[view, way, block],
            device_of(target),
        )

    def going(way, step):
        block = count - 1 - step + place if way == 0 else step - (count - 1 - place)
        target = place + 1 if way == 0 else place - 1
        return block, target, (block < count if way == 0 else block >= 0)

    def behind(way):
        return place > 0 if way == 0 else place < count - 1

    for step in range(count - 1):
        for way in range(2):
            block, target, inside = going(way, step)

            @pl.when(inside)
            def _():
                ready(block)
                for view in views:

                    @pl.when(behind(way))
                    def _():
                        leg(view, way, block, target, place).wait_recv()
                        value = owns[view](block) + came[view][block].astype(f32)
                        sent[view][block] = value.astype(sent[view].dtype)

                    @pl.when(jnp.logical_not(behind(way)))
                    def _():
                        sent[view][block] = owns[view](block).astype(sent[view].dtype)

                    leg(view, way, block, target, target).start()

        if between:
            between(step)

    ready(place)
    for way in range(2):

        @pl.when(behind(way))
        def _():
            for view in views:
                leg(view, way, place, lax.rem(place + 1, count), place).wait_recv()

    totals = []
    for view in views:
        total = owns[view](place)
        for way in range(2):
            value = came[view][place if way == 0 else count].astype(f32)
            total = total + jnp.where(behind(way), value, 0.0)
        totals.append(total)
    for step in range(count - 1):
        for way in range(2):
            block, target, inside = going(way, step)

            @pl.when(inside)
            def _():
                for view in views:
                    leg(view, way, block, target, target).wait_send()

    return totals


def front_kernel(
    packed_ref, tokens_ref, table_ref, out_ref, x_ref, own_sem, a_send, a_recv, send_sem, recv_sem, pass_sem, take_sem
):
    n_seq, n_dp, seq_index, dp_index = places()
    chips, chip, core = n_seq // 2, seq_index // 2, lax.rem(seq_index, 2)
    dp_peers = [lax.rem(dp_index + k, n_dp) for k in range(n_dp)]
    chip_peers = [lax.rem(chip + k, chips) for k in range(chips)]
    sibling = (dp_index, chip * 2 + 1 - core)
    greet(
        [(p, seq_index) for p in dp_peers[1:]]
        + [(dp_index, p * 2 + core) for p in chip_peers[1:]]
        + [sibling]
    )
    along = []
    for k in range(1, n_dp):
        copy = send(
            packed_ref.at[dp_peers[k]],
            table_ref.at[dp_index],
            a_send.at[k],
            a_recv.at[k],
            (dp_peers[k], seq_index),
        )
        copy.start()
        along.append(copy)
    x_ref[...] = norm_parts(tokens_ref[...].astype(f32))[0].astype(bf)
    own = [
        pltpu.make_async_copy(packed_ref.at[dp_index], table_ref.at[dp_index], own_sem.at[0]),
        pltpu.make_async_copy(x_ref, out_ref.at[seq_index], own_sem.at[1]),
    ]
    for copy in own:
        copy.start()
    pass_on, finish = spread_blocks(
        x_ref, out_ref, chips, chip, core, dp_index, sibling, send_sem, recv_sem, pass_sem, take_sem
    )
    pass_on()
    finish()
    for copy in along:
        copy.wait()
    for copy in own:
        copy.wait()


def spread_blocks(
    x_ref, out_ref, chips, chip, core, dp_index, sibling, send_sem, recv_sem, pass_sem, take_sem
):
    mine = out_ref.at[chip * 2 + core]
    copies = {}
    for k in range(chips - 1, 0, -1):
        device = (dp_index, lax.rem(chip + k, chips) * 2 + core)
        copies[k] = send(x_ref, mine, send_sem.at[k], recv_sem.at[k], device)
        copies[k].start()
    passed = [send(x_ref, mine, pass_sem.at[0], take_sem.at[0], sibling)]
    passed[0].start()

    def pass_on():
        for k in range(1, chips):
            copies[k].wait_recv()
            block = out_ref.at[lax.rem(chip + chips - k, chips) * 2 + core]
            onward = send(block, block, pass_sem.at[k], take_sem.at[k], sibling)
            onward.start()
            passed.append(onward)

    def finish():
        for copy in copies.values():
            copy.wait_send()
        for onward in passed:
            onward.wait()

    return pass_on, finish


def front(packed, x, collective_id):
    chips = lax.axis_size("seq") // 2
    n_dp = lax.axis_size("dp")
    return pl.pallas_call(
        front_kernel,
        out_shape=[
            jax.ShapeDtypeStruct(packed.shape, packed.dtype),
            jax.ShapeDtypeStruct((2 * chips,) + x.shape, x.dtype),
        ],
        in_specs=[VMEM, VMEM],
        out_specs=[ANY, ANY],
        scratch_shapes=[pltpu.VMEM(x.shape, bf), DMA((2,)), DMA((n_dp,)), DMA((n_dp,))]
        + [DMA((chips,))] * 4,
        compiler_params=comm_params(collective_id, 24),
        cost_estimate=takes(90),
        name="front",
    )(packed, x)


def sum_seq_kernel(x_ref, out_ref, taken, sent, arrived, pass_sem, take_sem, send_sem, recv_sem):
    n_seq, n_dp, seq_index, dp_index = places()
    chips, chip, core = n_seq // 2, seq_index // 2, lax.rem(seq_index, 2)
    peers = [lax.rem(chip + k, chips) for k in range(chips)]
    sibling = (dp_index, chip * 2 + 1 - core)
    greet([(dp_index, p * 2 + core) for p in peers[1:]] + [sibling])
    order = list(range(chips - 1, 0, -1)) + [0]
    passed = {}
    for k in order:
        block = x_ref.at[peers[k] * 2 + 1 - core]
        passed[k] = send(block, taken.at[k], pass_sem.at[k], take_sem.at[k], sibling)
        passed[k].start()
    copies = {}
    for k in order[:-1]:
        passed[k].wait_recv()
        own = x_ref[peers[k] * 2 + core].astype(f32)
        sent[k] = (own + taken[k].astype(f32)).astype(sent.dtype)
        device = (dp_index, peers[k] * 2 + core)
        copies[k] = send(sent.at[k], arrived.at[k], send_sem.at[k], recv_sem.at[k], device)
        copies[k].start()
    passed[0].wait_recv()
    total = x_ref[seq_index].astype(f32) + taken[0].astype(f32)
    for k in range(1, chips):
        copies[k].wait_recv()
        total = total + arrived[k].astype(f32)
    out_ref[...] = total
    for k in order:
        passed[k].wait_send()
    for k in order[:-1]:
        copies[k].wait_send()


def sum_seq(x, collective_id):
    blocks, rows, columns = x.shape
    chips = blocks // 2
    slots = pltpu.VMEM((chips, rows, columns), x.dtype)
    return pl.pallas_call(
        sum_seq_kernel,
        out_shape=jax.ShapeDtypeStruct((rows, columns), f32),
        in_specs=[VMEM],
        out_specs=VMEM,
        scratch_shapes=[slots, slots, slots] + [DMA((chips,))] * 4,
        compiler_params=comm_params(collective_id, 40),
        cost_estimate=takes(28),
        name="sum_seq",
    )(x)


def collect_kernel(
    qkv_ref, out_ref, qkv_sum, out_sum, qkv_sent, qkv_came, out_sent, out_came, total, own_sem,
    send_sem, recv_sem, a_send, a_recv
):
    n_seq, n_dp, seq_index, dp_index = places()
    seq_peers = [lax.rem(seq_index + k, n_seq) for k in range(n_seq)]
    greet(
        [(dp_index, p) for p in seq_peers[1:]]
        + [(lax.rem(dp_index + k, n_dp), seq_index) for k in range(1, n_dp)]
    )
    sums = relay_sum(
        [lambda block: qkv_ref[:, block].astype(f32), lambda block: out_ref[block].astype(f32)],
        [qkv_sent, out_sent],
        [qkv_came, out_came],
        dp_index,
        n_dp,
        lambda place: (place, seq_index),
        send_sem,
        recv_sem,
        lambda block: None,
    )
    total[...] = sums[0].astype(total.dtype)
    across = []
    for k in range(1, n_seq):
        copy = send(
            total.at[seq_peers[k]],
            qkv_sum.at[seq_index],
            a_send.at[k],
            a_recv.at[k],
            (dp_index, seq_peers[k]),
        )
        copy.start()
        across.append(copy)
    own = pltpu.make_async_copy(total.at[seq_index], qkv_sum.at[seq_index], own_sem)
    own.start()
    out_sum[...] = sums[1].astype(out_sum.dtype)
    for copy in across:
        copy.wait()
    own.wait()


def collect_attention(qkv, out, collective_id):
    n_seq = lax.axis_size("seq")
    n_dp = lax.axis_size("dp")
    tail = qkv.shape[2:]
    return pl.pallas_call(
        collect_kernel,
        out_shape=[
            jax.ShapeDtypeStruct((n_seq,) + tail, qkv.dtype),
            jax.ShapeDtypeStruct(out.shape[1:], out.dtype),
        ],
        in_specs=[VMEM, VMEM],
        out_specs=[VMEM, VMEM],
        scratch_shapes=[
            pltpu.VMEM((n_dp, n_seq) + tail, qkv.dtype),
            pltpu.VMEM((n_dp + 1, n_seq) + tail, qkv.dtype),
            pltpu.VMEM((n_dp,) + out.shape[1:], out.dtype),
            pltpu.VMEM((n_dp + 1,) + out.shape[1:], out.dtype),
            pltpu.VMEM((n_seq,) + tail, qkv.dtype),
            DMA,
            DMA((2, 2, n_dp)),
            DMA((2, 2, n_dp)),
            DMA((n_seq,)),
            DMA((n_seq,)),
        ],
        compiler_params=comm_params(collective_id, 48),
        cost_estimate=takes(75),
        name="collect_attention",
    )(qkv, out)


def ring_chip(place, chips):
    return jnp.where(place < chips // 2, 2 * place, 2 * (chips - 1 - place) + 1)


def ring_place(chip, chips):
    line = chip // 2
    return jnp.where(lax.rem(chip, 2) == 0, line, chips - 1 - line)


class Ring:
    def __init__(self, chips, chip, core, dp_index, send_sem, recv_sem):
        self.chips = chips
        self.place = ring_place(chip, chips)
        self.core = core
        self.dp_index = dp_index
        self.send_sem = send_sem
        self.recv_sem = recv_sem
        self.last = chips // 2

    def at(self, offset):
        return ring_chip(lax.rem(self.place + offset + self.chips, self.chips), self.chips)

    def device(self, way):
        return (self.dp_index, self.at(1 if way == 0 else -1) * 2 + self.core)

    def leg(self, view, way, step, src, dst):
        return send(
            src, dst, self.send_sem.at[view, way, step], self.recv_sem.at[view, way, step], self.device(way)
        )


def arrange_kernel(ff_blocks, units, ug_ref, down_ref, *refs):
    piece_ref = refs[-1]
    unit = units[pl.program_id(0)]
    rows, wide = piece_ref.shape[1:]
    sub, width = down_ref.shape[1:]
    groups = width // wide

    @pl.when((unit >= 4) & (unit < 4 + 2 * ff_blocks))
    def _():
        piece_ref[0] = ug_ref[0]

    @pl.when(unit >= 4 + 2 * ff_blocks)
    def _():
        for g in range(groups):
            piece_ref[0, g * sub : (g + 1) * sub, :] = down_ref[0, :, g * wide : (g + 1) * wide]

    if len(refs) == 3:
        qkv_ref, out_ref = refs[:2]
        blocks, _, columns = qkv_ref.shape
        step = columns // 3
        share = wide // step
        for u in range(3):

            @pl.when(unit == u)
            def _():
                for block in range(blocks):
                    g, h = block // share, block % share
                    piece_ref[0, g * sub : (g + 1) * sub, h * step : (h + 1) * step] = qkv_ref[
                        block, :, u * step : (u + 1) * step
                    ]

        @pl.when(unit == 3)
        def _():
            for g in range(groups):
                piece_ref[0, g * sub : (g + 1) * sub, :] = out_ref[:, g * wide : (g + 1) * wide]


def arrange(units, ug, down, attention):
    n_dp, slots = units.shape
    rows, wide = ug.shape[1:]
    sub, width = down.shape[1:]
    ff_blocks = down.shape[0]
    specs = [
        pl.BlockSpec(
            (1, rows, wide), lambda k, u: (jnp.clip(u[k] - 4, 0, 2 * ff_blocks - 1), 0, 0)
        ),
        pl.BlockSpec(
            (1, sub, width),
            lambda k, u: (jnp.clip(u[k] - 4 - 2 * ff_blocks, 0, ff_blocks - 1), 0, 0),
        ),
    ]
    if attention:
        specs.append(pl.BlockSpec(attention[0].shape, lambda k, u: (0, 0, 0)))
        specs.append(pl.BlockSpec(attention[1].shape, lambda k, u: (0, 0)))
    return pl.pallas_call(
        functools.partial(arrange_kernel, ff_blocks),
        out_shape=jax.ShapeDtypeStruct((n_dp * slots, rows, wide), bf),
        grid_spec=pltpu.PrefetchScalarGridSpec(
            num_scalar_prefetch=1,
            grid=(n_dp * slots,),
            in_specs=specs,
            out_specs=pl.BlockSpec((1, rows, wide), lambda k, u: (k, 0, 0)),
        ),
        compiler_params=pltpu.CompilerParams(vmem_limit_bytes=16 << 20),
        cost_estimate=takes(7),
        name="arrange",
    )(units.reshape(-1), ug, down, *attention).reshape(n_dp, slots, rows, wide)


def column_sums(refs, takens, sents, cames, send_sem, recv_sem, pass_sem, take_sem, between):
    n_seq, n_dp, seq_index, dp_index = places()
    core = lax.rem(seq_index, 2)
    sibling = (dp_index, seq_index + 1 - 2 * core)
    views = range(len(refs))

    def onward(view, block):
        return send(
            refs[view].at[1 - core, block],
            takens[view].at[block],
            pass_sem.at[view, block],
            take_sem.at[view, block],
            sibling,
        )

    for block in [b for k in range(n_dp // 2) for b in (n_dp - 1 - k, k)]:
        for view in views:
            onward(view, block).start()

    def ready(block):
        for view in views:
            onward(view, block).wait_recv()

    def own(view):
        return lambda block: refs[view][core, block].astype(f32) + takens[view][block].astype(f32)

    totals = relay_sum(
        [own(view) for view in views],
        sents,
        cames,
        dp_index,
        n_dp,
        lambda place: (place, seq_index),
        send_sem,
        recv_sem,
        ready,
        between,
    )
    for block in range(n_dp):
        for view in views:
            onward(view, block).wait_send()
    return totals


def ff_kernel(
    x_hbm, up_hbm, gate_hbm, down_hbm, cot_ref, ff_out, grad_out, down_grad, up_grad, gate_grad,
    x_ref, up_ref, gate_ref, down_ref, cot_all, hidden, up_low, gate_low, up_factor, gate_factor, stage, narrow, grad_stage,
    load_sem, grad_sem, stage_sem, narrow_sem, own_sem, send_sem, recv_sem, pass_sem, take_sem
):
    n_seq, n_dp, seq_index, dp_index = places()
    core = lax.rem(seq_index, 2)
    sibling = (dp_index, seq_index + 1 - 2 * core)
    loads = [
        pltpu.make_async_copy(src, dst, load_sem.at[k])
        for k, (src, dst) in enumerate(
            ((x_hbm, x_ref), (up_hbm, up_ref), (gate_hbm, gate_ref), (down_hbm, down_ref))
        )
    ]
    for load in loads:
        load.start()
    greet([(lax.rem(dp_index + k, n_dp), seq_index) for k in range(1, n_dp)] + [sibling])
    own = pltpu.make_async_copy(cot_ref, cot_all.at[core, dp_index], own_sem)
    own.start()
    own.wait()

    def onward(block):
        ref = cot_all.at[core, block]
        return send(ref, ref, pass_sem.at[block], take_sem.at[block], sibling)

    onward(dp_index).start()
    count, width = x_ref.shape
    columns = up_ref.shape[1]
    shard = cot_ref.shape[0]
    block_rows = 2 * shard
    blocks = count // block_rows

    def rows_of(b):
        return pl.ds(pl.multiple_of(b * block_rows, block_rows), block_rows)

    def times(left, right, left_axis, right_axis):
        return lax.dot_general(
            left, right, (((left_axis,), (right_axis,)), ((), ())), preferred_element_type=f32
        )

    def put(index, buffer, sem, value, dst):
        slot = lax.rem(index, 2)

        def copy(to):
            return pltpu.make_async_copy(buffer.at[slot], to, sem.at[slot])

        @pl.when(index >= 2)
        def _():
            copy(dst).wait()

        buffer[slot] = value
        copy(dst).start()

    def drain(buffer, sem, dst):
        for slot in range(2):
            pltpu.make_async_copy(buffer.at[slot], dst, sem.at[slot]).wait()

    def ahead(b, carry):
        at = rows_of(b)
        up = times(x_ref[at, :], up_ref[...], 1, 0)
        gate = times(x_ref[at, :], gate_ref[...], 1, 0)
        sig = jax.nn.sigmoid(gate)
        silu = gate * sig
        hidden[at, :] = (silu * up).astype(bf)
        up_factor[at, :] = silu
        gate_factor[at, :] = up * (sig + silu * (1.0 - sig))
        return carry

    def across(b, carry):
        at = rows_of(b)
        put(b, stage, stage_sem, times(hidden[at, :], down_ref[...], 1, 0).astype(bf), ff_out.at[at, :])
        return carry

    def back(place):
        ref = cot_all.at[1 - core, place]
        send(ref, ref, pass_sem.at[place], take_sem.at[place], sibling).wait_recv()
        lines = [
            pl.ds(pl.multiple_of((c * n_dp + place) * shard, shard), shard) for c in range(2)
        ]

        def both(source):
            return jnp.concatenate([source[line, :] for line in lines], axis=0)

        cot = jnp.concatenate([cot_all[c, place] for c in range(2)], axis=0)
        hidden_grad = times(cot, down_ref[...], 1, 1)
        up_part = (hidden_grad * both(up_factor)).astype(bf)
        gate_part = (hidden_grad * both(gate_factor)).astype(bf)
        value = times(up_part, up_ref[...], 1, 1) + times(gate_part, gate_ref[...], 1, 1)
        value = value.astype(bf)
        copies = []
        for c, line in enumerate(lines):
            up_low[line, :] = up_part[c * shard : (c + 1) * shard]
            gate_low[line, :] = gate_part[c * shard : (c + 1) * shard]
            grad_stage[c] = value[c * shard : (c + 1) * shard]
            copies.append(
                pltpu.make_async_copy(grad_stage.at[c], grad_out.at[line, :], grad_sem.at[c])
            )
            copies[c].start()
        for copy in copies:
            copy.wait()

    def back_at(distance):
        for place in (dp_index - distance, dp_index + distance):

            @pl.when((place >= 0) & (place < n_dp))
            def _():
                back(place)

    def work(step):
        if step == 1:
            for load in loads[:3]:
                load.wait()
            lax.fori_loop(0, blocks, ahead, 0)
            loads[3].wait()
        if step == 2 or n_dp == 2:
            back(dp_index)
        if step > 1:
            back_at(step - 1)
        if step == n_dp - 1:
            lax.fori_loop(0, blocks, across, 0)

    relay_gather(
        [lambda block: cot_all.at[core, block]],
        dp_index,
        n_dp,
        lambda place: (place, seq_index),
        send_sem,
        recv_sem,
        lambda block: onward(block).start(),
        during=work,
    )
    back_at(n_dp - 1)
    for block in range(n_dp):
        onward(block).wait_send()
    down_rows = min(256, columns)
    down_blocks = columns // down_rows
    cot_rows = cot_all[...].reshape(count, width)
    for b in range(down_blocks):
        at = slice(b * down_rows, (b + 1) * down_rows)
        value = times(hidden[:, at], cot_rows, 0, 0).astype(bf)
        put(b + blocks, stage.at[:, pl.ds(0, down_rows)], stage_sem, value, down_grad.at[at, :])
    side_blocks = width // 256
    for k, (low, out) in enumerate(((up_low, up_grad), (gate_low, gate_grad))):
        for b in range(side_blocks):
            at = slice(b * 256, (b + 1) * 256)
            value = times(x_ref[:, at], low[...], 0, 0).astype(bf)
            put(k * side_blocks + b, narrow, narrow_sem, value, out.at[at, :])
    drain(stage.at[:, pl.ds(0, down_rows)], stage_sem, down_grad.at[pl.ds(0, down_rows), :])
    drain(narrow, narrow_sem, gate_grad.at[pl.ds(0, 256), :])


def feed_forward(x, up, gate, down, cot, collective_id):
    n_dp = lax.axis_size("dp")
    count, width = x.shape
    columns = up.shape[1]
    shard = cot.shape[0]
    vmem = pltpu.VMEM
    low = lambda *shape: jax.ShapeDtypeStruct(shape, bf)
    return pl.pallas_call(
        ff_kernel,
        out_shape=[
            low(count, width),
            low(count, width),
            low(columns, width),
            low(width, columns),
            low(width, columns),
        ],
        in_specs=[ANY] * 4 + [VMEM],
        out_specs=[ANY] * 5,
        scratch_shapes=[
            vmem((count, width), bf),
            vmem((width, columns), bf),
            vmem((width, columns), bf),
            vmem((columns, width), bf),
            vmem((2, n_dp, shard, width), bf),
            vmem((count, columns), bf),
            vmem((count, columns), bf),
            vmem((count, columns), bf),
            vmem((count, columns), f32),
            vmem((count, columns), f32),
            vmem((2, 2 * shard, width), bf),
            vmem((2, 256, columns), bf),
            vmem((2, shard, width), bf),
            DMA((4,)),
            DMA((2,)),
            DMA((2,)),
            DMA((2,)),
            DMA,
            DMA((1, 2, n_dp)),
            DMA((1, 2, n_dp)),
            DMA((n_dp,)),
            DMA((n_dp,)),
        ],
        compiler_params=comm_params(collective_id, 58),
        cost_estimate=takes(60),
        name="feed_forward",
    )(x, up, gate, down, cot)


class BandSum:
    def __init__(self, band, owns, outs, scratch, chips, chip, core, dp_index, n_dp):
        self.begin, self.size = band
        self.owns, self.outs = owns, outs
        self.half_came, self.full_sent, self.full_came = scratch[0:3], scratch[3:6], scratch[6:9]
        self.mine, self.side_out = scratch[9:12], scratch[12]
        ring_send, ring_recv, self.side_send, self.side_recv, self.own_sem = scratch[13:]
        self.ring = Ring(chips, chip, core, dp_index, ring_send, ring_recv)
        self.chip, self.core, self.n_dp = chip, core, n_dp
        self.sibling = (dp_index, chip * 2 + 1 - core)
        self.blocks = outs[1].shape[0]
        self.pair = self.blocks // 2
        self.half = outs[0].shape[2] // 2

    def own(self, view, place, way):
        rows = pl.ds(self.begin, self.size)
        if view == 0:
            units = pl.ds(0, self.blocks) if way is None else pl.ds(way * self.pair, self.pair)
            return self.owns[0].at[units, place, rows, :]
        columns = pl.ds(0, self.blocks * self.half)
        if way is not None:
            columns = pl.ds(way * self.pair * self.half, self.pair * self.half)
        return self.owns[view].at[place, :, :, rows, columns]

    def leg(self, view, way, step):
        ring = self.ring
        if step == 0:
            src = self.own(view, ring.at(ring.last), way)
            return ring.leg(view, way, step, src, self.half_came[view].at[way])
        src = self.full_sent[view].at[step - 1, way]
        return ring.leg(view, way, step, src, self.full_came[view].at[step - 1, way])

    def own_copy(self, view, way, step):
        distance = self.ring.last - step
        if distance == 0:
            return pltpu.make_async_copy(
                self.own(view, self.chip, None), self.mine[view], self.own_sem.at[view, 0, step - 1]
            )
        src = self.own(view, self.ring.at(distance if way == 0 else -distance), None)
        return pltpu.make_async_copy(
            src, self.full_sent[view].at[step - 1, way], self.own_sem.at[view, way, step - 1]
        )

    def start(self):
        for view in range(3):
            for way in range(2):
                self.leg(view, way, 0).start()
        for step in range(1, self.ring.last + 1):
            for view in range(3):
                for way in range(2 if step < self.ring.last else 1):
                    self.own_copy(view, way, step).start()

    def steps(self):
        pair, half = self.pair, self.half
        for step in range(1, self.ring.last):
            for view in range(3):
                for way in range(2):
                    self.own_copy(view, way, step).wait()
                    self.leg(view, way, step - 1).wait_recv()
                    full = self.full_sent[view]
                    if step > 1:
                        value = full[step - 1, way].astype(f32)
                        value = value + self.full_came[view][step - 2, way].astype(f32)
                        full[step - 1, way] = value.astype(bf)
                    elif view == 0:
                        units = slice(way * pair, (way + 1) * pair)
                        value = full[0, way, units].astype(f32)
                        value = value + self.half_came[0][way].astype(f32)
                        full[0, way, units] = value.astype(bf)
                    else:
                        columns = slice(way * pair * half, (way + 1) * pair * half)
                        value = full[0, way, :, :, :, columns].astype(f32)
                        value = value + self.half_came[view][way].astype(f32)
                        full[0, way, :, :, :, columns] = value.astype(bf)
                    self.leg(view, way, step).start()

    def finish(self):
        ug_out, down_out = self.outs
        last, blocks, half = self.ring.last, self.blocks, self.half
        for view in range(3):
            self.own_copy(view, 0, last).wait()
            for way in range(2):
                self.leg(view, way, last - 1).wait_recv()
            if last > 1:
                came = [self.full_came[view][last - 2, way].astype(f32) for way in range(2)]
                value = self.mine[view][...].astype(f32) + came[0] + came[1]
            else:
                came = [self.half_came[view][way].astype(f32) for way in range(2)]
                other = jnp.concatenate(came, axis=0 if view == 0 else 3)
                value = self.mine[view][...].astype(f32) + other
            value = value.astype(bf)
            if view == 0:
                down_out[...] = value
                continue
            value = value.reshape(2, self.n_dp * self.size, blocks * half)
            for k in range(blocks):
                unit = (view - 1) * blocks + k

                @pl.when(self.core == 0)
                def _():
                    ug_out[unit, :, :half] = value[0, :, k * half : (k + 1) * half]
                    self.side_out[unit] = value[1, :, k * half : (k + 1) * half]

                @pl.when(self.core != 0)
                def _():
                    ug_out[unit, :, half:] = value[1, :, k * half : (k + 1) * half]
                    self.side_out[unit] = value[0, :, k * half : (k + 1) * half]

        place = pl.ds(pl.multiple_of(self.core * half, half), half)
        side = send(
            self.side_out, ug_out.at[:, :, place], self.side_send, self.side_recv, self.sibling
        )
        side.start()
        side.wait()

    def close(self):
        for step in range(self.ring.last):
            for view in range(3):
                for way in range(2):
                    self.leg(view, way, step).wait_send()


def grads_kernel(bands, late_slots, *refs):
    n_seq, n_dp, seq_index, dp_index = places()
    chips, chip, core = n_seq // 2, seq_index // 2, lax.rem(seq_index, 2)
    sibling = (dp_index, chip * 2 + 1 - core)
    refs = list(refs)

    def take(count):
        taken, refs[:count] = refs[:count], []
        return taken

    info, residual_ref, cot_ref = take(3)
    owns, x_refs = take(3), take(2)
    outs = [take(2) for _ in bands]
    grad_out, ff_out, tokens_out = take(3)
    late_out = take(1)[0] if late_slots else None
    next_out = take(len(bands) - 1) if late_slots else []
    scratch = [take(18) for _ in bands]
    takens, sents, cames = take(2), take(2), take(2)
    z_send, z_recv, x_pass, x_take = take(4)
    stage, token_own, token_send, token_recv, token_pass, token_take = take(6)
    greet(
        [(lax.rem(dp_index + k, n_dp), seq_index) for k in range(1, n_dp)]
        + [(dp_index, lax.rem(chip + k, chips) * 2 + core) for k in range(1, chips)]
        + [sibling]
    )
    sums = [
        BandSum(band, owns, out, memory, chips, chip, core, dp_index, n_dp)
        for band, out, memory in zip(bands, outs, scratch)
    ]
    sums[0].start()

    def between(step):
        if step == 0:
            sums[0].steps()
            for later in sums[1:]:
                later.start()

    norm_two_grad, ff_sum = column_sums(
        x_refs, takens, sents, cames, z_send, z_recv, x_pass, x_take, between
    )
    ff_out[...] = ff_sum
    residual = residual_ref[...]
    center = residual - jnp.mean(residual, axis=-1, keepdims=True)
    variance = jnp.mean(center * center, axis=-1, keepdims=True)
    scale_inv = lax.rsqrt(variance + norm_eps)
    grad = norm_back(center * scale_inv, scale_inv, norm_two_grad) + cot_ref[...].astype(f32)
    grad_out[...] = grad
    stage[...] = grad.astype(bf)
    own_tokens = pltpu.make_async_copy(stage, tokens_out.at[seq_index], token_own)
    own_tokens.start()
    pass_on, finish_tokens = spread_blocks(
        stage, tokens_out, chips, chip, core, dp_index, sibling,
        token_send, token_recv, token_pass, token_take,
    )
    for later in sums[1:]:
        later.steps()
    sums[0].finish()
    def fill(pair, target_ref):
        ug_ref, down_ref = pair
        blocks, size, width = down_ref.shape
        wide = ug_ref.shape[2]
        for k in range(n_dp * late_slots):
            unit = info[k]
            is_down = unit >= 4 + 2 * blocks
            for g in range(n_dp):
                rows = slice(g * size, (g + 1) * size)
                value = ug_ref[jnp.clip(unit - 4, 0, 2 * blocks - 1), rows, :]
                other = down_ref[
                    jnp.clip(unit - 4 - 2 * blocks, 0, blocks - 1), :, g * wide : (g + 1) * wide
                ]
                use_other = jnp.full(value.shape, is_down.astype(jnp.int32), jnp.int32) != 0
                target_ref[k // late_slots, k % late_slots, rows, :] = jnp.where(
                    use_other, other, value
                )

    along = []
    if late_slots:
        late_stage, late_send, late_recv, late_own = take(4)
        fill(outs[0], late_stage)
        for k in range(1, n_dp):
            target = lax.rem(dp_index + k, n_dp)
            along.append(
                send(
                    late_stage.at[target],
                    late_out.at[dp_index],
                    late_send.at[k],
                    late_recv.at[k],
                    (target, seq_index),
                )
            )
        along.append(
            pltpu.make_async_copy(late_stage.at[dp_index], late_out.at[dp_index], late_own)
        )
        for copy in along:
            copy.start()
    pass_on()
    for k, later in enumerate(sums[1:]):
        later.finish()
        if late_slots:
            fill(outs[k + 1], next_out[k])
    for band in sums:
        band.close()
    own_tokens.wait()
    finish_tokens()
    for copy in along:
        copy.wait()


def sum_grads(bands, late_units, residual, cot, sums, xs, collective_id):
    _, n_dp, shard, width = xs[0].shape
    chips = lax.axis_size("seq") // 2
    steps = chips // 2
    vmem = pltpu.VMEM
    blocks = sums[0].shape[0]
    wide = sums[1].shape[-1]
    half = wide // blocks
    late_slots = late_units.shape[1]
    out_shape, out_specs, scratch = [], [], []
    for _, size in bands:
        out_shape += [
            jax.ShapeDtypeStruct((2 * blocks, n_dp * size, 2 * half), bf),
            jax.ShapeDtypeStruct((blocks, size, width), bf),
        ]
        out_specs += [VMEM] * 2
        side = (2, n_dp, size)
        fulls = [(blocks, size, width), side + (wide,), side + (wide,)]
        halves = [(blocks // 2, size, width), side + (wide // 2,), side + (wide // 2,)]
        scratch += [vmem((2,) + s, bf) for s in halves]
        scratch += [vmem((max(steps - 1, 1), 2) + s, bf) for s in fulls] * 2
        scratch += [vmem(s, bf) for s in fulls]
        scratch += [
            vmem((2 * blocks, n_dp * size, half), bf),
            DMA((3, 2, steps)),
            DMA((3, 2, steps)),
            DMA,
            DMA,
            DMA((3, 2, steps)),
        ]
    out_shape += [jax.ShapeDtypeStruct((shard, width), f32)] * 2
    out_shape.append(jax.ShapeDtypeStruct((2 * chips, shard, width), bf))
    out_specs += [VMEM, VMEM, ANY]
    scratch += [vmem((n_dp, shard, width), bf)] * 4
    scratch += [vmem((n_dp + 1, shard, width), bf)] * 2
    scratch += [DMA((2, 2, n_dp))] * 2 + [DMA((2, n_dp))] * 2
    scratch += [vmem((shard, width), bf), DMA] + [DMA((chips,))] * 4
    if late_slots:
        piece = (n_dp, late_slots, n_dp * bands[0][1], 2 * half)
        out_shape.append(jax.ShapeDtypeStruct(piece, bf))
        out_specs.append(ANY)
        out_shape += [jax.ShapeDtypeStruct(piece, bf)] * (len(bands) - 1)
        out_specs += [VMEM] * (len(bands) - 1)
        scratch += [vmem(piece, bf), DMA((n_dp,)), DMA((n_dp,)), DMA]
    return pl.pallas_call(
        functools.partial(grads_kernel, bands, late_slots),
        out_shape=out_shape,
        in_specs=[pl.BlockSpec(memory_space=pltpu.SMEM), VMEM, VMEM] + [ANY] * 3 + [VMEM] * 2,
        out_specs=out_specs,
        scratch_shapes=scratch,
        compiler_params=comm_params(collective_id, 60),
        cost_estimate=takes(130),
        name="sum_grads",
    )(late_units.reshape(-1) if late_slots else jnp.zeros((1,), jnp.int32), residual, cot, *sums, *xs)


def attention_back_kernel(
    grad_ref, weight_ref, query_ref, key_ref, value_ref, mixed_ref, stat_ref, cos_ref, sin_ref, doc_row, doc_col, x_ref,
    qkv_out, qkv_weight_out, out_weight_out, mixed_grad, key_sum, value_sum
):
    seq_len, width = grad_ref.shape
    head_cols = query_ref.shape[1]
    heads = head_cols // HD
    block_rows = min(256, seq_len)
    scale = float(HD) ** (-0.5)

    def rows_of(b):
        return pl.ds(pl.multiple_of(b * block_rows, block_rows), block_rows)

    def times(left, right, left_axis, right_axis):
        return lax.dot_general(
            left, right, (((left_axis,), (right_axis,)), ((), ())), preferred_element_type=f32
        )

    def mix(b, carry):
        at = rows_of(b)
        mixed_grad[at, :] = times(grad_ref[at, :], weight_ref[...], 1, 1).astype(bf)
        return carry

    lax.fori_loop(0, seq_len // block_rows, mix, 0)
    key_sum[...] = jnp.zeros_like(key_sum)
    value_sum[...] = jnp.zeros_like(value_sum)

    def turned(grads, cosine, sine):
        scaled = grads * sine
        half = HD // 2
        other = jnp.concatenate([scaled[:, half:], -scaled[:, :half]], axis=-1)
        return grads * cosine + other

    def attend(b, carry):
        at = rows_of(b)
        begin = b * block_rows
        query_pos = begin + lax.broadcasted_iota(jnp.int32, (block_rows, seq_len), 0)
        key_pos = lax.broadcasted_iota(jnp.int32, (block_rows, seq_len), 1)
        allowed = (doc_col[at, :] == doc_row[...]) & (key_pos <= query_pos)
        for h in range(heads):
            place = slice(h * HD, (h + 1) * HD)
            query, part = query_ref[at, place], mixed_grad[at, place]
            scores = jnp.where(allowed, times(query, key_ref[:, place], 1, 1) * scale, masked_score)
            prob = jnp.exp(scores - stat_ref[at, h * HD : h * HD + 1])
            prob_grad = times(part, value_ref[:, place], 1, 1)
            inner = jnp.sum(prob * prob_grad, axis=-1, keepdims=True)
            score_grad = (prob * (prob_grad - inner) * scale).astype(bf)
            value_sum[:, place] += times(prob.astype(bf), part, 0, 0)
            key_sum[:, place] += times(score_grad, query, 0, 0)
            query_grad = times(score_grad, key_ref[:, place], 1, 0)
            qkv_out[at, place] = turned(query_grad, cos_ref[at, :], sin_ref[at, :]).astype(bf)
        return carry

    lax.fori_loop(0, seq_len // block_rows, attend, 0)

    def finish(b, carry):
        at = rows_of(b)
        for h in range(heads):
            place = slice(h * HD, (h + 1) * HD)
            grads = turned(key_sum[at, place], cos_ref[at, :], sin_ref[at, :])
            qkv_out[at, head_cols + h * HD : head_cols + (h + 1) * HD] = grads.astype(bf)
        qkv_out[at, 2 * head_cols :] = value_sum[at, :].astype(bf)
        return carry

    lax.fori_loop(0, seq_len // block_rows, finish, 0)
    columns = min(512, width)
    for c in range(width // columns):
        at = slice(c * columns, (c + 1) * columns)
        qkv_weight_out[at, :] = times(x_ref[:, at], qkv_out[...], 0, 0).astype(bf)
        out_weight_out[:, at] = times(mixed_ref[...], grad_ref[:, at], 0, 0).astype(bf)


def attention_back(grad, weight, query, key, value, mixed, stat, cosine, sine, doc, x):
    seq_len, width = grad.shape
    head_cols = query.shape[1]
    return pl.pallas_call(
        attention_back_kernel,
        out_shape=[
            jax.ShapeDtypeStruct((seq_len, 3 * head_cols), bf),
            jax.ShapeDtypeStruct((width, 3 * head_cols), bf),
            jax.ShapeDtypeStruct((head_cols, width), bf),
        ],
        in_specs=[VMEM] * 12,
        out_specs=[VMEM] * 3,
        scratch_shapes=[
            pltpu.VMEM((seq_len, head_cols), bf),
            pltpu.VMEM((seq_len, head_cols), f32),
            pltpu.VMEM((seq_len, head_cols), f32),
        ],
        compiler_params=pltpu.CompilerParams(vmem_limit_bytes=50 << 20),
        cost_estimate=takes(35),
        name="attention_back",
    )(grad, weight, query, key, value, mixed, stat, cosine, sine, doc[None, :], doc[:, None], x)


def turn_half(values):
    half = values.shape[-1] // 2
    return jnp.concatenate([-values[:, half:], values[:, :half]], axis=-1)


def forward_kernel(has_late, first_slots, ff_blocks, *refs):
    info, first_ref = refs[:2]
    refs = refs[2:]
    if has_late:
        late_ref, refs = refs[0], refs[1:]
    x1_ref, cos_ref, sin_ref, doc_row, doc_col, tokens_ref = refs[:6]
    refs = (None,) + refs
    qkv_all, out_all, query_out, key_out, value_out, mixed_out, stat_out, residual_out = refs[7:15]
    up_all, gate_all, down_all, x_all = refs[15:19]
    ug_all = (up_all, gate_all)
    att_stage, out_stage, part, taken, sent, arrived, x_stage = refs[19:26]
    mine_stage, given_stage, down_stage = refs[26:29]
    (own_sem, a_send, a_recv, w_send, w_recv, s_pass, s_take, s_send, s_recv,
     late_send, late_recv, late_own, stage_own, side_send, side_recv, ring_send, ring_recv,
     send_sem, recv_sem, pass_sem, take_sem) = refs[29:50]
    late_tables = refs[50:]
    n_seq, n_dp, seq_index, dp_index = places()
    chips, chip, core = n_seq // 2, seq_index // 2, lax.rem(seq_index, 2)
    sibling = (dp_index, chip * 2 + 1 - core)
    seq_peers = [lax.rem(seq_index + k, n_seq) for k in range(n_seq)]
    dp_peers = [lax.rem(dp_index + k, n_dp) for k in range(n_dp)]
    rows, wide = first_ref.shape[1:]
    sub = rows // n_dp
    half = wide // 2
    step_cols = att_stage.shape[2] // 3
    share = wide // step_cols
    tokens, width = tokens_ref.shape
    greet([(dp_index, p) for p in seq_peers[1:]] + [(p, seq_index) for p in dp_peers[1:]])

    def band(c):
        return pl.ds(c * sub, sub)

    def late_copies(c):
        copies = []
        for k in range(1, n_dp):
            copies.append(
                send(
                    late_ref.at[dp_peers[k], :, band(c)],
                    late_tables[c].at[dp_index],
                    late_send.at[c, k],
                    late_recv.at[c, k],
                    (dp_peers[k], seq_index),
                )
            )
        return copies

    def late_own_copy(c):
        return pltpu.make_async_copy(
            late_ref.at[dp_index, :, band(c)], late_tables[c].at[dp_index], late_own.at[c]
        )

    def late_start(c):
        if not has_late or c >= n_dp:
            return
        if c:
            for copy in late_copies(c - 1):
                copy.wait_send()
        for copy in late_copies(c):
            copy.start()
        late_own_copy(c).start()

    late_start(0)

    for u in range(3):
        for block in range(n_seq):
            g, h = block // share, block % share
            att_stage[block, :, u * step_cols : (u + 1) * step_cols] = first_ref[
                info[u], g * sub : (g + 1) * sub, h * step_cols : (h + 1) * step_cols
            ]
    for g in range(n_dp):
        out_stage[:, g * wide : (g + 1) * wide] = first_ref[info[3], g * sub : (g + 1) * sub, :]
    own = [
        pltpu.make_async_copy(att_stage.at[seq_index], qkv_all.at[seq_index, dp_index], own_sem.at[0]),
        pltpu.make_async_copy(out_stage, out_all.at[dp_index], own_sem.at[1]),
    ]
    across = []
    for k in range(1, n_seq):
        copy = send(
            att_stage.at[seq_peers[k]],
            qkv_all.at[seq_index, dp_index],
            a_send.at[k],
            a_recv.at[k],
            (dp_index, seq_peers[k]),
        )
        copy.start()
        across.append(copy)
    for copy in own:
        copy.start()
    for copy in own:
        copy.wait()
    for copy in across:
        copy.wait_recv()
    relay_gather(
        [lambda block: qkv_all.at[:, block], lambda block: out_all.at[block]],
        dp_index,
        n_dp,
        lambda place: (place, seq_index),
        w_send,
        w_recv,
        lambda block: None,
    )

    ring = Ring(chips, chip, core, dp_index, None, None)
    pair = ff_blocks // 2

    def ring_leg(c, view, way, step, arriving):
        distance = step if arriving else step - 1
        block = ring.at(-distance if way == 0 else distance)
        units = pl.ds(way * pair, pair) if step == ring.last else pl.ds(0, ff_blocks)
        if view == 0:
            ref = down_all.at[units, block, :, pl.ds(c * wide, wide)]
        else:
            columns = pl.ds(0, ff_blocks * half)
            if step == ring.last:
                columns = pl.ds(way * pair * half, pair * half)
            ref = ug_all[view - 1].at[block, :, band(c), columns]
        return send(
            ref, ref, ring_send.at[c, view, way, step - 1], ring_recv.at[c, view, way, step - 1],
            ring.device(way),
        )

    def side_copies(c):
        return [
            send(
                given_stage.at[c, k],
                ug_all[k].at[chip, core, band(c)],
                side_send.at[c, k],
                side_recv.at[c, k],
                sibling,
            )
            for k in range(2)
        ]

    def begin_band(c):
        if has_late:
            for copy in late_copies(c):
                copy.wait_recv()
            late_own_copy(c).wait()
            if c:
                late_start(c + 1)
            table = late_tables[c]
            late_slots = table.shape[1]
        for u in range(3 * ff_blocks):
            value = first_ref[info[4 + u], band(c), :]
            if has_late:
                code = info[4 + 3 * ff_blocks + u]
                other = table[code // late_slots, lax.rem(code, late_slots)]
                use_late = jnp.full(value.shape, info[4 + 6 * ff_blocks + u], jnp.int32) != 0
                value = jnp.where(use_late, other, value)
            if u < 2 * ff_blocks:
                left, right = value[:, :half], value[:, half:]
                k, j = u // ff_blocks, u % ff_blocks
                columns = slice(j * half, (j + 1) * half)

                @pl.when(core == 0)
                def _():
                    mine_stage[c, k, :, columns] = left
                    given_stage[c, k, :, columns] = right

                @pl.when(core != 0)
                def _():
                    mine_stage[c, k, :, columns] = right
                    given_stage[c, k, :, columns] = left
            else:
                down_stage[c, u - 2 * ff_blocks] = value
        for copy in side_copies(c):
            copy.start()
        local = [
            pltpu.make_async_copy(
                mine_stage.at[c, k], ug_all[k].at[chip, core, band(c)], stage_own.at[c, k]
            )
            for k in range(2)
        ]
        local.append(
            pltpu.make_async_copy(
                down_stage.at[c], down_all.at[:, chip, :, pl.ds(c * wide, wide)], stage_own.at[c, 2]
            )
        )
        for copy in local:
            copy.start()
        for copy in local:
            copy.wait()
        for copy in side_copies(c):
            copy.wait_recv()
        for view in range(3):
            for way in range(2):
                ring_leg(c, view, way, 1, False).start()

    def carry_band(c, step):
        for view in range(3):
            for way in range(2):
                ring_leg(c, view, way, step - 1, True).wait_recv()
                ring_leg(c, view, way, step, False).start()

    late_start(1)
    begin_band(0)

    seq_len = x1_ref.shape[0]
    heads = query_out.shape[1] // HD
    block_rows = min(256, seq_len)
    head_cols = heads * HD
    qkv_weight = qkv_all[...].reshape(width, 3 * head_cols)

    def project(b, carry):
        at = pl.ds(pl.multiple_of(b * block_rows, block_rows), block_rows)
        result = jnp.dot(x1_ref[at, :], qkv_weight, preferred_element_type=f32)
        cosine, sine = cos_ref[at, :], sin_ref[at, :]
        for h in range(heads):
            place = slice(h * HD, (h + 1) * HD)
            for part_id, out in ((0, query_out), (1, key_out)):
                begin = part_id * head_cols + h * HD
                values = result[:, begin : begin + HD]
                out[at, place] = (values * cosine + turn_half(values) * sine).astype(bf)
        value_out[at, :] = result[:, 2 * head_cols :].astype(bf)
        return carry

    lax.fori_loop(0, seq_len // block_rows, project, 0)

    def attend(b, carry):
        begin = pl.multiple_of(b * block_rows, block_rows)
        at = pl.ds(begin, block_rows)
        query_pos = begin + lax.broadcasted_iota(jnp.int32, (block_rows, seq_len), 0)
        key_pos = lax.broadcasted_iota(jnp.int32, (block_rows, seq_len), 1)
        allowed = (doc_col[at, :] == doc_row[...]) & (key_pos <= query_pos)
        for h in range(heads):
            place = slice(h * HD, (h + 1) * HD)
            scores = lax.dot_general(
                query_out[at, place],
                key_out[:, place],
                (((1,), (1,)), ((), ())),
                preferred_element_type=f32,
            )
            scores = jnp.where(allowed, scores * (float(HD) ** (-0.5)), masked_score)
            peak = jnp.max(scores, axis=-1, keepdims=True)
            raised = jnp.exp(scores - peak)
            total = jnp.sum(raised, axis=-1, keepdims=True)
            prob = (raised * (1.0 / total)).astype(bf)
            mixed = jnp.dot(prob, value_out[:, place], preferred_element_type=f32)
            mixed_out[at, place] = mixed.astype(bf)
            stat_out[at, place] = jnp.broadcast_to(peak + jnp.log(total), (block_rows, HD))
        return carry

    lax.fori_loop(0, seq_len // block_rows, attend, 0)
    out_weight = out_all[...].reshape(rows, width)

    def combine(b, carry):
        at = pl.ds(pl.multiple_of(b * tokens, tokens), tokens)
        part[b] = jnp.dot(mixed_out[at, :], out_weight, preferred_element_type=f32).astype(bf)
        return carry

    lax.fori_loop(0, n_seq, combine, 0)

    chip_peers = [lax.rem(chip + k, chips) for k in range(chips)]
    order = list(range(chips - 1, 0, -1)) + [0]
    passed = {}
    for k in order:
        block = part.at[chip_peers[k] * 2 + 1 - core]
        passed[k] = send(block, taken.at[k], s_pass.at[k], s_take.at[k], sibling)
        passed[k].start()
    copies = {}
    for k in order[:-1]:
        passed[k].wait_recv()
        value = part[chip_peers[k] * 2 + core].astype(f32)
        sent[k] = (value + taken[k].astype(f32)).astype(bf)
        device = (dp_index, chip_peers[k] * 2 + core)
        copies[k] = send(sent.at[k], arrived.at[k], s_send.at[k], s_recv.at[k], device)
        copies[k].start()

    begin_band(1)
    for step in range(2, ring.last + 1):
        carry_band(0, step)
    passed[0].wait_recv()
    total = part[seq_index].astype(f32) + taken[0].astype(f32)
    for k in range(1, chips):
        copies[k].wait_recv()
        total = total + arrived[k].astype(f32)
    residual = tokens_ref[...] + total
    residual_out[...] = residual
    center = residual - jnp.mean(residual, axis=-1, keepdims=True)
    spread = jnp.mean(center * center, axis=-1, keepdims=True)
    x_stage[...] = (center * lax.rsqrt(spread + norm_eps)).astype(bf)
    for c in range(2, n_dp):
        begin_band(c)
        for step in range(2, ring.last + 1):
            carry_band(c - 1, step)

    own_x = pltpu.make_async_copy(x_stage, x_all.at[core, dp_index], own_sem.at[3])
    own_x.start()
    own_x.wait()

    def onward(block):
        ref = x_all.at[core, block]
        return send(ref, ref, pass_sem.at[block], take_sem.at[block], sibling)

    onward(dp_index).start()
    relay_gather(
        [lambda block: x_all.at[core, block]],
        dp_index,
        n_dp,
        lambda place: (place, seq_index),
        send_sem,
        recv_sem,
        lambda block: onward(block).start(),
        lambda step: carry_band(n_dp - 1, 2) if step == 1 and ring.last > 1 else None,
    )
    for step in range(3, ring.last + 1):
        carry_band(n_dp - 1, step)
    for c in range(n_dp):
        for view in range(3):
            for way in range(2):
                ring_leg(c, view, way, ring.last, True).wait_recv()
                for step in range(1, ring.last + 1):
                    ring_leg(c, view, way, step, False).wait_send()
        for copy in side_copies(c):
            copy.wait_send()
        if has_late:
            if c == n_dp - 1:
                for copy in late_copies(c):
                    copy.wait_send()
    for block in range(n_dp):
        onward(block).wait_send()
        ref = x_all.at[1 - core, block]
        send(ref, ref, pass_sem.at[block], take_sem.at[block], sibling).wait_recv()
    for k in order:
        passed[k].wait_send()
    for k in order[:-1]:
        copies[k].wait_send()
    for copy in across:
        copy.wait_send()


def forward(info, first_table, late, x1, cosine, sine, doc, tokens, ff_blocks, first_slots, collective_id):
    n_seq = lax.axis_size("seq")
    n_dp = lax.axis_size("dp")
    chips = n_seq // 2
    rows, wide = first_table.shape[1:]
    sub = rows // n_dp
    half = wide // 2
    seq_len, width = x1.shape
    head_cols = width // n_seq
    shard = tokens.shape[0]
    steps = chips // 2
    vmem = pltpu.VMEM
    low = lambda *shape: jax.ShapeDtypeStruct(shape, bf)
    has_late = late is not None
    blocks = vmem((chips, shard, width), bf)
    return pl.pallas_call(
        functools.partial(forward_kernel, has_late, first_slots, ff_blocks),
        out_shape=[
            low(n_seq, n_dp, sub, 3 * head_cols),
            low(n_dp, sub, width),
            low(seq_len, head_cols),
            low(seq_len, head_cols),
            low(seq_len, head_cols),
            low(seq_len, head_cols),
            jax.ShapeDtypeStruct((seq_len, head_cols), f32),
            jax.ShapeDtypeStruct((shard, width), f32),
            low(chips, 2, rows, ff_blocks * half),
            low(chips, 2, rows, ff_blocks * half),
            low(ff_blocks, chips, sub, width),
            low(2, n_dp, shard, width),
        ],
        in_specs=[pl.BlockSpec(memory_space=pltpu.SMEM), VMEM]
        + [ANY] * has_late
        + [VMEM] * 6,
        out_specs=[VMEM] * 8 + [ANY] * 4,
        scratch_shapes=[
            vmem((n_seq, sub, 3 * head_cols), bf),
            vmem((sub, width), bf),
            vmem((n_seq, shard, width), bf),
            blocks,
            blocks,
            blocks,
            vmem((shard, width), bf),
            vmem((n_dp, 2, sub, ff_blocks * half), bf),
            vmem((n_dp, 2, sub, ff_blocks * half), bf),
            vmem((n_dp, ff_blocks, sub, wide), bf),
            DMA((4,)),
            DMA((n_seq,)),
            DMA((n_seq,)),
            DMA((2, 2, n_dp)),
            DMA((2, 2, n_dp)),
            DMA((chips,)),
            DMA((chips,)),
            DMA((chips,)),
            DMA((chips,)),
            DMA((n_dp, n_dp)),
            DMA((n_dp, n_dp)),
            DMA((n_dp,)),
            DMA((n_dp, 3)),
            DMA((n_dp, 2)),
            DMA((n_dp, 2)),
            DMA((n_dp, 3, 2, steps)),
            DMA((n_dp, 3, 2, steps)),
            DMA((1, 2, n_dp)),
            DMA((1, 2, n_dp)),
            DMA((n_dp,)),
            DMA((n_dp,)),
        ]
        + [vmem((n_dp, late.shape[1], sub, wide), bf) for _ in range(n_dp if has_late else 0)],
        compiler_params=comm_params(collective_id, 58),
        cost_estimate=takes(230),
        name="forward",
    )(
        info,
        first_table,
        *([late] if has_late else []),
        x1,
        cosine,
        sine,
        doc[None, :],
        doc[:, None],
        tokens,
    )


def local(block_input, cotangent, doc_lengths, owners, master, first_moment, second_moment):
    n_seq = lax.axis_size("seq")
    n_dp = lax.axis_size("dp")
    seq_index = lax.axis_index("seq")
    dp_index = lax.axis_index("dp")
    core = seq_index % 2
    _, shard_len, width = block_input.shape
    rows = master.shape[0]
    per_owner = master.shape[1]
    chips = n_seq // 2
    sub = rows // n_dp
    wide = width // n_dp
    half = chips * sub
    head_cols = H // n_seq * HD
    seq_len = shard_len * n_seq
    ff_blocks = FF // D
    first_slots = min(4, per_owner)
    unit_count = owners.shape[0]

    unit_slot = unit_slots(owners, per_owner)
    place = unit_slot - owners * per_owner
    all_slots = jnp.arange(n_dp * per_owner, dtype=jnp.int32)
    match = unit_slot[None, :] == all_slots[:, None]
    slot_unit = jnp.sum(
        jnp.where(match, jnp.arange(unit_count, dtype=jnp.int32)[None, :] + 1, 0), axis=1
    ) - 1
    slot_unit = slot_unit.reshape(n_dp, per_owner)
    own_units = lax.dynamic_index_in_dim(slot_unit, dp_index, 0, keepdims=False)
    is_col = (own_units >= 4) & (own_units < 4 + 2 * ff_blocks)


    tokens = block_input.astype(f32).reshape(shard_len, width)
    packed = pack(master, is_col.astype(jnp.int32), n_dp, n_seq, first_slots)
    first_table, normed_one_all = front(packed[0], block_input.reshape(shard_len, width), 2)
    first_table = first_table.reshape(n_dp * first_slots, rows, wide)
    normed_one_all = normed_one_all.reshape(seq_len, width)
    upstream = cotangent.reshape(shard_len, width)
    positions = jnp.arange(seq_len, dtype=jnp.int32)
    cosine, sine = rope_tables(positions.astype(f32), HD)
    doc_ends = jnp.cumsum(doc_lengths[0])
    doc = jnp.sum((positions[:, None] >= doc_ends[None, :]).astype(jnp.int32), axis=1)
    late_slots = per_owner - first_slots
    info = jnp.concatenate(
        [
            owners * first_slots + jnp.minimum(place, first_slots - 1),
            (owners * late_slots + jnp.maximum(place - first_slots, 0))[4:],
            (place >= first_slots)[4:],
        ]
    ).astype(jnp.int32)
    (
        qkv_weight,
        out_weight,
        queries,
        keys,
        values,
        attended_low,
        log_total,
        residual,
        up_weight,
        gate_weight,
        down_weight,
        normed_two_all,
    ) = forward(
        info,
        first_table,
        packed[1] if late_slots else None,
        normed_one_all,
        cosine,
        sine,
        doc,
        tokens,
        ff_blocks,
        first_slots,
        1,
    )
    qkv_weight = qkv_weight.reshape(width, 3 * head_cols)
    out_weight = out_weight.reshape(rows, width)
    normed_two, inv_two = norm_parts(residual)
    columns = ff_blocks * half
    up_weight = up_weight.reshape(width, columns)
    gate_weight = gate_weight.reshape(width, columns)
    down_weight = down_weight.reshape(columns, width)
    normed_two_all = normed_two_all.reshape(-1, width)
    ff_part, norm_two_part, down_grad, up_grad, gate_grad = feed_forward(
        normed_two_all, up_weight, gate_weight, down_weight, upstream, 7
    )
    side = (chips, 2, n_dp, sub, columns)
    sums = [
        down_grad.reshape(ff_blocks, chips, sub, width),
        up_grad.reshape(side),
        gate_grad.reshape(side),
    ]
    column = (2, n_dp, shard_len, width)
    bands = [(0, sub // 2), (sub // 2, sub // 2)] if sub % 32 == 0 else [(0, sub)]
    back = sum_grads(
        bands,
        slot_unit[:, first_slots:],
        residual,
        upstream,
        sums,
        [norm_two_part.reshape(column), ff_part.reshape(column)],
        5,
    )
    pieces = [back[2 * k : 2 * k + 2] for k in range(len(bands))]
    residual_grad, ff_out, residual_grad_all = back[2 * len(bands) : 2 * len(bands) + 3]
    residual_grad_all = residual_grad_all.reshape(seq_len, width)
    block_output = (residual + ff_out).astype(bf).reshape(block_input.shape)
    late_grads = []
    if late_slots:
        late_grads.append(back[2 * len(bands) + 3])
        for send_now in back[2 * len(bands) + 4 :]:
            send_now, residual_grad_all = lax.optimization_barrier((send_now, residual_grad_all))
            late_grads.append(lax.all_to_all(send_now, "dp", 0, 0))
    qkv_grad_low, qkv_wgrad, out_wgrad = attention_back(
        residual_grad_all,
        out_weight,
        queries,
        keys,
        values,
        attended_low,
        log_total,
        cosine,
        sine,
        doc,
        normed_one_all,
    )
    norm_one_part = jnp.einsum("tf,rf->tr", qkv_grad_low, qkv_weight, preferred_element_type=f32)
    norm_one_grad = sum_seq(norm_one_part.astype(bf).reshape(n_seq, shard_len, width), 3)
    qkv_piece, out_piece = collect_attention(
        qkv_wgrad.reshape(n_seq, n_dp, sub, 3 * head_cols), out_wgrad.reshape(n_dp, sub, width), 6
    )
    kinds = jnp.where(own_units < 0, 2, is_col.astype(jnp.int32)).astype(jnp.int32)
    kept = ()
    came = None
    for k, (begin, size) in enumerate(bands):
        rows_now = slice(begin, begin + size)
        attention = (qkv_piece[:, rows_now], out_piece[rows_now])
        send_now = arrange(slot_unit[:, :first_slots], *pieces[k], attention)
        if came is not None:
            send_now, came, norm_one_grad = lax.optimization_barrier(
                (send_now, came, norm_one_grad)
            )
        elif late_grads:
            send_now, late_grads[-1] = lax.optimization_barrier((send_now, late_grads[-1]))
        came = lax.all_to_all(send_now, "dp", 0, 0)
        kept = adam(
            kinds,
            [came] + late_grads[k : k + 1],
            master,
            first_moment,
            second_moment,
            n_dp,
            n_seq,
            first_slots,
            begin,
            kept,
        )
    owned_grads, new_first, new_second, new_master = kept
    tokens_again, norm_one_grad = lax.optimization_barrier((block_input, norm_one_grad))
    normed_one, inv_one = norm_parts(tokens_again.astype(f32).reshape(shard_len, width))
    input_grad = (residual_grad + norm_back(normed_one, inv_one, norm_one_grad)).reshape(
        block_input.shape
    )
    return (block_output, input_grad, owned_grads, new_first, new_second, new_master)


def solution(mesh):
    placed = (
        P("dp", "seq", None),
        P("dp", "seq", None),
        P("dp", None),
        P(),
        P("seq", "dp", None),
        P("seq", "dp", None),
        P("seq", "dp", None),
    )
    return jax.shard_map(
        local,
        mesh=mesh,
        in_specs=placed,
        out_specs=(
            P("dp", "seq", None),
            P("dp", "seq", None),
            P("seq", "dp", None),
            P("seq", "dp", None),
            P("seq", "dp", None),
            P("seq", "dp", None),
        ),
        check_vma=False,
    )
```

```python
import functools

import jax
import jax.numpy as jnp
import numpy as np
from jax import lax
from jax.experimental import pallas as pl
from jax.experimental.pallas import tpu as pltpu
from jax.sharding import PartitionSpec as P

D = 2048
H = 16
HD = 128
FF = 8192
STEP = 5
bf = jnp.bfloat16
f32 = jnp.float32
MESH = pl.DeviceIdType.MESH


norm_eps = 1e-05
rope_base = 10000.0
beta_one = 0.5
beta_two = 0.5
learn_rate = 0.01
decay_rate = 0.1
adam_eps = 1e-08
masked_score = -1000000000.0


def unit_slots(owners, per_owner):
    unit_count = owners.shape[0]
    unit_order = jnp.arange(unit_count, dtype=jnp.int32)
    matching = owners[:, None] == owners[None, :]
    before = unit_order[None, :] < unit_order[:, None]
    places = jnp.sum(jnp.where(matching & before, 1, 0), axis=1).astype(jnp.int32)
    return owners * per_owner + places


def norm_parts(values):
    center = values - jnp.mean(values, axis=-1, keepdims=True)
    spread = jnp.mean(center * center, axis=-1, keepdims=True)
    scale_inv = lax.rsqrt(spread + norm_eps)
    return (center * scale_inv, scale_inv)


def norm_back(normed, scale_inv, upstream):
    upstream_mean = jnp.mean(upstream, axis=-1, keepdims=True)
    cross_mean = jnp.mean(upstream * normed, axis=-1, keepdims=True)
    return scale_inv * (upstream - upstream_mean - normed * cross_mean)


def rope_tables(seq_len, head_dim):
    half_dim = head_dim // 2
    frequency = rope_base ** (-(np.arange(half_dim) * 2.0) / head_dim)
    angles = np.arange(seq_len)[:, None] * frequency[None, :]
    tables = [np.concatenate([half, half], axis=-1) for half in (np.cos(angles), np.sin(angles))]
    return [jnp.asarray(table.astype(np.float32)) for table in tables]


def pack_kernel(n_dp, chips, first_slots, flags, m_ref, *outs):
    rb, slots, width = m_ref.shape
    rows, wide = outs[0].shape[2:]
    sub = rows // n_dp
    start = pl.program_id(0) * rb
    target = start // sub
    inner = start % sub
    turned = jnp.swapaxes(m_ref[...], 0, 1).astype(bf)
    for s in range(slots):
        out = outs[0] if s < first_slots else outs[1]
        t = s if s < first_slots else s - first_slots
        x = turned[s]

        @pl.when(flags[s] == 1)
        def _():
            for d in range(n_dp):
                pieces = [
                    x[:, (2 * k + c) * rows + d * sub : (2 * k + c) * rows + (d + 1) * sub]
                    for c in range(2)
                    for k in range(chips)
                ]
                out[d, t, pl.ds(pl.multiple_of(start, rb), rb), :] = jnp.concatenate(pieces, axis=1)

        @pl.when(flags[s] == 0)
        def _():
            for g in range(n_dp):
                out[target, t, pl.ds(pl.multiple_of(g * sub + inner, rb), rb), :] = x[
                    :, g * wide : (g + 1) * wide
                ]


def pack(master, flags, n_dp, n_seq, first_slots):
    rows, slots, width = master.shape
    wide = width // n_dp
    rb = min(32, rows // n_dp)
    counts = [first_slots] + ([slots - first_slots] if slots > first_slots else [])
    return pl.pallas_call(
        functools.partial(pack_kernel, n_dp, n_seq // 2, first_slots),
        out_shape=[jax.ShapeDtypeStruct((n_dp, c, rows, wide), bf) for c in counts],
        grid_spec=pltpu.PrefetchScalarGridSpec(
            num_scalar_prefetch=1,
            grid=(rows // rb,),
            in_specs=[pl.BlockSpec((rb, slots, width), lambda i, f: (i, 0, 0))],
            out_specs=[
                pl.BlockSpec((n_dp, c, rows, wide), lambda i, f: (0, 0, 0, 0)) for c in counts
            ],
        ),
        compiler_params=pltpu.CompilerParams(vmem_limit_bytes=50 << 20),
        name="pack",
    )(flags, master)


def adam_kernel(n_dp, chips, first_slots, n_groups, n_kept, kinds, *refs):
    cols = refs[:n_groups]
    rws = refs[n_groups : 2 * n_groups]
    m_ref, f_ref, s_ref, keep_ref = refs[2 * n_groups : 2 * n_groups + 4]
    g_out, f_out, s_out, m_out, held = refs[2 * n_groups + 4 + n_kept :]
    rb, slots, width = m_ref.shape
    wide = width // n_dp
    rows = width // (2 * chips)
    sub = rows // n_dp
    half = chips * sub
    for s in range(slots):
        group = 0 if s < first_slots else 1
        t = s if group == 0 else s - first_slots

        @pl.when(kinds[s] == 1)
        def _():
            pieces = []
            for i in range(2 * chips):
                k, c = i // 2, i % 2
                for d in range(n_dp):
                    begin = c * half + k * sub
                    pieces.append(cols[group][d, t, :, begin : begin + sub])
            held[s] = jnp.concatenate(pieces, axis=1).astype(f32)

        @pl.when(kinds[s] == 0)
        def _():
            for g in range(n_dp):
                held[s, :, g * wide : (g + 1) * wide] = rws[group][0, t, g, :, :].astype(f32)

        @pl.when(kinds[s] == 2)
        def _():
            held[s] = jnp.zeros((rb, width), f32)

    grad = jnp.swapaxes(held[...], 0, 1)
    keep = keep_ref[...] > 0.0
    g_out[...] = grad
    first = jnp.where(keep, beta_one * f_ref[...] + (1.0 - beta_one) * grad, 0.0)
    f_out[...] = first
    second = jnp.where(keep, beta_two * s_ref[...] + (1.0 - beta_two) * grad * grad, 0.0)
    s_out[...] = second
    fixed_first = first * (1.0 / (1.0 - beta_one**STEP))
    fixed_second = second * (1.0 / (1.0 - beta_two**STEP))
    old = m_ref[...]
    root = fixed_second * lax.rsqrt(jnp.maximum(fixed_second, 1e-37))
    step = fixed_first * pl.reciprocal(root + adam_eps, approx=True) + decay_rate * old
    m_out[...] = jnp.where(keep, old - learn_rate * step, 0.0)


def adam(kinds, grads, master, first_moment, second_moment, n_dp, n_seq, first_slots, begin, kept):
    rows, slots, width = master.shape
    wide = width // n_dp
    sub = rows // n_dp
    size = grads[0].shape[2] // n_dp
    rb = min(16, size)
    steps = size // rb
    state = pl.BlockSpec(
        (rb, slots, width), lambda d, i, k: (d * (sub // rb) + begin // rb + i, 0, 0)
    )
    cols = [
        pl.BlockSpec((n_dp, g.shape[1], rb, wide), lambda d, i, k: (0, 0, d * steps + i, 0))
        for g in grads
    ]
    rws = [
        pl.BlockSpec((1, g.shape[1], n_dp, rb, wide), lambda d, i, k: (d, 0, 0, i, 0)) for g in grads
    ]
    keep = jnp.broadcast_to((kinds != 2).astype(f32)[None, :, None], (1, slots, width))
    first_kept = 1 + 2 * len(grads) + 4
    return pl.pallas_call(
        functools.partial(adam_kernel, n_dp, n_seq // 2, first_slots, len(grads), len(kept)),
        out_shape=[jax.ShapeDtypeStruct(master.shape, f32)] * 4,
        grid_spec=pltpu.PrefetchScalarGridSpec(
            num_scalar_prefetch=1,
            grid=(n_dp, steps),
            in_specs=cols
            + rws
            + [state] * 3
            + [pl.BlockSpec((1, slots, width), lambda d, i, k: (0, 0, 0))]
            + [pl.BlockSpec(memory_space=pl.ANY)] * len(kept),
            out_specs=[state] * 4,
            scratch_shapes=[pltpu.VMEM((slots, rb, width), f32)],
        ),
        input_output_aliases={first_kept + k: k for k in range(len(kept))},
        compiler_params=pltpu.CompilerParams(vmem_limit_bytes=50 << 20),
        cost_estimate=pl.CostEstimate(
            flops=0, bytes_accessed=int(150e6 * size / sub), transcendentals=0
        ),
        name="adam",
    )(
        kinds,
        *grads,
        *[g.reshape(n_dp, g.shape[1], n_dp, size, wide) for g in grads],
        master,
        first_moment,
        second_moment,
        keep,
        *kept,
    )


ANY = pl.BlockSpec(memory_space=pl.ANY)
VMEM = pl.BlockSpec(memory_space=pltpu.VMEM)
DMA = pltpu.SemaphoreType.DMA


def comm_params(collective_id, mib):
    return pltpu.CompilerParams(
        collective_id=collective_id, has_side_effects=True, vmem_limit_bytes=mib << 20
    )


def takes(microseconds):
    return pl.CostEstimate(flops=0, bytes_accessed=int(microseconds * 3e6), transcendentals=0)


def places():
    n_seq = lax.axis_size("seq")
    n_dp = lax.axis_size("dp")
    return n_seq, n_dp, lax.axis_index("seq"), lax.axis_index("dp")


def greet(devices):
    barrier = pltpu.get_barrier_semaphore()
    for device in devices:
        pl.semaphore_signal(barrier, inc=1, device_id=device, device_id_type=MESH)
    pl.semaphore_wait(barrier, len(devices))


def send(src, dst, send_sem, recv_sem, device):
    return pltpu.make_async_remote_copy(
        src_ref=src,
        dst_ref=dst,
        send_sem=send_sem,
        recv_sem=recv_sem,
        device_id=device,
        device_id_type=MESH,
    )


def relay_gather(views, place, count, device_of, send_sem, recv_sem, arrived, between=None, during=None):
    def leg(view, way, step, block, target):
        ref = views[view](block)
        return send(ref, ref, send_sem.at[view, way, step], recv_sem.at[view, way, step], device_of(target))

    def going(way, step):
        block = place - (step - 1) if way == 0 else place + (step - 1)
        target = place + 1 if way == 0 else place - 1
        inside = (block >= 0) & (block < count) & (target >= 0) & (target < count)
        return block, target, inside

    for step in range(1, count):
        for way in range(2):
            block, target, inside = going(way, step)

            @pl.when(inside)
            def _():
                for view in range(len(views)):
                    leg(view, way, step, block, target).start()

        if during:
            during(step)

        for way in range(2):
            block = place - step if way == 0 else place + step

            @pl.when((block >= 0) & (block < count))
            def _():
                for view in range(len(views)):
                    leg(view, way, step, block, lax.rem(place + 1, count)).wait_recv()
                arrived(block)

        if between:
            between(step)

    for step in range(1, count):
        for way in range(2):
            block, target, inside = going(way, step)

            @pl.when(inside)
            def _():
                for view in range(len(views)):
                    leg(view, way, step, block, target).wait_send()


def relay_sum(owns, sent, came, place, count, device_of, send_sem, recv_sem, ready, between=None):
    views = range(len(owns))

    def spot(way, block, receiver):
        return jnp.where(block == receiver, count, block) if way else block

    def leg(view, way, block, target, receiver):
        return send(
            sent[view].at[block],
            came[view].at[spot(way, block, receiver)],
            send_sem.at[view, way, block],
            recv_sem.at[view, way, block],
            device_of(target),
        )

    def going(way, step):
        block = count - 1 - step + place if way == 0 else step - (count - 1 - place)
        target = place + 1 if way == 0 else place - 1
        return block, target, (block < count if way == 0 else block >= 0)

    def behind(way):
        return place > 0 if way == 0 else place < count - 1

    for step in range(count - 1):
        for way in range(2):
            block, target, inside = going(way, step)

            @pl.when(inside)
            def _():
                ready(block)
                for view in views:

                    @pl.when(behind(way))
                    def _():
                        leg(view, way, block, target, place).wait_recv()
                        value = owns[view](block) + came[view][block].astype(f32)
                        sent[view][block] = value.astype(sent[view].dtype)

                    @pl.when(jnp.logical_not(behind(way)))
                    def _():
                        sent[view][block] = owns[view](block).astype(sent[view].dtype)

                    leg(view, way, block, target, target).start()

        if between:
            between(step)

    ready(place)
    for way in range(2):

        @pl.when(behind(way))
        def _():
            for view in views:
                leg(view, way, place, lax.rem(place + 1, count), place).wait_recv()

    totals = []
    for view in views:
        total = owns[view](place)
        for way in range(2):
            value = came[view][place if way == 0 else count].astype(f32)
            total = total + jnp.where(behind(way), value, 0.0)
        totals.append(total)
    for step in range(count - 1):
        for way in range(2):
            block, target, inside = going(way, step)

            @pl.when(inside)
            def _():
                for view in views:
                    leg(view, way, block, target, target).wait_send()

    return totals


def front_kernel(
    packed_ref, tokens_ref, table_ref, out_ref, x_ref, own_sem, a_send, a_recv, send_sem, recv_sem, pass_sem, take_sem
):
    n_seq, n_dp, seq_index, dp_index = places()
    chips, chip, core = n_seq // 2, seq_index // 2, lax.rem(seq_index, 2)
    dp_peers = [lax.rem(dp_index + k, n_dp) for k in range(n_dp)]
    chip_peers = [lax.rem(chip + k, chips) for k in range(chips)]
    sibling = (dp_index, chip * 2 + 1 - core)
    greet(
        [(p, seq_index) for p in dp_peers[1:]]
        + [(dp_index, p * 2 + core) for p in chip_peers[1:]]
        + [sibling]
    )
    along = []
    for k in range(1, n_dp):
        copy = send(
            packed_ref.at[dp_peers[k]],
            table_ref.at[dp_index],
            a_send.at[k],
            a_recv.at[k],
            (dp_peers[k], seq_index),
        )
        copy.start()
        along.append(copy)
    x_ref[...] = norm_parts(tokens_ref[...].astype(f32))[0].astype(bf)
    own = [
        pltpu.make_async_copy(packed_ref.at[dp_index], table_ref.at[dp_index], own_sem.at[0]),
        pltpu.make_async_copy(x_ref, out_ref.at[seq_index], own_sem.at[1]),
    ]
    for copy in own:
        copy.start()
    pass_on, finish = spread_blocks(
        x_ref, out_ref, chips, chip, core, dp_index, sibling, send_sem, recv_sem, pass_sem, take_sem
    )
    pass_on()
    finish()
    for copy in along:
        copy.wait()
    for copy in own:
        copy.wait()


def spread_blocks(
    x_ref, out_ref, chips, chip, core, dp_index, sibling, send_sem, recv_sem, pass_sem, take_sem
):
    mine = out_ref.at[chip * 2 + core]
    copies = {}
    for k in range(chips - 1, 0, -1):
        device = (dp_index, lax.rem(chip + k, chips) * 2 + core)
        copies[k] = send(x_ref, mine, send_sem.at[k], recv_sem.at[k], device)
        copies[k].start()
    passed = [send(x_ref, mine, pass_sem.at[0], take_sem.at[0], sibling)]
    passed[0].start()

    def pass_on():
        for k in range(1, chips):
            copies[k].wait_recv()
            block = out_ref.at[lax.rem(chip + chips - k, chips) * 2 + core]
            onward = send(block, block, pass_sem.at[k], take_sem.at[k], sibling)
            onward.start()
            passed.append(onward)

    def finish():
        for copy in copies.values():
            copy.wait_send()
        for onward in passed:
            onward.wait()

    return pass_on, finish


def front(packed, x, collective_id):
    chips = lax.axis_size("seq") // 2
    n_dp = lax.axis_size("dp")
    return pl.pallas_call(
        front_kernel,
        out_shape=[
            jax.ShapeDtypeStruct(packed.shape, packed.dtype),
            jax.ShapeDtypeStruct((2 * chips,) + x.shape, x.dtype),
        ],
        in_specs=[VMEM, VMEM],
        out_specs=[ANY, ANY],
        scratch_shapes=[pltpu.VMEM(x.shape, bf), DMA((2,)), DMA((n_dp,)), DMA((n_dp,))]
        + [DMA((chips,))] * 4,
        compiler_params=comm_params(collective_id, 24),
        cost_estimate=takes(90),
        name="front",
    )(packed, x)


def sum_seq_kernel(x_ref, out_ref, taken, sent, arrived, pass_sem, take_sem, send_sem, recv_sem):
    n_seq, n_dp, seq_index, dp_index = places()
    chips, chip, core = n_seq // 2, seq_index // 2, lax.rem(seq_index, 2)
    peers = [lax.rem(chip + k, chips) for k in range(chips)]
    sibling = (dp_index, chip * 2 + 1 - core)
    greet([(dp_index, p * 2 + core) for p in peers[1:]] + [sibling])
    order = list(range(chips - 1, 0, -1)) + [0]
    passed = {}
    for k in order:
        block = x_ref.at[peers[k] * 2 + 1 - core]
        passed[k] = send(block, taken.at[k], pass_sem.at[k], take_sem.at[k], sibling)
        passed[k].start()
    copies = {}
    for k in order[:-1]:
        passed[k].wait_recv()
        own = x_ref[peers[k] * 2 + core].astype(f32)
        sent[k] = (own + taken[k].astype(f32)).astype(sent.dtype)
        device = (dp_index, peers[k] * 2 + core)
        copies[k] = send(sent.at[k], arrived.at[k], send_sem.at[k], recv_sem.at[k], device)
        copies[k].start()
    passed[0].wait_recv()
    total = x_ref[seq_index].astype(f32) + taken[0].astype(f32)
    for k in range(1, chips):
        copies[k].wait_recv()
        total = total + arrived[k].astype(f32)
    out_ref[...] = total
    for k in order:
        passed[k].wait_send()
    for k in order[:-1]:
        copies[k].wait_send()


def sum_seq(x, collective_id):
    blocks, rows, columns = x.shape
    chips = blocks // 2
    slots = pltpu.VMEM((chips, rows, columns), x.dtype)
    return pl.pallas_call(
        sum_seq_kernel,
        out_shape=jax.ShapeDtypeStruct((rows, columns), f32),
        in_specs=[VMEM],
        out_specs=VMEM,
        scratch_shapes=[slots, slots, slots] + [DMA((chips,))] * 4,
        compiler_params=comm_params(collective_id, 40),
        cost_estimate=takes(28),
        name="sum_seq",
    )(x)


def collect_kernel(
    qkv_ref, out_ref, qkv_sum, out_sum, qkv_sent, qkv_came, out_sent, out_came, total, own_sem,
    send_sem, recv_sem, a_send, a_recv
):
    n_seq, n_dp, seq_index, dp_index = places()
    seq_peers = [lax.rem(seq_index + k, n_seq) for k in range(n_seq)]
    greet(
        [(dp_index, p) for p in seq_peers[1:]]
        + [(lax.rem(dp_index + k, n_dp), seq_index) for k in range(1, n_dp)]
    )
    sums = relay_sum(
        [lambda block: qkv_ref[:, block].astype(f32), lambda block: out_ref[block].astype(f32)],
        [qkv_sent, out_sent],
        [qkv_came, out_came],
        dp_index,
        n_dp,
        lambda place: (place, seq_index),
        send_sem,
        recv_sem,
        lambda block: None,
    )
    total[...] = sums[0].astype(total.dtype)
    across = []
    for k in range(1, n_seq):
        copy = send(
            total.at[seq_peers[k]],
            qkv_sum.at[seq_index],
            a_send.at[k],
            a_recv.at[k],
            (dp_index, seq_peers[k]),
        )
        copy.start()
        across.append(copy)
    own = pltpu.make_async_copy(total.at[seq_index], qkv_sum.at[seq_index], own_sem)
    own.start()
    out_sum[...] = sums[1].astype(out_sum.dtype)
    for copy in across:
        copy.wait()
    own.wait()


def collect_attention(qkv, out, collective_id):
    n_seq = lax.axis_size("seq")
    n_dp = lax.axis_size("dp")
    tail = qkv.shape[2:]
    return pl.pallas_call(
        collect_kernel,
        out_shape=[
            jax.ShapeDtypeStruct((n_seq,) + tail, qkv.dtype),
            jax.ShapeDtypeStruct(out.shape[1:], out.dtype),
        ],
        in_specs=[VMEM, VMEM],
        out_specs=[VMEM, VMEM],
        scratch_shapes=[
            pltpu.VMEM((n_dp, n_seq) + tail, qkv.dtype),
            pltpu.VMEM((n_dp + 1, n_seq) + tail, qkv.dtype),
            pltpu.VMEM((n_dp,) + out.shape[1:], out.dtype),
            pltpu.VMEM((n_dp + 1,) + out.shape[1:], out.dtype),
            pltpu.VMEM((n_seq,) + tail, qkv.dtype),
            DMA,
            DMA((2, 2, n_dp)),
            DMA((2, 2, n_dp)),
            DMA((n_seq,)),
            DMA((n_seq,)),
        ],
        compiler_params=comm_params(collective_id, 48),
        cost_estimate=takes(75),
        name="collect_attention",
    )(qkv, out)


def ring_chip(place, chips):
    return jnp.where(place < chips // 2, 2 * place, 2 * (chips - 1 - place) + 1)


def ring_place(chip, chips):
    line = chip // 2
    return jnp.where(lax.rem(chip, 2) == 0, line, chips - 1 - line)


class Ring:
    def __init__(self, chips, chip, core, dp_index, send_sem, recv_sem):
        self.chips = chips
        self.place = ring_place(chip, chips)
        self.core = core
        self.dp_index = dp_index
        self.send_sem = send_sem
        self.recv_sem = recv_sem
        self.last = chips // 2

    def at(self, offset):
        return ring_chip(lax.rem(self.place + offset + self.chips, self.chips), self.chips)

    def device(self, way):
        return (self.dp_index, self.at(1 if way == 0 else -1) * 2 + self.core)

    def leg(self, view, way, step, src, dst):
        return send(
            src, dst, self.send_sem.at[view, way, step], self.recv_sem.at[view, way, step], self.device(way)
        )


def arrange_kernel(ff_blocks, units, ug_ref, down_ref, *refs):
    piece_ref = refs[-1]
    unit = units[pl.program_id(0)]
    rows, wide = piece_ref.shape[1:]
    sub, width = down_ref.shape[1:]
    groups = width // wide

    @pl.when((unit >= 4) & (unit < 4 + 2 * ff_blocks))
    def _():
        piece_ref[0] = ug_ref[0]

    @pl.when(unit >= 4 + 2 * ff_blocks)
    def _():
        for g in range(groups):
            piece_ref[0, g * sub : (g + 1) * sub, :] = down_ref[0, :, g * wide : (g + 1) * wide]

    if len(refs) == 3:
        qkv_ref, out_ref = refs[:2]
        blocks, _, columns = qkv_ref.shape
        step = columns // 3
        share = wide // step
        for u in range(3):

            @pl.when(unit == u)
            def _():
                for block in range(blocks):
                    g, h = block // share, block % share
                    piece_ref[0, g * sub : (g + 1) * sub, h * step : (h + 1) * step] = qkv_ref[
                        block, :, u * step : (u + 1) * step
                    ]

        @pl.when(unit == 3)
        def _():
            for g in range(groups):
                piece_ref[0, g * sub : (g + 1) * sub, :] = out_ref[:, g * wide : (g + 1) * wide]


def arrange(units, ug, down, attention):
    n_dp, slots = units.shape
    rows, wide = ug.shape[1:]
    sub, width = down.shape[1:]
    ff_blocks = down.shape[0]
    specs = [
        pl.BlockSpec(
            (1, rows, wide), lambda k, u: (jnp.clip(u[k] - 4, 0, 2 * ff_blocks - 1), 0, 0)
        ),
        pl.BlockSpec(
            (1, sub, width),
            lambda k, u: (jnp.clip(u[k] - 4 - 2 * ff_blocks, 0, ff_blocks - 1), 0, 0),
        ),
    ]
    if attention:
        specs.append(pl.BlockSpec(attention[0].shape, lambda k, u: (0, 0, 0)))
        specs.append(pl.BlockSpec(attention[1].shape, lambda k, u: (0, 0)))
    return pl.pallas_call(
        functools.partial(arrange_kernel, ff_blocks),
        out_shape=jax.ShapeDtypeStruct((n_dp * slots, rows, wide), bf),
        grid_spec=pltpu.PrefetchScalarGridSpec(
            num_scalar_prefetch=1,
            grid=(n_dp * slots,),
            in_specs=specs,
            out_specs=pl.BlockSpec((1, rows, wide), lambda k, u: (k, 0, 0)),
        ),
        compiler_params=pltpu.CompilerParams(vmem_limit_bytes=16 << 20),
        cost_estimate=takes(7),
        name="arrange",
    )(units.reshape(-1), ug, down, *attention).reshape(n_dp, slots, rows, wide)


def column_sums(refs, takens, sents, cames, send_sem, recv_sem, pass_sem, take_sem, between):
    n_seq, n_dp, seq_index, dp_index = places()
    core = lax.rem(seq_index, 2)
    sibling = (dp_index, seq_index + 1 - 2 * core)
    views = range(len(refs))

    def onward(view, block):
        return send(
            refs[view].at[1 - core, block],
            takens[view].at[block],
            pass_sem.at[view, block],
            take_sem.at[view, block],
            sibling,
        )

    for block in [b for k in range(n_dp // 2) for b in (n_dp - 1 - k, k)]:
        for view in views:
            onward(view, block).start()

    def ready(block):
        for view in views:
            onward(view, block).wait_recv()

    def own(view):
        return lambda block: refs[view][core, block].astype(f32) + takens[view][block].astype(f32)

    totals = relay_sum(
        [own(view) for view in views],
        sents,
        cames,
        dp_index,
        n_dp,
        lambda place: (place, seq_index),
        send_sem,
        recv_sem,
        ready,
        between,
    )
    for block in range(n_dp):
        for view in views:
            onward(view, block).wait_send()
    return totals


def ff_kernel(
    x_hbm, up_hbm, gate_hbm, down_hbm, cot_ref, ff_out, grad_out, down_grad, up_grad, gate_grad,
    x_ref, up_ref, gate_ref, down_ref, cot_all, hidden, up_low, gate_low, up_factor, gate_factor, stage, narrow, grad_stage,
    load_sem, grad_sem, stage_sem, narrow_sem, own_sem, send_sem, recv_sem, pass_sem, take_sem
):
    n_seq, n_dp, seq_index, dp_index = places()
    core = lax.rem(seq_index, 2)
    sibling = (dp_index, seq_index + 1 - 2 * core)
    loads = [
        pltpu.make_async_copy(src, dst, load_sem.at[k])
        for k, (src, dst) in enumerate(
            ((x_hbm, x_ref), (up_hbm, up_ref), (gate_hbm, gate_ref), (down_hbm, down_ref))
        )
    ]
    for load in loads:
        load.start()
    greet([(lax.rem(dp_index + k, n_dp), seq_index) for k in range(1, n_dp)] + [sibling])
    own = pltpu.make_async_copy(cot_ref, cot_all.at[core, dp_index], own_sem)
    own.start()
    own.wait()

    def onward(block):
        ref = cot_all.at[core, block]
        return send(ref, ref, pass_sem.at[block], take_sem.at[block], sibling)

    onward(dp_index).start()
    count, width = x_ref.shape
    columns = up_ref.shape[1]
    shard = cot_ref.shape[0]
    block_rows = 2 * shard
    blocks = count // block_rows

    def rows_of(b):
        return pl.ds(pl.multiple_of(b * block_rows, block_rows), block_rows)

    def times(left, right, left_axis, right_axis):
        return lax.dot_general(
            left, right, (((left_axis,), (right_axis,)), ((), ())), preferred_element_type=f32
        )

    def put(index, buffer, sem, value, dst):
        slot = lax.rem(index, 2)

        def copy(to):
            return pltpu.make_async_copy(buffer.at[slot], to, sem.at[slot])

        @pl.when(index >= 2)
        def _():
            copy(dst).wait()

        buffer[slot] = value
        copy(dst).start()

    def drain(buffer, sem, dst):
        for slot in range(2):
            pltpu.make_async_copy(buffer.at[slot], dst, sem.at[slot]).wait()

    def ahead(b, carry):
        at = rows_of(b)
        up = times(x_ref[at, :], up_ref[...], 1, 0)
        gate = times(x_ref[at, :], gate_ref[...], 1, 0)
        sig = jax.nn.sigmoid(gate)
        silu = gate * sig
        hidden[at, :] = (silu * up).astype(bf)
        up_factor[at, :] = silu
        gate_factor[at, :] = up * (sig + silu * (1.0 - sig))
        return carry

    def across(b, carry):
        at = rows_of(b)
        put(b, stage, stage_sem, times(hidden[at, :], down_ref[...], 1, 0).astype(bf), ff_out.at[at, :])
        return carry

    def back(place):
        ref = cot_all.at[1 - core, place]
        send(ref, ref, pass_sem.at[place], take_sem.at[place], sibling).wait_recv()
        lines = [
            pl.ds(pl.multiple_of((c * n_dp + place) * shard, shard), shard) for c in range(2)
        ]

        def both(source):
            return jnp.concatenate([source[line, :] for line in lines], axis=0)

        cot = jnp.concatenate([cot_all[c, place] for c in range(2)], axis=0)
        hidden_grad = times(cot, down_ref[...], 1, 1)
        up_part = (hidden_grad * both(up_factor)).astype(bf)
        gate_part = (hidden_grad * both(gate_factor)).astype(bf)
        value = times(up_part, up_ref[...], 1, 1) + times(gate_part, gate_ref[...], 1, 1)
        value = value.astype(bf)
        copies = []
        for c, line in enumerate(lines):
            up_low[line, :] = up_part[c * shard : (c + 1) * shard]
            gate_low[line, :] = gate_part[c * shard : (c + 1) * shard]
            grad_stage[c] = value[c * shard : (c + 1) * shard]
            copies.append(
                pltpu.make_async_copy(grad_stage.at[c], grad_out.at[line, :], grad_sem.at[c])
            )
            copies[c].start()
        for copy in copies:
            copy.wait()

    def back_at(distance):
        for place in (dp_index - distance, dp_index + distance):

            @pl.when((place >= 0) & (place < n_dp))
            def _():
                back(place)

    def work(step):
        if step == 1:
            for load in loads[:3]:
                load.wait()
            lax.fori_loop(0, blocks, ahead, 0)
            loads[3].wait()
        if step == 2 or n_dp == 2:
            back(dp_index)
        if step > 1:
            back_at(step - 1)
        if step == n_dp - 1:
            lax.fori_loop(0, blocks, across, 0)

    relay_gather(
        [lambda block: cot_all.at[core, block]],
        dp_index,
        n_dp,
        lambda place: (place, seq_index),
        send_sem,
        recv_sem,
        lambda block: onward(block).start(),
        during=work,
    )
    back_at(n_dp - 1)
    for block in range(n_dp):
        onward(block).wait_send()
    down_rows = min(256, columns)
    down_blocks = columns // down_rows
    cot_rows = cot_all[...].reshape(count, width)
    for b in range(down_blocks):
        at = slice(b * down_rows, (b + 1) * down_rows)
        value = times(hidden[:, at], cot_rows, 0, 0).astype(bf)
        put(b + blocks, stage.at[:, pl.ds(0, down_rows)], stage_sem, value, down_grad.at[at, :])
    side_blocks = width // 256
    for k, (low, out) in enumerate(((up_low, up_grad), (gate_low, gate_grad))):
        for b in range(side_blocks):
            at = slice(b * 256, (b + 1) * 256)
            value = times(x_ref[:, at], low[...], 0, 0).astype(bf)
            put(k * side_blocks + b, narrow, narrow_sem, value, out.at[at, :])
    drain(stage.at[:, pl.ds(0, down_rows)], stage_sem, down_grad.at[pl.ds(0, down_rows), :])
    drain(narrow, narrow_sem, gate_grad.at[pl.ds(0, 256), :])


def feed_forward(x, up, gate, down, cot, collective_id):
    n_dp = lax.axis_size("dp")
    count, width = x.shape
    columns = up.shape[1]
    shard = cot.shape[0]
    vmem = pltpu.VMEM
    low = lambda *shape: jax.ShapeDtypeStruct(shape, bf)
    return pl.pallas_call(
        ff_kernel,
        out_shape=[
            low(count, width),
            low(count, width),
            low(columns, width),
            low(width, columns),
            low(width, columns),
        ],
        in_specs=[ANY] * 4 + [VMEM],
        out_specs=[ANY] * 5,
        scratch_shapes=[
            vmem((count, width), bf),
            vmem((width, columns), bf),
            vmem((width, columns), bf),
            vmem((columns, width), bf),
            vmem((2, n_dp, shard, width), bf),
            vmem((count, columns), bf),
            vmem((count, columns), bf),
            vmem((count, columns), bf),
            vmem((count, columns), f32),
            vmem((count, columns), f32),
            vmem((2, 2 * shard, width), bf),
            vmem((2, 256, columns), bf),
            vmem((2, shard, width), bf),
            DMA((4,)),
            DMA((2,)),
            DMA((2,)),
            DMA((2,)),
            DMA,
            DMA((1, 2, n_dp)),
            DMA((1, 2, n_dp)),
            DMA((n_dp,)),
            DMA((n_dp,)),
        ],
        compiler_params=comm_params(collective_id, 58),
        cost_estimate=takes(60),
        name="feed_forward",
    )(x, up, gate, down, cot)


class BandSum:
    def __init__(self, band, owns, outs, scratch, chips, chip, core, dp_index, n_dp):
        self.begin, self.size = band
        self.owns, self.outs = owns, outs
        self.half_came, self.full_sent, self.full_came = scratch[0:3], scratch[3:6], scratch[6:9]
        self.mine, self.side_out = scratch[9:12], scratch[12]
        ring_send, ring_recv, self.side_send, self.side_recv, self.own_sem = scratch[13:]
        self.ring = Ring(chips, chip, core, dp_index, ring_send, ring_recv)
        self.chip, self.core, self.n_dp = chip, core, n_dp
        self.sibling = (dp_index, chip * 2 + 1 - core)
        self.blocks = outs[1].shape[0]
        self.pair = self.blocks // 2
        self.half = outs[0].shape[2] // 2

    def own(self, view, place, way):
        rows = pl.ds(self.begin, self.size)
        if view == 0:
            units = pl.ds(0, self.blocks) if way is None else pl.ds(way * self.pair, self.pair)
            return self.owns[0].at[units, place, rows, :]
        columns = pl.ds(0, self.blocks * self.half)
        if way is not None:
            columns = pl.ds(way * self.pair * self.half, self.pair * self.half)
        return self.owns[view].at[place, :, :, rows, columns]

    def leg(self, view, way, step):
        ring = self.ring
        if step == 0:
            src = self.own(view, ring.at(ring.last), way)
            return ring.leg(view, way, step, src, self.half_came[view].at[way])
        src = self.full_sent[view].at[step - 1, way]
        return ring.leg(view, way, step, src, self.full_came[view].at[step - 1, way])

    def own_copy(self, view, way, step):
        distance = self.ring.last - step
        if distance == 0:
            return pltpu.make_async_copy(
                self.own(view, self.chip, None), self.mine[view], self.own_sem.at[view, 0, step - 1]
            )
        src = self.own(view, self.ring.at(distance if way == 0 else -distance), None)
        return pltpu.make_async_copy(
            src, self.full_sent[view].at[step - 1, way], self.own_sem.at[view, way, step - 1]
        )

    def start(self):
        for view in range(3):
            for way in range(2):
                self.leg(view, way, 0).start()
        for step in range(1, self.ring.last + 1):
            for view in range(3):
                for way in range(2 if step < self.ring.last else 1):
                    self.own_copy(view, way, step).start()

    def steps(self):
        pair, half = self.pair, self.half
        for step in range(1, self.ring.last):
            for view in range(3):
                for way in range(2):
                    self.own_copy(view, way, step).wait()
                    self.leg(view, way, step - 1).wait_recv()
                    full = self.full_sent[view]
                    if step > 1:
                        value = full[step - 1, way].astype(f32)
                        value = value + self.full_came[view][step - 2, way].astype(f32)
                        full[step - 1, way] = value.astype(bf)
                    elif view == 0:
                        units = slice(way * pair, (way + 1) * pair)
                        value = full[0, way, units].astype(f32)
                        value = value + self.half_came[0][way].astype(f32)
                        full[0, way, units] = value.astype(bf)
                    else:
                        columns = slice(way * pair * half, (way + 1) * pair * half)
                        value = full[0, way, :, :, :, columns].astype(f32)
                        value = value + self.half_came[view][way].astype(f32)
                        full[0, way, :, :, :, columns] = value.astype(bf)
                    self.leg(view, way, step).start()

    def finish(self):
        ug_out, down_out = self.outs
        last, blocks, half = self.ring.last, self.blocks, self.half
        for view in range(3):
            self.own_copy(view, 0, last).wait()
            for way in range(2):
                self.leg(view, way, last - 1).wait_recv()
            if last > 1:
                came = [self.full_came[view][last - 2, way].astype(f32) for way in range(2)]
                value = self.mine[view][...].astype(f32) + came[0] + came[1]
            else:
                came = [self.half_came[view][way].astype(f32) for way in range(2)]
                other = jnp.concatenate(came, axis=0 if view == 0 else 3)
                value = self.mine[view][...].astype(f32) + other
            value = value.astype(bf)
            if view == 0:
                down_out[...] = value
                continue
            value = value.reshape(2, self.n_dp * self.size, blocks * half)
            for k in range(blocks):
                unit = (view - 1) * blocks + k

                @pl.when(self.core == 0)
                def _():
                    ug_out[unit, :, :half] = value[0, :, k * half : (k + 1) * half]
                    self.side_out[unit] = value[1, :, k * half : (k + 1) * half]

                @pl.when(self.core != 0)
                def _():
                    ug_out[unit, :, half:] = value[1, :, k * half : (k + 1) * half]
                    self.side_out[unit] = value[0, :, k * half : (k + 1) * half]

        place = pl.ds(pl.multiple_of(self.core * half, half), half)
        side = send(
            self.side_out, ug_out.at[:, :, place], self.side_send, self.side_recv, self.sibling
        )
        side.start()
        side.wait()

    def close(self):
        for step in range(self.ring.last):
            for view in range(3):
                for way in range(2):
                    self.leg(view, way, step).wait_send()


def grads_kernel(bands, late_slots, *refs):
    n_seq, n_dp, seq_index, dp_index = places()
    chips, chip, core = n_seq // 2, seq_index // 2, lax.rem(seq_index, 2)
    sibling = (dp_index, chip * 2 + 1 - core)
    refs = list(refs)

    def take(count):
        taken, refs[:count] = refs[:count], []
        return taken

    info, residual_ref, cot_ref = take(3)
    owns, x_refs = take(3), take(2)
    outs = [take(2) for _ in bands]
    grad_out, ff_out, tokens_out = take(3)
    late_out = take(1)[0] if late_slots else None
    next_out = take(len(bands) - 1) if late_slots else []
    scratch = [take(18) for _ in bands]
    takens, sents, cames = take(2), take(2), take(2)
    z_send, z_recv, x_pass, x_take = take(4)
    stage, token_own, token_send, token_recv, token_pass, token_take = take(6)
    greet(
        [(lax.rem(dp_index + k, n_dp), seq_index) for k in range(1, n_dp)]
        + [(dp_index, lax.rem(chip + k, chips) * 2 + core) for k in range(1, chips)]
        + [sibling]
    )
    sums = [
        BandSum(band, owns, out, memory, chips, chip, core, dp_index, n_dp)
        for band, out, memory in zip(bands, outs, scratch)
    ]
    sums[0].start()

    def between(step):
        if step == 0:
            sums[0].steps()
            for later in sums[1:]:
                later.start()
        if step == n_dp - 2:
            for later in sums[1:]:
                later.steps()

    norm_two_grad, ff_sum = column_sums(
        x_refs, takens, sents, cames, z_send, z_recv, x_pass, x_take, between
    )
    ff_out[...] = ff_sum
    residual = residual_ref[...]
    center = residual - jnp.mean(residual, axis=-1, keepdims=True)
    variance = jnp.mean(center * center, axis=-1, keepdims=True)
    scale_inv = lax.rsqrt(variance + norm_eps)
    grad = norm_back(center * scale_inv, scale_inv, norm_two_grad) + cot_ref[...].astype(f32)
    grad_out[...] = grad
    stage[...] = grad.astype(bf)
    own_tokens = pltpu.make_async_copy(stage, tokens_out.at[seq_index], token_own)
    own_tokens.start()
    pass_on, finish_tokens = spread_blocks(
        stage, tokens_out, chips, chip, core, dp_index, sibling,
        token_send, token_recv, token_pass, token_take,
    )
    sums[0].finish()
    def fill(pair, target_ref):
        ug_ref, down_ref = pair
        blocks, size, width = down_ref.shape
        wide = ug_ref.shape[2]
        for k in range(n_dp * late_slots):
            unit = info[k]
            is_down = unit >= 4 + 2 * blocks
            for g in range(n_dp):
                rows = slice(g * size, (g + 1) * size)
                value = ug_ref[jnp.clip(unit - 4, 0, 2 * blocks - 1), rows, :]
                other = down_ref[
                    jnp.clip(unit - 4 - 2 * blocks, 0, blocks - 1), :, g * wide : (g + 1) * wide
                ]
                use_other = jnp.full(value.shape, is_down.astype(jnp.int32), jnp.int32) != 0
                target_ref[k // late_slots, k % late_slots, rows, :] = jnp.where(
                    use_other, other, value
                )

    along = []
    if late_slots:
        late_stage, late_send, late_recv, late_own = take(4)
        fill(outs[0], late_stage)
        for k in range(1, n_dp):
            target = lax.rem(dp_index + k, n_dp)
            along.append(
                send(
                    late_stage.at[target],
                    late_out.at[dp_index],
                    late_send.at[k],
                    late_recv.at[k],
                    (target, seq_index),
                )
            )
        along.append(
            pltpu.make_async_copy(late_stage.at[dp_index], late_out.at[dp_index], late_own)
        )
        for copy in along:
            copy.start()
    pass_on()
    for k, later in enumerate(sums[1:]):
        later.finish()
        if late_slots:
            fill(outs[k + 1], next_out[k])
    for band in sums:
        band.close()
    own_tokens.wait()
    finish_tokens()
    for copy in along:
        copy.wait()


def sum_grads(bands, late_units, residual, cot, sums, xs, collective_id):
    _, n_dp, shard, width = xs[0].shape
    chips = lax.axis_size("seq") // 2
    steps = chips // 2
    vmem = pltpu.VMEM
    blocks = sums[0].shape[0]
    wide = sums[1].shape[-1]
    half = wide // blocks
    late_slots = late_units.shape[1]
    out_shape, out_specs, scratch = [], [], []
    for _, size in bands:
        out_shape += [
            jax.ShapeDtypeStruct((2 * blocks, n_dp * size, 2 * half), bf),
            jax.ShapeDtypeStruct((blocks, size, width), bf),
        ]
        out_specs += [VMEM] * 2
        side = (2, n_dp, size)
        fulls = [(blocks, size, width), side + (wide,), side + (wide,)]
        halves = [(blocks // 2, size, width), side + (wide // 2,), side + (wide // 2,)]
        scratch += [vmem((2,) + s, bf) for s in halves]
        scratch += [vmem((max(steps - 1, 1), 2) + s, bf) for s in fulls] * 2
        scratch += [vmem(s, bf) for s in fulls]
        scratch += [
            vmem((2 * blocks, n_dp * size, half), bf),
            DMA((3, 2, steps)),
            DMA((3, 2, steps)),
            DMA,
            DMA,
            DMA((3, 2, steps)),
        ]
    out_shape += [jax.ShapeDtypeStruct((shard, width), f32)] * 2
    out_shape.append(jax.ShapeDtypeStruct((2 * chips, shard, width), bf))
    out_specs += [VMEM, VMEM, ANY]
    scratch += [vmem((n_dp, shard, width), bf)] * 4
    scratch += [vmem((n_dp + 1, shard, width), bf)] * 2
    scratch += [DMA((2, 2, n_dp))] * 2 + [DMA((2, n_dp))] * 2
    scratch += [vmem((shard, width), bf), DMA] + [DMA((chips,))] * 4
    if late_slots:
        piece = (n_dp, late_slots, n_dp * bands[0][1], 2 * half)
        out_shape.append(jax.ShapeDtypeStruct(piece, bf))
        out_specs.append(ANY)
        out_shape += [jax.ShapeDtypeStruct(piece, bf)] * (len(bands) - 1)
        out_specs += [VMEM] * (len(bands) - 1)
        scratch += [vmem(piece, bf), DMA((n_dp,)), DMA((n_dp,)), DMA]
    return pl.pallas_call(
        functools.partial(grads_kernel, bands, late_slots),
        out_shape=out_shape,
        in_specs=[pl.BlockSpec(memory_space=pltpu.SMEM), VMEM, VMEM] + [ANY] * 3 + [VMEM] * 2,
        out_specs=out_specs,
        scratch_shapes=scratch,
        compiler_params=comm_params(collective_id, 60),
        cost_estimate=takes(130),
        name="sum_grads",
    )(late_units.reshape(-1) if late_slots else jnp.zeros((1,), jnp.int32), residual, cot, *sums, *xs)


def attention_back_kernel(
    grad_ref, weight_ref, query_ref, key_ref, value_ref, mixed_ref, stat_ref, cos_ref, sin_ref, doc_row, doc_col, x_ref,
    qkv_out, qkv_weight_out, out_weight_out, mixed_grad, key_sum, value_sum
):
    seq_len, width = grad_ref.shape
    head_cols = query_ref.shape[1]
    heads = head_cols // HD
    block_rows = min(256, seq_len)
    scale = float(HD) ** (-0.5)

    def rows_of(b):
        return pl.ds(pl.multiple_of(b * block_rows, block_rows), block_rows)

    def times(left, right, left_axis, right_axis):
        return lax.dot_general(
            left, right, (((left_axis,), (right_axis,)), ((), ())), preferred_element_type=f32
        )

    def mix(b, carry):
        at = rows_of(b)
        mixed_grad[at, :] = times(grad_ref[at, :], weight_ref[...], 1, 1).astype(bf)
        return carry

    lax.fori_loop(0, seq_len // block_rows, mix, 0)
    key_sum[...] = jnp.zeros_like(key_sum)
    value_sum[...] = jnp.zeros_like(value_sum)

    def turned(grads, cosine, sine):
        scaled = grads * sine
        half = HD // 2
        other = jnp.concatenate([scaled[:, half:], -scaled[:, :half]], axis=-1)
        return grads * cosine + other

    def attend(b, carry):
        at = rows_of(b)
        begin = b * block_rows
        query_pos = begin + lax.broadcasted_iota(jnp.int32, (block_rows, seq_len), 0)
        key_pos = lax.broadcasted_iota(jnp.int32, (block_rows, seq_len), 1)
        allowed = (doc_col[at, :] == doc_row[...]) & (key_pos <= query_pos)
        for h in range(heads):
            place = slice(h * HD, (h + 1) * HD)
            query, part = query_ref[at, place], mixed_grad[at, place]
            scores = jnp.where(allowed, times(query, key_ref[:, place], 1, 1) * scale, masked_score)
            prob = jnp.exp(scores - stat_ref[at, h * HD : h * HD + 1])
            prob_grad = times(part, value_ref[:, place], 1, 1)
            inner = jnp.sum(prob * prob_grad, axis=-1, keepdims=True)
            score_grad = (prob * (prob_grad - inner) * scale).astype(bf)
            value_sum[:, place] += times(prob.astype(bf), part, 0, 0)
            key_sum[:, place] += times(score_grad, query, 0, 0)
            query_grad = times(score_grad, key_ref[:, place], 1, 0)
            qkv_out[at, place] = turned(query_grad, cos_ref[at, :], sin_ref[at, :]).astype(bf)
        return carry

    lax.fori_loop(0, seq_len // block_rows, attend, 0)

    def finish(b, carry):
        at = rows_of(b)
        for h in range(heads):
            place = slice(h * HD, (h + 1) * HD)
            grads = turned(key_sum[at, place], cos_ref[at, :], sin_ref[at, :])
            qkv_out[at, head_cols + h * HD : head_cols + (h + 1) * HD] = grads.astype(bf)
        qkv_out[at, 2 * head_cols :] = value_sum[at, :].astype(bf)
        return carry

    lax.fori_loop(0, seq_len // block_rows, finish, 0)
    columns = min(512, width)
    for c in range(width // columns):
        at = slice(c * columns, (c + 1) * columns)
        qkv_weight_out[at, :] = times(x_ref[:, at], qkv_out[...], 0, 0).astype(bf)
        out_weight_out[:, at] = times(mixed_ref[...], grad_ref[:, at], 0, 0).astype(bf)


def attention_back(grad, weight, query, key, value, mixed, stat, cosine, sine, doc, x):
    seq_len, width = grad.shape
    head_cols = query.shape[1]
    return pl.pallas_call(
        attention_back_kernel,
        out_shape=[
            jax.ShapeDtypeStruct((seq_len, 3 * head_cols), bf),
            jax.ShapeDtypeStruct((width, 3 * head_cols), bf),
            jax.ShapeDtypeStruct((head_cols, width), bf),
        ],
        in_specs=[VMEM] * 12,
        out_specs=[VMEM] * 3,
        scratch_shapes=[
            pltpu.VMEM((seq_len, head_cols), bf),
            pltpu.VMEM((seq_len, head_cols), f32),
            pltpu.VMEM((seq_len, head_cols), f32),
        ],
        compiler_params=pltpu.CompilerParams(vmem_limit_bytes=50 << 20),
        cost_estimate=takes(35),
        name="attention_back",
    )(grad, weight, query, key, value, mixed, stat, cosine, sine, doc[None, :], doc[:, None], x)


def turn_half(values):
    half = values.shape[-1] // 2
    return jnp.concatenate([-values[:, half:], values[:, :half]], axis=-1)


def forward_kernel(has_late, first_slots, ff_blocks, *refs):
    info, first_ref = refs[:2]
    refs = refs[2:]
    if has_late:
        late_ref, refs = refs[0], refs[1:]
    x1_ref, cos_ref, sin_ref, doc_row, doc_col, tokens_ref = refs[:6]
    refs = (None,) + refs
    qkv_all, out_all, query_out, key_out, value_out, mixed_out, stat_out, residual_out = refs[7:15]
    up_all, gate_all, down_all, x_all = refs[15:19]
    ug_all = (up_all, gate_all)
    att_stage, out_stage, part, taken, sent, arrived, x_stage = refs[19:26]
    mine_stage, given_stage, down_stage = refs[26:29]
    (own_sem, a_send, a_recv, w_send, w_recv, s_pass, s_take, s_send, s_recv,
     late_send, late_recv, late_own, stage_own, side_send, side_recv, ring_send, ring_recv,
     send_sem, recv_sem, pass_sem, take_sem) = refs[29:50]
    late_tables = refs[50:-2]
    x1_hbm, x1_ref, x1_sem = x1_ref, refs[-2], refs[-1]
    x1_copy = pltpu.make_async_copy(x1_hbm, x1_ref, x1_sem)
    x1_copy.start()
    n_seq, n_dp, seq_index, dp_index = places()
    chips, chip, core = n_seq // 2, seq_index // 2, lax.rem(seq_index, 2)
    sibling = (dp_index, chip * 2 + 1 - core)
    seq_peers = [lax.rem(seq_index + k, n_seq) for k in range(n_seq)]
    dp_peers = [lax.rem(dp_index + k, n_dp) for k in range(n_dp)]
    rows, wide = first_ref.shape[1:]
    sub = rows // n_dp
    half = wide // 2
    step_cols = att_stage.shape[2] // 3
    share = wide // step_cols
    tokens, width = tokens_ref.shape
    greet([(dp_index, p) for p in seq_peers[1:]] + [(p, seq_index) for p in dp_peers[1:]])

    def band(c):
        return pl.ds(c * sub, sub)

    def late_copies(c):
        copies = []
        for k in range(1, n_dp):
            copies.append(
                send(
                    late_ref.at[dp_peers[k], :, band(c)],
                    late_tables[c].at[dp_index],
                    late_send.at[c, k],
                    late_recv.at[c, k],
                    (dp_peers[k], seq_index),
                )
            )
        return copies

    def late_own_copy(c):
        return pltpu.make_async_copy(
            late_ref.at[dp_index, :, band(c)], late_tables[c].at[dp_index], late_own.at[c]
        )

    def late_start(c):
        if not has_late or c >= n_dp:
            return
        if c:
            for copy in late_copies(c - 1):
                copy.wait_send()
        for copy in late_copies(c):
            copy.start()
        late_own_copy(c).start()

    late_start(0)

    for u in range(3):
        for block in range(n_seq):
            g, h = block // share, block % share
            att_stage[block, :, u * step_cols : (u + 1) * step_cols] = first_ref[
                info[u], g * sub : (g + 1) * sub, h * step_cols : (h + 1) * step_cols
            ]
    for g in range(n_dp):
        out_stage[:, g * wide : (g + 1) * wide] = first_ref[info[3], g * sub : (g + 1) * sub, :]
    own = [
        pltpu.make_async_copy(att_stage.at[seq_index], qkv_all.at[seq_index, dp_index], own_sem.at[0]),
        pltpu.make_async_copy(out_stage, out_all.at[dp_index], own_sem.at[1]),
    ]
    across = []
    for k in range(1, n_seq):
        copy = send(
            att_stage.at[seq_peers[k]],
            qkv_all.at[seq_index, dp_index],
            a_send.at[k],
            a_recv.at[k],
            (dp_index, seq_peers[k]),
        )
        copy.start()
        across.append(copy)
    for copy in own:
        copy.start()
    for copy in own:
        copy.wait()
    for copy in across:
        copy.wait_recv()
    relay_gather(
        [lambda block: qkv_all.at[:, block], lambda block: out_all.at[block]],
        dp_index,
        n_dp,
        lambda place: (place, seq_index),
        w_send,
        w_recv,
        lambda block: None,
    )

    ring = Ring(chips, chip, core, dp_index, None, None)
    pair = ff_blocks // 2

    def ring_leg(c, view, way, step, arriving):
        distance = step if arriving else step - 1
        block = ring.at(-distance if way == 0 else distance)
        units = pl.ds(way * pair, pair) if step == ring.last else pl.ds(0, ff_blocks)
        if view == 0:
            ref = down_all.at[units, block, :, pl.ds(c * wide, wide)]
        else:
            columns = pl.ds(0, ff_blocks * half)
            if step == ring.last:
                columns = pl.ds(way * pair * half, pair * half)
            ref = ug_all[view - 1].at[block, :, band(c), columns]
        return send(
            ref, ref, ring_send.at[c, view, way, step - 1], ring_recv.at[c, view, way, step - 1],
            ring.device(way),
        )

    def side_copies(c):
        return [
            send(
                given_stage.at[c, k],
                ug_all[k].at[chip, core, band(c)],
                side_send.at[c, k],
                side_recv.at[c, k],
                sibling,
            )
            for k in range(2)
        ]

    def begin_band(c):
        if has_late:
            for copy in late_copies(c):
                copy.wait_recv()
            late_own_copy(c).wait()
            if c:
                late_start(c + 1)
            table = late_tables[c]
            late_slots = table.shape[1]
        for u in range(3 * ff_blocks):
            value = first_ref[info[4 + u], band(c), :]
            if has_late:
                code = info[4 + 3 * ff_blocks + u]
                other = table[code // late_slots, lax.rem(code, late_slots)]
                use_late = jnp.full(value.shape, info[4 + 6 * ff_blocks + u], jnp.int32) != 0
                value = jnp.where(use_late, other, value)
            if u < 2 * ff_blocks:
                left, right = value[:, :half], value[:, half:]
                k, j = u // ff_blocks, u % ff_blocks
                columns = slice(j * half, (j + 1) * half)

                @pl.when(core == 0)
                def _():
                    mine_stage[c, k, :, columns] = left
                    given_stage[c, k, :, columns] = right

                @pl.when(core != 0)
                def _():
                    mine_stage[c, k, :, columns] = right
                    given_stage[c, k, :, columns] = left
            else:
                down_stage[c, u - 2 * ff_blocks] = value
        for copy in side_copies(c):
            copy.start()
        local = [
            pltpu.make_async_copy(
                mine_stage.at[c, k], ug_all[k].at[chip, core, band(c)], stage_own.at[c, k]
            )
            for k in range(2)
        ]
        local.append(
            pltpu.make_async_copy(
                down_stage.at[c], down_all.at[:, chip, :, pl.ds(c * wide, wide)], stage_own.at[c, 2]
            )
        )
        for copy in local:
            copy.start()
        for copy in local:
            copy.wait()
        for copy in side_copies(c):
            copy.wait_recv()
        for view in range(3):
            for way in range(2):
                ring_leg(c, view, way, 1, False).start()

    def carry_band(c, step):
        for view in range(3):
            for way in range(2):
                ring_leg(c, view, way, step - 1, True).wait_recv()
                ring_leg(c, view, way, step, False).start()

    late_start(1)
    begin_band(0)

    x1_copy.wait()
    seq_len = x1_ref.shape[0]
    heads = query_out.shape[1] // HD
    block_rows = min(256, seq_len)
    head_cols = heads * HD
    qkv_weight = qkv_all[...].reshape(width, 3 * head_cols)

    def project(b, carry):
        at = pl.ds(pl.multiple_of(b * block_rows, block_rows), block_rows)
        result = jnp.dot(x1_ref[at, :], qkv_weight, preferred_element_type=f32)
        cosine, sine = cos_ref[at, :], sin_ref[at, :]
        for h in range(heads):
            place = slice(h * HD, (h + 1) * HD)
            for part_id, out in ((0, query_out), (1, key_out)):
                begin = part_id * head_cols + h * HD
                values = result[:, begin : begin + HD]
                out[at, place] = (values * cosine + turn_half(values) * sine).astype(bf)
        value_out[at, :] = result[:, 2 * head_cols :].astype(bf)
        return carry

    lax.fori_loop(0, seq_len // block_rows, project, 0)

    def attend(b, carry):
        begin = pl.multiple_of(b * block_rows, block_rows)
        at = pl.ds(begin, block_rows)
        query_pos = begin + lax.broadcasted_iota(jnp.int32, (block_rows, seq_len), 0)
        key_pos = lax.broadcasted_iota(jnp.int32, (block_rows, seq_len), 1)
        allowed = (doc_col[at, :] == doc_row[...]) & (key_pos <= query_pos)
        for h in range(heads):
            place = slice(h * HD, (h + 1) * HD)
            scores = lax.dot_general(
                query_out[at, place],
                key_out[:, place],
                (((1,), (1,)), ((), ())),
                preferred_element_type=f32,
            )
            scores = jnp.where(allowed, scores * (float(HD) ** (-0.5)), masked_score)
            peak = jnp.max(scores, axis=-1, keepdims=True)
            raised = jnp.exp(scores - peak)
            total = jnp.sum(raised, axis=-1, keepdims=True)
            prob = (raised * (1.0 / total)).astype(bf)
            mixed = jnp.dot(prob, value_out[:, place], preferred_element_type=f32)
            mixed_out[at, place] = mixed.astype(bf)
            stat_out[at, place] = jnp.broadcast_to(peak + jnp.log(total), (block_rows, HD))
        return carry

    lax.fori_loop(0, seq_len // block_rows, attend, 0)
    out_weight = out_all[...].reshape(rows, width)

    def combine(b, carry):
        at = pl.ds(pl.multiple_of(b * tokens, tokens), tokens)
        part[b] = jnp.dot(mixed_out[at, :], out_weight, preferred_element_type=f32).astype(bf)
        return carry

    lax.fori_loop(0, n_seq, combine, 0)

    chip_peers = [lax.rem(chip + k, chips) for k in range(chips)]
    order = list(range(chips - 1, 0, -1)) + [0]
    passed = {}
    for k in order:
        block = part.at[chip_peers[k] * 2 + 1 - core]
        passed[k] = send(block, taken.at[k], s_pass.at[k], s_take.at[k], sibling)
        passed[k].start()
    copies = {}
    for k in order[:-1]:
        passed[k].wait_recv()
        value = part[chip_peers[k] * 2 + core].astype(f32)
        sent[k] = (value + taken[k].astype(f32)).astype(bf)
        device = (dp_index, chip_peers[k] * 2 + core)
        copies[k] = send(sent.at[k], arrived.at[k], s_send.at[k], s_recv.at[k], device)
        copies[k].start()

    begin_band(1)
    for step in range(2, ring.last + 1):
        carry_band(0, step)
    passed[0].wait_recv()
    total = part[seq_index].astype(f32) + taken[0].astype(f32)
    for k in range(1, chips):
        copies[k].wait_recv()
        total = total + arrived[k].astype(f32)
    residual = tokens_ref[...].astype(f32) + total
    residual_out[...] = residual
    center = residual - jnp.mean(residual, axis=-1, keepdims=True)
    spread = jnp.mean(center * center, axis=-1, keepdims=True)
    x_stage[...] = (center * lax.rsqrt(spread + norm_eps)).astype(bf)
    for c in range(2, n_dp):
        begin_band(c)
        for step in range(2, ring.last + 1):
            carry_band(c - 1, step)

    own_x = pltpu.make_async_copy(x_stage, x_all.at[core, dp_index], own_sem.at[3])
    own_x.start()
    own_x.wait()

    def onward(block):
        ref = x_all.at[core, block]
        return send(ref, ref, pass_sem.at[block], take_sem.at[block], sibling)

    onward(dp_index).start()
    relay_gather(
        [lambda block: x_all.at[core, block]],
        dp_index,
        n_dp,
        lambda place: (place, seq_index),
        send_sem,
        recv_sem,
        lambda block: onward(block).start(),
        lambda step: carry_band(n_dp - 1, 2) if step == 1 and ring.last > 1 else None,
    )
    for step in range(3, ring.last + 1):
        carry_band(n_dp - 1, step)
    for c in range(n_dp):
        for view in range(3):
            for way in range(2):
                ring_leg(c, view, way, ring.last, True).wait_recv()
                for step in range(1, ring.last + 1):
                    ring_leg(c, view, way, step, False).wait_send()
        for copy in side_copies(c):
            copy.wait_send()
        if has_late:
            if c == n_dp - 1:
                for copy in late_copies(c):
                    copy.wait_send()
    for block in range(n_dp):
        onward(block).wait_send()
        ref = x_all.at[1 - core, block]
        send(ref, ref, pass_sem.at[block], take_sem.at[block], sibling).wait_recv()
    for k in order:
        passed[k].wait_send()
    for k in order[:-1]:
        copies[k].wait_send()
    for copy in across:
        copy.wait_send()


def forward(info, first_table, late, x1, cosine, sine, doc, tokens, ff_blocks, first_slots, collective_id):
    n_seq = lax.axis_size("seq")
    n_dp = lax.axis_size("dp")
    chips = n_seq // 2
    rows, wide = first_table.shape[1:]
    sub = rows // n_dp
    half = wide // 2
    seq_len, width = x1.shape
    head_cols = width // n_seq
    shard = tokens.shape[0]
    steps = chips // 2
    vmem = pltpu.VMEM
    low = lambda *shape: jax.ShapeDtypeStruct(shape, bf)
    has_late = late is not None
    blocks = vmem((chips, shard, width), bf)
    return pl.pallas_call(
        functools.partial(forward_kernel, has_late, first_slots, ff_blocks),
        out_shape=[
            low(n_seq, n_dp, sub, 3 * head_cols),
            low(n_dp, sub, width),
            low(seq_len, head_cols),
            low(seq_len, head_cols),
            low(seq_len, head_cols),
            low(seq_len, head_cols),
            jax.ShapeDtypeStruct((seq_len, head_cols), f32),
            jax.ShapeDtypeStruct((shard, width), f32),
            low(chips, 2, rows, ff_blocks * half),
            low(chips, 2, rows, ff_blocks * half),
            low(ff_blocks, chips, sub, width),
            low(2, n_dp, shard, width),
        ],
        in_specs=[pl.BlockSpec(memory_space=pltpu.SMEM), VMEM]
        + [ANY] * has_late
        + [ANY]
        + [VMEM] * 5,
        out_specs=[VMEM] * 8 + [ANY] * 4,
        scratch_shapes=[
            vmem((n_seq, sub, 3 * head_cols), bf),
            vmem((sub, width), bf),
            vmem((n_seq, shard, width), bf),
            blocks,
            blocks,
            blocks,
            vmem((shard, width), bf),
            vmem((n_dp, 2, sub, ff_blocks * half), bf),
            vmem((n_dp, 2, sub, ff_blocks * half), bf),
            vmem((n_dp, ff_blocks, sub, wide), bf),
            DMA((4,)),
            DMA((n_seq,)),
            DMA((n_seq,)),
            DMA((2, 2, n_dp)),
            DMA((2, 2, n_dp)),
            DMA((chips,)),
            DMA((chips,)),
            DMA((chips,)),
            DMA((chips,)),
            DMA((n_dp, n_dp)),
            DMA((n_dp, n_dp)),
            DMA((n_dp,)),
            DMA((n_dp, 3)),
            DMA((n_dp, 2)),
            DMA((n_dp, 2)),
            DMA((n_dp, 3, 2, steps)),
            DMA((n_dp, 3, 2, steps)),
            DMA((1, 2, n_dp)),
            DMA((1, 2, n_dp)),
            DMA((n_dp,)),
            DMA((n_dp,)),
        ]
        + [vmem((n_dp, late.shape[1], sub, wide), bf) for _ in range(n_dp if has_late else 0)]
        + [vmem((seq_len, width), bf), DMA],
        compiler_params=comm_params(collective_id, 58),
        cost_estimate=takes(230),
        name="forward",
    )(
        info,
        first_table,
        *([late] if has_late else []),
        x1,
        cosine,
        sine,
        doc[None, :],
        doc[:, None],
        tokens,
    )


def local(block_input, cotangent, doc_lengths, owners, master, first_moment, second_moment):
    n_seq = lax.axis_size("seq")
    n_dp = lax.axis_size("dp")
    seq_index = lax.axis_index("seq")
    dp_index = lax.axis_index("dp")
    core = seq_index % 2
    _, shard_len, width = block_input.shape
    rows = master.shape[0]
    per_owner = master.shape[1]
    chips = n_seq // 2
    sub = rows // n_dp
    wide = width // n_dp
    half = chips * sub
    head_cols = H // n_seq * HD
    seq_len = shard_len * n_seq
    ff_blocks = FF // D
    first_slots = min(4, per_owner)
    unit_count = owners.shape[0]

    unit_slot = unit_slots(owners, per_owner)
    place = unit_slot - owners * per_owner
    all_slots = jnp.arange(n_dp * per_owner, dtype=jnp.int32)
    match = unit_slot[None, :] == all_slots[:, None]
    slot_unit = jnp.sum(
        jnp.where(match, jnp.arange(unit_count, dtype=jnp.int32)[None, :] + 1, 0), axis=1
    ) - 1
    slot_unit = slot_unit.reshape(n_dp, per_owner)
    own_units = lax.dynamic_index_in_dim(slot_unit, dp_index, 0, keepdims=False)
    is_col = (own_units >= 4) & (own_units < 4 + 2 * ff_blocks)


    tokens = block_input.reshape(shard_len, width)
    packed = pack(master, is_col.astype(jnp.int32), n_dp, n_seq, first_slots)
    first_table, normed_one_all = front(packed[0], tokens, 2)
    first_table = first_table.reshape(n_dp * first_slots, rows, wide)
    normed_one_all = normed_one_all.reshape(seq_len, width)
    upstream = cotangent.reshape(shard_len, width)
    positions = jnp.arange(seq_len, dtype=jnp.int32)
    cosine, sine = rope_tables(seq_len, HD)
    doc_ends = jnp.cumsum(doc_lengths[0])
    doc = jnp.sum((positions[:, None] >= doc_ends[None, :]).astype(jnp.int32), axis=1)
    late_slots = per_owner - first_slots
    info = jnp.concatenate(
        [
            owners * first_slots + jnp.minimum(place, first_slots - 1),
            (owners * late_slots + jnp.maximum(place - first_slots, 0))[4:],
            (place >= first_slots)[4:],
        ]
    ).astype(jnp.int32)
    (
        qkv_weight,
        out_weight,
        queries,
        keys,
        values,
        attended_low,
        log_total,
        residual,
        up_weight,
        gate_weight,
        down_weight,
        normed_two_all,
    ) = forward(
        info,
        first_table,
        packed[1] if late_slots else None,
        normed_one_all,
        cosine,
        sine,
        doc,
        tokens,
        ff_blocks,
        first_slots,
        1,
    )
    qkv_weight = qkv_weight.reshape(width, 3 * head_cols)
    out_weight = out_weight.reshape(rows, width)
    normed_two, inv_two = norm_parts(residual)
    columns = ff_blocks * half
    up_weight = up_weight.reshape(width, columns)
    gate_weight = gate_weight.reshape(width, columns)
    down_weight = down_weight.reshape(columns, width)
    normed_two_all = normed_two_all.reshape(-1, width)
    ff_part, norm_two_part, down_grad, up_grad, gate_grad = feed_forward(
        normed_two_all, up_weight, gate_weight, down_weight, upstream, 7
    )
    side = (chips, 2, n_dp, sub, columns)
    sums = [
        down_grad.reshape(ff_blocks, chips, sub, width),
        up_grad.reshape(side),
        gate_grad.reshape(side),
    ]
    column = (2, n_dp, shard_len, width)
    bands = [(0, sub // 2), (sub // 2, sub // 2)] if sub % 32 == 0 else [(0, sub)]
    back = sum_grads(
        bands,
        slot_unit[:, first_slots:],
        residual,
        upstream,
        sums,
        [norm_two_part.reshape(column), ff_part.reshape(column)],
        5,
    )
    pieces = [back[2 * k : 2 * k + 2] for k in range(len(bands))]
    residual_grad, ff_out, residual_grad_all = back[2 * len(bands) : 2 * len(bands) + 3]
    residual_grad_all = residual_grad_all.reshape(seq_len, width)
    block_output = (residual + ff_out).astype(bf).reshape(block_input.shape)
    late_grads = []
    if late_slots:
        late_grads.append(back[2 * len(bands) + 3])
        for send_now in back[2 * len(bands) + 4 :]:
            send_now, residual_grad_all = lax.optimization_barrier((send_now, residual_grad_all))
            late_grads.append(lax.all_to_all(send_now, "dp", 0, 0))
    qkv_grad_low, qkv_wgrad, out_wgrad = attention_back(
        residual_grad_all,
        out_weight,
        queries,
        keys,
        values,
        attended_low,
        log_total,
        cosine,
        sine,
        doc,
        normed_one_all,
    )
    norm_one_part = jnp.einsum("tf,rf->tr", qkv_grad_low, qkv_weight, preferred_element_type=f32)
    norm_one_grad = sum_seq(norm_one_part.astype(bf).reshape(n_seq, shard_len, width), 3)
    qkv_piece, out_piece = collect_attention(
        qkv_wgrad.reshape(n_seq, n_dp, sub, 3 * head_cols), out_wgrad.reshape(n_dp, sub, width), 6
    )
    kinds = jnp.where(own_units < 0, 2, is_col.astype(jnp.int32)).astype(jnp.int32)
    kept = ()
    came = None
    for k, (begin, size) in enumerate(bands):
        rows_now = slice(begin, begin + size)
        attention = (qkv_piece[:, rows_now], out_piece[rows_now])
        send_now = arrange(slot_unit[:, :first_slots], *pieces[k], attention)
        if came is not None:
            send_now, came, norm_one_grad = lax.optimization_barrier(
                (send_now, came, norm_one_grad)
            )
        elif late_grads:
            send_now, late_grads[-1] = lax.optimization_barrier((send_now, late_grads[-1]))
        came = lax.all_to_all(send_now, "dp", 0, 0)
        kept = adam(
            kinds,
            [came] + late_grads[k : k + 1],
            master,
            first_moment,
            second_moment,
            n_dp,
            n_seq,
            first_slots,
            begin,
            kept,
        )
    owned_grads, new_first, new_second, new_master = kept
    tokens_again, norm_one_grad = lax.optimization_barrier((block_input, norm_one_grad))
    normed_one, inv_one = norm_parts(tokens_again.astype(f32).reshape(shard_len, width))
    input_grad = (residual_grad + norm_back(normed_one, inv_one, norm_one_grad)).reshape(
        block_input.shape
    )
    return (block_output, input_grad, owned_grads, new_first, new_second, new_master)


def solution(mesh):
    placed = (
        P("dp", "seq", None),
        P("dp", "seq", None),
        P("dp", None),
        P(),
        P("seq", "dp", None),
        P("seq", "dp", None),
        P("seq", "dp", None),
    )
    return jax.shard_map(
        local,
        mesh=mesh,
        in_specs=placed,
        out_specs=(
            P("dp", "seq", None),
            P("dp", "seq", None),
            P("seq", "dp", None),
            P("seq", "dp", None),
            P("seq", "dp", None),
            P("seq", "dp", None),
        ),
        check_vma=False,
    )
```

```python
import functools

import jax
import jax.numpy as jnp
import numpy as np
from jax import lax
from jax.experimental import pallas as pl
from jax.experimental.pallas import tpu as pltpu
from jax.sharding import PartitionSpec as P

D = 2048
H = 16
HD = 128
FF = 8192
STEP = 5
bf = jnp.bfloat16
f32 = jnp.float32
MESH = pl.DeviceIdType.MESH


norm_eps = 1e-05
rope_base = 10000.0
beta_one = 0.5
beta_two = 0.5
learn_rate = 0.01
decay_rate = 0.1
adam_eps = 1e-08
masked_score = -1000000000.0


def unit_slots(owners, per_owner):
    unit_count = owners.shape[0]
    unit_order = jnp.arange(unit_count, dtype=jnp.int32)
    matching = owners[:, None] == owners[None, :]
    before = unit_order[None, :] < unit_order[:, None]
    places = jnp.sum(jnp.where(matching & before, 1, 0), axis=1).astype(jnp.int32)
    return owners * per_owner + places


def norm_parts(values):
    center = values - jnp.mean(values, axis=-1, keepdims=True)
    spread = jnp.mean(center * center, axis=-1, keepdims=True)
    scale_inv = lax.rsqrt(spread + norm_eps)
    return (center * scale_inv, scale_inv)


def norm_back(normed, scale_inv, upstream):
    upstream_mean = jnp.mean(upstream, axis=-1, keepdims=True)
    cross_mean = jnp.mean(upstream * normed, axis=-1, keepdims=True)
    return scale_inv * (upstream - upstream_mean - normed * cross_mean)


def rope_tables(seq_len, head_dim):
    half_dim = head_dim // 2
    frequency = rope_base ** (-(np.arange(half_dim) * 2.0) / head_dim)
    angles = np.arange(seq_len)[:, None] * frequency[None, :]
    tables = [np.concatenate([half, half], axis=-1) for half in (np.cos(angles), np.sin(angles))]
    return [jnp.asarray(table.astype(np.float32)) for table in tables]


def pack_kernel(n_dp, chips, first_slots, flags, m_ref, *outs):
    rb, slots, width = m_ref.shape
    rows, wide = outs[0].shape[2:]
    sub = rows // n_dp
    start = pl.program_id(0) * rb
    target = start // sub
    inner = start % sub
    turned = jnp.swapaxes(m_ref[...], 0, 1).astype(bf)
    for s in range(slots):
        out = outs[0] if s < first_slots else outs[1]
        t = s if s < first_slots else s - first_slots
        x = turned[s]

        @pl.when(flags[s] == 1)
        def _():
            for d in range(n_dp):
                pieces = [
                    x[:, (2 * k + c) * rows + d * sub : (2 * k + c) * rows + (d + 1) * sub]
                    for c in range(2)
                    for k in range(chips)
                ]
                out[d, t, pl.ds(pl.multiple_of(start, rb), rb), :] = jnp.concatenate(pieces, axis=1)

        @pl.when(flags[s] == 0)
        def _():
            for g in range(n_dp):
                out[target, t, pl.ds(pl.multiple_of(g * sub + inner, rb), rb), :] = x[
                    :, g * wide : (g + 1) * wide
                ]


def pack(master, flags, n_dp, n_seq, first_slots):
    rows, slots, width = master.shape
    wide = width // n_dp
    rb = min(32, rows // n_dp)
    counts = [first_slots] + ([slots - first_slots] if slots > first_slots else [])
    return pl.pallas_call(
        functools.partial(pack_kernel, n_dp, n_seq // 2, first_slots),
        out_shape=[jax.ShapeDtypeStruct((n_dp, c, rows, wide), bf) for c in counts],
        grid_spec=pltpu.PrefetchScalarGridSpec(
            num_scalar_prefetch=1,
            grid=(rows // rb,),
            in_specs=[pl.BlockSpec((rb, slots, width), lambda i, f: (i, 0, 0))],
            out_specs=[
                pl.BlockSpec((n_dp, c, rows, wide), lambda i, f: (0, 0, 0, 0)) for c in counts
            ],
        ),
        compiler_params=pltpu.CompilerParams(vmem_limit_bytes=50 << 20),
        name="pack",
    )(flags, master)


def adam_kernel(n_dp, chips, first_slots, n_groups, n_kept, kinds, *refs):
    cols = refs[:n_groups]
    rws = refs[n_groups : 2 * n_groups]
    m_ref, f_ref, s_ref, keep_ref = refs[2 * n_groups : 2 * n_groups + 4]
    g_out, f_out, s_out, m_out, held = refs[2 * n_groups + 4 + n_kept :]
    rb, slots, width = m_ref.shape
    wide = width // n_dp
    rows = width // (2 * chips)
    sub = rows // n_dp
    half = chips * sub
    for s in range(slots):
        group = 0 if s < first_slots else 1
        t = s if group == 0 else s - first_slots

        @pl.when(kinds[s] == 1)
        def _():
            pieces = []
            for i in range(2 * chips):
                k, c = i // 2, i % 2
                for d in range(n_dp):
                    begin = c * half + k * sub
                    pieces.append(cols[group][d, t, :, begin : begin + sub])
            held[s] = jnp.concatenate(pieces, axis=1).astype(f32)

        @pl.when(kinds[s] == 0)
        def _():
            for g in range(n_dp):
                held[s, :, g * wide : (g + 1) * wide] = rws[group][0, t, g, :, :].astype(f32)

        @pl.when(kinds[s] == 2)
        def _():
            held[s] = jnp.zeros((rb, width), f32)

    grad = jnp.swapaxes(held[...], 0, 1)
    keep = keep_ref[...] > 0.0
    g_out[...] = grad
    first = jnp.where(keep, beta_one * f_ref[...] + (1.0 - beta_one) * grad, 0.0)
    f_out[...] = first
    second = jnp.where(keep, beta_two * s_ref[...] + (1.0 - beta_two) * grad * grad, 0.0)
    s_out[...] = second
    fixed_first = first * (1.0 / (1.0 - beta_one**STEP))
    fixed_second = second * (1.0 / (1.0 - beta_two**STEP))
    old = m_ref[...]
    root = fixed_second * lax.rsqrt(jnp.maximum(fixed_second, 1e-37))
    step = fixed_first * pl.reciprocal(root + adam_eps, approx=True) + decay_rate * old
    m_out[...] = jnp.where(keep, old - learn_rate * step, 0.0)


def adam(kinds, grads, master, first_moment, second_moment, n_dp, n_seq, first_slots, begin, kept):
    rows, slots, width = master.shape
    wide = width // n_dp
    sub = rows // n_dp
    size = grads[0].shape[2] // n_dp
    rb = min(16, size)
    steps = size // rb
    state = pl.BlockSpec(
        (rb, slots, width), lambda d, i, k: (d * (sub // rb) + begin // rb + i, 0, 0)
    )
    cols = [
        pl.BlockSpec((n_dp, g.shape[1], rb, wide), lambda d, i, k: (0, 0, d * steps + i, 0))
        for g in grads
    ]
    rws = [
        pl.BlockSpec((1, g.shape[1], n_dp, rb, wide), lambda d, i, k: (d, 0, 0, i, 0)) for g in grads
    ]
    keep = jnp.broadcast_to((kinds != 2).astype(f32)[None, :, None], (1, slots, width))
    first_kept = 1 + 2 * len(grads) + 4
    return pl.pallas_call(
        functools.partial(adam_kernel, n_dp, n_seq // 2, first_slots, len(grads), len(kept)),
        out_shape=[jax.ShapeDtypeStruct(master.shape, f32)] * 4,
        grid_spec=pltpu.PrefetchScalarGridSpec(
            num_scalar_prefetch=1,
            grid=(n_dp, steps),
            in_specs=cols
            + rws
            + [state] * 3
            + [pl.BlockSpec((1, slots, width), lambda d, i, k: (0, 0, 0))]
            + [pl.BlockSpec(memory_space=pl.ANY)] * len(kept),
            out_specs=[state] * 4,
            scratch_shapes=[pltpu.VMEM((slots, rb, width), f32)],
        ),
        input_output_aliases={first_kept + k: k for k in range(len(kept))},
        compiler_params=pltpu.CompilerParams(vmem_limit_bytes=50 << 20),
        cost_estimate=pl.CostEstimate(
            flops=0, bytes_accessed=int(150e6 * size / sub), transcendentals=0
        ),
        name="adam",
    )(
        kinds,
        *grads,
        *[g.reshape(n_dp, g.shape[1], n_dp, size, wide) for g in grads],
        master,
        first_moment,
        second_moment,
        keep,
        *kept,
    )


ANY = pl.BlockSpec(memory_space=pl.ANY)
VMEM = pl.BlockSpec(memory_space=pltpu.VMEM)
DMA = pltpu.SemaphoreType.DMA


def comm_params(collective_id, mib):
    return pltpu.CompilerParams(
        collective_id=collective_id, has_side_effects=True, vmem_limit_bytes=mib << 20
    )


def takes(microseconds):
    return pl.CostEstimate(flops=0, bytes_accessed=int(microseconds * 3e6), transcendentals=0)


def places():
    n_seq = lax.axis_size("seq")
    n_dp = lax.axis_size("dp")
    return n_seq, n_dp, lax.axis_index("seq"), lax.axis_index("dp")


def greet(devices):
    barrier = pltpu.get_barrier_semaphore()
    for device in devices:
        pl.semaphore_signal(barrier, inc=1, device_id=device, device_id_type=MESH)
    pl.semaphore_wait(barrier, len(devices))


def send(src, dst, send_sem, recv_sem, device):
    return pltpu.make_async_remote_copy(
        src_ref=src,
        dst_ref=dst,
        send_sem=send_sem,
        recv_sem=recv_sem,
        device_id=device,
        device_id_type=MESH,
    )


def relay_gather(views, place, count, device_of, send_sem, recv_sem, arrived, between=None, during=None):
    def leg(view, way, step, block, target):
        ref = views[view](block)
        return send(ref, ref, send_sem.at[view, way, step], recv_sem.at[view, way, step], device_of(target))

    def going(way, step):
        block = place - (step - 1) if way == 0 else place + (step - 1)
        target = place + 1 if way == 0 else place - 1
        inside = (block >= 0) & (block < count) & (target >= 0) & (target < count)
        return block, target, inside

    for step in range(1, count):
        for way in range(2):
            block, target, inside = going(way, step)

            @pl.when(inside)
            def _():
                for view in range(len(views)):
                    leg(view, way, step, block, target).start()

        if during:
            during(step)

        for way in range(2):
            block = place - step if way == 0 else place + step

            @pl.when((block >= 0) & (block < count))
            def _():
                for view in range(len(views)):
                    leg(view, way, step, block, lax.rem(place + 1, count)).wait_recv()
                arrived(block)

        if between:
            between(step)

    for step in range(1, count):
        for way in range(2):
            block, target, inside = going(way, step)

            @pl.when(inside)
            def _():
                for view in range(len(views)):
                    leg(view, way, step, block, target).wait_send()


def relay_sum(owns, sent, came, place, count, device_of, send_sem, recv_sem, ready, between=None):
    views = range(len(owns))

    def spot(way, block, receiver):
        return jnp.where(block == receiver, count, block) if way else block

    def leg(view, way, block, target, receiver):
        return send(
            sent[view].at[block],
            came[view].at[spot(way, block, receiver)],
            send_sem.at[view, way, block],
            recv_sem.at[view, way, block],
            device_of(target),
        )

    def going(way, step):
        block = count - 1 - step + place if way == 0 else step - (count - 1 - place)
        target = place + 1 if way == 0 else place - 1
        return block, target, (block < count if way == 0 else block >= 0)

    def behind(way):
        return place > 0 if way == 0 else place < count - 1

    for step in range(count - 1):
        for way in range(2):
            block, target, inside = going(way, step)

            @pl.when(inside)
            def _():
                ready(block)
                for view in views:

                    @pl.when(behind(way))
                    def _():
                        leg(view, way, block, target, place).wait_recv()
                        value = owns[view](block) + came[view][block].astype(f32)
                        sent[view][block] = value.astype(sent[view].dtype)

                    @pl.when(jnp.logical_not(behind(way)))
                    def _():
                        sent[view][block] = owns[view](block).astype(sent[view].dtype)

                    leg(view, way, block, target, target).start()

        if between:
            between(step)

    ready(place)
    for way in range(2):

        @pl.when(behind(way))
        def _():
            for view in views:
                leg(view, way, place, lax.rem(place + 1, count), place).wait_recv()

    totals = []
    for view in views:
        total = owns[view](place)
        for way in range(2):
            value = came[view][place if way == 0 else count].astype(f32)
            total = total + jnp.where(behind(way), value, 0.0)
        totals.append(total)
    for step in range(count - 1):
        for way in range(2):
            block, target, inside = going(way, step)

            @pl.when(inside)
            def _():
                for view in views:
                    leg(view, way, block, target, target).wait_send()

    return totals


def front_kernel(
    packed_ref, tokens_ref, table_ref, out_ref, x_ref, own_sem, a_send, a_recv, send_sem, recv_sem, pass_sem, take_sem
):
    n_seq, n_dp, seq_index, dp_index = places()
    chips, chip, core = n_seq // 2, seq_index // 2, lax.rem(seq_index, 2)
    dp_peers = [lax.rem(dp_index + k, n_dp) for k in range(n_dp)]
    chip_peers = [lax.rem(chip + k, chips) for k in range(chips)]
    sibling = (dp_index, chip * 2 + 1 - core)
    greet(
        [(p, seq_index) for p in dp_peers[1:]]
        + [(dp_index, p * 2 + core) for p in chip_peers[1:]]
        + [sibling]
    )
    along = []
    for k in range(1, n_dp):
        copy = send(
            packed_ref.at[dp_peers[k]],
            table_ref.at[dp_index],
            a_send.at[k],
            a_recv.at[k],
            (dp_peers[k], seq_index),
        )
        copy.start()
        along.append(copy)
    x_ref[...] = norm_parts(tokens_ref[...].astype(f32))[0].astype(bf)
    own = [
        pltpu.make_async_copy(packed_ref.at[dp_index], table_ref.at[dp_index], own_sem.at[0]),
        pltpu.make_async_copy(x_ref, out_ref.at[seq_index], own_sem.at[1]),
    ]
    for copy in own:
        copy.start()
    pass_on, finish = spread_blocks(
        x_ref, out_ref, chips, chip, core, dp_index, sibling, send_sem, recv_sem, pass_sem, take_sem
    )
    pass_on()
    finish()
    for copy in along:
        copy.wait()
    for copy in own:
        copy.wait()


def spread_blocks(
    x_ref, out_ref, chips, chip, core, dp_index, sibling, send_sem, recv_sem, pass_sem, take_sem
):
    mine = out_ref.at[chip * 2 + core]
    copies = {}
    for k in range(chips - 1, 0, -1):
        device = (dp_index, lax.rem(chip + k, chips) * 2 + core)
        copies[k] = send(x_ref, mine, send_sem.at[k], recv_sem.at[k], device)
        copies[k].start()
    passed = [send(x_ref, mine, pass_sem.at[0], take_sem.at[0], sibling)]
    passed[0].start()

    def pass_on():
        for k in range(1, chips):
            copies[k].wait_recv()
            block = out_ref.at[lax.rem(chip + chips - k, chips) * 2 + core]
            onward = send(block, block, pass_sem.at[k], take_sem.at[k], sibling)
            onward.start()
            passed.append(onward)

    def finish():
        for copy in copies.values():
            copy.wait_send()
        for onward in passed:
            onward.wait()

    return pass_on, finish


def front(packed, x, collective_id):
    chips = lax.axis_size("seq") // 2
    n_dp = lax.axis_size("dp")
    return pl.pallas_call(
        front_kernel,
        out_shape=[
            jax.ShapeDtypeStruct(packed.shape, packed.dtype),
            jax.ShapeDtypeStruct((2 * chips,) + x.shape, x.dtype),
        ],
        in_specs=[VMEM, VMEM],
        out_specs=[ANY, ANY],
        scratch_shapes=[pltpu.VMEM(x.shape, bf), DMA((2,)), DMA((n_dp,)), DMA((n_dp,))]
        + [DMA((chips,))] * 4,
        compiler_params=comm_params(collective_id, 24),
        cost_estimate=takes(90),
        name="front",
    )(packed, x)


def sum_seq_kernel(x_ref, out_ref, taken, sent, arrived, pass_sem, take_sem, send_sem, recv_sem):
    n_seq, n_dp, seq_index, dp_index = places()
    chips, chip, core = n_seq // 2, seq_index // 2, lax.rem(seq_index, 2)
    peers = [lax.rem(chip + k, chips) for k in range(chips)]
    sibling = (dp_index, chip * 2 + 1 - core)
    greet([(dp_index, p * 2 + core) for p in peers[1:]] + [sibling])
    order = list(range(chips - 1, 0, -1)) + [0]
    passed = {}
    for k in order:
        block = x_ref.at[peers[k] * 2 + 1 - core]
        passed[k] = send(block, taken.at[k], pass_sem.at[k], take_sem.at[k], sibling)
        passed[k].start()
    copies = {}
    for k in order[:-1]:
        passed[k].wait_recv()
        own = x_ref[peers[k] * 2 + core].astype(f32)
        sent[k] = (own + taken[k].astype(f32)).astype(sent.dtype)
        device = (dp_index, peers[k] * 2 + core)
        copies[k] = send(sent.at[k], arrived.at[k], send_sem.at[k], recv_sem.at[k], device)
        copies[k].start()
    passed[0].wait_recv()
    total = x_ref[seq_index].astype(f32) + taken[0].astype(f32)
    for k in range(1, chips):
        copies[k].wait_recv()
        total = total + arrived[k].astype(f32)
    out_ref[...] = total
    for k in order:
        passed[k].wait_send()
    for k in order[:-1]:
        copies[k].wait_send()


def sum_seq(x, collective_id):
    blocks, rows, columns = x.shape
    chips = blocks // 2
    slots = pltpu.VMEM((chips, rows, columns), x.dtype)
    return pl.pallas_call(
        sum_seq_kernel,
        out_shape=jax.ShapeDtypeStruct((rows, columns), f32),
        in_specs=[VMEM],
        out_specs=VMEM,
        scratch_shapes=[slots, slots, slots] + [DMA((chips,))] * 4,
        compiler_params=comm_params(collective_id, 40),
        cost_estimate=takes(28),
        name="sum_seq",
    )(x)


def collect_kernel(
    qkv_ref, out_ref, qkv_sum, out_sum, qkv_sent, qkv_came, out_sent, out_came, total, own_sem,
    send_sem, recv_sem, a_send, a_recv
):
    n_seq, n_dp, seq_index, dp_index = places()
    seq_peers = [lax.rem(seq_index + k, n_seq) for k in range(n_seq)]
    greet(
        [(dp_index, p) for p in seq_peers[1:]]
        + [(lax.rem(dp_index + k, n_dp), seq_index) for k in range(1, n_dp)]
    )
    sums = relay_sum(
        [lambda block: qkv_ref[:, block].astype(f32), lambda block: out_ref[block].astype(f32)],
        [qkv_sent, out_sent],
        [qkv_came, out_came],
        dp_index,
        n_dp,
        lambda place: (place, seq_index),
        send_sem,
        recv_sem,
        lambda block: None,
    )
    total[...] = sums[0].astype(total.dtype)
    across = []
    for k in range(1, n_seq):
        copy = send(
            total.at[seq_peers[k]],
            qkv_sum.at[seq_index],
            a_send.at[k],
            a_recv.at[k],
            (dp_index, seq_peers[k]),
        )
        copy.start()
        across.append(copy)
    own = pltpu.make_async_copy(total.at[seq_index], qkv_sum.at[seq_index], own_sem)
    own.start()
    out_sum[...] = sums[1].astype(out_sum.dtype)
    for copy in across:
        copy.wait()
    own.wait()


def collect_attention(qkv, out, collective_id):
    n_seq = lax.axis_size("seq")
    n_dp = lax.axis_size("dp")
    tail = qkv.shape[2:]
    return pl.pallas_call(
        collect_kernel,
        out_shape=[
            jax.ShapeDtypeStruct((n_seq,) + tail, qkv.dtype),
            jax.ShapeDtypeStruct(out.shape[1:], out.dtype),
        ],
        in_specs=[VMEM, VMEM],
        out_specs=[VMEM, VMEM],
        scratch_shapes=[
            pltpu.VMEM((n_dp, n_seq) + tail, qkv.dtype),
            pltpu.VMEM((n_dp + 1, n_seq) + tail, qkv.dtype),
            pltpu.VMEM((n_dp,) + out.shape[1:], out.dtype),
            pltpu.VMEM((n_dp + 1,) + out.shape[1:], out.dtype),
            pltpu.VMEM((n_seq,) + tail, qkv.dtype),
            DMA,
            DMA((2, 2, n_dp)),
            DMA((2, 2, n_dp)),
            DMA((n_seq,)),
            DMA((n_seq,)),
        ],
        compiler_params=comm_params(collective_id, 48),
        cost_estimate=takes(75),
        name="collect_attention",
    )(qkv, out)


def ring_chip(place, chips):
    return jnp.where(place < chips // 2, 2 * place, 2 * (chips - 1 - place) + 1)


def ring_place(chip, chips):
    line = chip // 2
    return jnp.where(lax.rem(chip, 2) == 0, line, chips - 1 - line)


class Ring:
    def __init__(self, chips, chip, core, dp_index, send_sem, recv_sem):
        self.chips = chips
        self.place = ring_place(chip, chips)
        self.core = core
        self.dp_index = dp_index
        self.send_sem = send_sem
        self.recv_sem = recv_sem
        self.last = chips // 2

    def at(self, offset):
        return ring_chip(lax.rem(self.place + offset + self.chips, self.chips), self.chips)

    def device(self, way):
        return (self.dp_index, self.at(1 if way == 0 else -1) * 2 + self.core)

    def leg(self, view, way, step, src, dst):
        return send(
            src, dst, self.send_sem.at[view, way, step], self.recv_sem.at[view, way, step], self.device(way)
        )


def arrange_kernel(ff_blocks, units, ug_ref, down_ref, *refs):
    piece_ref = refs[-1]
    unit = units[pl.program_id(0)]
    rows, wide = piece_ref.shape[1:]
    sub, width = down_ref.shape[1:]
    groups = width // wide

    @pl.when((unit >= 4) & (unit < 4 + 2 * ff_blocks))
    def _():
        piece_ref[0] = ug_ref[0]

    @pl.when(unit >= 4 + 2 * ff_blocks)
    def _():
        for g in range(groups):
            piece_ref[0, g * sub : (g + 1) * sub, :] = down_ref[0, :, g * wide : (g + 1) * wide]

    if len(refs) == 3:
        qkv_ref, out_ref = refs[:2]
        blocks, _, columns = qkv_ref.shape
        step = columns // 3
        share = wide // step
        for u in range(3):

            @pl.when(unit == u)
            def _():
                for block in range(blocks):
                    g, h = block // share, block % share
                    piece_ref[0, g * sub : (g + 1) * sub, h * step : (h + 1) * step] = qkv_ref[
                        block, :, u * step : (u + 1) * step
                    ]

        @pl.when(unit == 3)
        def _():
            for g in range(groups):
                piece_ref[0, g * sub : (g + 1) * sub, :] = out_ref[:, g * wide : (g + 1) * wide]


def arrange(units, ug, down, attention):
    n_dp, slots = units.shape
    rows, wide = ug.shape[1:]
    sub, width = down.shape[1:]
    ff_blocks = down.shape[0]
    specs = [
        pl.BlockSpec(
            (1, rows, wide), lambda k, u: (jnp.clip(u[k] - 4, 0, 2 * ff_blocks - 1), 0, 0)
        ),
        pl.BlockSpec(
            (1, sub, width),
            lambda k, u: (jnp.clip(u[k] - 4 - 2 * ff_blocks, 0, ff_blocks - 1), 0, 0),
        ),
    ]
    if attention:
        specs.append(pl.BlockSpec(attention[0].shape, lambda k, u: (0, 0, 0)))
        specs.append(pl.BlockSpec(attention[1].shape, lambda k, u: (0, 0)))
    return pl.pallas_call(
        functools.partial(arrange_kernel, ff_blocks),
        out_shape=jax.ShapeDtypeStruct((n_dp * slots, rows, wide), bf),
        grid_spec=pltpu.PrefetchScalarGridSpec(
            num_scalar_prefetch=1,
            grid=(n_dp * slots,),
            in_specs=specs,
            out_specs=pl.BlockSpec((1, rows, wide), lambda k, u: (k, 0, 0)),
        ),
        compiler_params=pltpu.CompilerParams(vmem_limit_bytes=16 << 20),
        cost_estimate=takes(7),
        name="arrange",
    )(units.reshape(-1), ug, down, *attention).reshape(n_dp, slots, rows, wide)


def column_sums(refs, takens, sents, cames, send_sem, recv_sem, pass_sem, take_sem, between):
    n_seq, n_dp, seq_index, dp_index = places()
    core = lax.rem(seq_index, 2)
    sibling = (dp_index, seq_index + 1 - 2 * core)
    views = range(len(refs))

    def onward(view, block):
        return send(
            refs[view].at[1 - core, block],
            takens[view].at[block],
            pass_sem.at[view, block],
            take_sem.at[view, block],
            sibling,
        )

    for block in [b for k in range(n_dp // 2) for b in (n_dp - 1 - k, k)]:
        for view in views:
            onward(view, block).start()

    def ready(block):
        for view in views:
            onward(view, block).wait_recv()

    def own(view):
        return lambda block: refs[view][core, block].astype(f32) + takens[view][block].astype(f32)

    totals = relay_sum(
        [own(view) for view in views],
        sents,
        cames,
        dp_index,
        n_dp,
        lambda place: (place, seq_index),
        send_sem,
        recv_sem,
        ready,
        between,
    )
    for block in range(n_dp):
        for view in views:
            onward(view, block).wait_send()
    return totals


def ff_kernel(
    x_hbm, up_hbm, gate_hbm, down_hbm, cot_ref, ff_out, grad_out, down_grad, up_grad, gate_grad,
    x_ref, up_ref, gate_ref, down_ref, cot_all, hidden, up_low, gate_low, up_factor, gate_factor, stage, narrow, grad_stage,
    load_sem, grad_sem, stage_sem, narrow_sem, own_sem, send_sem, recv_sem, pass_sem, take_sem
):
    n_seq, n_dp, seq_index, dp_index = places()
    core = lax.rem(seq_index, 2)
    sibling = (dp_index, seq_index + 1 - 2 * core)
    loads = [
        pltpu.make_async_copy(src, dst, load_sem.at[k])
        for k, (src, dst) in enumerate(
            ((x_hbm, x_ref), (up_hbm, up_ref), (gate_hbm, gate_ref), (down_hbm, down_ref))
        )
    ]
    for load in loads:
        load.start()
    greet([(lax.rem(dp_index + k, n_dp), seq_index) for k in range(1, n_dp)] + [sibling])
    own = pltpu.make_async_copy(cot_ref, cot_all.at[core, dp_index], own_sem)
    own.start()
    own.wait()

    def onward(block):
        ref = cot_all.at[core, block]
        return send(ref, ref, pass_sem.at[block], take_sem.at[block], sibling)

    onward(dp_index).start()
    count, width = x_ref.shape
    columns = up_ref.shape[1]
    shard = cot_ref.shape[0]
    block_rows = 2 * shard
    blocks = count // block_rows

    def rows_of(b):
        return pl.ds(pl.multiple_of(b * block_rows, block_rows), block_rows)

    def times(left, right, left_axis, right_axis):
        return lax.dot_general(
            left, right, (((left_axis,), (right_axis,)), ((), ())), preferred_element_type=f32
        )

    def put(index, buffer, sem, value, dst):
        slot = lax.rem(index, 2)

        def copy(to):
            return pltpu.make_async_copy(buffer.at[slot], to, sem.at[slot])

        @pl.when(index >= 2)
        def _():
            copy(dst).wait()

        buffer[slot] = value
        copy(dst).start()

    def drain(buffer, sem, dst):
        for slot in range(2):
            pltpu.make_async_copy(buffer.at[slot], dst, sem.at[slot]).wait()

    def ahead(b, carry):
        at = rows_of(b)
        up = times(x_ref[at, :], up_ref[...], 1, 0)
        gate = times(x_ref[at, :], gate_ref[...], 1, 0)
        sig = jax.nn.sigmoid(gate)
        silu = gate * sig
        hidden[at, :] = (silu * up).astype(bf)
        up_factor[at, :] = silu
        gate_factor[at, :] = up * (sig + silu * (1.0 - sig))
        return carry

    def across(b, carry):
        at = rows_of(b)
        put(b, stage, stage_sem, times(hidden[at, :], down_ref[...], 1, 0).astype(bf), ff_out.at[at, :])
        return carry

    def back(place):
        ref = cot_all.at[1 - core, place]
        send(ref, ref, pass_sem.at[place], take_sem.at[place], sibling).wait_recv()
        lines = [
            pl.ds(pl.multiple_of((c * n_dp + place) * shard, shard), shard) for c in range(2)
        ]

        def both(source):
            return jnp.concatenate([source[line, :] for line in lines], axis=0)

        cot = jnp.concatenate([cot_all[c, place] for c in range(2)], axis=0)
        hidden_grad = times(cot, down_ref[...], 1, 1)
        up_part = (hidden_grad * both(up_factor)).astype(bf)
        gate_part = (hidden_grad * both(gate_factor)).astype(bf)
        value = times(up_part, up_ref[...], 1, 1) + times(gate_part, gate_ref[...], 1, 1)
        value = value.astype(bf)
        copies = []
        for c, line in enumerate(lines):
            up_low[line, :] = up_part[c * shard : (c + 1) * shard]
            gate_low[line, :] = gate_part[c * shard : (c + 1) * shard]
            grad_stage[c] = value[c * shard : (c + 1) * shard]
            copies.append(
                pltpu.make_async_copy(grad_stage.at[c], grad_out.at[line, :], grad_sem.at[c])
            )
            copies[c].start()
        for copy in copies:
            copy.wait()

    def back_at(distance):
        for place in (dp_index - distance, dp_index + distance):

            @pl.when((place >= 0) & (place < n_dp))
            def _():
                back(place)

    def work(step):
        if step == 1:
            for load in loads[:3]:
                load.wait()
            lax.fori_loop(0, blocks, ahead, 0)
            loads[3].wait()
        if step == 2 or n_dp == 2:
            back(dp_index)
        if step > 1:
            back_at(step - 1)
        if step == n_dp - 1:
            lax.fori_loop(0, blocks, across, 0)

    relay_gather(
        [lambda block: cot_all.at[core, block]],
        dp_index,
        n_dp,
        lambda place: (place, seq_index),
        send_sem,
        recv_sem,
        lambda block: onward(block).start(),
        during=work,
    )
    back_at(n_dp - 1)
    for block in range(n_dp):
        onward(block).wait_send()
    down_rows = min(256, columns)
    down_blocks = columns // down_rows
    cot_rows = cot_all[...].reshape(count, width)
    for b in range(down_blocks):
        at = slice(b * down_rows, (b + 1) * down_rows)
        value = times(hidden[:, at], cot_rows, 0, 0).astype(bf)
        put(b + blocks, stage.at[:, pl.ds(0, down_rows)], stage_sem, value, down_grad.at[at, :])
    side_blocks = width // 256
    for k, (low, out) in enumerate(((up_low, up_grad), (gate_low, gate_grad))):
        for b in range(side_blocks):
            at = slice(b * 256, (b + 1) * 256)
            value = times(x_ref[:, at], low[...], 0, 0).astype(bf)
            put(k * side_blocks + b, narrow, narrow_sem, value, out.at[at, :])
    drain(stage.at[:, pl.ds(0, down_rows)], stage_sem, down_grad.at[pl.ds(0, down_rows), :])
    drain(narrow, narrow_sem, gate_grad.at[pl.ds(0, 256), :])


def feed_forward(x, up, gate, down, cot, collective_id):
    n_dp = lax.axis_size("dp")
    count, width = x.shape
    columns = up.shape[1]
    shard = cot.shape[0]
    vmem = pltpu.VMEM
    low = lambda *shape: jax.ShapeDtypeStruct(shape, bf)
    return pl.pallas_call(
        ff_kernel,
        out_shape=[
            low(count, width),
            low(count, width),
            low(columns, width),
            low(width, columns),
            low(width, columns),
        ],
        in_specs=[ANY] * 4 + [VMEM],
        out_specs=[ANY] * 5,
        scratch_shapes=[
            vmem((count, width), bf),
            vmem((width, columns), bf),
            vmem((width, columns), bf),
            vmem((columns, width), bf),
            vmem((2, n_dp, shard, width), bf),
            vmem((count, columns), bf),
            vmem((count, columns), bf),
            vmem((count, columns), bf),
            vmem((count, columns), f32),
            vmem((count, columns), f32),
            vmem((2, 2 * shard, width), bf),
            vmem((2, 256, columns), bf),
            vmem((2, shard, width), bf),
            DMA((4,)),
            DMA((2,)),
            DMA((2,)),
            DMA((2,)),
            DMA,
            DMA((1, 2, n_dp)),
            DMA((1, 2, n_dp)),
            DMA((n_dp,)),
            DMA((n_dp,)),
        ],
        compiler_params=comm_params(collective_id, 58),
        cost_estimate=takes(60),
        name="feed_forward",
    )(x, up, gate, down, cot)


class BandSum:
    def __init__(self, band, owns, outs, scratch, chips, chip, core, dp_index, n_dp):
        self.begin, self.size = band
        self.owns, self.outs = owns, outs
        self.half_came, self.full_sent, self.full_came = scratch[0:3], scratch[3:6], scratch[6:9]
        self.mine, self.side_out = scratch[9:12], scratch[12]
        ring_send, ring_recv, self.side_send, self.side_recv, self.own_sem = scratch[13:]
        self.ring = Ring(chips, chip, core, dp_index, ring_send, ring_recv)
        self.chip, self.core, self.n_dp = chip, core, n_dp
        self.sibling = (dp_index, chip * 2 + 1 - core)
        self.blocks = outs[1].shape[0]
        self.pair = self.blocks // 2
        self.half = outs[0].shape[2] // 2

    def own(self, view, place, way):
        rows = pl.ds(self.begin, self.size)
        if view == 0:
            units = pl.ds(0, self.blocks) if way is None else pl.ds(way * self.pair, self.pair)
            return self.owns[0].at[units, place, rows, :]
        columns = pl.ds(0, self.blocks * self.half)
        if way is not None:
            columns = pl.ds(way * self.pair * self.half, self.pair * self.half)
        return self.owns[view].at[place, :, :, rows, columns]

    def leg(self, view, way, step):
        ring = self.ring
        if step == 0:
            src = self.own(view, ring.at(ring.last), way)
            return ring.leg(view, way, step, src, self.half_came[view].at[way])
        src = self.full_sent[view].at[step - 1, way]
        return ring.leg(view, way, step, src, self.full_came[view].at[step - 1, way])

    def own_copy(self, view, way, step):
        distance = self.ring.last - step
        if distance == 0:
            return pltpu.make_async_copy(
                self.own(view, self.chip, None), self.mine[view], self.own_sem.at[view, 0, step - 1]
            )
        src = self.own(view, self.ring.at(distance if way == 0 else -distance), None)
        return pltpu.make_async_copy(
            src, self.full_sent[view].at[step - 1, way], self.own_sem.at[view, way, step - 1]
        )

    def start(self):
        for view in range(3):
            for way in range(2):
                self.leg(view, way, 0).start()
        for step in range(1, self.ring.last + 1):
            for view in range(3):
                for way in range(2 if step < self.ring.last else 1):
                    self.own_copy(view, way, step).start()

    def steps(self):
        pair, half = self.pair, self.half
        for step in range(1, self.ring.last):
            for view in range(3):
                for way in range(2):
                    self.own_copy(view, way, step).wait()
                    self.leg(view, way, step - 1).wait_recv()
                    full = self.full_sent[view]
                    if step > 1:
                        value = full[step - 1, way].astype(f32)
                        value = value + self.full_came[view][step - 2, way].astype(f32)
                        full[step - 1, way] = value.astype(bf)
                    elif view == 0:
                        units = slice(way * pair, (way + 1) * pair)
                        value = full[0, way, units].astype(f32)
                        value = value + self.half_came[0][way].astype(f32)
                        full[0, way, units] = value.astype(bf)
                    else:
                        columns = slice(way * pair * half, (way + 1) * pair * half)
                        value = full[0, way, :, :, :, columns].astype(f32)
                        value = value + self.half_came[view][way].astype(f32)
                        full[0, way, :, :, :, columns] = value.astype(bf)
                    self.leg(view, way, step).start()

    def finish(self):
        ug_out, down_out = self.outs
        last, blocks, half = self.ring.last, self.blocks, self.half
        for view in range(3):
            self.own_copy(view, 0, last).wait()
            for way in range(2):
                self.leg(view, way, last - 1).wait_recv()
            if last > 1:
                came = [self.full_came[view][last - 2, way].astype(f32) for way in range(2)]
                value = self.mine[view][...].astype(f32) + came[0] + came[1]
            else:
                came = [self.half_came[view][way].astype(f32) for way in range(2)]
                other = jnp.concatenate(came, axis=0 if view == 0 else 3)
                value = self.mine[view][...].astype(f32) + other
            value = value.astype(bf)
            if view == 0:
                down_out[...] = value
                continue
            value = value.reshape(2, self.n_dp * self.size, blocks * half)
            for k in range(blocks):
                unit = (view - 1) * blocks + k

                @pl.when(self.core == 0)
                def _():
                    ug_out[unit, :, :half] = value[0, :, k * half : (k + 1) * half]
                    self.side_out[unit] = value[1, :, k * half : (k + 1) * half]

                @pl.when(self.core != 0)
                def _():
                    ug_out[unit, :, half:] = value[1, :, k * half : (k + 1) * half]
                    self.side_out[unit] = value[0, :, k * half : (k + 1) * half]

        place = pl.ds(pl.multiple_of(self.core * half, half), half)
        side = send(
            self.side_out, ug_out.at[:, :, place], self.side_send, self.side_recv, self.sibling
        )
        side.start()
        side.wait()

    def close(self):
        for step in range(self.ring.last):
            for view in range(3):
                for way in range(2):
                    self.leg(view, way, step).wait_send()


def grads_kernel(bands, late_slots, *refs):
    n_seq, n_dp, seq_index, dp_index = places()
    chips, chip, core = n_seq // 2, seq_index // 2, lax.rem(seq_index, 2)
    sibling = (dp_index, chip * 2 + 1 - core)
    refs = list(refs)

    def take(count):
        taken, refs[:count] = refs[:count], []
        return taken

    info, residual_ref, cot_ref = take(3)
    owns, x_refs = take(3), take(2)
    outs = [take(2) for _ in bands]
    grad_out, ff_out, tokens_out = take(3)
    late_out = take(1)[0] if late_slots else None
    next_out = take(len(bands) - 1) if late_slots else []
    scratch = [take(18) for _ in bands]
    takens, sents, cames = take(2), take(2), take(2)
    z_send, z_recv, x_pass, x_take = take(4)
    stage, token_own, token_send, token_recv, token_pass, token_take = take(6)
    greet(
        [(lax.rem(dp_index + k, n_dp), seq_index) for k in range(1, n_dp)]
        + [(dp_index, lax.rem(chip + k, chips) * 2 + core) for k in range(1, chips)]
        + [sibling]
    )
    sums = [
        BandSum(band, owns, out, memory, chips, chip, core, dp_index, n_dp)
        for band, out, memory in zip(bands, outs, scratch)
    ]
    sums[0].start()

    def between(step):
        if step == 0:
            sums[0].steps()
            for later in sums[1:]:
                later.start()
        if step == n_dp - 2:
            for later in sums[1:]:
                later.steps()

    norm_two_grad, ff_sum = column_sums(
        x_refs, takens, sents, cames, z_send, z_recv, x_pass, x_take, between
    )
    ff_out[...] = ff_sum
    residual = residual_ref[...]
    center = residual - jnp.mean(residual, axis=-1, keepdims=True)
    variance = jnp.mean(center * center, axis=-1, keepdims=True)
    scale_inv = lax.rsqrt(variance + norm_eps)
    grad = norm_back(center * scale_inv, scale_inv, norm_two_grad) + cot_ref[...].astype(f32)
    grad_out[...] = grad
    stage[...] = grad.astype(bf)
    own_tokens = pltpu.make_async_copy(stage, tokens_out.at[seq_index], token_own)
    own_tokens.start()
    pass_on, finish_tokens = spread_blocks(
        stage, tokens_out, chips, chip, core, dp_index, sibling,
        token_send, token_recv, token_pass, token_take,
    )
    sums[0].finish()
    def fill(pair, target_ref):
        ug_ref, down_ref = pair
        blocks, size, width = down_ref.shape
        wide = ug_ref.shape[2]
        for k in range(n_dp * late_slots):
            unit = info[k]
            is_down = unit >= 4 + 2 * blocks
            for g in range(n_dp):
                rows = slice(g * size, (g + 1) * size)
                value = ug_ref[jnp.clip(unit - 4, 0, 2 * blocks - 1), rows, :]
                other = down_ref[
                    jnp.clip(unit - 4 - 2 * blocks, 0, blocks - 1), :, g * wide : (g + 1) * wide
                ]
                use_other = jnp.full(value.shape, is_down.astype(jnp.int32), jnp.int32) != 0
                target_ref[k // late_slots, k % late_slots, rows, :] = jnp.where(
                    use_other, other, value
                )

    along = []
    if late_slots:
        late_stage, late_send, late_recv, late_own = take(4)
        fill(outs[0], late_stage)
        for k in range(1, n_dp):
            target = lax.rem(dp_index + k, n_dp)
            along.append(
                send(
                    late_stage.at[target],
                    late_out.at[dp_index],
                    late_send.at[k],
                    late_recv.at[k],
                    (target, seq_index),
                )
            )
        along.append(
            pltpu.make_async_copy(late_stage.at[dp_index], late_out.at[dp_index], late_own)
        )
        for copy in along:
            copy.start()
    pass_on()
    for k, later in enumerate(sums[1:]):
        later.finish()
        if late_slots:
            fill(outs[k + 1], next_out[k])
    for band in sums:
        band.close()
    own_tokens.wait()
    finish_tokens()
    for copy in along:
        copy.wait()


def sum_grads(bands, late_units, residual, cot, sums, xs, collective_id):
    _, n_dp, shard, width = xs[0].shape
    chips = lax.axis_size("seq") // 2
    steps = chips // 2
    vmem = pltpu.VMEM
    blocks = sums[0].shape[0]
    wide = sums[1].shape[-1]
    half = wide // blocks
    late_slots = late_units.shape[1]
    out_shape, out_specs, scratch = [], [], []
    for _, size in bands:
        out_shape += [
            jax.ShapeDtypeStruct((2 * blocks, n_dp * size, 2 * half), bf),
            jax.ShapeDtypeStruct((blocks, size, width), bf),
        ]
        out_specs += [VMEM] * 2
        side = (2, n_dp, size)
        fulls = [(blocks, size, width), side + (wide,), side + (wide,)]
        halves = [(blocks // 2, size, width), side + (wide // 2,), side + (wide // 2,)]
        scratch += [vmem((2,) + s, bf) for s in halves]
        scratch += [vmem((max(steps - 1, 1), 2) + s, bf) for s in fulls] * 2
        scratch += [vmem(s, bf) for s in fulls]
        scratch += [
            vmem((2 * blocks, n_dp * size, half), bf),
            DMA((3, 2, steps)),
            DMA((3, 2, steps)),
            DMA,
            DMA,
            DMA((3, 2, steps)),
        ]
    out_shape += [jax.ShapeDtypeStruct((shard, width), f32)] * 2
    out_shape.append(jax.ShapeDtypeStruct((2 * chips, shard, width), bf))
    out_specs += [VMEM, VMEM, ANY]
    scratch += [vmem((n_dp, shard, width), bf)] * 4
    scratch += [vmem((n_dp + 1, shard, width), bf)] * 2
    scratch += [DMA((2, 2, n_dp))] * 2 + [DMA((2, n_dp))] * 2
    scratch += [vmem((shard, width), bf), DMA] + [DMA((chips,))] * 4
    if late_slots:
        piece = (n_dp, late_slots, n_dp * bands[0][1], 2 * half)
        out_shape.append(jax.ShapeDtypeStruct(piece, bf))
        out_specs.append(ANY)
        out_shape += [jax.ShapeDtypeStruct(piece, bf)] * (len(bands) - 1)
        out_specs += [VMEM] * (len(bands) - 1)
        scratch += [vmem(piece, bf), DMA((n_dp,)), DMA((n_dp,)), DMA]
    return pl.pallas_call(
        functools.partial(grads_kernel, bands, late_slots),
        out_shape=out_shape,
        in_specs=[pl.BlockSpec(memory_space=pltpu.SMEM), VMEM, VMEM] + [ANY] * 3 + [VMEM] * 2,
        out_specs=out_specs,
        scratch_shapes=scratch,
        compiler_params=comm_params(collective_id, 60),
        cost_estimate=takes(130),
        name="sum_grads",
    )(late_units.reshape(-1) if late_slots else jnp.zeros((1,), jnp.int32), residual, cot, *sums, *xs)


def attention_back_kernel(
    grad_ref, weight_ref, query_ref, key_ref, value_ref, mixed_ref, stat_ref, cos_ref, sin_ref, doc_row, doc_col, x_ref,
    qkv_out, qkv_weight_out, out_weight_out, mixed_grad, key_sum, value_sum
):
    seq_len, width = grad_ref.shape
    head_cols = query_ref.shape[1]
    heads = head_cols // HD
    block_rows = min(256, seq_len)
    scale = float(HD) ** (-0.5)

    def rows_of(b):
        return pl.ds(pl.multiple_of(b * block_rows, block_rows), block_rows)

    def times(left, right, left_axis, right_axis):
        return lax.dot_general(
            left, right, (((left_axis,), (right_axis,)), ((), ())), preferred_element_type=f32
        )

    def mix(b, carry):
        at = rows_of(b)
        mixed_grad[at, :] = times(grad_ref[at, :], weight_ref[...], 1, 1).astype(bf)
        return carry

    lax.fori_loop(0, seq_len // block_rows, mix, 0)
    key_sum[...] = jnp.zeros_like(key_sum)
    value_sum[...] = jnp.zeros_like(value_sum)

    def turned(grads, cosine, sine):
        scaled = grads * sine
        half = HD // 2
        other = jnp.concatenate([scaled[:, half:], -scaled[:, :half]], axis=-1)
        return grads * cosine + other

    def attend(b, carry):
        at = rows_of(b)
        begin = b * block_rows
        query_pos = begin + lax.broadcasted_iota(jnp.int32, (block_rows, seq_len), 0)
        key_pos = lax.broadcasted_iota(jnp.int32, (block_rows, seq_len), 1)
        allowed = (doc_col[at, :] == doc_row[...]) & (key_pos <= query_pos)
        for h in range(heads):
            place = slice(h * HD, (h + 1) * HD)
            query, part = query_ref[at, place], mixed_grad[at, place]
            scores = jnp.where(allowed, times(query, key_ref[:, place], 1, 1) * scale, masked_score)
            prob = jnp.exp(scores - stat_ref[at, h * HD : h * HD + 1])
            prob_grad = times(part, value_ref[:, place], 1, 1)
            inner = jnp.sum(prob * prob_grad, axis=-1, keepdims=True)
            score_grad = (prob * (prob_grad - inner) * scale).astype(bf)
            value_sum[:, place] += times(prob.astype(bf), part, 0, 0)
            key_sum[:, place] += times(score_grad, query, 0, 0)
            query_grad = times(score_grad, key_ref[:, place], 1, 0)
            qkv_out[at, place] = turned(query_grad, cos_ref[at, :], sin_ref[at, :]).astype(bf)
        return carry

    lax.fori_loop(0, seq_len // block_rows, attend, 0)

    def finish(b, carry):
        at = rows_of(b)
        for h in range(heads):
            place = slice(h * HD, (h + 1) * HD)
            grads = turned(key_sum[at, place], cos_ref[at, :], sin_ref[at, :])
            qkv_out[at, head_cols + h * HD : head_cols + (h + 1) * HD] = grads.astype(bf)
        qkv_out[at, 2 * head_cols :] = value_sum[at, :].astype(bf)
        return carry

    lax.fori_loop(0, seq_len // block_rows, finish, 0)
    columns = min(512, width)
    for c in range(width // columns):
        at = slice(c * columns, (c + 1) * columns)
        qkv_weight_out[at, :] = times(x_ref[:, at], qkv_out[...], 0, 0).astype(bf)
        out_weight_out[:, at] = times(mixed_ref[...], grad_ref[:, at], 0, 0).astype(bf)


def attention_back(grad, weight, query, key, value, mixed, stat, cosine, sine, doc, x):
    seq_len, width = grad.shape
    head_cols = query.shape[1]
    return pl.pallas_call(
        attention_back_kernel,
        out_shape=[
            jax.ShapeDtypeStruct((seq_len, 3 * head_cols), bf),
            jax.ShapeDtypeStruct((width, 3 * head_cols), bf),
            jax.ShapeDtypeStruct((head_cols, width), bf),
        ],
        in_specs=[VMEM] * 12,
        out_specs=[VMEM] * 3,
        scratch_shapes=[
            pltpu.VMEM((seq_len, head_cols), bf),
            pltpu.VMEM((seq_len, head_cols), f32),
            pltpu.VMEM((seq_len, head_cols), f32),
        ],
        compiler_params=pltpu.CompilerParams(vmem_limit_bytes=50 << 20),
        cost_estimate=takes(35),
        name="attention_back",
    )(grad, weight, query, key, value, mixed, stat, cosine, sine, doc[None, :], doc[:, None], x)


def turn_half(values):
    half = values.shape[-1] // 2
    return jnp.concatenate([-values[:, half:], values[:, :half]], axis=-1)


def forward_kernel(has_late, first_slots, ff_blocks, *refs):
    info, first_ref = refs[:2]
    refs = refs[2:]
    if has_late:
        late_ref, refs = refs[0], refs[1:]
    x1_ref, cos_ref, sin_ref, doc_row, doc_col, tokens_ref = refs[:6]
    refs = (None,) + refs
    qkv_all, out_all, query_out, key_out, value_out, mixed_out, stat_out, residual_out = refs[7:15]
    up_all, gate_all, down_all, x_all = refs[15:19]
    ug_all = (up_all, gate_all)
    att_stage, out_stage, part, taken, sent, arrived, x_stage = refs[19:26]
    mine_stage, given_stage, down_stage = refs[26:29]
    (own_sem, a_send, a_recv, w_send, w_recv, s_pass, s_take, s_send, s_recv,
     late_send, late_recv, late_own, stage_own, side_send, side_recv, ring_send, ring_recv,
     send_sem, recv_sem, pass_sem, take_sem) = refs[29:50]
    late_tables = refs[50:-2]
    x1_hbm, x1_ref, x1_sem = x1_ref, refs[-2], refs[-1]
    x1_copy = pltpu.make_async_copy(x1_hbm, x1_ref, x1_sem)
    x1_copy.start()
    n_seq, n_dp, seq_index, dp_index = places()
    chips, chip, core = n_seq // 2, seq_index // 2, lax.rem(seq_index, 2)
    sibling = (dp_index, chip * 2 + 1 - core)
    seq_peers = [lax.rem(seq_index + k, n_seq) for k in range(n_seq)]
    dp_peers = [lax.rem(dp_index + k, n_dp) for k in range(n_dp)]
    rows, wide = first_ref.shape[1:]
    sub = rows // n_dp
    half = wide // 2
    step_cols = att_stage.shape[2] // 3
    share = wide // step_cols
    tokens, width = tokens_ref.shape
    greet([(dp_index, p) for p in seq_peers[1:]] + [(p, seq_index) for p in dp_peers[1:]])

    def band(c):
        return pl.ds(c * sub, sub)

    def late_copies(c):
        copies = []
        for k in range(1, n_dp):
            copies.append(
                send(
                    late_ref.at[dp_peers[k], :, band(c)],
                    late_tables[c].at[dp_index],
                    late_send.at[c, k],
                    late_recv.at[c, k],
                    (dp_peers[k], seq_index),
                )
            )
        return copies

    def late_own_copy(c):
        return pltpu.make_async_copy(
            late_ref.at[dp_index, :, band(c)], late_tables[c].at[dp_index], late_own.at[c]
        )

    def late_start(c):
        if not has_late or c >= n_dp:
            return
        if c and c < max(2, n_dp - 1):
            for copy in late_copies(c - 1):
                copy.wait_send()
        for copy in late_copies(c):
            copy.start()
        late_own_copy(c).start()

    late_start(0)

    for u in range(3):
        for block in range(n_seq):
            g, h = block // share, block % share
            att_stage[block, :, u * step_cols : (u + 1) * step_cols] = first_ref[
                info[u], g * sub : (g + 1) * sub, h * step_cols : (h + 1) * step_cols
            ]
    for g in range(n_dp):
        out_stage[:, g * wide : (g + 1) * wide] = first_ref[info[3], g * sub : (g + 1) * sub, :]
    own = [
        pltpu.make_async_copy(att_stage.at[seq_index], qkv_all.at[seq_index, dp_index], own_sem.at[0]),
        pltpu.make_async_copy(out_stage, out_all.at[dp_index], own_sem.at[1]),
    ]
    across = []
    for k in range(1, n_seq):
        copy = send(
            att_stage.at[seq_peers[k]],
            qkv_all.at[seq_index, dp_index],
            a_send.at[k],
            a_recv.at[k],
            (dp_index, seq_peers[k]),
        )
        copy.start()
        across.append(copy)
    for copy in own:
        copy.start()
    for copy in own:
        copy.wait()
    for copy in across:
        copy.wait_recv()
    relay_gather(
        [lambda block: qkv_all.at[:, block], lambda block: out_all.at[block]],
        dp_index,
        n_dp,
        lambda place: (place, seq_index),
        w_send,
        w_recv,
        lambda block: None,
    )

    ring = Ring(chips, chip, core, dp_index, None, None)
    pair = ff_blocks // 2

    def ring_leg(c, view, way, step, arriving):
        distance = step if arriving else step - 1
        block = ring.at(-distance if way == 0 else distance)
        units = pl.ds(way * pair, pair) if step == ring.last else pl.ds(0, ff_blocks)
        if view == 0:
            ref = down_all.at[units, block, :, pl.ds(c * wide, wide)]
        else:
            columns = pl.ds(0, ff_blocks * half)
            if step == ring.last:
                columns = pl.ds(way * pair * half, pair * half)
            ref = ug_all[view - 1].at[block, :, band(c), columns]
        return send(
            ref, ref, ring_send.at[c, view, way, step - 1], ring_recv.at[c, view, way, step - 1],
            ring.device(way),
        )

    def side_copies(c):
        return [
            send(
                given_stage.at[c, k],
                ug_all[k].at[chip, core, band(c)],
                side_send.at[c, k],
                side_recv.at[c, k],
                sibling,
            )
            for k in range(2)
        ]

    def begin_band(c):
        if has_late:
            for copy in late_copies(c):
                copy.wait_recv()
            late_own_copy(c).wait()
            if c and (c + 1 < n_dp - 1 or n_dp == 3):
                late_start(c + 1)
            if c and c + 1 == n_dp - 2:
                late_start(n_dp - 1)
            table = late_tables[c]
            late_slots = table.shape[1]
        for u in range(3 * ff_blocks):
            value = first_ref[info[4 + u], band(c), :]
            if has_late:
                code = info[4 + 3 * ff_blocks + u]
                other = table[code // late_slots, lax.rem(code, late_slots)]
                use_late = jnp.full(value.shape, info[4 + 6 * ff_blocks + u], jnp.int32) != 0
                value = jnp.where(use_late, other, value)
            if u < 2 * ff_blocks:
                left, right = value[:, :half], value[:, half:]
                k, j = u // ff_blocks, u % ff_blocks
                columns = slice(j * half, (j + 1) * half)

                @pl.when(core == 0)
                def _():
                    mine_stage[c, k, :, columns] = left
                    given_stage[c, k, :, columns] = right

                @pl.when(core != 0)
                def _():
                    mine_stage[c, k, :, columns] = right
                    given_stage[c, k, :, columns] = left
            else:
                down_stage[c, u - 2 * ff_blocks] = value
        for copy in side_copies(c):
            copy.start()
        local = [
            pltpu.make_async_copy(
                mine_stage.at[c, k], ug_all[k].at[chip, core, band(c)], stage_own.at[c, k]
            )
            for k in range(2)
        ]
        local.append(
            pltpu.make_async_copy(
                down_stage.at[c], down_all.at[:, chip, :, pl.ds(c * wide, wide)], stage_own.at[c, 2]
            )
        )
        for copy in local:
            copy.start()
        for copy in local:
            copy.wait()
        for copy in side_copies(c):
            copy.wait_recv()
        for view in range(3):
            for way in range(2):
                ring_leg(c, view, way, 1, False).start()

    def carry_band(c, step):
        for view in range(3):
            for way in range(2):
                ring_leg(c, view, way, step - 1, True).wait_recv()
                ring_leg(c, view, way, step, False).start()

    late_start(1)
    begin_band(0)

    x1_copy.wait()
    seq_len = x1_ref.shape[0]
    heads = query_out.shape[1] // HD
    block_rows = min(256, seq_len)
    head_cols = heads * HD
    qkv_weight = qkv_all[...].reshape(width, 3 * head_cols)

    def project(b, carry):
        at = pl.ds(pl.multiple_of(b * block_rows, block_rows), block_rows)
        result = jnp.dot(x1_ref[at, :], qkv_weight, preferred_element_type=f32)
        cosine, sine = cos_ref[at, :], sin_ref[at, :]
        for h in range(heads):
            place = slice(h * HD, (h + 1) * HD)
            for part_id, out in ((0, query_out), (1, key_out)):
                begin = part_id * head_cols + h * HD
                values = result[:, begin : begin + HD]
                out[at, place] = (values * cosine + turn_half(values) * sine).astype(bf)
        value_out[at, :] = result[:, 2 * head_cols :].astype(bf)
        return carry

    lax.fori_loop(0, seq_len // block_rows, project, 0)

    def attend(b, carry):
        begin = pl.multiple_of(b * block_rows, block_rows)
        at = pl.ds(begin, block_rows)
        query_pos = begin + lax.broadcasted_iota(jnp.int32, (block_rows, seq_len), 0)
        key_pos = lax.broadcasted_iota(jnp.int32, (block_rows, seq_len), 1)
        allowed = (doc_col[at, :] == doc_row[...]) & (key_pos <= query_pos)
        for h in range(heads):
            place = slice(h * HD, (h + 1) * HD)
            scores = lax.dot_general(
                query_out[at, place],
                key_out[:, place],
                (((1,), (1,)), ((), ())),
                preferred_element_type=f32,
            )
            scores = jnp.where(allowed, scores * (float(HD) ** (-0.5)), masked_score)
            peak = jnp.max(scores, axis=-1, keepdims=True)
            raised = jnp.exp(scores - peak)
            total = jnp.sum(raised, axis=-1, keepdims=True)
            prob = (raised * (1.0 / total)).astype(bf)
            mixed = jnp.dot(prob, value_out[:, place], preferred_element_type=f32)
            mixed_out[at, place] = mixed.astype(bf)
            stat_out[at, place] = jnp.broadcast_to(peak + jnp.log(total), (block_rows, HD))
        return carry

    lax.fori_loop(0, seq_len // block_rows, attend, 0)
    out_weight = out_all[...].reshape(rows, width)

    def combine(b, carry):
        at = pl.ds(pl.multiple_of(b * tokens, tokens), tokens)
        part[b] = jnp.dot(mixed_out[at, :], out_weight, preferred_element_type=f32).astype(bf)
        return carry

    lax.fori_loop(0, n_seq, combine, 0)

    chip_peers = [lax.rem(chip + k, chips) for k in range(chips)]
    order = list(range(chips - 1, 0, -1)) + [0]
    passed = {}
    for k in order:
        block = part.at[chip_peers[k] * 2 + 1 - core]
        passed[k] = send(block, taken.at[k], s_pass.at[k], s_take.at[k], sibling)
        passed[k].start()
    copies = {}
    for k in order[:-1]:
        passed[k].wait_recv()
        value = part[chip_peers[k] * 2 + core].astype(f32)
        sent[k] = (value + taken[k].astype(f32)).astype(bf)
        device = (dp_index, chip_peers[k] * 2 + core)
        copies[k] = send(sent.at[k], arrived.at[k], s_send.at[k], s_recv.at[k], device)
        copies[k].start()

    begin_band(1)
    for step in range(2, ring.last + 1):
        carry_band(0, step)
    passed[0].wait_recv()
    total = part[seq_index].astype(f32) + taken[0].astype(f32)
    for k in range(1, chips):
        copies[k].wait_recv()
        total = total + arrived[k].astype(f32)
    residual = tokens_ref[...].astype(f32) + total
    residual_out[...] = residual
    center = residual - jnp.mean(residual, axis=-1, keepdims=True)
    spread = jnp.mean(center * center, axis=-1, keepdims=True)
    x_stage[...] = (center * lax.rsqrt(spread + norm_eps)).astype(bf)
    for c in range(2, n_dp - 1):
        begin_band(c)
        for step in range(2, ring.last + 1):
            carry_band(c - 1, step)

    def last_band():
        begin_band(n_dp - 1)
        for step in range(2, ring.last + 1):
            carry_band(n_dp - 2, step)

    own_x = pltpu.make_async_copy(x_stage, x_all.at[core, dp_index], own_sem.at[3])
    own_x.start()
    own_x.wait()

    def onward(block):
        ref = x_all.at[core, block]
        return send(ref, ref, pass_sem.at[block], take_sem.at[block], sibling)

    onward(dp_index).start()
    relay_gather(
        [lambda block: x_all.at[core, block]],
        dp_index,
        n_dp,
        lambda place: (place, seq_index),
        send_sem,
        recv_sem,
        lambda block: onward(block).start(),
        lambda step: last_band() if step == 1 else None,
    )
    for step in range(2, ring.last + 1):
        carry_band(n_dp - 1, step)
    for c in range(n_dp):
        for view in range(3):
            for way in range(2):
                ring_leg(c, view, way, ring.last, True).wait_recv()
                for step in range(1, ring.last + 1):
                    ring_leg(c, view, way, step, False).wait_send()
        for copy in side_copies(c):
            copy.wait_send()
        if has_late:
            if c >= max(1, n_dp - 2):
                for copy in late_copies(c):
                    copy.wait_send()
    for block in range(n_dp):
        onward(block).wait_send()
        ref = x_all.at[1 - core, block]
        send(ref, ref, pass_sem.at[block], take_sem.at[block], sibling).wait_recv()
    for k in order:
        passed[k].wait_send()
    for k in order[:-1]:
        copies[k].wait_send()
    for copy in across:
        copy.wait_send()


def forward(info, first_table, late, x1, cosine, sine, doc, tokens, ff_blocks, first_slots, collective_id):
    n_seq = lax.axis_size("seq")
    n_dp = lax.axis_size("dp")
    chips = n_seq // 2
    rows, wide = first_table.shape[1:]
    sub = rows // n_dp
    half = wide // 2
    seq_len, width = x1.shape
    head_cols = width // n_seq
    shard = tokens.shape[0]
    steps = chips // 2
    vmem = pltpu.VMEM
    low = lambda *shape: jax.ShapeDtypeStruct(shape, bf)
    has_late = late is not None
    blocks = vmem((chips, shard, width), bf)
    return pl.pallas_call(
        functools.partial(forward_kernel, has_late, first_slots, ff_blocks),
        out_shape=[
            low(n_seq, n_dp, sub, 3 * head_cols),
            low(n_dp, sub, width),
            low(seq_len, head_cols),
            low(seq_len, head_cols),
            low(seq_len, head_cols),
            low(seq_len, head_cols),
            jax.ShapeDtypeStruct((seq_len, head_cols), f32),
            jax.ShapeDtypeStruct((shard, width), f32),
            low(chips, 2, rows, ff_blocks * half),
            low(chips, 2, rows, ff_blocks * half),
            low(ff_blocks, chips, sub, width),
            low(2, n_dp, shard, width),
        ],
        in_specs=[pl.BlockSpec(memory_space=pltpu.SMEM), VMEM]
        + [ANY] * has_late
        + [ANY]
        + [VMEM] * 5,
        out_specs=[VMEM] * 8 + [ANY] * 4,
        scratch_shapes=[
            vmem((n_seq, sub, 3 * head_cols), bf),
            vmem((sub, width), bf),
            vmem((n_seq, shard, width), bf),
            blocks,
            blocks,
            blocks,
            vmem((shard, width), bf),
            vmem((n_dp, 2, sub, ff_blocks * half), bf),
            vmem((n_dp, 2, sub, ff_blocks * half), bf),
            vmem((n_dp, ff_blocks, sub, wide), bf),
            DMA((4,)),
            DMA((n_seq,)),
            DMA((n_seq,)),
            DMA((2, 2, n_dp)),
            DMA((2, 2, n_dp)),
            DMA((chips,)),
            DMA((chips,)),
            DMA((chips,)),
            DMA((chips,)),
            DMA((n_dp, n_dp)),
            DMA((n_dp, n_dp)),
            DMA((n_dp,)),
            DMA((n_dp, 3)),
            DMA((n_dp, 2)),
            DMA((n_dp, 2)),
            DMA((n_dp, 3, 2, steps)),
            DMA((n_dp, 3, 2, steps)),
            DMA((1, 2, n_dp)),
            DMA((1, 2, n_dp)),
            DMA((n_dp,)),
            DMA((n_dp,)),
        ]
        + [vmem((n_dp, late.shape[1], sub, wide), bf) for _ in range(n_dp if has_late else 0)]
        + [vmem((seq_len, width), bf), DMA],
        compiler_params=comm_params(collective_id, 58),
        cost_estimate=takes(230),
        name="forward",
    )(
        info,
        first_table,
        *([late] if has_late else []),
        x1,
        cosine,
        sine,
        doc[None, :],
        doc[:, None],
        tokens,
    )


def local(block_input, cotangent, doc_lengths, owners, master, first_moment, second_moment):
    n_seq = lax.axis_size("seq")
    n_dp = lax.axis_size("dp")
    seq_index = lax.axis_index("seq")
    dp_index = lax.axis_index("dp")
    core = seq_index % 2
    _, shard_len, width = block_input.shape
    rows = master.shape[0]
    per_owner = master.shape[1]
    chips = n_seq // 2
    sub = rows // n_dp
    wide = width // n_dp
    half = chips * sub
    head_cols = H // n_seq * HD
    seq_len = shard_len * n_seq
    ff_blocks = FF // D
    first_slots = min(4, per_owner)
    unit_count = owners.shape[0]

    unit_slot = unit_slots(owners, per_owner)
    place = unit_slot - owners * per_owner
    all_slots = jnp.arange(n_dp * per_owner, dtype=jnp.int32)
    match = unit_slot[None, :] == all_slots[:, None]
    slot_unit = jnp.sum(
        jnp.where(match, jnp.arange(unit_count, dtype=jnp.int32)[None, :] + 1, 0), axis=1
    ) - 1
    slot_unit = slot_unit.reshape(n_dp, per_owner)
    own_units = lax.dynamic_index_in_dim(slot_unit, dp_index, 0, keepdims=False)
    is_col = (own_units >= 4) & (own_units < 4 + 2 * ff_blocks)


    tokens = block_input.reshape(shard_len, width)
    packed = pack(master, is_col.astype(jnp.int32), n_dp, n_seq, first_slots)
    first_table, normed_one_all = front(packed[0], tokens, 2)
    first_table = first_table.reshape(n_dp * first_slots, rows, wide)
    normed_one_all = normed_one_all.reshape(seq_len, width)
    upstream = cotangent.reshape(shard_len, width)
    positions = jnp.arange(seq_len, dtype=jnp.int32)
    cosine, sine = rope_tables(seq_len, HD)
    doc_ends = jnp.cumsum(doc_lengths[0])
    doc = jnp.sum((positions[:, None] >= doc_ends[None, :]).astype(jnp.int32), axis=1)
    late_slots = per_owner - first_slots
    info = jnp.concatenate(
        [
            owners * first_slots + jnp.minimum(place, first_slots - 1),
            (owners * late_slots + jnp.maximum(place - first_slots, 0))[4:],
            (place >= first_slots)[4:],
        ]
    ).astype(jnp.int32)
    (
        qkv_weight,
        out_weight,
        queries,
        keys,
        values,
        attended_low,
        log_total,
        residual,
        up_weight,
        gate_weight,
        down_weight,
        normed_two_all,
    ) = forward(
        info,
        first_table,
        packed[1] if late_slots else None,
        normed_one_all,
        cosine,
        sine,
        doc,
        tokens,
        ff_blocks,
        first_slots,
        1,
    )
    qkv_weight = qkv_weight.reshape(width, 3 * head_cols)
    out_weight = out_weight.reshape(rows, width)
    normed_two, inv_two = norm_parts(residual)
    columns = ff_blocks * half
    up_weight = up_weight.reshape(width, columns)
    gate_weight = gate_weight.reshape(width, columns)
    down_weight = down_weight.reshape(columns, width)
    normed_two_all = normed_two_all.reshape(-1, width)
    ff_part, norm_two_part, down_grad, up_grad, gate_grad = feed_forward(
        normed_two_all, up_weight, gate_weight, down_weight, upstream, 7
    )
    side = (chips, 2, n_dp, sub, columns)
    sums = [
        down_grad.reshape(ff_blocks, chips, sub, width),
        up_grad.reshape(side),
        gate_grad.reshape(side),
    ]
    column = (2, n_dp, shard_len, width)
    bands = [(0, sub // 2), (sub // 2, sub // 2)] if sub % 32 == 0 else [(0, sub)]
    back = sum_grads(
        bands,
        slot_unit[:, first_slots:],
        residual,
        upstream,
        sums,
        [norm_two_part.reshape(column), ff_part.reshape(column)],
        5,
    )
    pieces = [back[2 * k : 2 * k + 2] for k in range(len(bands))]
    residual_grad, ff_out, residual_grad_all = back[2 * len(bands) : 2 * len(bands) + 3]
    residual_grad_all = residual_grad_all.reshape(seq_len, width)
    block_output = (residual + ff_out).astype(bf).reshape(block_input.shape)
    late_grads = []
    if late_slots:
        late_grads.append(back[2 * len(bands) + 3])
        for send_now in back[2 * len(bands) + 4 :]:
            send_now, residual_grad_all = lax.optimization_barrier((send_now, residual_grad_all))
            late_grads.append(lax.all_to_all(send_now, "dp", 0, 0))
    qkv_grad_low, qkv_wgrad, out_wgrad = attention_back(
        residual_grad_all,
        out_weight,
        queries,
        keys,
        values,
        attended_low,
        log_total,
        cosine,
        sine,
        doc,
        normed_one_all,
    )
    norm_one_part = jnp.einsum("tf,rf->tr", qkv_grad_low, qkv_weight, preferred_element_type=f32)
    norm_one_grad = sum_seq(norm_one_part.astype(bf).reshape(n_seq, shard_len, width), 3)
    qkv_piece, out_piece = collect_attention(
        qkv_wgrad.reshape(n_seq, n_dp, sub, 3 * head_cols), out_wgrad.reshape(n_dp, sub, width), 6
    )
    kinds = jnp.where(own_units < 0, 2, is_col.astype(jnp.int32)).astype(jnp.int32)
    kept = ()
    came = None
    for k, (begin, size) in enumerate(bands):
        rows_now = slice(begin, begin + size)
        attention = (qkv_piece[:, rows_now], out_piece[rows_now])
        send_now = arrange(slot_unit[:, :first_slots], *pieces[k], attention)
        if came is not None:
            send_now, came, norm_one_grad = lax.optimization_barrier(
                (send_now, came, norm_one_grad)
            )
        elif late_grads:
            send_now, late_grads[-1] = lax.optimization_barrier((send_now, late_grads[-1]))
        came = lax.all_to_all(send_now, "dp", 0, 0)
        kept = adam(
            kinds,
            [came] + late_grads[k : k + 1],
            master,
            first_moment,
            second_moment,
            n_dp,
            n_seq,
            first_slots,
            begin,
            kept,
        )
    owned_grads, new_first, new_second, new_master = kept
    tokens_again, norm_one_grad = lax.optimization_barrier((block_input, norm_one_grad))
    normed_one, inv_one = norm_parts(tokens_again.astype(f32).reshape(shard_len, width))
    input_grad = (residual_grad + norm_back(normed_one, inv_one, norm_one_grad)).reshape(
        block_input.shape
    )
    return (block_output, input_grad, owned_grads, new_first, new_second, new_master)


def solution(mesh):
    placed = (
        P("dp", "seq", None),
        P("dp", "seq", None),
        P("dp", None),
        P(),
        P("seq", "dp", None),
        P("seq", "dp", None),
        P("seq", "dp", None),
    )
    return jax.shard_map(
        local,
        mesh=mesh,
        in_specs=placed,
        out_specs=(
            P("dp", "seq", None),
            P("dp", "seq", None),
            P("seq", "dp", None),
            P("seq", "dp", None),
            P("seq", "dp", None),
            P("seq", "dp", None),
        ),
        check_vma=False,
    )
```

```python
import functools

import jax
import jax.numpy as jnp
import numpy as np
from jax import lax
from jax.experimental import pallas as pl
from jax.experimental.pallas import tpu as pltpu
from jax.sharding import PartitionSpec as P

D = 2048
H = 16
HD = 128
FF = 8192
STEP = 5
bf = jnp.bfloat16
f32 = jnp.float32
MESH = pl.DeviceIdType.MESH


norm_eps = 1e-05
rope_base = 10000.0
beta_one = 0.5
beta_two = 0.5
learn_rate = 0.01
decay_rate = 0.1
adam_eps = 1e-08
masked_score = -1000000000.0


def unit_slots(owners, per_owner):
    unit_count = owners.shape[0]
    unit_order = jnp.arange(unit_count, dtype=jnp.int32)
    matching = owners[:, None] == owners[None, :]
    before = unit_order[None, :] < unit_order[:, None]
    places = jnp.sum(jnp.where(matching & before, 1, 0), axis=1).astype(jnp.int32)
    return owners * per_owner + places


def norm_parts(values):
    center = values - jnp.mean(values, axis=-1, keepdims=True)
    spread = jnp.mean(center * center, axis=-1, keepdims=True)
    scale_inv = lax.rsqrt(spread + norm_eps)
    return (center * scale_inv, scale_inv)


def norm_back(normed, scale_inv, upstream):
    upstream_mean = jnp.mean(upstream, axis=-1, keepdims=True)
    cross_mean = jnp.mean(upstream * normed, axis=-1, keepdims=True)
    return scale_inv * (upstream - upstream_mean - normed * cross_mean)


def rope_tables(seq_len, head_dim):
    half_dim = head_dim // 2
    frequency = rope_base ** (-(np.arange(half_dim) * 2.0) / head_dim)
    angles = np.arange(seq_len)[:, None] * frequency[None, :]
    tables = [np.concatenate([half, half], axis=-1) for half in (np.cos(angles), np.sin(angles))]
    return [jnp.asarray(table.astype(np.float32)) for table in tables]


def pack_kernel(n_dp, chips, first_slots, flags, m_ref, *outs):
    rb, slots, width = m_ref.shape
    rows, wide = outs[0].shape[2:]
    sub = rows // n_dp
    start = pl.program_id(0) * rb
    target = start // sub
    inner = start % sub
    turned = jnp.swapaxes(m_ref[...], 0, 1).astype(bf)
    for s in range(slots):
        out = outs[0] if s < first_slots else outs[1]
        t = s if s < first_slots else s - first_slots
        x = turned[s]

        @pl.when(flags[s] == 1)
        def _():
            for d in range(n_dp):
                pieces = [
                    x[:, (2 * k + c) * rows + d * sub : (2 * k + c) * rows + (d + 1) * sub]
                    for c in range(2)
                    for k in range(chips)
                ]
                out[d, t, pl.ds(pl.multiple_of(start, rb), rb), :] = jnp.concatenate(pieces, axis=1)

        @pl.when(flags[s] == 0)
        def _():
            for g in range(n_dp):
                out[target, t, pl.ds(pl.multiple_of(g * sub + inner, rb), rb), :] = x[
                    :, g * wide : (g + 1) * wide
                ]


def pack(master, flags, n_dp, n_seq, first_slots):
    rows, slots, width = master.shape
    wide = width // n_dp
    rb = min(32, rows // n_dp)
    counts = [first_slots] + ([slots - first_slots] if slots > first_slots else [])
    return pl.pallas_call(
        functools.partial(pack_kernel, n_dp, n_seq // 2, first_slots),
        out_shape=[jax.ShapeDtypeStruct((n_dp, c, rows, wide), bf) for c in counts],
        grid_spec=pltpu.PrefetchScalarGridSpec(
            num_scalar_prefetch=1,
            grid=(rows // rb,),
            in_specs=[pl.BlockSpec((rb, slots, width), lambda i, f: (i, 0, 0))],
            out_specs=[
                pl.BlockSpec((n_dp, c, rows, wide), lambda i, f: (0, 0, 0, 0)) for c in counts
            ],
        ),
        compiler_params=pltpu.CompilerParams(vmem_limit_bytes=50 << 20),
        name="pack",
    )(flags, master)


def adam_kernel(n_dp, chips, first_slots, n_groups, n_kept, kinds, *refs):
    cols = refs[:n_groups]
    rws = refs[n_groups : 2 * n_groups]
    m_ref, f_ref, s_ref, keep_ref = refs[2 * n_groups : 2 * n_groups + 4]
    g_out, f_out, s_out, m_out, held = refs[2 * n_groups + 4 + n_kept :]
    rb, slots, width = m_ref.shape
    wide = width // n_dp
    rows = width // (2 * chips)
    sub = rows // n_dp
    half = chips * sub
    for s in range(slots):
        group = 0 if s < first_slots else 1
        t = s if group == 0 else s - first_slots

        @pl.when(kinds[s] == 1)
        def _():
            pieces = []
            for i in range(2 * chips):
                k, c = i // 2, i % 2
                for d in range(n_dp):
                    begin = c * half + k * sub
                    pieces.append(cols[group][d, t, :, begin : begin + sub])
            held[s] = jnp.concatenate(pieces, axis=1).astype(f32)

        @pl.when(kinds[s] == 0)
        def _():
            for g in range(n_dp):
                held[s, :, g * wide : (g + 1) * wide] = rws[group][0, t, g, :, :].astype(f32)

        @pl.when(kinds[s] == 2)
        def _():
            held[s] = jnp.zeros((rb, width), f32)

    grad = jnp.swapaxes(held[...], 0, 1)
    keep = keep_ref[...] > 0.0
    g_out[...] = grad
    first = jnp.where(keep, beta_one * f_ref[...] + (1.0 - beta_one) * grad, 0.0)
    f_out[...] = first
    second = jnp.where(keep, beta_two * s_ref[...] + (1.0 - beta_two) * grad * grad, 0.0)
    s_out[...] = second
    fixed_first = first * (1.0 / (1.0 - beta_one**STEP))
    fixed_second = second * (1.0 / (1.0 - beta_two**STEP))
    old = m_ref[...]
    root = fixed_second * lax.rsqrt(jnp.maximum(fixed_second, 1e-37))
    step = fixed_first * pl.reciprocal(root + adam_eps, approx=True) + decay_rate * old
    m_out[...] = jnp.where(keep, old - learn_rate * step, 0.0)


def adam(kinds, grads, master, first_moment, second_moment, n_dp, n_seq, first_slots, begin, kept):
    rows, slots, width = master.shape
    wide = width // n_dp
    sub = rows // n_dp
    size = grads[0].shape[2] // n_dp
    rb = min(16, size)
    steps = size // rb
    state = pl.BlockSpec(
        (rb, slots, width), lambda d, i, k: (d * (sub // rb) + begin // rb + i, 0, 0)
    )
    cols = [
        pl.BlockSpec((n_dp, g.shape[1], rb, wide), lambda d, i, k: (0, 0, d * steps + i, 0))
        for g in grads
    ]
    rws = [
        pl.BlockSpec((1, g.shape[1], n_dp, rb, wide), lambda d, i, k: (d, 0, 0, i, 0)) for g in grads
    ]
    keep = jnp.broadcast_to((kinds != 2).astype(f32)[None, :, None], (1, slots, width))
    first_kept = 1 + 2 * len(grads) + 4
    return pl.pallas_call(
        functools.partial(adam_kernel, n_dp, n_seq // 2, first_slots, len(grads), len(kept)),
        out_shape=[jax.ShapeDtypeStruct(master.shape, f32)] * 4,
        grid_spec=pltpu.PrefetchScalarGridSpec(
            num_scalar_prefetch=1,
            grid=(n_dp, steps),
            in_specs=cols
            + rws
            + [state] * 3
            + [pl.BlockSpec((1, slots, width), lambda d, i, k: (0, 0, 0))]
            + [pl.BlockSpec(memory_space=pl.ANY)] * len(kept),
            out_specs=[state] * 4,
            scratch_shapes=[pltpu.VMEM((slots, rb, width), f32)],
        ),
        input_output_aliases={first_kept + k: k for k in range(len(kept))},
        compiler_params=pltpu.CompilerParams(vmem_limit_bytes=50 << 20),
        cost_estimate=pl.CostEstimate(
            flops=0, bytes_accessed=int(150e6 * size / sub), transcendentals=0
        ),
        name="adam",
    )(
        kinds,
        *grads,
        *[g.reshape(n_dp, g.shape[1], n_dp, size, wide) for g in grads],
        master,
        first_moment,
        second_moment,
        keep,
        *kept,
    )


ANY = pl.BlockSpec(memory_space=pl.ANY)
VMEM = pl.BlockSpec(memory_space=pltpu.VMEM)
DMA = pltpu.SemaphoreType.DMA


def comm_params(collective_id, mib):
    return pltpu.CompilerParams(
        collective_id=collective_id, has_side_effects=True, vmem_limit_bytes=mib << 20
    )


def takes(microseconds):
    return pl.CostEstimate(flops=0, bytes_accessed=int(microseconds * 3e6), transcendentals=0)


def places():
    n_seq = lax.axis_size("seq")
    n_dp = lax.axis_size("dp")
    return n_seq, n_dp, lax.axis_index("seq"), lax.axis_index("dp")


def greet(devices):
    barrier = pltpu.get_barrier_semaphore()
    for device in devices:
        pl.semaphore_signal(barrier, inc=1, device_id=device, device_id_type=MESH)
    pl.semaphore_wait(barrier, len(devices))


def send(src, dst, send_sem, recv_sem, device):
    return pltpu.make_async_remote_copy(
        src_ref=src,
        dst_ref=dst,
        send_sem=send_sem,
        recv_sem=recv_sem,
        device_id=device,
        device_id_type=MESH,
    )


def relay_gather(views, place, count, device_of, send_sem, recv_sem, arrived, between=None, during=None):
    def leg(view, way, step, block, target):
        ref = views[view](block)
        return send(ref, ref, send_sem.at[view, way, step], recv_sem.at[view, way, step], device_of(target))

    def going(way, step):
        block = place - (step - 1) if way == 0 else place + (step - 1)
        target = place + 1 if way == 0 else place - 1
        inside = (block >= 0) & (block < count) & (target >= 0) & (target < count)
        return block, target, inside

    for step in range(1, count):
        for way in range(2):
            block, target, inside = going(way, step)

            @pl.when(inside)
            def _():
                for view in range(len(views)):
                    leg(view, way, step, block, target).start()

        if during:
            during(step)

        for way in range(2):
            block = place - step if way == 0 else place + step

            @pl.when((block >= 0) & (block < count))
            def _():
                for view in range(len(views)):
                    leg(view, way, step, block, lax.rem(place + 1, count)).wait_recv()
                arrived(block)

        if between:
            between(step)

    for step in range(1, count):
        for way in range(2):
            block, target, inside = going(way, step)

            @pl.when(inside)
            def _():
                for view in range(len(views)):
                    leg(view, way, step, block, target).wait_send()


def relay_sum(owns, sent, came, place, count, device_of, send_sem, recv_sem, ready, between=None):
    views = range(len(owns))

    def spot(way, block, receiver):
        return jnp.where(block == receiver, count, block) if way else block

    def leg(view, way, block, target, receiver):
        return send(
            sent[view].at[block],
            came[view].at[spot(way, block, receiver)],
            send_sem.at[view, way, block],
            recv_sem.at[view, way, block],
            device_of(target),
        )

    def going(way, step):
        block = count - 1 - step + place if way == 0 else step - (count - 1 - place)
        target = place + 1 if way == 0 else place - 1
        return block, target, (block < count if way == 0 else block >= 0)

    def behind(way):
        return place > 0 if way == 0 else place < count - 1

    for step in range(count - 1):
        for way in range(2):
            block, target, inside = going(way, step)

            @pl.when(inside)
            def _():
                ready(block)
                for view in views:

                    @pl.when(behind(way))
                    def _():
                        leg(view, way, block, target, place).wait_recv()
                        value = owns[view](block) + came[view][block].astype(f32)
                        sent[view][block] = value.astype(sent[view].dtype)

                    @pl.when(jnp.logical_not(behind(way)))
                    def _():
                        sent[view][block] = owns[view](block).astype(sent[view].dtype)

                    leg(view, way, block, target, target).start()

        if between:
            between(step)

    ready(place)
    for way in range(2):

        @pl.when(behind(way))
        def _():
            for view in views:
                leg(view, way, place, lax.rem(place + 1, count), place).wait_recv()

    totals = []
    for view in views:
        total = owns[view](place)
        for way in range(2):
            value = came[view][place if way == 0 else count].astype(f32)
            total = total + jnp.where(behind(way), value, 0.0)
        totals.append(total)
    for step in range(count - 1):
        for way in range(2):
            block, target, inside = going(way, step)

            @pl.when(inside)
            def _():
                for view in views:
                    leg(view, way, block, target, target).wait_send()

    return totals


def front_kernel(
    packed_ref, tokens_ref, table_ref, out_ref, x_ref, own_sem, a_send, a_recv, send_sem, recv_sem, pass_sem, take_sem
):
    n_seq, n_dp, seq_index, dp_index = places()
    chips, chip, core = n_seq // 2, seq_index // 2, lax.rem(seq_index, 2)
    dp_peers = [lax.rem(dp_index + k, n_dp) for k in range(n_dp)]
    chip_peers = [lax.rem(chip + k, chips) for k in range(chips)]
    sibling = (dp_index, chip * 2 + 1 - core)
    greet(
        [(p, seq_index) for p in dp_peers[1:]]
        + [(dp_index, p * 2 + core) for p in chip_peers[1:]]
        + [sibling]
    )
    along = []
    for k in range(1, n_dp):
        copy = send(
            packed_ref.at[dp_peers[k]],
            table_ref.at[dp_index],
            a_send.at[k],
            a_recv.at[k],
            (dp_peers[k], seq_index),
        )
        copy.start()
        along.append(copy)
    x_ref[...] = norm_parts(tokens_ref[...].astype(f32))[0].astype(bf)
    own = [
        pltpu.make_async_copy(packed_ref.at[dp_index], table_ref.at[dp_index], own_sem.at[0]),
        pltpu.make_async_copy(x_ref, out_ref.at[seq_index], own_sem.at[1]),
    ]
    for copy in own:
        copy.start()
    pass_on, finish = spread_blocks(
        x_ref, out_ref, chips, chip, core, dp_index, sibling, send_sem, recv_sem, pass_sem, take_sem
    )
    pass_on()
    finish()
    for copy in along:
        copy.wait()
    for copy in own:
        copy.wait()


def spread_blocks(
    x_ref, out_ref, chips, chip, core, dp_index, sibling, send_sem, recv_sem, pass_sem, take_sem
):
    mine = out_ref.at[chip * 2 + core]
    copies = {}
    for k in range(chips - 1, 0, -1):
        device = (dp_index, lax.rem(chip + k, chips) * 2 + core)
        copies[k] = send(x_ref, mine, send_sem.at[k], recv_sem.at[k], device)
        copies[k].start()
    passed = [send(x_ref, mine, pass_sem.at[0], take_sem.at[0], sibling)]
    passed[0].start()

    def pass_on():
        for k in range(1, chips):
            copies[k].wait_recv()
            block = out_ref.at[lax.rem(chip + chips - k, chips) * 2 + core]
            onward = send(block, block, pass_sem.at[k], take_sem.at[k], sibling)
            onward.start()
            passed.append(onward)

    def finish():
        for copy in copies.values():
            copy.wait_send()
        for onward in passed:
            onward.wait()

    return pass_on, finish


def front(packed, x, collective_id):
    chips = lax.axis_size("seq") // 2
    n_dp = lax.axis_size("dp")
    return pl.pallas_call(
        front_kernel,
        out_shape=[
            jax.ShapeDtypeStruct(packed.shape, packed.dtype),
            jax.ShapeDtypeStruct((2 * chips,) + x.shape, x.dtype),
        ],
        in_specs=[ANY, VMEM],
        out_specs=[ANY, ANY],
        scratch_shapes=[pltpu.VMEM(x.shape, bf), DMA((2,)), DMA((n_dp,)), DMA((n_dp,))]
        + [DMA((chips,))] * 4,
        compiler_params=comm_params(collective_id, 24),
        cost_estimate=takes(90),
        name="front",
    )(packed, x)


def sum_seq_kernel(x_ref, out_ref, taken, sent, arrived, pass_sem, take_sem, send_sem, recv_sem):
    n_seq, n_dp, seq_index, dp_index = places()
    chips, chip, core = n_seq // 2, seq_index // 2, lax.rem(seq_index, 2)
    peers = [lax.rem(chip + k, chips) for k in range(chips)]
    sibling = (dp_index, chip * 2 + 1 - core)
    greet([(dp_index, p * 2 + core) for p in peers[1:]] + [sibling])
    order = list(range(chips - 1, 0, -1)) + [0]
    passed = {}
    for k in order:
        block = x_ref.at[peers[k] * 2 + 1 - core]
        passed[k] = send(block, taken.at[k], pass_sem.at[k], take_sem.at[k], sibling)
        passed[k].start()
    copies = {}
    for k in order[:-1]:
        passed[k].wait_recv()
        own = x_ref[peers[k] * 2 + core].astype(f32)
        sent[k] = (own + taken[k].astype(f32)).astype(sent.dtype)
        device = (dp_index, peers[k] * 2 + core)
        copies[k] = send(sent.at[k], arrived.at[k], send_sem.at[k], recv_sem.at[k], device)
        copies[k].start()
    passed[0].wait_recv()
    total = x_ref[seq_index].astype(f32) + taken[0].astype(f32)
    for k in range(1, chips):
        copies[k].wait_recv()
        total = total + arrived[k].astype(f32)
    out_ref[...] = total
    for k in order:
        passed[k].wait_send()
    for k in order[:-1]:
        copies[k].wait_send()


def sum_seq(x, collective_id):
    blocks, rows, columns = x.shape
    chips = blocks // 2
    slots = pltpu.VMEM((chips, rows, columns), x.dtype)
    return pl.pallas_call(
        sum_seq_kernel,
        out_shape=jax.ShapeDtypeStruct((rows, columns), f32),
        in_specs=[VMEM],
        out_specs=VMEM,
        scratch_shapes=[slots, slots, slots] + [DMA((chips,))] * 4,
        compiler_params=comm_params(collective_id, 40),
        cost_estimate=takes(28),
        name="sum_seq",
    )(x)


def collect_kernel(
    qkv_ref, out_ref, qkv_sum, out_sum, qkv_sent, qkv_came, out_sent, out_came, total, own_sem,
    send_sem, recv_sem, a_send, a_recv
):
    n_seq, n_dp, seq_index, dp_index = places()
    seq_peers = [lax.rem(seq_index + k, n_seq) for k in range(n_seq)]
    greet(
        [(dp_index, p) for p in seq_peers[1:]]
        + [(lax.rem(dp_index + k, n_dp), seq_index) for k in range(1, n_dp)]
    )
    sums = relay_sum(
        [lambda block: qkv_ref[:, block].astype(f32), lambda block: out_ref[block].astype(f32)],
        [qkv_sent, out_sent],
        [qkv_came, out_came],
        dp_index,
        n_dp,
        lambda place: (place, seq_index),
        send_sem,
        recv_sem,
        lambda block: None,
    )
    total[...] = sums[0].astype(total.dtype)
    across = []
    for k in range(1, n_seq):
        copy = send(
            total.at[seq_peers[k]],
            qkv_sum.at[seq_index],
            a_send.at[k],
            a_recv.at[k],
            (dp_index, seq_peers[k]),
        )
        copy.start()
        across.append(copy)
    own = pltpu.make_async_copy(total.at[seq_index], qkv_sum.at[seq_index], own_sem)
    own.start()
    out_sum[...] = sums[1].astype(out_sum.dtype)
    for copy in across:
        copy.wait()
    own.wait()


def collect_attention(qkv, out, collective_id):
    n_seq = lax.axis_size("seq")
    n_dp = lax.axis_size("dp")
    tail = qkv.shape[2:]
    return pl.pallas_call(
        collect_kernel,
        out_shape=[
            jax.ShapeDtypeStruct((n_seq,) + tail, qkv.dtype),
            jax.ShapeDtypeStruct(out.shape[1:], out.dtype),
        ],
        in_specs=[VMEM, VMEM],
        out_specs=[VMEM, VMEM],
        scratch_shapes=[
            pltpu.VMEM((n_dp, n_seq) + tail, qkv.dtype),
            pltpu.VMEM((n_dp + 1, n_seq) + tail, qkv.dtype),
            pltpu.VMEM((n_dp,) + out.shape[1:], out.dtype),
            pltpu.VMEM((n_dp + 1,) + out.shape[1:], out.dtype),
            pltpu.VMEM((n_seq,) + tail, qkv.dtype),
            DMA,
            DMA((2, 2, n_dp)),
            DMA((2, 2, n_dp)),
            DMA((n_seq,)),
            DMA((n_seq,)),
        ],
        compiler_params=comm_params(collective_id, 48),
        cost_estimate=takes(75),
        name="collect_attention",
    )(qkv, out)


def ring_chip(place, chips):
    return jnp.where(place < chips // 2, 2 * place, 2 * (chips - 1 - place) + 1)


def ring_place(chip, chips):
    line = chip // 2
    return jnp.where(lax.rem(chip, 2) == 0, line, chips - 1 - line)


class Ring:
    def __init__(self, chips, chip, core, dp_index, send_sem, recv_sem):
        self.chips = chips
        self.place = ring_place(chip, chips)
        self.core = core
        self.dp_index = dp_index
        self.send_sem = send_sem
        self.recv_sem = recv_sem
        self.last = chips // 2

    def at(self, offset):
        return ring_chip(lax.rem(self.place + offset + self.chips, self.chips), self.chips)

    def device(self, way):
        return (self.dp_index, self.at(1 if way == 0 else -1) * 2 + self.core)

    def leg(self, view, way, step, src, dst):
        return send(
            src, dst, self.send_sem.at[view, way, step], self.recv_sem.at[view, way, step], self.device(way)
        )


def arrange_kernel(ff_blocks, units, ug_ref, down_ref, *refs):
    piece_ref = refs[-1]
    unit = units[pl.program_id(0)]
    rows, wide = piece_ref.shape[1:]
    sub, width = down_ref.shape[1:]
    groups = width // wide

    @pl.when((unit >= 4) & (unit < 4 + 2 * ff_blocks))
    def _():
        piece_ref[0] = ug_ref[0]

    @pl.when(unit >= 4 + 2 * ff_blocks)
    def _():
        for g in range(groups):
            piece_ref[0, g * sub : (g + 1) * sub, :] = down_ref[0, :, g * wide : (g + 1) * wide]

    if len(refs) == 3:
        qkv_ref, out_ref = refs[:2]
        blocks, _, columns = qkv_ref.shape
        step = columns // 3
        share = wide // step
        for u in range(3):

            @pl.when(unit == u)
            def _():
                for block in range(blocks):
                    g, h = block // share, block % share
                    piece_ref[0, g * sub : (g + 1) * sub, h * step : (h + 1) * step] = qkv_ref[
                        block, :, u * step : (u + 1) * step
                    ]

        @pl.when(unit == 3)
        def _():
            for g in range(groups):
                piece_ref[0, g * sub : (g + 1) * sub, :] = out_ref[:, g * wide : (g + 1) * wide]


def arrange(units, ug, down, attention):
    n_dp, slots = units.shape
    rows, wide = ug.shape[1:]
    sub, width = down.shape[1:]
    ff_blocks = down.shape[0]
    specs = [
        pl.BlockSpec(
            (1, rows, wide), lambda k, u: (jnp.clip(u[k] - 4, 0, 2 * ff_blocks - 1), 0, 0)
        ),
        pl.BlockSpec(
            (1, sub, width),
            lambda k, u: (jnp.clip(u[k] - 4 - 2 * ff_blocks, 0, ff_blocks - 1), 0, 0),
        ),
    ]
    if attention:
        specs.append(pl.BlockSpec(attention[0].shape, lambda k, u: (0, 0, 0)))
        specs.append(pl.BlockSpec(attention[1].shape, lambda k, u: (0, 0)))
    return pl.pallas_call(
        functools.partial(arrange_kernel, ff_blocks),
        out_shape=jax.ShapeDtypeStruct((n_dp * slots, rows, wide), bf),
        grid_spec=pltpu.PrefetchScalarGridSpec(
            num_scalar_prefetch=1,
            grid=(n_dp * slots,),
            in_specs=specs,
            out_specs=pl.BlockSpec((1, rows, wide), lambda k, u: (k, 0, 0)),
        ),
        compiler_params=pltpu.CompilerParams(vmem_limit_bytes=16 << 20),
        cost_estimate=takes(7),
        name="arrange",
    )(units.reshape(-1), ug, down, *attention).reshape(n_dp, slots, rows, wide)


def column_sums(refs, takens, sents, cames, send_sem, recv_sem, pass_sem, take_sem, between):
    n_seq, n_dp, seq_index, dp_index = places()
    core = lax.rem(seq_index, 2)
    sibling = (dp_index, seq_index + 1 - 2 * core)
    views = range(len(refs))

    def onward(view, block):
        return send(
            refs[view].at[1 - core, block],
            takens[view].at[block],
            pass_sem.at[view, block],
            take_sem.at[view, block],
            sibling,
        )

    for block in [b for k in range(n_dp // 2) for b in (n_dp - 1 - k, k)]:
        for view in views:
            onward(view, block).start()

    def ready(block):
        for view in views:
            onward(view, block).wait_recv()

    def own(view):
        return lambda block: refs[view][core, block].astype(f32) + takens[view][block].astype(f32)

    totals = relay_sum(
        [own(view) for view in views],
        sents,
        cames,
        dp_index,
        n_dp,
        lambda place: (place, seq_index),
        send_sem,
        recv_sem,
        ready,
        between,
    )
    for block in range(n_dp):
        for view in views:
            onward(view, block).wait_send()
    return totals


def ff_kernel(
    x_hbm, up_hbm, gate_hbm, down_hbm, cot_ref, ff_out, grad_out, down_grad, up_grad, gate_grad,
    x_ref, up_ref, gate_ref, down_ref, cot_all, hidden, up_low, gate_low, up_factor, gate_factor, stage, narrow, grad_stage,
    load_sem, grad_sem, stage_sem, narrow_sem, own_sem, send_sem, recv_sem, pass_sem, take_sem
):
    n_seq, n_dp, seq_index, dp_index = places()
    core = lax.rem(seq_index, 2)
    sibling = (dp_index, seq_index + 1 - 2 * core)
    loads = [
        pltpu.make_async_copy(src, dst, load_sem.at[k])
        for k, (src, dst) in enumerate(
            ((x_hbm, x_ref), (up_hbm, up_ref), (gate_hbm, gate_ref), (down_hbm, down_ref))
        )
    ]
    for load in loads:
        load.start()
    greet([(lax.rem(dp_index + k, n_dp), seq_index) for k in range(1, n_dp)] + [sibling])
    own = pltpu.make_async_copy(cot_ref, cot_all.at[core, dp_index], own_sem)
    own.start()
    own.wait()

    def onward(block):
        ref = cot_all.at[core, block]
        return send(ref, ref, pass_sem.at[block], take_sem.at[block], sibling)

    onward(dp_index).start()
    count, width = x_ref.shape
    columns = up_ref.shape[1]
    shard = cot_ref.shape[0]
    block_rows = 2 * shard
    blocks = count // block_rows

    def rows_of(b):
        return pl.ds(pl.multiple_of(b * block_rows, block_rows), block_rows)

    def times(left, right, left_axis, right_axis):
        return lax.dot_general(
            left, right, (((left_axis,), (right_axis,)), ((), ())), preferred_element_type=f32
        )

    def put(index, buffer, sem, value, dst):
        slot = lax.rem(index, 2)

        def copy(to):
            return pltpu.make_async_copy(buffer.at[slot], to, sem.at[slot])

        @pl.when(index >= 2)
        def _():
            copy(dst).wait()

        buffer[slot] = value
        copy(dst).start()

    def drain(buffer, sem, dst):
        for slot in range(2):
            pltpu.make_async_copy(buffer.at[slot], dst, sem.at[slot]).wait()

    def ahead(b, carry):
        at = rows_of(b)
        up = times(x_ref[at, :], up_ref[...], 1, 0)
        gate = times(x_ref[at, :], gate_ref[...], 1, 0)
        sig = jax.nn.sigmoid(gate)
        silu = gate * sig
        hidden[at, :] = (silu * up).astype(bf)
        up_factor[at, :] = silu
        gate_factor[at, :] = up * (sig + silu * (1.0 - sig))
        return carry

    def across(b, carry):
        at = rows_of(b)
        put(b, stage, stage_sem, times(hidden[at, :], down_ref[...], 1, 0).astype(bf), ff_out.at[at, :])
        return carry

    def back(place):
        ref = cot_all.at[1 - core, place]
        send(ref, ref, pass_sem.at[place], take_sem.at[place], sibling).wait_recv()
        lines = [
            pl.ds(pl.multiple_of((c * n_dp + place) * shard, shard), shard) for c in range(2)
        ]

        def both(source):
            return jnp.concatenate([source[line, :] for line in lines], axis=0)

        cot = jnp.concatenate([cot_all[c, place] for c in range(2)], axis=0)
        hidden_grad = times(cot, down_ref[...], 1, 1)
        up_part = (hidden_grad * both(up_factor)).astype(bf)
        gate_part = (hidden_grad * both(gate_factor)).astype(bf)
        value = times(up_part, up_ref[...], 1, 1) + times(gate_part, gate_ref[...], 1, 1)
        value = value.astype(bf)
        copies = []
        for c, line in enumerate(lines):
            up_low[line, :] = up_part[c * shard : (c + 1) * shard]
            gate_low[line, :] = gate_part[c * shard : (c + 1) * shard]
            grad_stage[c] = value[c * shard : (c + 1) * shard]
            copies.append(
                pltpu.make_async_copy(grad_stage.at[c], grad_out.at[line, :], grad_sem.at[c])
            )
            copies[c].start()
        for copy in copies:
            copy.wait()

    def back_at(distance):
        for place in (dp_index - distance, dp_index + distance):

            @pl.when((place >= 0) & (place < n_dp))
            def _():
                back(place)

    def work(step):
        if step == 1:
            for load in loads[:3]:
                load.wait()
            lax.fori_loop(0, blocks, ahead, 0)
            loads[3].wait()
        if step == 2 or n_dp == 2:
            back(dp_index)
        if step > 1:
            back_at(step - 1)
        if step == n_dp - 1:
            lax.fori_loop(0, blocks, across, 0)

    relay_gather(
        [lambda block: cot_all.at[core, block]],
        dp_index,
        n_dp,
        lambda place: (place, seq_index),
        send_sem,
        recv_sem,
        lambda block: onward(block).start(),
        during=work,
    )
    back_at(n_dp - 1)
    for block in range(n_dp):
        onward(block).wait_send()
    down_rows = min(256, columns)
    down_blocks = columns // down_rows
    cot_rows = cot_all[...].reshape(count, width)
    for b in range(down_blocks):
        at = slice(b * down_rows, (b + 1) * down_rows)
        value = times(hidden[:, at], cot_rows, 0, 0).astype(bf)
        put(b + blocks, stage.at[:, pl.ds(0, down_rows)], stage_sem, value, down_grad.at[at, :])
    side_blocks = width // 256
    for k, (low, out) in enumerate(((up_low, up_grad), (gate_low, gate_grad))):
        for b in range(side_blocks):
            at = slice(b * 256, (b + 1) * 256)
            value = times(x_ref[:, at], low[...], 0, 0).astype(bf)
            put(k * side_blocks + b, narrow, narrow_sem, value, out.at[at, :])
    drain(stage.at[:, pl.ds(0, down_rows)], stage_sem, down_grad.at[pl.ds(0, down_rows), :])
    drain(narrow, narrow_sem, gate_grad.at[pl.ds(0, 256), :])


def feed_forward(x, up, gate, down, cot, collective_id):
    n_dp = lax.axis_size("dp")
    count, width = x.shape
    columns = up.shape[1]
    shard = cot.shape[0]
    vmem = pltpu.VMEM
    low = lambda *shape: jax.ShapeDtypeStruct(shape, bf)
    return pl.pallas_call(
        ff_kernel,
        out_shape=[
            low(count, width),
            low(count, width),
            low(columns, width),
            low(width, columns),
            low(width, columns),
        ],
        in_specs=[ANY] * 4 + [VMEM],
        out_specs=[ANY] * 5,
        scratch_shapes=[
            vmem((count, width), bf),
            vmem((width, columns), bf),
            vmem((width, columns), bf),
            vmem((columns, width), bf),
            vmem((2, n_dp, shard, width), bf),
            vmem((count, columns), bf),
            vmem((count, columns), bf),
            vmem((count, columns), bf),
            vmem((count, columns), f32),
            vmem((count, columns), f32),
            vmem((2, 2 * shard, width), bf),
            vmem((2, 256, columns), bf),
            vmem((2, shard, width), bf),
            DMA((4,)),
            DMA((2,)),
            DMA((2,)),
            DMA((2,)),
            DMA,
            DMA((1, 2, n_dp)),
            DMA((1, 2, n_dp)),
            DMA((n_dp,)),
            DMA((n_dp,)),
        ],
        compiler_params=comm_params(collective_id, 58),
        cost_estimate=takes(60),
        name="feed_forward",
    )(x, up, gate, down, cot)


class BandSum:
    def __init__(self, band, owns, outs, scratch, chips, chip, core, dp_index, n_dp):
        self.begin, self.size = band
        self.owns, self.outs = owns, outs
        self.half_came, self.full_sent, self.full_came = scratch[0:3], scratch[3:6], scratch[6:9]
        self.mine, self.side_out = scratch[9:12], scratch[12]
        ring_send, ring_recv, self.side_send, self.side_recv, self.own_sem = scratch[13:]
        self.ring = Ring(chips, chip, core, dp_index, ring_send, ring_recv)
        self.chip, self.core, self.n_dp = chip, core, n_dp
        self.sibling = (dp_index, chip * 2 + 1 - core)
        self.blocks = outs[1].shape[0]
        self.pair = self.blocks // 2
        self.half = outs[0].shape[2] // 2

    def own(self, view, place, way):
        rows = pl.ds(self.begin, self.size)
        if view == 0:
            units = pl.ds(0, self.blocks) if way is None else pl.ds(way * self.pair, self.pair)
            return self.owns[0].at[units, place, rows, :]
        columns = pl.ds(0, self.blocks * self.half)
        if way is not None:
            columns = pl.ds(way * self.pair * self.half, self.pair * self.half)
        return self.owns[view].at[place, :, :, rows, columns]

    def leg(self, view, way, step):
        ring = self.ring
        if step == 0:
            src = self.own(view, ring.at(ring.last), way)
            return ring.leg(view, way, step, src, self.half_came[view].at[way])
        src = self.full_sent[view].at[step - 1, way]
        return ring.leg(view, way, step, src, self.full_came[view].at[step - 1, way])

    def own_copy(self, view, way, step):
        distance = self.ring.last - step
        if distance == 0:
            return pltpu.make_async_copy(
                self.own(view, self.chip, None), self.mine[view], self.own_sem.at[view, 0, step - 1]
            )
        src = self.own(view, self.ring.at(distance if way == 0 else -distance), None)
        return pltpu.make_async_copy(
            src, self.full_sent[view].at[step - 1, way], self.own_sem.at[view, way, step - 1]
        )

    def start(self):
        for view in range(3):
            for way in range(2):
                self.leg(view, way, 0).start()
        for step in range(1, self.ring.last + 1):
            for view in range(3):
                for way in range(2 if step < self.ring.last else 1):
                    self.own_copy(view, way, step).start()

    def steps(self):
        pair, half = self.pair, self.half
        for step in range(1, self.ring.last):
            for view in range(3):
                for way in range(2):
                    self.own_copy(view, way, step).wait()
                    self.leg(view, way, step - 1).wait_recv()
                    full = self.full_sent[view]
                    if step > 1:
                        value = full[step - 1, way].astype(f32)
                        value = value + self.full_came[view][step - 2, way].astype(f32)
                        full[step - 1, way] = value.astype(bf)
                    elif view == 0:
                        units = slice(way * pair, (way + 1) * pair)
                        value = full[0, way, units].astype(f32)
                        value = value + self.half_came[0][way].astype(f32)
                        full[0, way, units] = value.astype(bf)
                    else:
                        columns = slice(way * pair * half, (way + 1) * pair * half)
                        value = full[0, way, :, :, :, columns].astype(f32)
                        value = value + self.half_came[view][way].astype(f32)
                        full[0, way, :, :, :, columns] = value.astype(bf)
                    self.leg(view, way, step).start()

    def finish(self):
        ug_out, down_out = self.outs
        last, blocks, half = self.ring.last, self.blocks, self.half
        for view in range(3):
            self.own_copy(view, 0, last).wait()
            for way in range(2):
                self.leg(view, way, last - 1).wait_recv()
            if last > 1:
                came = [self.full_came[view][last - 2, way].astype(f32) for way in range(2)]
                value = self.mine[view][...].astype(f32) + came[0] + came[1]
            else:
                came = [self.half_came[view][way].astype(f32) for way in range(2)]
                other = jnp.concatenate(came, axis=0 if view == 0 else 3)
                value = self.mine[view][...].astype(f32) + other
            value = value.astype(bf)
            if view == 0:
                down_out[...] = value
                continue
            value = value.reshape(2, self.n_dp * self.size, blocks * half)
            for k in range(blocks):
                unit = (view - 1) * blocks + k

                @pl.when(self.core == 0)
                def _():
                    ug_out[unit, :, :half] = value[0, :, k * half : (k + 1) * half]
                    self.side_out[unit] = value[1, :, k * half : (k + 1) * half]

                @pl.when(self.core != 0)
                def _():
                    ug_out[unit, :, half:] = value[1, :, k * half : (k + 1) * half]
                    self.side_out[unit] = value[0, :, k * half : (k + 1) * half]

        place = pl.ds(pl.multiple_of(self.core * half, half), half)
        side = send(
            self.side_out, ug_out.at[:, :, place], self.side_send, self.side_recv, self.sibling
        )
        side.start()
        side.wait()

    def close(self):
        for step in range(self.ring.last):
            for view in range(3):
                for way in range(2):
                    self.leg(view, way, step).wait_send()


def grads_kernel(bands, late_slots, *refs):
    n_seq, n_dp, seq_index, dp_index = places()
    chips, chip, core = n_seq // 2, seq_index // 2, lax.rem(seq_index, 2)
    sibling = (dp_index, chip * 2 + 1 - core)
    refs = list(refs)

    def take(count):
        taken, refs[:count] = refs[:count], []
        return taken

    info, residual_ref, cot_ref = take(3)
    owns, x_refs = take(3), take(2)
    outs = [take(2) for _ in bands]
    grad_out, ff_out, tokens_out = take(3)
    late_out = take(1)[0] if late_slots else None
    next_out = take(len(bands) - 1) if late_slots else []
    scratch = [take(18) for _ in bands]
    takens, sents, cames = take(2), take(2), take(2)
    z_send, z_recv, x_pass, x_take = take(4)
    stage, token_own, token_send, token_recv, token_pass, token_take = take(6)
    greet(
        [(lax.rem(dp_index + k, n_dp), seq_index) for k in range(1, n_dp)]
        + [(dp_index, lax.rem(chip + k, chips) * 2 + core) for k in range(1, chips)]
        + [sibling]
    )
    sums = [
        BandSum(band, owns, out, memory, chips, chip, core, dp_index, n_dp)
        for band, out, memory in zip(bands, outs, scratch)
    ]
    sums[0].start()

    def between(step):
        if step == 0:
            sums[0].steps()
            for later in sums[1:]:
                later.start()
        if step == n_dp - 2:
            for later in sums[1:]:
                later.steps()

    norm_two_grad, ff_sum = column_sums(
        x_refs, takens, sents, cames, z_send, z_recv, x_pass, x_take, between
    )
    ff_out[...] = ff_sum
    residual = residual_ref[...]
    center = residual - jnp.mean(residual, axis=-1, keepdims=True)
    variance = jnp.mean(center * center, axis=-1, keepdims=True)
    scale_inv = lax.rsqrt(variance + norm_eps)
    grad = norm_back(center * scale_inv, scale_inv, norm_two_grad) + cot_ref[...].astype(f32)
    grad_out[...] = grad
    stage[...] = grad.astype(bf)
    own_tokens = pltpu.make_async_copy(stage, tokens_out.at[seq_index], token_own)
    own_tokens.start()
    pass_on, finish_tokens = spread_blocks(
        stage, tokens_out, chips, chip, core, dp_index, sibling,
        token_send, token_recv, token_pass, token_take,
    )
    sums[0].finish()
    def fill(pair, target_ref):
        ug_ref, down_ref = pair
        blocks, size, width = down_ref.shape
        wide = ug_ref.shape[2]
        for k in range(n_dp * late_slots):
            unit = info[k]
            is_down = unit >= 4 + 2 * blocks
            for g in range(n_dp):
                rows = slice(g * size, (g + 1) * size)
                value = ug_ref[jnp.clip(unit - 4, 0, 2 * blocks - 1), rows, :]
                other = down_ref[
                    jnp.clip(unit - 4 - 2 * blocks, 0, blocks - 1), :, g * wide : (g + 1) * wide
                ]
                use_other = jnp.full(value.shape, is_down.astype(jnp.int32), jnp.int32) != 0
                target_ref[k // late_slots, k % late_slots, rows, :] = jnp.where(
                    use_other, other, value
                )

    along = []
    if late_slots:
        late_stage, late_send, late_recv, late_own = take(4)
        fill(outs[0], late_stage)
        for k in range(1, n_dp):
            target = lax.rem(dp_index + k, n_dp)
            along.append(
                send(
                    late_stage.at[target],
                    late_out.at[dp_index],
                    late_send.at[k],
                    late_recv.at[k],
                    (target, seq_index),
                )
            )
        along.append(
            pltpu.make_async_copy(late_stage.at[dp_index], late_out.at[dp_index], late_own)
        )
        for copy in along:
            copy.start()
    pass_on()
    for k, later in enumerate(sums[1:]):
        later.finish()
        if late_slots:
            fill(outs[k + 1], next_out[k])
    for band in sums:
        band.close()
    own_tokens.wait()
    finish_tokens()
    for copy in along:
        copy.wait()


def sum_grads(bands, late_units, residual, cot, sums, xs, collective_id):
    _, n_dp, shard, width = xs[0].shape
    chips = lax.axis_size("seq") // 2
    steps = chips // 2
    vmem = pltpu.VMEM
    blocks = sums[0].shape[0]
    wide = sums[1].shape[-1]
    half = wide // blocks
    late_slots = late_units.shape[1]
    out_shape, out_specs, scratch = [], [], []
    for _, size in bands:
        out_shape += [
            jax.ShapeDtypeStruct((2 * blocks, n_dp * size, 2 * half), bf),
            jax.ShapeDtypeStruct((blocks, size, width), bf),
        ]
        out_specs += [VMEM] * 2
        side = (2, n_dp, size)
        fulls = [(blocks, size, width), side + (wide,), side + (wide,)]
        halves = [(blocks // 2, size, width), side + (wide // 2,), side + (wide // 2,)]
        scratch += [vmem((2,) + s, bf) for s in halves]
        scratch += [vmem((max(steps - 1, 1), 2) + s, bf) for s in fulls] * 2
        scratch += [vmem(s, bf) for s in fulls]
        scratch += [
            vmem((2 * blocks, n_dp * size, half), bf),
            DMA((3, 2, steps)),
            DMA((3, 2, steps)),
            DMA,
            DMA,
            DMA((3, 2, steps)),
        ]
    out_shape += [jax.ShapeDtypeStruct((shard, width), f32)] * 2
    out_shape.append(jax.ShapeDtypeStruct((2 * chips, shard, width), bf))
    out_specs += [VMEM, VMEM, ANY]
    scratch += [vmem((n_dp, shard, width), bf)] * 4
    scratch += [vmem((n_dp + 1, shard, width), bf)] * 2
    scratch += [DMA((2, 2, n_dp))] * 2 + [DMA((2, n_dp))] * 2
    scratch += [vmem((shard, width), bf), DMA] + [DMA((chips,))] * 4
    if late_slots:
        piece = (n_dp, late_slots, n_dp * bands[0][1], 2 * half)
        out_shape.append(jax.ShapeDtypeStruct(piece, bf))
        out_specs.append(ANY)
        out_shape += [jax.ShapeDtypeStruct(piece, bf)] * (len(bands) - 1)
        out_specs += [VMEM] * (len(bands) - 1)
        scratch += [vmem(piece, bf), DMA((n_dp,)), DMA((n_dp,)), DMA]
    return pl.pallas_call(
        functools.partial(grads_kernel, bands, late_slots),
        out_shape=out_shape,
        in_specs=[pl.BlockSpec(memory_space=pltpu.SMEM), VMEM, VMEM] + [ANY] * 3 + [VMEM] * 2,
        out_specs=out_specs,
        scratch_shapes=scratch,
        compiler_params=comm_params(collective_id, 60),
        cost_estimate=takes(130),
        name="sum_grads",
    )(late_units.reshape(-1) if late_slots else jnp.zeros((1,), jnp.int32), residual, cot, *sums, *xs)


def attention_back_kernel(
    grad_ref, weight_ref, query_ref, key_ref, value_ref, mixed_ref, stat_ref, cos_ref, sin_ref, doc_row, doc_col, x_ref,
    qkv_out, qkv_weight_out, out_weight_out, mixed_grad, key_sum, value_sum
):
    seq_len, width = grad_ref.shape
    head_cols = query_ref.shape[1]
    heads = head_cols // HD
    block_rows = min(256, seq_len)
    scale = float(HD) ** (-0.5)

    def rows_of(b):
        return pl.ds(pl.multiple_of(b * block_rows, block_rows), block_rows)

    def times(left, right, left_axis, right_axis):
        return lax.dot_general(
            left, right, (((left_axis,), (right_axis,)), ((), ())), preferred_element_type=f32
        )

    def mix(b, carry):
        at = rows_of(b)
        mixed_grad[at, :] = times(grad_ref[at, :], weight_ref[...], 1, 1).astype(bf)
        return carry

    lax.fori_loop(0, seq_len // block_rows, mix, 0)
    key_sum[...] = jnp.zeros_like(key_sum)
    value_sum[...] = jnp.zeros_like(value_sum)

    def turned(grads, cosine, sine):
        scaled = grads * sine
        half = HD // 2
        other = jnp.concatenate([scaled[:, half:], -scaled[:, :half]], axis=-1)
        return grads * cosine + other

    def attend(b, carry):
        at = rows_of(b)
        begin = b * block_rows
        query_pos = begin + lax.broadcasted_iota(jnp.int32, (block_rows, seq_len), 0)
        key_pos = lax.broadcasted_iota(jnp.int32, (block_rows, seq_len), 1)
        allowed = (doc_col[at, :] == doc_row[...]) & (key_pos <= query_pos)
        for h in range(heads):
            place = slice(h * HD, (h + 1) * HD)
            query, part = query_ref[at, place], mixed_grad[at, place]
            scores = jnp.where(allowed, times(query, key_ref[:, place], 1, 1) * scale, masked_score)
            prob = jnp.exp(scores - stat_ref[at, h * HD : h * HD + 1])
            prob_grad = times(part, value_ref[:, place], 1, 1)
            inner = jnp.sum(prob * prob_grad, axis=-1, keepdims=True)
            score_grad = (prob * (prob_grad - inner) * scale).astype(bf)
            value_sum[:, place] += times(prob.astype(bf), part, 0, 0)
            key_sum[:, place] += times(score_grad, query, 0, 0)
            query_grad = times(score_grad, key_ref[:, place], 1, 0)
            qkv_out[at, place] = turned(query_grad, cos_ref[at, :], sin_ref[at, :]).astype(bf)
        return carry

    lax.fori_loop(0, seq_len // block_rows, attend, 0)

    def finish(b, carry):
        at = rows_of(b)
        for h in range(heads):
            place = slice(h * HD, (h + 1) * HD)
            grads = turned(key_sum[at, place], cos_ref[at, :], sin_ref[at, :])
            qkv_out[at, head_cols + h * HD : head_cols + (h + 1) * HD] = grads.astype(bf)
        qkv_out[at, 2 * head_cols :] = value_sum[at, :].astype(bf)
        return carry

    lax.fori_loop(0, seq_len // block_rows, finish, 0)
    columns = min(512, width)
    for c in range(width // columns):
        at = slice(c * columns, (c + 1) * columns)
        qkv_weight_out[at, :] = times(x_ref[:, at], qkv_out[...], 0, 0).astype(bf)
        out_weight_out[:, at] = times(mixed_ref[...], grad_ref[:, at], 0, 0).astype(bf)


def attention_back(grad, weight, query, key, value, mixed, stat, cosine, sine, doc, x):
    seq_len, width = grad.shape
    head_cols = query.shape[1]
    return pl.pallas_call(
        attention_back_kernel,
        out_shape=[
            jax.ShapeDtypeStruct((seq_len, 3 * head_cols), bf),
            jax.ShapeDtypeStruct((width, 3 * head_cols), bf),
            jax.ShapeDtypeStruct((head_cols, width), bf),
        ],
        in_specs=[VMEM] * 12,
        out_specs=[VMEM] * 3,
        scratch_shapes=[
            pltpu.VMEM((seq_len, head_cols), bf),
            pltpu.VMEM((seq_len, head_cols), f32),
            pltpu.VMEM((seq_len, head_cols), f32),
        ],
        compiler_params=pltpu.CompilerParams(vmem_limit_bytes=50 << 20),
        cost_estimate=takes(35),
        name="attention_back",
    )(grad, weight, query, key, value, mixed, stat, cosine, sine, doc[None, :], doc[:, None], x)


def turn_half(values):
    half = values.shape[-1] // 2
    return jnp.concatenate([-values[:, half:], values[:, :half]], axis=-1)


def forward_kernel(has_late, first_slots, ff_blocks, *refs):
    info, first_ref = refs[:2]
    refs = refs[2:]
    if has_late:
        late_ref, refs = refs[0], refs[1:]
    x1_ref, cos_ref, sin_ref, doc_row, doc_col, tokens_ref = refs[:6]
    refs = (None,) + refs
    qkv_all, out_all, query_out, key_out, value_out, mixed_out, stat_out, residual_out = refs[7:15]
    up_all, gate_all, down_all, x_all = refs[15:19]
    ug_all = (up_all, gate_all)
    att_stage, out_stage, part, taken, sent, arrived, x_stage = refs[19:26]
    mine_stage, given_stage, down_stage = refs[26:29]
    (own_sem, a_send, a_recv, w_send, w_recv, s_pass, s_take, s_send, s_recv,
     late_send, late_recv, late_own, stage_own, side_send, side_recv, ring_send, ring_recv,
     send_sem, recv_sem, pass_sem, take_sem) = refs[29:50]
    late_tables = refs[50:-2]
    x1_hbm, x1_ref, x1_sem = x1_ref, refs[-2], refs[-1]
    x1_copy = pltpu.make_async_copy(x1_hbm, x1_ref, x1_sem)
    x1_copy.start()
    n_seq, n_dp, seq_index, dp_index = places()
    chips, chip, core = n_seq // 2, seq_index // 2, lax.rem(seq_index, 2)
    sibling = (dp_index, chip * 2 + 1 - core)
    seq_peers = [lax.rem(seq_index + k, n_seq) for k in range(n_seq)]
    dp_peers = [lax.rem(dp_index + k, n_dp) for k in range(n_dp)]
    rows, wide = first_ref.shape[1:]
    sub = rows // n_dp
    half = wide // 2
    step_cols = att_stage.shape[2] // 3
    share = wide // step_cols
    tokens, width = tokens_ref.shape
    greet([(dp_index, p) for p in seq_peers[1:]] + [(p, seq_index) for p in dp_peers[1:]])

    def band(c):
        return pl.ds(c * sub, sub)

    def late_copies(c):
        copies = []
        for k in range(1, n_dp):
            copies.append(
                send(
                    late_ref.at[dp_peers[k], :, band(c)],
                    late_tables[c].at[dp_index],
                    late_send.at[c, k],
                    late_recv.at[c, k],
                    (dp_peers[k], seq_index),
                )
            )
        return copies

    def late_own_copy(c):
        return pltpu.make_async_copy(
            late_ref.at[dp_index, :, band(c)], late_tables[c].at[dp_index], late_own.at[c]
        )

    def late_start(c):
        if not has_late or c >= n_dp:
            return
        if c and c < max(2, n_dp - 1):
            for copy in late_copies(c - 1):
                copy.wait_send()
        for copy in late_copies(c):
            copy.start()
        late_own_copy(c).start()

    late_start(0)

    for u in range(3):
        for block in range(n_seq):
            g, h = block // share, block % share
            att_stage[block, :, u * step_cols : (u + 1) * step_cols] = first_ref[
                info[u], g * sub : (g + 1) * sub, h * step_cols : (h + 1) * step_cols
            ]
    for g in range(n_dp):
        out_stage[:, g * wide : (g + 1) * wide] = first_ref[info[3], g * sub : (g + 1) * sub, :]
    own = [
        pltpu.make_async_copy(att_stage.at[seq_index], qkv_all.at[seq_index, dp_index], own_sem.at[0]),
        pltpu.make_async_copy(out_stage, out_all.at[dp_index], own_sem.at[1]),
    ]
    across = []
    for k in range(1, n_seq):
        copy = send(
            att_stage.at[seq_peers[k]],
            qkv_all.at[seq_index, dp_index],
            a_send.at[k],
            a_recv.at[k],
            (dp_index, seq_peers[k]),
        )
        copy.start()
        across.append(copy)
    for copy in own:
        copy.start()
    for copy in own:
        copy.wait()
    for copy in across:
        copy.wait_recv()
    relay_gather(
        [lambda block: qkv_all.at[:, block], lambda block: out_all.at[block]],
        dp_index,
        n_dp,
        lambda place: (place, seq_index),
        w_send,
        w_recv,
        lambda block: None,
    )

    ring = Ring(chips, chip, core, dp_index, None, None)
    pair = ff_blocks // 2

    def ring_leg(c, view, way, step, arriving):
        distance = step if arriving else step - 1
        block = ring.at(-distance if way == 0 else distance)
        units = pl.ds(way * pair, pair) if step == ring.last else pl.ds(0, ff_blocks)
        if view == 0:
            ref = down_all.at[units, block, :, pl.ds(c * wide, wide)]
        else:
            columns = pl.ds(0, ff_blocks * half)
            if step == ring.last:
                columns = pl.ds(way * pair * half, pair * half)
            ref = ug_all[view - 1].at[block, :, band(c), columns]
        return send(
            ref, ref, ring_send.at[c, view, way, step - 1], ring_recv.at[c, view, way, step - 1],
            ring.device(way),
        )

    def side_copies(c):
        return [
            send(
                given_stage.at[c, k],
                ug_all[k].at[chip, core, band(c)],
                side_send.at[c, k],
                side_recv.at[c, k],
                sibling,
            )
            for k in range(2)
        ]

    def begin_band(c):
        if has_late:
            for copy in late_copies(c):
                copy.wait_recv()
            late_own_copy(c).wait()
            if c and (c + 1 < n_dp - 1 or n_dp == 3):
                late_start(c + 1)
            if c and c + 1 == n_dp - 2:
                late_start(n_dp - 1)
            table = late_tables[c]
            late_slots = table.shape[1]
        for u in range(3 * ff_blocks):
            value = first_ref[info[4 + u], band(c), :]
            if has_late:
                code = info[4 + 3 * ff_blocks + u]
                other = table[code // late_slots, lax.rem(code, late_slots)]
                use_late = jnp.full(value.shape, info[4 + 6 * ff_blocks + u], jnp.int32) != 0
                value = jnp.where(use_late, other, value)
            if u < 2 * ff_blocks:
                left, right = value[:, :half], value[:, half:]
                k, j = u // ff_blocks, u % ff_blocks
                columns = slice(j * half, (j + 1) * half)

                @pl.when(core == 0)
                def _():
                    mine_stage[c, k, :, columns] = left
                    given_stage[c, k, :, columns] = right

                @pl.when(core != 0)
                def _():
                    mine_stage[c, k, :, columns] = right
                    given_stage[c, k, :, columns] = left
            else:
                down_stage[c, u - 2 * ff_blocks] = value
        for copy in side_copies(c):
            copy.start()
        local = [
            pltpu.make_async_copy(
                mine_stage.at[c, k], ug_all[k].at[chip, core, band(c)], stage_own.at[c, k]
            )
            for k in range(2)
        ]
        local.append(
            pltpu.make_async_copy(
                down_stage.at[c], down_all.at[:, chip, :, pl.ds(c * wide, wide)], stage_own.at[c, 2]
            )
        )
        for copy in local:
            copy.start()
        for copy in local:
            copy.wait()
        for copy in side_copies(c):
            copy.wait_recv()
        for view in range(3):
            for way in range(2):
                ring_leg(c, view, way, 1, False).start()

    def carry_band(c, step):
        for view in range(3):
            for way in range(2):
                ring_leg(c, view, way, step - 1, True).wait_recv()
                ring_leg(c, view, way, step, False).start()

    late_start(1)
    begin_band(0)

    x1_copy.wait()
    seq_len = x1_ref.shape[0]
    heads = query_out.shape[1] // HD
    block_rows = min(256, seq_len)
    head_cols = heads * HD
    qkv_weight = qkv_all[...].reshape(width, 3 * head_cols)

    def project(b, carry):
        at = pl.ds(pl.multiple_of(b * block_rows, block_rows), block_rows)
        result = jnp.dot(x1_ref[at, :], qkv_weight, preferred_element_type=f32)
        cosine, sine = cos_ref[at, :], sin_ref[at, :]
        for h in range(heads):
            place = slice(h * HD, (h + 1) * HD)
            for part_id, out in ((0, query_out), (1, key_out)):
                begin = part_id * head_cols + h * HD
                values = result[:, begin : begin + HD]
                out[at, place] = (values * cosine + turn_half(values) * sine).astype(bf)
        value_out[at, :] = result[:, 2 * head_cols :].astype(bf)
        return carry

    lax.fori_loop(0, seq_len // block_rows, project, 0)

    def attend(b, carry):
        begin = pl.multiple_of(b * block_rows, block_rows)
        at = pl.ds(begin, block_rows)
        query_pos = begin + lax.broadcasted_iota(jnp.int32, (block_rows, seq_len), 0)
        key_pos = lax.broadcasted_iota(jnp.int32, (block_rows, seq_len), 1)
        allowed = (doc_col[at, :] == doc_row[...]) & (key_pos <= query_pos)
        for h in range(heads):
            place = slice(h * HD, (h + 1) * HD)
            scores = lax.dot_general(
                query_out[at, place],
                key_out[:, place],
                (((1,), (1,)), ((), ())),
                preferred_element_type=f32,
            )
            scores = jnp.where(allowed, scores * (float(HD) ** (-0.5)), masked_score)
            peak = jnp.max(scores, axis=-1, keepdims=True)
            raised = jnp.exp(scores - peak)
            total = jnp.sum(raised, axis=-1, keepdims=True)
            prob = (raised * (1.0 / total)).astype(bf)
            mixed = jnp.dot(prob, value_out[:, place], preferred_element_type=f32)
            mixed_out[at, place] = mixed.astype(bf)
            stat_out[at, place] = jnp.broadcast_to(peak + jnp.log(total), (block_rows, HD))
        return carry

    lax.fori_loop(0, seq_len // block_rows, attend, 0)
    out_weight = out_all[...].reshape(rows, width)

    def combine(b, carry):
        at = pl.ds(pl.multiple_of(b * tokens, tokens), tokens)
        part[b] = jnp.dot(mixed_out[at, :], out_weight, preferred_element_type=f32).astype(bf)
        return carry

    lax.fori_loop(0, n_seq, combine, 0)

    chip_peers = [lax.rem(chip + k, chips) for k in range(chips)]
    order = list(range(chips - 1, 0, -1)) + [0]
    passed = {}
    for k in order:
        block = part.at[chip_peers[k] * 2 + 1 - core]
        passed[k] = send(block, taken.at[k], s_pass.at[k], s_take.at[k], sibling)
        passed[k].start()
    copies = {}
    for k in order[:-1]:
        passed[k].wait_recv()
        value = part[chip_peers[k] * 2 + core].astype(f32)
        sent[k] = (value + taken[k].astype(f32)).astype(bf)
        device = (dp_index, chip_peers[k] * 2 + core)
        copies[k] = send(sent.at[k], arrived.at[k], s_send.at[k], s_recv.at[k], device)
        copies[k].start()

    begin_band(1)
    for step in range(2, ring.last + 1):
        carry_band(0, step)
    passed[0].wait_recv()
    total = part[seq_index].astype(f32) + taken[0].astype(f32)
    for k in range(1, chips):
        copies[k].wait_recv()
        total = total + arrived[k].astype(f32)
    residual = tokens_ref[...].astype(f32) + total
    residual_out[...] = residual
    center = residual - jnp.mean(residual, axis=-1, keepdims=True)
    spread = jnp.mean(center * center, axis=-1, keepdims=True)
    x_stage[...] = (center * lax.rsqrt(spread + norm_eps)).astype(bf)
    for c in range(2, n_dp - 1):
        begin_band(c)
        for step in range(2, ring.last + 1):
            carry_band(c - 1, step)

    def last_band():
        begin_band(n_dp - 1)
        for step in range(2, ring.last + 1):
            carry_band(n_dp - 2, step)

    own_x = pltpu.make_async_copy(x_stage, x_all.at[core, dp_index], own_sem.at[3])
    own_x.start()
    own_x.wait()

    def onward(block):
        ref = x_all.at[core, block]
        return send(ref, ref, pass_sem.at[block], take_sem.at[block], sibling)

    onward(dp_index).start()
    relay_gather(
        [lambda block: x_all.at[core, block]],
        dp_index,
        n_dp,
        lambda place: (place, seq_index),
        send_sem,
        recv_sem,
        lambda block: onward(block).start(),
        lambda step: last_band() if step == 1 else None,
    )
    for step in range(2, ring.last + 1):
        carry_band(n_dp - 1, step)
    for c in range(n_dp):
        for view in range(3):
            for way in range(2):
                ring_leg(c, view, way, ring.last, True).wait_recv()
                for step in range(1, ring.last + 1):
                    ring_leg(c, view, way, step, False).wait_send()
        for copy in side_copies(c):
            copy.wait_send()
        if has_late:
            if c >= max(1, n_dp - 2):
                for copy in late_copies(c):
                    copy.wait_send()
    for block in range(n_dp):
        onward(block).wait_send()
        ref = x_all.at[1 - core, block]
        send(ref, ref, pass_sem.at[block], take_sem.at[block], sibling).wait_recv()
    for k in order:
        passed[k].wait_send()
    for k in order[:-1]:
        copies[k].wait_send()
    for copy in across:
        copy.wait_send()


def forward(info, first_table, late, x1, cosine, sine, doc, tokens, ff_blocks, first_slots, collective_id):
    n_seq = lax.axis_size("seq")
    n_dp = lax.axis_size("dp")
    chips = n_seq // 2
    rows, wide = first_table.shape[1:]
    sub = rows // n_dp
    half = wide // 2
    seq_len, width = x1.shape
    head_cols = width // n_seq
    shard = tokens.shape[0]
    steps = chips // 2
    vmem = pltpu.VMEM
    low = lambda *shape: jax.ShapeDtypeStruct(shape, bf)
    has_late = late is not None
    blocks = vmem((chips, shard, width), bf)
    return pl.pallas_call(
        functools.partial(forward_kernel, has_late, first_slots, ff_blocks),
        out_shape=[
            low(n_seq, n_dp, sub, 3 * head_cols),
            low(n_dp, sub, width),
            low(seq_len, head_cols),
            low(seq_len, head_cols),
            low(seq_len, head_cols),
            low(seq_len, head_cols),
            jax.ShapeDtypeStruct((seq_len, head_cols), f32),
            jax.ShapeDtypeStruct((shard, width), f32),
            low(chips, 2, rows, ff_blocks * half),
            low(chips, 2, rows, ff_blocks * half),
            low(ff_blocks, chips, sub, width),
            low(2, n_dp, shard, width),
        ],
        in_specs=[pl.BlockSpec(memory_space=pltpu.SMEM), VMEM]
        + [ANY] * has_late
        + [ANY]
        + [VMEM] * 5,
        out_specs=[VMEM] * 8 + [ANY] * 4,
        scratch_shapes=[
            vmem((n_seq, sub, 3 * head_cols), bf),
            vmem((sub, width), bf),
            vmem((n_seq, shard, width), bf),
            blocks,
            blocks,
            blocks,
            vmem((shard, width), bf),
            vmem((n_dp, 2, sub, ff_blocks * half), bf),
            vmem((n_dp, 2, sub, ff_blocks * half), bf),
            vmem((n_dp, ff_blocks, sub, wide), bf),
            DMA((4,)),
            DMA((n_seq,)),
            DMA((n_seq,)),
            DMA((2, 2, n_dp)),
            DMA((2, 2, n_dp)),
            DMA((chips,)),
            DMA((chips,)),
            DMA((chips,)),
            DMA((chips,)),
            DMA((n_dp, n_dp)),
            DMA((n_dp, n_dp)),
            DMA((n_dp,)),
            DMA((n_dp, 3)),
            DMA((n_dp, 2)),
            DMA((n_dp, 2)),
            DMA((n_dp, 3, 2, steps)),
            DMA((n_dp, 3, 2, steps)),
            DMA((1, 2, n_dp)),
            DMA((1, 2, n_dp)),
            DMA((n_dp,)),
            DMA((n_dp,)),
        ]
        + [vmem((n_dp, late.shape[1], sub, wide), bf) for _ in range(n_dp if has_late else 0)]
        + [vmem((seq_len, width), bf), DMA],
        compiler_params=comm_params(collective_id, 58),
        cost_estimate=takes(230),
        name="forward",
    )(
        info,
        first_table,
        *([late] if has_late else []),
        x1,
        cosine,
        sine,
        doc[None, :],
        doc[:, None],
        tokens,
    )


def local(block_input, cotangent, doc_lengths, owners, master, first_moment, second_moment):
    n_seq = lax.axis_size("seq")
    n_dp = lax.axis_size("dp")
    seq_index = lax.axis_index("seq")
    dp_index = lax.axis_index("dp")
    core = seq_index % 2
    _, shard_len, width = block_input.shape
    rows = master.shape[0]
    per_owner = master.shape[1]
    chips = n_seq // 2
    sub = rows // n_dp
    wide = width // n_dp
    half = chips * sub
    head_cols = H // n_seq * HD
    seq_len = shard_len * n_seq
    ff_blocks = FF // D
    first_slots = min(4, per_owner)
    unit_count = owners.shape[0]

    unit_slot = unit_slots(owners, per_owner)
    place = unit_slot - owners * per_owner
    all_slots = jnp.arange(n_dp * per_owner, dtype=jnp.int32)
    match = unit_slot[None, :] == all_slots[:, None]
    slot_unit = jnp.sum(
        jnp.where(match, jnp.arange(unit_count, dtype=jnp.int32)[None, :] + 1, 0), axis=1
    ) - 1
    slot_unit = slot_unit.reshape(n_dp, per_owner)
    own_units = lax.dynamic_index_in_dim(slot_unit, dp_index, 0, keepdims=False)
    is_col = (own_units >= 4) & (own_units < 4 + 2 * ff_blocks)


    tokens = block_input.reshape(shard_len, width)
    packed = pack(master, is_col.astype(jnp.int32), n_dp, n_seq, first_slots)
    first_table, normed_one_all = front(packed[0], tokens, 2)
    first_table = first_table.reshape(n_dp * first_slots, rows, wide)
    normed_one_all = normed_one_all.reshape(seq_len, width)
    upstream = cotangent.reshape(shard_len, width)
    positions = jnp.arange(seq_len, dtype=jnp.int32)
    cosine, sine = rope_tables(seq_len, HD)
    doc_ends = jnp.cumsum(doc_lengths[0])
    doc = jnp.sum((positions[:, None] >= doc_ends[None, :]).astype(jnp.int32), axis=1)
    late_slots = per_owner - first_slots
    info = jnp.concatenate(
        [
            owners * first_slots + jnp.minimum(place, first_slots - 1),
            (owners * late_slots + jnp.maximum(place - first_slots, 0))[4:],
            (place >= first_slots)[4:],
        ]
    ).astype(jnp.int32)
    (
        qkv_weight,
        out_weight,
        queries,
        keys,
        values,
        attended_low,
        log_total,
        residual,
        up_weight,
        gate_weight,
        down_weight,
        normed_two_all,
    ) = forward(
        info,
        first_table,
        packed[1] if late_slots else None,
        normed_one_all,
        cosine,
        sine,
        doc,
        tokens,
        ff_blocks,
        first_slots,
        1,
    )
    qkv_weight = qkv_weight.reshape(width, 3 * head_cols)
    out_weight = out_weight.reshape(rows, width)
    normed_two, inv_two = norm_parts(residual)
    columns = ff_blocks * half
    up_weight = up_weight.reshape(width, columns)
    gate_weight = gate_weight.reshape(width, columns)
    down_weight = down_weight.reshape(columns, width)
    normed_two_all = normed_two_all.reshape(-1, width)
    ff_part, norm_two_part, down_grad, up_grad, gate_grad = feed_forward(
        normed_two_all, up_weight, gate_weight, down_weight, upstream, 7
    )
    side = (chips, 2, n_dp, sub, columns)
    sums = [
        down_grad.reshape(ff_blocks, chips, sub, width),
        up_grad.reshape(side),
        gate_grad.reshape(side),
    ]
    column = (2, n_dp, shard_len, width)
    bands = [(0, sub // 2), (sub // 2, sub // 2)] if sub % 32 == 0 else [(0, sub)]
    back = sum_grads(
        bands,
        slot_unit[:, first_slots:],
        residual,
        upstream,
        sums,
        [norm_two_part.reshape(column), ff_part.reshape(column)],
        5,
    )
    pieces = [back[2 * k : 2 * k + 2] for k in range(len(bands))]
    residual_grad, ff_out, residual_grad_all = back[2 * len(bands) : 2 * len(bands) + 3]
    residual_grad_all = residual_grad_all.reshape(seq_len, width)
    block_output = (residual + ff_out).astype(bf).reshape(block_input.shape)
    late_grads = []
    if late_slots:
        late_grads.append(back[2 * len(bands) + 3])
        for send_now in back[2 * len(bands) + 4 :]:
            send_now, residual_grad_all = lax.optimization_barrier((send_now, residual_grad_all))
            late_grads.append(lax.all_to_all(send_now, "dp", 0, 0))
    qkv_grad_low, qkv_wgrad, out_wgrad = attention_back(
        residual_grad_all,
        out_weight,
        queries,
        keys,
        values,
        attended_low,
        log_total,
        cosine,
        sine,
        doc,
        normed_one_all,
    )
    norm_one_part = jnp.einsum("tf,rf->tr", qkv_grad_low, qkv_weight, preferred_element_type=f32)
    norm_one_grad = sum_seq(norm_one_part.astype(bf).reshape(n_seq, shard_len, width), 3)
    qkv_piece, out_piece = collect_attention(
        qkv_wgrad.reshape(n_seq, n_dp, sub, 3 * head_cols), out_wgrad.reshape(n_dp, sub, width), 6
    )
    kinds = jnp.where(own_units < 0, 2, is_col.astype(jnp.int32)).astype(jnp.int32)
    kept = ()
    came = None
    for k, (begin, size) in enumerate(bands):
        rows_now = slice(begin, begin + size)
        attention = (qkv_piece[:, rows_now], out_piece[rows_now])
        send_now = arrange(slot_unit[:, :first_slots], *pieces[k], attention)
        if came is not None:
            send_now, came, norm_one_grad = lax.optimization_barrier(
                (send_now, came, norm_one_grad)
            )
        elif late_grads:
            send_now, late_grads[-1] = lax.optimization_barrier((send_now, late_grads[-1]))
        came = lax.all_to_all(send_now, "dp", 0, 0)
        kept = adam(
            kinds,
            [came] + late_grads[k : k + 1],
            master,
            first_moment,
            second_moment,
            n_dp,
            n_seq,
            first_slots,
            begin,
            kept,
        )
    owned_grads, new_first, new_second, new_master = kept
    tokens_again, norm_one_grad = lax.optimization_barrier((block_input, norm_one_grad))
    normed_one, inv_one = norm_parts(tokens_again.astype(f32).reshape(shard_len, width))
    input_grad = (residual_grad + norm_back(normed_one, inv_one, norm_one_grad)).reshape(
        block_input.shape
    )
    return (block_output, input_grad, owned_grads, new_first, new_second, new_master)


def solution(mesh):
    placed = (
        P("dp", "seq", None),
        P("dp", "seq", None),
        P("dp", None),
        P(),
        P("seq", "dp", None),
        P("seq", "dp", None),
        P("seq", "dp", None),
    )
    return jax.shard_map(
        local,
        mesh=mesh,
        in_specs=placed,
        out_specs=(
            P("dp", "seq", None),
            P("dp", "seq", None),
            P("seq", "dp", None),
            P("seq", "dp", None),
            P("seq", "dp", None),
            P("seq", "dp", None),
        ),
        check_vma=False,
    )
```
